32 devices in a mesh: tm: 8 (over z, x), heads: 4 (over y, core).
Axes of the slice: x: 2, y: 2, z: 4, core: 2. Of those that a mesh axis runs over, the one named last changes fastest.
Arguments:
- slab_tokens: bfloat16 [4096, 3584], P('tm', 'heads'), may hold values from -14 to 14
- memory: bfloat16 [4096, 3584], P('tm', 'heads'), may hold values from -14 to 14
- query_weight: bfloat16 [3584, 3584], P(None, 'heads'), may hold values from -0.09375 to 0.09375
- key_weight: bfloat16 [3584, 512], P(None, 'heads'), may hold values from -0.09375 to 0.09375
- value_weight: bfloat16 [3584, 512], P(None, 'heads'), may hold values from -0.09375 to 0.09375
- query_down: bfloat16 [16, 3584], replicated, may hold values from -0.09375 to 0.09375
- query_up: bfloat16 [16, 3584], P(None, 'heads'), may hold values from -1.5 to 1.5
- value_down: bfloat16 [16, 3584], replicated, may hold values from -0.09375 to 0.09375
- value_up: bfloat16 [16, 512], P(None, 'heads'), may hold values from -1.5 to 1.5
- tag_weight: bfloat16 [3584, 8], P('heads'), may hold values from -0.75 to 0.75
- retrieval: int32 [32, 8], P('tm'), may hold values from 0 to 31, as said below
- boundary: int32 [32], P('tm'), may hold values from 0 to 127
- grad_tags: float32 [4096, 8], P('tm'), may hold values from -0.375 to 0.375
Outputs:
- tag_logits: float32 [4096, 8], P('tm')
- query_down_grad: float32 [16, 3584], P(None, 'heads')
- query_up_grad: float32 [16, 3584], P(None, 'heads')
- value_down_grad: float32 [16, 3584], P(None, 'heads')
- value_up_grad: float32 [16, 512], P(None, 'heads')
The draws below stay inside these ranges and needn't reach their ends.
Inputs may be any that keep to these rules, and one draw needn't show every extreme that they name: `retrieval`: each row names 8 different memory blocks; the rows of one index of tm name at most 1 different blocks held by any one index of tm.
All inputs are finite; a program needn't handle non-finite values.
Results may differ from the reference program's by a relative error of at most 0.035.
The reference program's roundings to bfloat16 on the way (of `queries`, `probs_low`, `attended`, `attended_grad`, `score_grad` and `query_grad`) count: a program that leaves them out, or rounds other values in their place, can miss the bound.
Values may be sent and summed in bfloat16 or wider, within the bound.
No kernel may reach another device: no remote copies, remote signals or barrier semaphores. Data moves between devices by JAX's collectives and lax.ppermute only.
A program may use at most 128 MiB of HBM per device.

```python
import jax
import jax.numpy as jnp
from jax import lax

D = 3584
HEADS = 28
KVH = 4
HD = 128
RANK = 16
TOP = 8
BLK = 128
CAP = 1
TAGS = 8
MB_DEV = 4
SPANS = 32
TOKENS = 4096
NMEM = 32
MEMTOK = 4096
N_TM = 8


def draw_slab_tokens(key, part):
    key = jax.random.fold_in(key, 11)
    first_key = jax.random.fold_in(key, 0)
    values = jax.random.normal(first_key, (TOKENS, D), jnp.float32)
    return jnp.clip(values, -14.0, 14.0).astype(jnp.bfloat16)


def draw_memory(key, part):
    key = jax.random.fold_in(key, 12)
    first_key = jax.random.fold_in(key, 0)
    values = jax.random.normal(first_key, (MEMTOK, D), jnp.float32)
    return jnp.clip(values, -14.0, 14.0).astype(jnp.bfloat16)


def draw_retrieval(key, part):
    key = jax.random.fold_in(key, 31)
    rank_key, noise_key, owner_key, offset_key = jax.random.split(key, 4)
    block_total = MB_DEV * N_TM
    per_device = SPANS // N_TM
    order = jax.random.permutation(rank_key, block_total)
    popular = 2 ** 15 // (order + 1)
    noise = jax.random.randint(noise_key, (SPANS, block_total), 0, 2 ** 17)
    span_ids = jnp.arange(SPANS, dtype=jnp.int32)[:, None]
    device_ids = span_ids // per_device
    first_span = span_ids % per_device == 0
    block_ids = jnp.arange(block_total, dtype=jnp.int32)[None, :]
    owners = block_ids // MB_DEV
    within = block_ids % MB_DEV
    offset_table = jax.random.randint(offset_key, (N_TM, N_TM), 0, MB_DEV)
    pair_offset = offset_table[device_ids, owners]
    allowed = (within - pair_offset) % MB_DEV < CAP
    offsets = jax.random.randint(owner_key, (N_TM,), 0, N_TM)
    forced_owner = (device_ids + jnp.take(offsets, device_ids)) % N_TM
    forced = first_span & (owners == forced_owner) & allowed
    scores = noise + popular[None, :] + forced.astype(jnp.int32) * 2 ** 18
    scores = jnp.where(allowed, scores * block_total + block_ids, -1 - block_ids)
    chosen = lax.top_k(scores, TOP)[1]
    return chosen.astype(jnp.int32)


def with_ends(result, key, least, largest):
    longest = result.shape.index(max(result.shape))
    spots = []
    for shift in (0, 1):
        where = [jax.random.randint(jax.random.fold_in(key, axis), (), 0, length) for axis, length in enumerate(result.shape)]
        where[longest] = (where[longest] + shift) % result.shape[longest]
        spots.append(tuple(where))
    return result.at[spots[0]].set(least).at[spots[1]].set(largest)


def levels(stream_key, extent, shards, smallest, high):
    level = 1.0
    for position, blocks in shards:
        steps = jax.random.uniform(jax.random.fold_in(jax.random.fold_in(stream_key, 6), position), (blocks,), jnp.float32, smallest / len(shards), high / len(shards))
        level = level * jnp.repeat(jnp.exp(steps), extent[position] // blocks).reshape((-1,) + (1,) * (len(extent) - 1 - position))
    return level


def centred(stream_key, shape, scale, most, cuts=(), kind=jnp.bfloat16):
    entries = scale * jax.random.normal(stream_key, shape, jnp.float32)
    if cuts:
        entries = entries * levels(stream_key, shape, cuts, -0.22, 0.18)
    return jnp.clip(entries, -most, most).astype(kind)


def setup_inputs(seed: int = 0) -> dict:
    keys = jax.random.split(jax.random.key(seed), 14)
    slab_tokens = draw_slab_tokens(jax.random.fold_in(keys[13], 71), 0)
    memory = draw_memory(jax.random.fold_in(keys[13], 71), 0)
    query_weight = centred(keys[2], (D, HEADS * HD), D ** -0.5, 0.09375, ((1, 4),))
    key_weight = centred(keys[3], (D, KVH * HD), D ** -0.5, 0.09375, ((1, 4),))
    value_weight = centred(keys[4], (D, KVH * HD), D ** -0.5, 0.09375, ((1, 4),))
    query_down = centred(keys[5], (RANK, D), D ** -0.5, 0.09375)
    query_up = centred(keys[6], (RANK, HEADS * HD), RANK ** -0.5, 1.5, ((1, 4),))
    value_down = centred(keys[7], (RANK, D), D ** -0.5, 0.09375)
    value_up = centred(keys[8], (RANK, KVH * HD), RANK ** -0.5, 1.5, ((1, 4),))
    tag_weight = centred(keys[9], (HEADS * HD, TAGS), 64 ** -0.5, 0.75, ((0, 4),))
    retrieval = draw_retrieval(jax.random.fold_in(keys[13], 71), 0)
    boundary = with_ends(jax.random.randint(keys[11], (SPANS,), 0, BLK), jax.random.fold_in(keys[11], 1), 0, BLK - 1).astype(jnp.int32)
    grad_tags = centred(keys[12], (TOKENS, TAGS), (4.0 / TOKENS ** 0.5), 0.375, ((0, 8),), jnp.float32)
    return dict(slab_tokens=slab_tokens, memory=memory, query_weight=query_weight, key_weight=key_weight, value_weight=value_weight, query_down=query_down, query_up=query_up, value_down=value_down, value_up=value_up, tag_weight=tag_weight, retrieval=retrieval, boundary=boundary, grad_tags=grad_tags)


HIGHEST = lax.Precision.HIGHEST


def attend(query, all_keys, all_values, split_row, out_grad):
    span_count, row_count, query_width = query.shape
    key_count, kv_width = all_keys.shape[1], all_keys.shape[2]
    kv_heads = kv_width // HD
    group_size = query_width // kv_width
    score_scale = HD ** -0.5
    query_heads = query.astype(jnp.float32).reshape(span_count, row_count, kv_heads, group_size, HD)
    key_heads = all_keys.astype(jnp.float32).reshape(span_count, key_count, kv_heads, HD)
    value_heads = all_values.astype(jnp.float32).reshape(span_count, key_count, kv_heads, HD)
    grad_heads = out_grad.astype(jnp.float32).reshape(span_count, row_count, kv_heads, group_size, HD)
    scores = jnp.einsum("crngd,cknd->cngrk", query_heads, key_heads, precision=HIGHEST) * score_scale
    row_ids = jnp.arange(row_count, dtype=jnp.int32)[:, None]
    col_ids = jnp.arange(BLK, dtype=jnp.int32)[None, :]
    edge_at = split_row[:, None, None]
    local_seen = (col_ids <= row_ids) & ((col_ids >= edge_at) | (row_ids < edge_at))
    visible = jnp.concatenate([jnp.ones((span_count, row_count, key_count - BLK), jnp.bool_), local_seen], axis=2)
    scores = jnp.where(visible[:, None, None], scores, -jnp.inf)
    row_max = jnp.max(scores, axis=-1, keepdims=True)
    weights = jnp.exp(scores - row_max)
    probs = weights / jnp.sum(weights, axis=-1, keepdims=True)
    probs_low = probs.astype(jnp.bfloat16).astype(jnp.float32)
    attended = jnp.einsum("cngrk,cknd->crngd", probs_low, value_heads, precision=HIGHEST).astype(jnp.bfloat16)
    prob_grad = jnp.einsum("crngd,cknd->cngrk", grad_heads, value_heads, precision=HIGHEST)
    row_dot = jnp.sum(grad_heads * attended.astype(jnp.float32), axis=-1)
    row_dot = jnp.transpose(row_dot, (0, 2, 3, 1))[..., None]
    score_grad = (probs * (prob_grad - row_dot) * score_scale).astype(jnp.bfloat16).astype(jnp.float32)
    query_grad = jnp.einsum("cngrk,cknd->crngd", score_grad, key_heads, precision=HIGHEST).astype(jnp.bfloat16)
    value_grad = jnp.einsum("cngrk,crngd->cknd", probs_low, grad_heads, precision=HIGHEST)
    return (attended.reshape(span_count, row_count, query_width),
            query_grad.reshape(span_count, row_count, query_width),
            value_grad.reshape(span_count, key_count, kv_width))


def reference(slab_tokens, memory, query_weight, key_weight, value_weight, query_down, query_up, value_down, value_up, tag_weight, retrieval, boundary, grad_tags):
    def project(left_side, right_side):
        return jnp.dot(left_side, right_side, preferred_element_type=jnp.float32)

    low_query = project(slab_tokens, query_down.T).astype(jnp.bfloat16)
    low_value = project(slab_tokens, value_down.T).astype(jnp.bfloat16)
    memory_low = project(memory, value_down.T).astype(jnp.bfloat16)
    queries = (project(slab_tokens, query_weight) + project(low_query, query_up)).astype(jnp.bfloat16)
    keys_local = project(slab_tokens, key_weight).astype(jnp.bfloat16)
    values_local = (project(slab_tokens, value_weight) + project(low_value, value_up)).astype(jnp.bfloat16)
    memory_keys = project(memory, key_weight).astype(jnp.bfloat16)
    memory_values = (project(memory, value_weight) + project(memory_low, value_up)).astype(jnp.bfloat16)
    kv_width = key_weight.shape[1]
    query_width = query_weight.shape[1]
    attended_grad = jnp.dot(grad_tags, tag_weight.astype(jnp.float32).T, precision=HIGHEST).astype(jnp.bfloat16)
    block_keys = memory_keys.reshape(NMEM, BLK, kv_width)
    block_values = memory_values.reshape(NMEM, BLK, kv_width)

    def span_step(memory_grad, inputs):
        query_block, key_block, value_block, grad_block, block_ids, split_row = inputs
        all_keys = jnp.concatenate([block_keys[block_ids].reshape(TOP * BLK, kv_width), key_block], 0)
        all_values = jnp.concatenate([block_values[block_ids].reshape(TOP * BLK, kv_width), value_block], 0)
        attended, query_grad, value_grad = attend(query_block[None], all_keys[None], all_values[None], split_row[None], grad_block[None])
        slot_grad = value_grad[0, :TOP * BLK].reshape(TOP, BLK, kv_width)
        memory_grad = memory_grad.at[block_ids].add(slot_grad)
        return memory_grad, (attended[0], query_grad[0], value_grad[0, TOP * BLK:])

    start_grad = jnp.zeros((NMEM, BLK, kv_width), jnp.float32)
    memory_grad, (attended, query_grad, local_grad) = lax.scan(
        span_step, start_grad,
        (queries.reshape(SPANS, BLK, query_width), keys_local.reshape(SPANS, BLK, kv_width),
         values_local.reshape(SPANS, BLK, kv_width), attended_grad.reshape(SPANS, BLK, query_width),
         retrieval, boundary))
    attended = attended.reshape(TOKENS, query_width)
    query_grad = query_grad.reshape(TOKENS, query_width)
    local_grad = local_grad.reshape(TOKENS, kv_width)
    memory_grad = memory_grad.reshape(MEMTOK, kv_width)
    tag_logits = project(attended, tag_weight)
    up_wide = value_up.astype(jnp.float32)
    query_low_grad = project(query_grad, query_up.T).astype(jnp.bfloat16)
    value_low_grad = jnp.dot(local_grad, up_wide.T, precision=HIGHEST).astype(jnp.bfloat16)
    memory_low_grad = jnp.dot(memory_grad, up_wide.T, precision=HIGHEST).astype(jnp.bfloat16)
    query_up_grad = project(low_query.T, query_grad)
    value_up_grad = (jnp.dot(low_value.astype(jnp.float32).T, local_grad, precision=HIGHEST)
                     + jnp.dot(memory_low.astype(jnp.float32).T, memory_grad, precision=HIGHEST))
    query_down_grad = project(query_low_grad.T, slab_tokens)
    value_down_grad = project(value_low_grad.T, slab_tokens) + project(memory_low_grad.T, memory)
    return tag_logits, query_down_grad, query_up_grad, value_down_grad, value_up_grad
```

```python
import jax
import jax.numpy as jnp
from jax import lax
from jax.experimental import pallas as pl
from jax.experimental.pallas import tpu as pltpu
from jax.sharding import PartitionSpec as P

HD = 128
RANK = 16
TOP = 8
BLK = 128
CAP = 1


HIGHEST = lax.Precision.HIGHEST


def attend(query, all_keys, all_values, split_row, out_grad):
    span_count, row_count, query_width = query.shape
    key_count, kv_width = (all_keys.shape[1], all_keys.shape[2])
    kv_heads = kv_width // HD
    group_size = query_width // kv_width
    score_scale = HD ** (-0.5)
    query_heads = query.reshape(span_count, row_count, kv_heads, group_size, HD)
    key_heads = all_keys.reshape(span_count, key_count, kv_heads, HD)
    value_heads = all_values.reshape(span_count, key_count, kv_heads, HD)
    grad_heads = out_grad.reshape(span_count, row_count, kv_heads, group_size, HD)
    scores = (
        jnp.einsum("crngd,cknd->cngrk", query_heads, key_heads, preferred_element_type=jnp.float32)
        * score_scale
    )
    row_ids = jnp.arange(row_count, dtype=jnp.int32)[:, None]
    col_ids = jnp.arange(BLK, dtype=jnp.int32)[None, :]
    edge_at = split_row[:, None, None]
    local_seen = (col_ids <= row_ids) & ((col_ids >= edge_at) | (row_ids < edge_at))
    visible = jnp.concatenate(
        [jnp.ones((span_count, row_count, key_count - BLK), jnp.bool_), local_seen], axis=2
    )
    scores = jnp.where(visible[:, None, None], scores, -jnp.inf)
    row_max = jnp.max(scores, axis=-1, keepdims=True)
    weights = jnp.exp(scores - row_max)
    probs = weights / jnp.sum(weights, axis=-1, keepdims=True)
    probs_low = probs.astype(jnp.bfloat16)
    attended = jnp.einsum(
        "cngrk,cknd->crngd", probs_low, value_heads, preferred_element_type=jnp.float32
    ).astype(jnp.bfloat16)
    prob_grad = jnp.einsum(
        "crngd,cknd->cngrk", grad_heads, value_heads, preferred_element_type=jnp.float32
    )
    row_dot = jnp.sum(grad_heads.astype(jnp.float32) * attended.astype(jnp.float32), axis=-1)
    row_dot = jnp.transpose(row_dot, (0, 2, 3, 1))[..., None]
    score_grad = (probs * (prob_grad - row_dot) * score_scale).astype(jnp.bfloat16)
    query_grad = jnp.einsum(
        "cngrk,cknd->crngd", score_grad, key_heads, preferred_element_type=jnp.float32
    ).astype(jnp.bfloat16)
    value_grad = jnp.einsum(
        "cngrk,crngd->cknd", probs_low, grad_heads, preferred_element_type=jnp.float32
    )
    return (
        attended.reshape(span_count, row_count, query_width),
        query_grad.reshape(span_count, row_count, query_width),
        value_grad.reshape(span_count, key_count, kv_width),
    )


def choose_slots(needed, places):
    slot_ids = jnp.arange(CAP, dtype=jnp.int32)
    return needed[:, None, :] * (places[:, None, :] == slot_ids[None, :, None]).astype(jnp.int32)


def general(
    slab_tokens,
    memory,
    query_weight,
    key_weight,
    value_weight,
    query_down,
    query_up,
    value_down,
    value_up,
    tag_weight,
    retrieval,
    boundary,
    grad_tags,
):
    tok_rows = slab_tokens.shape[0]
    mem_rows = memory.shape[0]
    query_width = query_weight.shape[1]
    kv_width = key_weight.shape[1]
    span_count = tok_rows // BLK
    block_count = mem_rows // BLK
    pair_weight = jnp.concatenate([key_weight, value_weight], 1)
    adapter_pair = jnp.concatenate([query_down, value_down], 0)
    contract_last = (((1,), (1,)), ((), ()))
    contract_first = (((0,), (0,)), ((), ()))
    token_piece = lax.all_gather(slab_tokens, "heads", axis=1, tiled=True)
    memory_piece = lax.all_gather(memory, "heads", axis=1, tiled=True)
    query_acc = jnp.dot(token_piece, query_weight, preferred_element_type=jnp.float32)
    pair_acc = jnp.dot(token_piece, pair_weight, preferred_element_type=jnp.float32)
    low_acc = lax.dot_general(
        token_piece, adapter_pair, contract_last, preferred_element_type=jnp.float32
    )
    memory_acc = jnp.dot(memory_piece, pair_weight, preferred_element_type=jnp.float32)
    memory_low_acc = lax.dot_general(
        memory_piece, adapter_pair[RANK:], contract_last, preferred_element_type=jnp.float32
    )
    query_acc, pair_acc, low_acc, memory_acc, memory_low_acc = (
        query_acc,
        pair_acc,
        low_acc,
        memory_acc,
        memory_low_acc,
    )
    low_tokens = low_acc.astype(jnp.bfloat16)
    low_query = low_tokens[:, :RANK]
    low_value = low_tokens[:, RANK:]
    queries = (query_acc + jnp.dot(low_query, query_up, preferred_element_type=jnp.float32)).astype(
        jnp.bfloat16
    )
    keys_local = pair_acc[:, :kv_width].astype(jnp.bfloat16)
    values_local = (
        pair_acc[:, kv_width:] + jnp.dot(low_value, value_up, preferred_element_type=jnp.float32)
    ).astype(jnp.bfloat16)
    memory_low = memory_low_acc.astype(jnp.bfloat16)
    memory_pair = (
        jnp.concatenate(
            [
                memory_acc[:, :kv_width],
                memory_acc[:, kv_width:]
                + jnp.dot(memory_low, value_up, preferred_element_type=jnp.float32),
            ],
            1,
        )
        .astype(jnp.bfloat16)
        .reshape(block_count, BLK, 2 * kv_width)
    )
    peer_count = lax.axis_size("tm")
    every_block = jnp.arange(peer_count * block_count, dtype=jnp.int32)
    wanted = (
        jnp.any(retrieval.reshape(-1, 1) == every_block[None, :], axis=0)
        .astype(jnp.int32)
        .reshape(peer_count, block_count)
    )
    places = jnp.cumsum(wanted, axis=1) - wanted
    requested = choose_slots(wanted, places)
    asked_for = lax.all_to_all(requested, "tm", split_axis=0, concat_axis=0, tiled=True)
    rows_needed = retrieval // block_count * CAP + jnp.take(places.reshape(-1), retrieval)
    asked_low = asked_for.astype(jnp.bfloat16)
    outgoing = jnp.einsum(
        "rcm,mbw->rcbw", asked_low, memory_pair, preferred_element_type=jnp.float32
    ).astype(jnp.bfloat16)
    fetched = lax.all_to_all(outgoing, "tm", split_axis=0, concat_axis=0, tiled=True)
    slot_rows = fetched.reshape(peer_count * CAP, BLK, 2 * kv_width)
    picked = jnp.take(slot_rows, rows_needed.reshape(-1), axis=0).reshape(
        span_count, TOP * BLK, 2 * kv_width
    )
    all_keys = jnp.concatenate(
        [picked[..., :kv_width], keys_local.reshape(span_count, BLK, kv_width)], 1
    )
    all_values = jnp.concatenate(
        [picked[..., kv_width:], values_local.reshape(span_count, BLK, kv_width)], 1
    )
    attended_grad = lax.dot_general(
        grad_tags, tag_weight.astype(jnp.float32), contract_last, precision=HIGHEST
    ).astype(jnp.bfloat16)
    attended, query_grad, value_grad = attend(
        queries.reshape(span_count, BLK, query_width),
        all_keys,
        all_values,
        boundary,
        attended_grad.reshape(span_count, BLK, query_width),
    )
    attended = attended.reshape(tok_rows, query_width)
    query_grad = query_grad.reshape(tok_rows, query_width)
    logits_out = lax.psum(
        jnp.dot(attended, tag_weight, preferred_element_type=jnp.float32), "heads"
    )
    local_grad = value_grad[:, TOP * BLK :].reshape(tok_rows, kv_width)
    slot_grads = value_grad[:, : TOP * BLK].reshape(span_count * TOP, BLK * kv_width)
    slot_hits = (
        rows_needed.reshape(-1, 1) == jnp.arange(peer_count * CAP, dtype=jnp.int32)[None, :]
    ).astype(jnp.float32)
    grad_buffer = lax.dot_general(slot_hits, slot_grads, contract_first, precision=HIGHEST).reshape(
        peer_count * CAP, BLK, kv_width
    )
    up_wide = value_up.astype(jnp.float32)
    returned = lax.all_to_all(
        grad_buffer.reshape(peer_count, CAP, BLK, kv_width),
        "tm",
        split_axis=0,
        concat_axis=0,
        tiled=True,
    )
    owned_grad = jnp.einsum(
        "rcm,rcbw->mbw", asked_for.astype(jnp.float32), returned, precision=HIGHEST
    ).reshape(mem_rows, kv_width)
    memory_cot = lax.dot_general(up_wide, owned_grad, contract_last, precision=HIGHEST)
    up_memory = lax.dot_general(
        memory_low.astype(jnp.float32), owned_grad, contract_first, precision=HIGHEST
    )
    query_cot = lax.dot_general(
        query_up, query_grad, contract_last, preferred_element_type=jnp.float32
    )
    value_cot = lax.dot_general(up_wide, local_grad, contract_last, precision=HIGHEST)
    query_cot, value_cot, memory_cot = lax.psum((query_cot, value_cot, memory_cot), "heads")
    query_down_grad = jnp.dot(
        query_cot.astype(jnp.bfloat16), slab_tokens, preferred_element_type=jnp.float32
    )
    value_down_grad = jnp.dot(
        value_cot.astype(jnp.bfloat16), slab_tokens, preferred_element_type=jnp.float32
    ) + jnp.dot(memory_cot.astype(jnp.bfloat16), memory, preferred_element_type=jnp.float32)
    query_up_grad = lax.dot_general(
        low_query, query_grad, contract_first, preferred_element_type=jnp.float32
    )
    value_up_grad = (
        lax.dot_general(
            low_value.astype(jnp.float32), local_grad, contract_first, precision=HIGHEST
        )
        + up_memory
    )
    query_down_grad, query_up_grad, value_down_grad, value_up_grad = lax.psum(
        (query_down_grad, query_up_grad, value_down_grad, value_up_grad), "tm"
    )
    return (logits_out, query_down_grad, query_up_grad, value_down_grad, value_up_grad)


LOG2E = 1.4426950408889634
NT = (((1,), (1,)), ((), ()))
PACK = 2 * BLK + RANK
VMEM_BYTES = 56 * 1024 * 1024


def dot_nt(a, b, precision=None):
    return lax.dot_general(a, b, NT, precision=precision, preferred_element_type=jnp.float32)


def dot_nn(a, b, precision=None):
    return jnp.dot(a, b, precision=precision, preferred_element_type=jnp.float32)


def memory_kernel(pieces, readers, place_ref, asked_ref, *refs):
    tokens = refs[: 4 * pieces]
    wk_ref, wv_ref, down_ref, up_ref, out_ref, pair_ref = refs[4 * pieces :]
    width = tokens[0].shape[1]
    rows = tokens[0].shape[0]
    for part in range(pieces):
        acc = None
        low = None
        for j in range(4):
            start = pl.multiple_of(lax.bitwise_xor(place_ref[0], j) * width, width)
            x = tokens[4 * part + j][...]
            w = jnp.concatenate([wk_ref[pl.ds(start, width), :], wv_ref[pl.ds(start, width), :]], 1)
            term = dot_nn(x, w)
            low_term = dot_nt(x, down_ref[:, pl.ds(start, width)])
            acc = term if acc is None else acc + term
            low = low_term if low is None else low + low_term
        low_b = low.astype(jnp.bfloat16)
        values = (acc[:, HD:] + dot_nn(low_b, up_ref[...])).astype(jnp.bfloat16)
        keys = acc[:, :HD].astype(jnp.bfloat16)
        low_t = jnp.transpose(low).astype(jnp.bfloat16)
        for b in range(rows // BLK):
            m = part * (rows // BLK) + b
            pair_ref[m, 0:BLK, :] = keys[b * BLK : (b + 1) * BLK]
            pair_ref[m, BLK : 2 * BLK, :] = values[b * BLK : (b + 1) * BLK]
            pair_ref[m, 2 * BLK : PACK, :] = low_t[:, b * BLK : (b + 1) * BLK]
    for r in range(readers):
        out_ref[r] = pair_ref[asked_ref[r]]


def span_kernel(spans, owners, heads, place_ref, bound_ref, x0, x1, x2, x3, wq_hbm, wk_hbm, wv_hbm, qd_hbm, vd_hbm,
                qup_ref, vup_ref, tag_ref, grad_ref, grad_t_ref, got_ref, mcot_in, qg_in, vg_in,
                cot_ref, mcot_ref, qg_ref, vg_ref,
                wq_s, wkv_s, wv_s, qd_s, vd_s, q_s, k_own, v_own, low_s, k_all, v_all, p_s, att_s, dq_s, dv_s, sems):
    width = x0.shape[1]
    tokens = (x0, x1, x2, x3)
    copies = []
    for j in range(4):
        start = pl.multiple_of(lax.bitwise_xor(place_ref[0], j) * width, width)
        here = pl.ds(start, width)
        group = [
            pltpu.make_async_copy(wq_hbm.at[here, :], wq_s.at[j], sems.at[j, 0]),
            pltpu.make_async_copy(wk_hbm.at[here, :], wkv_s.at[j], sems.at[j, 1]),
            pltpu.make_async_copy(wv_hbm.at[here, :], wv_s.at[j], sems.at[j, 2]),
            pltpu.make_async_copy(qd_hbm.at[:, here], qd_s.at[j], sems.at[j, 3]),
            pltpu.make_async_copy(vd_hbm.at[:, here], vd_s.at[j], sems.at[j, 4]),
        ]
        for c in group:
            c.start()
        copies.append(group)
    for b in range(owners):
        k_all[b * BLK : (b + 1) * BLK, :] = got_ref[b, 0:BLK, :]
        v_all[b * BLK : (b + 1) * BLK, :] = got_ref[b, BLK : 2 * BLK, :]
    q_acc = None
    for j in range(4):
        for c in copies[j]:
            c.wait()
        x = tokens[j][...]
        q_term = dot_nn(x, wq_s[j])
        kv_term = dot_nn(x, jnp.concatenate([wkv_s[j], wv_s[j]], 1))
        low_term = dot_nt(x, jnp.concatenate([qd_s[j], vd_s[j]], 0))
        if q_acc is None:
            q_acc, kv_acc, low_acc = q_term, kv_term, low_term
        else:
            q_acc, kv_acc, low_acc = q_acc + q_term, kv_acc + kv_term, low_acc + low_term
    low = low_acc.astype(jnp.bfloat16)
    q_s[...] = (q_acc + dot_nn(low[:, :RANK], qup_ref[...])).astype(jnp.bfloat16)
    k_own[...] = kv_acc[:, :HD].astype(jnp.bfloat16)
    v_own[...] = (kv_acc[:, HD:] + dot_nn(low[:, RANK:], vup_ref[...])).astype(jnp.bfloat16)
    low_s[...] = jnp.transpose(low_acc).astype(jnp.bfloat16)
    dv_s[...] = jnp.zeros_like(dv_s)
    qg_ref[...] = qg_in[...]
    vg_ref[...] = vg_in[...]
    seen = owners * BLK
    scale = HD ** (-0.5)
    up_wide = vup_ref[...].astype(jnp.float32)

    def span_step(c, carry):
        first = pl.multiple_of(c * BLK, BLK)
        rows = pl.ds(first, BLK)
        k_all[seen:, :] = k_own[rows, :]
        v_all[seen:, :] = v_own[rows, :]
        edge = bound_ref[c]
        row_ids = lax.broadcasted_iota(jnp.int32, (BLK, BLK), 0)
        col_ids = lax.broadcasted_iota(jnp.int32, (BLK, BLK), 1)
        visible = (col_ids <= row_ids) & ((col_ids >= edge) | (row_ids < edge))
        keys = k_all[...]
        values = v_all[...]
        for h in range(heads):
            cols = slice(h * HD, (h + 1) * HD)
            g = grad_ref[rows, cols]
            s = dot_nt(q_s[rows, cols], keys)
            s = jnp.concatenate([s[:, :seen], jnp.where(visible, s[:, seen:], -jnp.inf)], 1)
            top = jnp.max(s, axis=1, keepdims=True)
            w = jnp.exp2((s - top) * (scale * LOG2E))
            probs = w * (1.0 / jnp.sum(w, axis=1, keepdims=True))
            probs_low = probs.astype(jnp.bfloat16)
            att = dot_nn(probs_low, values).astype(jnp.bfloat16)
            dp = dot_nt(g, values)
            dot = jnp.sum(g.astype(jnp.float32) * att.astype(jnp.float32), axis=1, keepdims=True)
            ds = (probs * ((dp - dot) * scale)).astype(jnp.bfloat16)
            dq_s[:, cols] = dot_nn(ds, keys).astype(jnp.bfloat16)
            att_s[:, cols] = att
            p_s[h * BLK : (h + 1) * BLK, :] = probs_low
        g_t = jnp.concatenate([grad_t_ref[h * HD : (h + 1) * HD, rows] for h in range(heads)], 1)
        dv = dot_nn(g_t, p_s[...])
        dv_s[...] += dv[:, :seen]
        dv_own = dv[:, seen:]
        low_v = low_s[RANK:, rows].astype(jnp.float32)
        dq = dq_s[...]
        cot_ref[0:RANK, rows] = dot_nt(qup_ref[...], dq)
        cot_ref[RANK : 2 * RANK, rows] = dot_nn(up_wide, dv_own, HIGHEST)
        cot_ref[2 * RANK :, rows] = dot_nt(tag_ref[...], att_s[...])
        qg_ref[...] += dot_nn(low_s[0:RANK, rows], dq)
        vg_ref[...] += dot_nt(low_v, dv_own, HIGHEST)
        return carry

    lax.fori_loop(0, spans, span_step, 0)
    dv = dv_s[...]
    mcot = dot_nn(up_wide, dv, HIGHEST)
    low_m = jnp.concatenate([got_ref[b, 2 * BLK : PACK, :] for b in range(owners)], 1).astype(jnp.float32)
    vg_ref[...] += dot_nt(low_m, dv, HIGHEST)
    for b in range(owners):
        mcot_ref[b] = mcot_in[b] + mcot[:, b * BLK : (b + 1) * BLK]


def swap(x, bit):
    return lax.ppermute(x, "heads", [(i, i ^ bit) for i in range(4)])


def gather_parts(x):
    far = swap(x, 2)
    near = swap(x, 1)
    return x, near, far, swap(far, 1)


def heads_sum(x):
    x = x + swap(x, 1)
    return x + swap(x, 2)


def smem():
    return pl.BlockSpec(memory_space=pltpu.SMEM)


def vmem():
    return pl.BlockSpec(memory_space=pltpu.VMEM)


def fast(
    slab_tokens,
    memory,
    query_weight,
    key_weight,
    value_weight,
    query_down,
    query_up,
    value_down,
    value_up,
    tag_weight,
    retrieval,
    boundary,
    grad_tags,
):
    tok_rows, width = slab_tokens.shape
    mem_rows = memory.shape[0]
    query_width = query_weight.shape[1]
    heads = query_width // HD
    spans = tok_rows // BLK
    blocks = mem_rows // BLK
    peers = lax.axis_size("tm")
    f32 = jnp.float32
    bf16 = jnp.bfloat16
    mem_cuts, tok_cuts = 2, 2

    mem_parts = [gather_parts(m) for m in jnp.split(memory, mem_cuts, 0)]
    tok_parts = [gather_parts(x) for x in jnp.split(slab_tokens, tok_cuts, 0)]

    named = retrieval[0]
    owner_ids = jnp.arange(peers, dtype=jnp.int32)
    wanted = jnp.sum(
        jnp.where(named[None, :] // blocks == owner_ids[:, None], named[None, :] % blocks, 0), axis=1
    ).astype(jnp.int32)
    asked = lax.all_to_all(wanted, "tm", split_axis=0, concat_axis=0, tiled=True)
    place = lax.axis_index("heads").astype(jnp.int32).reshape(1)

    tag_t = tag_weight.T
    wide_tag = tag_t.astype(f32)
    grad_t = lax.dot_general(
        wide_tag, grad_tags, (((0,), (1,)), ((), ())), precision=HIGHEST
    ).astype(bf16)
    grad = lax.dot_general(grad_tags, wide_tag, (((1,), (0,)), ((), ())), precision=HIGHEST).astype(bf16)

    outgoing = pl.pallas_call(
        lambda *refs: memory_kernel(mem_cuts, peers, *refs),
        out_shape=jax.ShapeDtypeStruct((peers, PACK, HD), bf16),
        in_specs=[smem(), smem()] + [vmem()] * (4 * mem_cuts + 4),
        out_specs=vmem(),
        scratch_shapes=[pltpu.VMEM((blocks, PACK, HD), bf16)],
        compiler_params=pltpu.CompilerParams(vmem_limit_bytes=VMEM_BYTES),
        name="memory_pairs",
    )(place, asked, *[p for part in mem_parts for p in part], key_weight, value_weight, value_down, value_up)
    got = lax.all_to_all(outgoing, "tm", split_axis=0, concat_axis=0, tiled=True)

    rows = tok_rows // tok_cuts
    cut_spans = spans // tok_cuts
    seen = peers * BLK
    mcot = jnp.zeros((peers, RANK, BLK), f32)
    query_up_grad = jnp.zeros((RANK, query_width), f32)
    value_up_grad = jnp.zeros((RANK, HD), f32)
    cots = []
    anywhere = pl.BlockSpec(memory_space=pl.ANY)
    call = pl.pallas_call(
        lambda *refs: span_kernel(cut_spans, peers, heads, *refs),
        out_shape=(
            jax.ShapeDtypeStruct((2 * RANK + tag_t.shape[0], rows), f32),
            jax.ShapeDtypeStruct((peers, RANK, BLK), f32),
            jax.ShapeDtypeStruct((RANK, query_width), f32),
            jax.ShapeDtypeStruct((RANK, HD), f32),
        ),
        in_specs=[smem(), smem()] + [vmem()] * 4 + [anywhere] * 5 + [vmem()] * 9,
        out_specs=(vmem(),) * 4,
        scratch_shapes=[
            pltpu.VMEM((4, width, query_width), bf16),
            pltpu.VMEM((4, width, HD), bf16),
            pltpu.VMEM((4, width, HD), bf16),
            pltpu.VMEM((4, RANK, width), bf16),
            pltpu.VMEM((4, RANK, width), bf16),
            pltpu.VMEM((rows, query_width), bf16),
            pltpu.VMEM((rows, HD), bf16),
            pltpu.VMEM((rows, HD), bf16),
            pltpu.VMEM((2 * RANK, rows), bf16),
            pltpu.VMEM((seen + BLK, HD), bf16),
            pltpu.VMEM((seen + BLK, HD), bf16),
            pltpu.VMEM((heads * BLK, seen + BLK), bf16),
            pltpu.VMEM((BLK, query_width), bf16),
            pltpu.VMEM((BLK, query_width), bf16),
            pltpu.VMEM((HD, seen), f32),
            pltpu.SemaphoreType.DMA((4, 5)),
        ],
        compiler_params=pltpu.CompilerParams(vmem_limit_bytes=VMEM_BYTES),
        name="span_attention",
    )
    for t in range(tok_cuts):
        cut = slice(t * rows, (t + 1) * rows)
        cot, mcot, query_up_grad, value_up_grad = call(
            place, boundary[t * cut_spans : (t + 1) * cut_spans], *tok_parts[t],
            query_weight, key_weight, value_weight, query_down, value_down,
            query_up, value_up, tag_t, grad[cut], grad_t[:, cut], got, mcot, query_up_grad, value_up_grad,
        )
        cots.append(cot)
    cot = heads_sum(jnp.concatenate(cots, 1))
    logits = cot[2 * RANK :].T
    back = lax.all_to_all(mcot, "tm", split_axis=0, concat_axis=0, tiled=True)
    block_ids = jnp.arange(blocks, dtype=jnp.int32)
    hits = (asked[:, None] == block_ids[None, :])[:, :, None, None]
    owned = jnp.sum(jnp.where(hits, back[:, None], 0.0), axis=0)
    owned = heads_sum(owned)
    owned = jnp.transpose(owned, (1, 0, 2)).reshape(RANK, mem_rows)
    query_down_grad = jnp.dot(cot[:RANK].astype(bf16), slab_tokens, preferred_element_type=f32)
    value_down_grad = jnp.dot(
        cot[RANK : 2 * RANK].astype(bf16), slab_tokens, preferred_element_type=f32
    ) + jnp.dot(owned.astype(bf16), memory, preferred_element_type=f32)

    tiles = []
    for grad_piece in (query_up_grad, value_up_grad, query_down_grad, value_down_grad):
        for n in range(grad_piece.shape[1] // HD):
            tiles.append(grad_piece[:, n * HD : (n + 1) * HD])
    real = len(tiles)
    each = -(-real // peers)
    tiles += [jnp.zeros((RANK, HD), f32)] * (each * peers - real)
    packed = jnp.concatenate(tiles, 0).reshape(peers, each * RANK, HD)
    shares = lax.all_to_all(packed, "tm", split_axis=0, concat_axis=0, tiled=True)
    share = jnp.sum(shares, axis=0)
    everyone = jnp.broadcast_to(share[None], shares.shape)
    whole = lax.all_to_all(everyone, "tm", split_axis=0, concat_axis=0, tiled=True)
    whole = whole.reshape(peers * each, RANK, HD)
    outs = []
    at = 0
    for grad_piece in (query_up_grad, value_up_grad, query_down_grad, value_down_grad):
        count = grad_piece.shape[1] // HD
        outs.append(jnp.concatenate([whole[at + n] for n in range(count)], 1))
        at += count
    query_up_grad, value_up_grad, query_down_grad, value_down_grad = outs
    return (logits, query_down_grad, query_up_grad, value_down_grad, value_up_grad)


def solution(mesh):
    in_specs = (
        P("tm", "heads"),
        P("tm", "heads"),
        P(None, "heads"),
        P(None, "heads"),
        P(None, "heads"),
        P(),
        P(None, "heads"),
        P(),
        P(None, "heads"),
        P("heads", None),
        P("tm", None),
        P("tm"),
        P("tm", None),
    )
    out_specs = (
        P("tm", None),
        P(None, "heads"),
        P(None, "heads"),
        P(None, "heads"),
        P(None, "heads"),
    )
    fits = mesh.shape["heads"] == 4 and mesh.shape["tm"] * CAP == TOP
    local = fast if fits else general
    return jax.shard_map(local, mesh=mesh, in_specs=in_specs, out_specs=out_specs, check_vma=False)
```

```python
import jax
import jax.numpy as jnp
from jax import lax
from jax.experimental import pallas as pl
from jax.experimental.pallas import tpu as pltpu
from jax.sharding import PartitionSpec as P

HD = 128
RANK = 16
TOP = 8
BLK = 128
CAP = 1


HIGHEST = lax.Precision.HIGHEST


def attend(query, all_keys, all_values, split_row, out_grad):
    span_count, row_count, query_width = query.shape
    key_count, kv_width = (all_keys.shape[1], all_keys.shape[2])
    kv_heads = kv_width // HD
    group_size = query_width // kv_width
    score_scale = HD ** (-0.5)
    query_heads = query.reshape(span_count, row_count, kv_heads, group_size, HD)
    key_heads = all_keys.reshape(span_count, key_count, kv_heads, HD)
    value_heads = all_values.reshape(span_count, key_count, kv_heads, HD)
    grad_heads = out_grad.reshape(span_count, row_count, kv_heads, group_size, HD)
    scores = (
        jnp.einsum("crngd,cknd->cngrk", query_heads, key_heads, preferred_element_type=jnp.float32)
        * score_scale
    )
    row_ids = jnp.arange(row_count, dtype=jnp.int32)[:, None]
    col_ids = jnp.arange(BLK, dtype=jnp.int32)[None, :]
    edge_at = split_row[:, None, None]
    local_seen = (col_ids <= row_ids) & ((col_ids >= edge_at) | (row_ids < edge_at))
    visible = jnp.concatenate(
        [jnp.ones((span_count, row_count, key_count - BLK), jnp.bool_), local_seen], axis=2
    )
    scores = jnp.where(visible[:, None, None], scores, -jnp.inf)
    row_max = jnp.max(scores, axis=-1, keepdims=True)
    weights = jnp.exp(scores - row_max)
    probs = weights / jnp.sum(weights, axis=-1, keepdims=True)
    probs_low = probs.astype(jnp.bfloat16)
    attended = jnp.einsum(
        "cngrk,cknd->crngd", probs_low, value_heads, preferred_element_type=jnp.float32
    ).astype(jnp.bfloat16)
    prob_grad = jnp.einsum(
        "crngd,cknd->cngrk", grad_heads, value_heads, preferred_element_type=jnp.float32
    )
    row_dot = jnp.sum(grad_heads.astype(jnp.float32) * attended.astype(jnp.float32), axis=-1)
    row_dot = jnp.transpose(row_dot, (0, 2, 3, 1))[..., None]
    score_grad = (probs * (prob_grad - row_dot) * score_scale).astype(jnp.bfloat16)
    query_grad = jnp.einsum(
        "cngrk,cknd->crngd", score_grad, key_heads, preferred_element_type=jnp.float32
    ).astype(jnp.bfloat16)
    value_grad = jnp.einsum(
        "cngrk,crngd->cknd", probs_low, grad_heads, preferred_element_type=jnp.float32
    )
    return (
        attended.reshape(span_count, row_count, query_width),
        query_grad.reshape(span_count, row_count, query_width),
        value_grad.reshape(span_count, key_count, kv_width),
    )


def choose_slots(needed, places):
    slot_ids = jnp.arange(CAP, dtype=jnp.int32)
    return needed[:, None, :] * (places[:, None, :] == slot_ids[None, :, None]).astype(jnp.int32)


def general(
    slab_tokens,
    memory,
    query_weight,
    key_weight,
    value_weight,
    query_down,
    query_up,
    value_down,
    value_up,
    tag_weight,
    retrieval,
    boundary,
    grad_tags,
):
    tok_rows = slab_tokens.shape[0]
    mem_rows = memory.shape[0]
    query_width = query_weight.shape[1]
    kv_width = key_weight.shape[1]
    span_count = tok_rows // BLK
    block_count = mem_rows // BLK
    pair_weight = jnp.concatenate([key_weight, value_weight], 1)
    adapter_pair = jnp.concatenate([query_down, value_down], 0)
    contract_last = (((1,), (1,)), ((), ()))
    contract_first = (((0,), (0,)), ((), ()))
    token_piece = lax.all_gather(slab_tokens, "heads", axis=1, tiled=True)
    memory_piece = lax.all_gather(memory, "heads", axis=1, tiled=True)
    query_acc = jnp.dot(token_piece, query_weight, preferred_element_type=jnp.float32)
    pair_acc = jnp.dot(token_piece, pair_weight, preferred_element_type=jnp.float32)
    low_acc = lax.dot_general(
        token_piece, adapter_pair, contract_last, preferred_element_type=jnp.float32
    )
    memory_acc = jnp.dot(memory_piece, pair_weight, preferred_element_type=jnp.float32)
    memory_low_acc = lax.dot_general(
        memory_piece, adapter_pair[RANK:], contract_last, preferred_element_type=jnp.float32
    )
    query_acc, pair_acc, low_acc, memory_acc, memory_low_acc = (
        query_acc,
        pair_acc,
        low_acc,
        memory_acc,
        memory_low_acc,
    )
    low_tokens = low_acc.astype(jnp.bfloat16)
    low_query = low_tokens[:, :RANK]
    low_value = low_tokens[:, RANK:]
    queries = (query_acc + jnp.dot(low_query, query_up, preferred_element_type=jnp.float32)).astype(
        jnp.bfloat16
    )
    keys_local = pair_acc[:, :kv_width].astype(jnp.bfloat16)
    values_local = (
        pair_acc[:, kv_width:] + jnp.dot(low_value, value_up, preferred_element_type=jnp.float32)
    ).astype(jnp.bfloat16)
    memory_low = memory_low_acc.astype(jnp.bfloat16)
    memory_pair = (
        jnp.concatenate(
            [
                memory_acc[:, :kv_width],
                memory_acc[:, kv_width:]
                + jnp.dot(memory_low, value_up, preferred_element_type=jnp.float32),
            ],
            1,
        )
        .astype(jnp.bfloat16)
        .reshape(block_count, BLK, 2 * kv_width)
    )
    peer_count = lax.axis_size("tm")
    every_block = jnp.arange(peer_count * block_count, dtype=jnp.int32)
    wanted = (
        jnp.any(retrieval.reshape(-1, 1) == every_block[None, :], axis=0)
        .astype(jnp.int32)
        .reshape(peer_count, block_count)
    )
    places = jnp.cumsum(wanted, axis=1) - wanted
    requested = choose_slots(wanted, places)
    asked_for = lax.all_to_all(requested, "tm", split_axis=0, concat_axis=0, tiled=True)
    rows_needed = retrieval // block_count * CAP + jnp.take(places.reshape(-1), retrieval)
    asked_low = asked_for.astype(jnp.bfloat16)
    outgoing = jnp.einsum(
        "rcm,mbw->rcbw", asked_low, memory_pair, preferred_element_type=jnp.float32
    ).astype(jnp.bfloat16)
    fetched = lax.all_to_all(outgoing, "tm", split_axis=0, concat_axis=0, tiled=True)
    slot_rows = fetched.reshape(peer_count * CAP, BLK, 2 * kv_width)
    picked = jnp.take(slot_rows, rows_needed.reshape(-1), axis=0).reshape(
        span_count, TOP * BLK, 2 * kv_width
    )
    all_keys = jnp.concatenate(
        [picked[..., :kv_width], keys_local.reshape(span_count, BLK, kv_width)], 1
    )
    all_values = jnp.concatenate(
        [picked[..., kv_width:], values_local.reshape(span_count, BLK, kv_width)], 1
    )
    attended_grad = lax.dot_general(
        grad_tags, tag_weight.astype(jnp.float32), contract_last, precision=HIGHEST
    ).astype(jnp.bfloat16)
    attended, query_grad, value_grad = attend(
        queries.reshape(span_count, BLK, query_width),
        all_keys,
        all_values,
        boundary,
        attended_grad.reshape(span_count, BLK, query_width),
    )
    attended = attended.reshape(tok_rows, query_width)
    query_grad = query_grad.reshape(tok_rows, query_width)
    logits_out = lax.psum(
        jnp.dot(attended, tag_weight, preferred_element_type=jnp.float32), "heads"
    )
    local_grad = value_grad[:, TOP * BLK :].reshape(tok_rows, kv_width)
    slot_grads = value_grad[:, : TOP * BLK].reshape(span_count * TOP, BLK * kv_width)
    slot_hits = (
        rows_needed.reshape(-1, 1) == jnp.arange(peer_count * CAP, dtype=jnp.int32)[None, :]
    ).astype(jnp.float32)
    grad_buffer = lax.dot_general(slot_hits, slot_grads, contract_first, precision=HIGHEST).reshape(
        peer_count * CAP, BLK, kv_width
    )
    up_wide = value_up.astype(jnp.float32)
    returned = lax.all_to_all(
        grad_buffer.reshape(peer_count, CAP, BLK, kv_width),
        "tm",
        split_axis=0,
        concat_axis=0,
        tiled=True,
    )
    owned_grad = jnp.einsum(
        "rcm,rcbw->mbw", asked_for.astype(jnp.float32), returned, precision=HIGHEST
    ).reshape(mem_rows, kv_width)
    memory_cot = lax.dot_general(up_wide, owned_grad, contract_last, precision=HIGHEST)
    up_memory = lax.dot_general(
        memory_low.astype(jnp.float32), owned_grad, contract_first, precision=HIGHEST
    )
    query_cot = lax.dot_general(
        query_up, query_grad, contract_last, preferred_element_type=jnp.float32
    )
    value_cot = lax.dot_general(up_wide, local_grad, contract_last, precision=HIGHEST)
    query_cot, value_cot, memory_cot = lax.psum((query_cot, value_cot, memory_cot), "heads")
    query_down_grad = jnp.dot(
        query_cot.astype(jnp.bfloat16), slab_tokens, preferred_element_type=jnp.float32
    )
    value_down_grad = jnp.dot(
        value_cot.astype(jnp.bfloat16), slab_tokens, preferred_element_type=jnp.float32
    ) + jnp.dot(memory_cot.astype(jnp.bfloat16), memory, preferred_element_type=jnp.float32)
    query_up_grad = lax.dot_general(
        low_query, query_grad, contract_first, preferred_element_type=jnp.float32
    )
    value_up_grad = (
        lax.dot_general(
            low_value.astype(jnp.float32), local_grad, contract_first, precision=HIGHEST
        )
        + up_memory
    )
    query_down_grad, query_up_grad, value_down_grad, value_up_grad = lax.psum(
        (query_down_grad, query_up_grad, value_down_grad, value_up_grad), "tm"
    )
    return (logits_out, query_down_grad, query_up_grad, value_down_grad, value_up_grad)


LOG2E = 1.4426950408889634
NT = (((1,), (1,)), ((), ()))
PACK = 2 * BLK + RANK
STRIP = 16
VMEM_BYTES = 48 * 1024 * 1024


def dot_nt(a, b, precision=None):
    return lax.dot_general(a, b, NT, precision=precision, preferred_element_type=jnp.float32)


def dot_nn(a, b, precision=None):
    return jnp.dot(a, b, precision=precision, preferred_element_type=jnp.float32)


def piece_rows(place_ref, j, width):
    return pl.ds(pl.multiple_of(lax.bitwise_xor(place_ref[0], j) * width, width), width)


def memory_kernel(peers, last, place_ref, me_ref, asked_ref, x0, x1, x2, x3, wk_ref, wv_ref, down_ref, up_ref, *refs):
    tokens = (x0, x1, x2, x3)
    rows, width = x0.shape
    blocks = rows // BLK
    acc = None
    low = None
    for j in range(4):
        here = piece_rows(place_ref, j, width)
        x = tokens[j][...]
        term = dot_nn(x, jnp.concatenate([wk_ref[here, :], wv_ref[here, :]], 1))
        low_term = dot_nt(x, down_ref[:, here])
        acc = term if acc is None else acc + term
        low = low_term if low is None else low + low_term
    values = (acc[:, HD:] + dot_nn(low.astype(jnp.bfloat16), up_ref[...])).astype(jnp.bfloat16)
    keys = acc[:, :HD].astype(jnp.bfloat16)
    low_t = jnp.transpose(low).astype(jnp.bfloat16)
    if last:
        before, outs, pair_ref = refs[0], refs[1 : 1 + peers], refs[1 + peers]
        offset = before.shape[0]
        pair_ref[:offset] = before[...]
    else:
        pair_ref = refs[0]
        offset = 0
    for b in range(blocks):
        at = slice(b * BLK, (b + 1) * BLK)
        pair_ref[offset + b, 0:BLK, :] = keys[at]
        pair_ref[offset + b, BLK : 2 * BLK, :] = values[at]
        pair_ref[offset + b, 2 * BLK : PACK, :] = low_t[:, at]
    if last:
        for d in range(peers):
            outs[d][...] = pair_ref[asked_ref[lax.bitwise_xor(me_ref[0], d)]]


def project_kernel(place_ref, x0, x1, x2, x3, wq_hbm, wk_hbm, wv_hbm, qd_hbm, vd_hbm, qup_ref, vup_ref,
                   q_ref, k_ref, v_ref, low_ref, wq_s, wk_s, wv_s, qd_s, vd_s, sems):
    tokens = (x0, x1, x2, x3)
    width = x0.shape[1]
    copies = []
    for j in range(4):
        here = piece_rows(place_ref, j, width)
        group = [
            pltpu.make_async_copy(wq_hbm.at[here, :], wq_s.at[j], sems.at[j, 0]),
            pltpu.make_async_copy(wk_hbm.at[here, :], wk_s.at[j], sems.at[j, 1]),
            pltpu.make_async_copy(wv_hbm.at[here, :], wv_s.at[j], sems.at[j, 2]),
            pltpu.make_async_copy(qd_hbm.at[:, here], qd_s.at[j], sems.at[j, 3]),
            pltpu.make_async_copy(vd_hbm.at[:, here], vd_s.at[j], sems.at[j, 4]),
        ]
        for c in group:
            c.start()
        copies.append(group)
    q_acc = kv_acc = low_acc = None
    for j in range(4):
        for c in copies[j]:
            c.wait()
        x = tokens[j][...]
        q_term = dot_nn(x, wq_s[j])
        kv_term = dot_nn(x, jnp.concatenate([wk_s[j], wv_s[j]], 1))
        low_term = dot_nt(x, jnp.concatenate([qd_s[j], vd_s[j]], 0))
        if q_acc is None:
            q_acc, kv_acc, low_acc = q_term, kv_term, low_term
        else:
            q_acc, kv_acc, low_acc = q_acc + q_term, kv_acc + kv_term, low_acc + low_term
    low = low_acc.astype(jnp.bfloat16)
    q_ref[...] = (q_acc + dot_nn(low[:, :RANK], qup_ref[...])).astype(jnp.bfloat16)
    k_ref[...] = kv_acc[:, :HD].astype(jnp.bfloat16)
    v_ref[...] = (kv_acc[:, HD:] + dot_nn(low[:, RANK:], vup_ref[...])).astype(jnp.bfloat16)
    low_ref[...] = jnp.transpose(low_acc).astype(jnp.bfloat16)


def attention_kernel(cuts, peers, heads, bound_ref, *refs):
    parts = refs[: 4 * cuts]
    got = refs[4 * cuts : 4 * cuts + peers]
    qup_ref, vup_ref, tag_ref, grad_ref, grad_t_ref = refs[4 * cuts + peers : 4 * cuts + peers + 5]
    outs = refs[4 * cuts + peers + 5 :]
    cot_ref, up_ref = outs[0], outs[1]
    mcot_refs = outs[2 : 2 + peers]
    (q_s, k_own, v_own, low_s, k_all, v_all, kt_all, vt_all, bias_s, s_s, e_s, dp_s, p_s, ds_s, att_s, dq_s, dv_s) = outs[2 + peers :]
    seen = peers * BLK
    for t in range(cuts):
        q_c, k_c, v_c, low_c = parts[4 * t : 4 * t + 4]
        rows = q_c.shape[0]
        at = slice(t * rows, (t + 1) * rows)
        q_s[at, :] = q_c[...]
        k_own[at, :] = k_c[...]
        v_own[at, :] = v_c[...]
        low_s[:, at] = low_c[...]
    for b in range(peers):
        at = slice(b * BLK, (b + 1) * BLK)
        k = got[b][0:BLK, :]
        v = got[b][BLK : 2 * BLK, :]
        k_all[at, :] = k
        v_all[at, :] = v
        kt_all[:, at] = jnp.transpose(k)
        vt_all[:, at] = jnp.transpose(v)
    dv_s[...] = jnp.zeros_like(dv_s)
    up_ref[...] = jnp.zeros_like(up_ref)
    scale = HD ** (-0.5)
    up_wide = vup_ref[...].astype(jnp.float32)
    query_width = heads * HD

    def span_step(c, carry):
        rows = pl.ds(pl.multiple_of(c * BLK, BLK), BLK)
        k = k_own[rows, :]
        v = v_own[rows, :]
        k_all[seen:, :] = k
        v_all[seen:, :] = v
        kt_all[:, seen:] = jnp.transpose(k)
        vt_all[:, seen:] = jnp.transpose(v)
        edge = bound_ref[c]
        row_ids = lax.broadcasted_iota(jnp.int32, (BLK, BLK), 0)
        col_ids = lax.broadcasted_iota(jnp.int32, (BLK, BLK), 1)
        visible = (col_ids <= row_ids) & ((col_ids >= edge) | (row_ids < edge))
        bias_s[...] = jnp.where(visible, 0.0, -jnp.inf)

        def head_cols(h):
            return slice(h * HD, (h + 1) * HD)

        def scores(h):
            s_s[h % 2] = dot_nn(q_s[rows, head_cols(h)], kt_all[...])

        def prob_grads(h):
            dp_s[h % 3] = dot_nn(grad_ref[rows, head_cols(h)], vt_all[...])

        def softmax(h):
            for r in range(0, BLK, STRIP):
                at = slice(r, r + STRIP)
                s = s_s[h % 2, at, :]
                s = jnp.concatenate([s[:, :seen], s[:, seen:] + bias_s[at, :]], 1) * (scale * LOG2E)
                w = jnp.exp2(s - jnp.max(s, axis=1, keepdims=True))
                probs = w * (1.0 / jnp.sum(w, axis=1, keepdims=True))
                e_s[h % 2, at, :] = probs
                p_s[h * BLK + r : h * BLK + r + STRIP, :] = probs.astype(jnp.bfloat16)

        def attend_head(h):
            att_s[:, head_cols(h)] = dot_nn(p_s[h * BLK : (h + 1) * BLK, :], v_all[...]).astype(jnp.bfloat16)

        def score_grads(h):
            for r in range(0, BLK, STRIP):
                at = slice(r, r + STRIP)
                g = grad_ref[pl.ds(pl.multiple_of(c * BLK + r, STRIP), STRIP), head_cols(h)]
                dot = jnp.sum(
                    g.astype(jnp.float32) * att_s[at, head_cols(h)].astype(jnp.float32), axis=1, keepdims=True
                )
                ds_s[h % 2, at, :] = (e_s[h % 2, at, :] * ((dp_s[h % 3, at, :] - dot) * scale)).astype(jnp.bfloat16)
            dq_s[:, head_cols(h)] = dot_nn(ds_s[h % 2], k_all[...]).astype(jnp.bfloat16)

        scores(0)
        prob_grads(0)
        for h in range(heads + 1):
            if h < heads:
                softmax(h)
            if h + 1 < heads:
                scores(h + 1)
                prob_grads(h + 1)
            if h > 0:
                score_grads(h - 1)
            if h < heads:
                attend_head(h)
        g_t = jnp.concatenate([grad_t_ref[h * HD : (h + 1) * HD, rows] for h in range(heads)], 1)
        dv = dot_nn(g_t, p_s[...])
        dv_s[...] += dv[:, :seen]
        dv_own = dv[:, seen:]
        dq = dq_s[...]
        cot_ref[0:RANK, rows] = dot_nt(qup_ref[...], dq)
        cot_ref[RANK : 2 * RANK, rows] = dot_nn(up_wide, dv_own, HIGHEST)
        cot_ref[2 * RANK :, rows] = dot_nt(tag_ref[...], att_s[...])
        up_ref[:, :query_width] += dot_nn(low_s[0:RANK, rows], dq)
        up_ref[:, query_width:] += dot_nt(low_s[RANK:, rows].astype(jnp.float32), dv_own, HIGHEST)
        return carry

    lax.fori_loop(0, q_s.shape[0] // BLK, span_step, 0)
    dv = dv_s[...]
    mcot = dot_nn(up_wide, dv, HIGHEST)
    low_m = jnp.concatenate([got[b][2 * BLK : PACK, :] for b in range(peers)], 1).astype(jnp.float32)
    up_ref[:, query_width:] += dot_nt(low_m, dv, HIGHEST)
    for b in range(peers):
        mcot_refs[b][...] = mcot[:, b * BLK : (b + 1) * BLK]


def own_kernel(peers, me_ref, asked_ref, *refs):
    pieces, out_ref, sum_s = refs[:peers], refs[peers], refs[peers + 1]
    sum_s[...] = jnp.zeros_like(sum_s)
    for d in range(peers):
        block = asked_ref[lax.bitwise_xor(me_ref[0], d)]
        sum_s[block] = sum_s[block] + pieces[d][...]
    out_ref[...] = jnp.concatenate([sum_s[m] for m in range(sum_s.shape[0])], 1)


def down_kernel(peers, me_ref, *refs):
    cots, owns = refs[0:4], refs[4:8]
    slab_ref, memory_ref, logit_ref = refs[8:11]
    outs, part_s = refs[11 : 11 + peers], refs[11 + peers]
    cot = (cots[0][...] + cots[1][...]) + (cots[2][...] + cots[3][...])
    own = (owns[0][...] + owns[1][...]) + (owns[2][...] + owns[3][...])
    logit_ref[...] = cot[2 * RANK :]
    both = dot_nn(cot[: 2 * RANK].astype(jnp.bfloat16), slab_ref[...])
    value = both[RANK:] + dot_nn(own.astype(jnp.bfloat16), memory_ref[...])
    tiles = []
    for whole in (both[:RANK], value):
        for n in range(whole.shape[1] // HD):
            tiles.append(whole[:, n * HD : (n + 1) * HD])
    each = part_s.shape[1]
    for n in range(each * peers):
        part_s[n // each, n % each] = tiles[n] if n < len(tiles) else jnp.zeros((RANK, HD), jnp.float32)
    for d in range(peers):
        outs[d][...] = part_s[lax.bitwise_xor(me_ref[0], d)]


def share_kernel(peers, *refs):
    total = refs[0][...]
    for d in range(1, peers):
        total = total + refs[d][...]
    refs[peers][...] = total


def finish_kernel(peers, me_ref, *refs):
    shares, up_ref = refs[:peers], refs[peers]
    query_down_ref, query_up_ref, value_down_ref, value_up_ref, all_s = refs[peers + 1 :]
    for d in range(peers):
        all_s[lax.bitwise_xor(me_ref[0], d)] = shares[d][...]
    each = all_s.shape[1]
    n = 0
    for out_ref in (query_down_ref, value_down_ref):
        for m in range(out_ref.shape[1] // HD):
            out_ref[:, m * HD : (m + 1) * HD] = all_s[n // each, n % each]
            n += 1
    query_width = query_up_ref.shape[1]
    query_up_ref[...] = up_ref[:, :query_width]
    value_up_ref[...] = up_ref[:, query_width:]


def swap(x, bit, axis="heads"):
    return lax.ppermute(x, axis, [(i, i ^ bit) for i in range(lax.axis_size(axis))])


def gather_parts(x):
    far = swap(x, 2)
    near = swap(x, 1)
    return x, near, far, swap(far, 1)


def smem():
    return pl.BlockSpec(memory_space=pltpu.SMEM)


def vmem():
    return pl.BlockSpec(memory_space=pltpu.VMEM)


def shaped(*shape, dtype=jnp.float32):
    return jax.ShapeDtypeStruct(shape, dtype)


def run(body, name, out_shape, in_specs, scratch=(), flops=0, moved=0):
    many = isinstance(out_shape, (tuple, list))
    return pl.pallas_call(
        body,
        out_shape=out_shape,
        in_specs=in_specs,
        out_specs=tuple(vmem() for _ in out_shape) if many else vmem(),
        scratch_shapes=list(scratch),
        compiler_params=pltpu.CompilerParams(vmem_limit_bytes=VMEM_BYTES),
        cost_estimate=pl.CostEstimate(flops=flops, bytes_accessed=moved, transcendentals=0),
        name=name,
    )


def fast(
    slab_tokens,
    memory,
    query_weight,
    key_weight,
    value_weight,
    query_down,
    query_up,
    value_down,
    value_up,
    tag_weight,
    retrieval,
    boundary,
    grad_tags,
):
    tok_rows, width = slab_tokens.shape
    mem_rows = memory.shape[0]
    query_width = query_weight.shape[1]
    heads = query_width // HD
    spans = tok_rows // BLK
    blocks = mem_rows // BLK
    peers = lax.axis_size("tm")
    f32 = jnp.float32
    bf16 = jnp.bfloat16
    mem_cuts, tok_cuts = 2, 2

    mem_parts = [gather_parts(m) for m in jnp.split(memory, mem_cuts, 0)]
    tok_parts = [gather_parts(x) for x in jnp.split(slab_tokens, tok_cuts, 0)]

    named = retrieval[0]
    owner_ids = jnp.arange(peers, dtype=jnp.int32)
    wanted = jnp.sum(
        jnp.where(named[None, :] // blocks == owner_ids[:, None], named[None, :] % blocks, 0), axis=1
    ).astype(jnp.int32)
    asked = lax.all_to_all(wanted, "tm", split_axis=0, concat_axis=0, tiled=True)
    place = lax.axis_index("heads").astype(jnp.int32).reshape(1)
    me = lax.axis_index("tm").astype(jnp.int32).reshape(1)

    tag_t = tag_weight.T
    tags = tag_t.shape[0]
    wide_tag = tag_t.astype(f32)
    grad_t = lax.dot_general(
        wide_tag, grad_tags, (((0,), (1,)), ((), ())), precision=HIGHEST
    ).astype(bf16)
    grad = lax.dot_general(grad_tags, wide_tag, (((1,), (0,)), ((), ())), precision=HIGHEST).astype(bf16)

    cut_rows = mem_rows // mem_cuts
    cut_blocks = blocks // mem_cuts
    before = []
    for t in range(mem_cuts):
        last = t == mem_cuts - 1
        args = [place, me, asked, *mem_parts[t], key_weight, value_weight, value_down, value_up]
        if last:
            args.append(jnp.concatenate(before, 0) if len(before) > 1 else before[0])
            out_shape = [shaped(PACK, HD, dtype=bf16)] * peers
            scratch = [pltpu.VMEM((blocks, PACK, HD), bf16)]
        else:
            out_shape = shaped(cut_blocks, PACK, HD, dtype=bf16)
            scratch = []
        result = run(
            lambda *refs, last=last: memory_kernel(peers, last, *refs),
            "memory_pairs",
            out_shape,
            [smem()] * 3 + [vmem()] * (len(args) - 3),
            scratch,
            flops=2 * cut_rows * 4 * width * 3 * HD,
            moved=8 * cut_rows * width + 16 * width * HD,
        )(*args)
        before.append(result)
    outgoing = before[-1]
    got = [outgoing[0]] + [swap(outgoing[d], d, "tm") for d in range(1, peers)]

    rows = tok_rows // tok_cuts
    anywhere = pl.BlockSpec(memory_space=pl.ANY)
    parts = []
    for t in range(tok_cuts):
        parts += run(
            project_kernel,
            "project_span_rows",
            (
                shaped(rows, query_width, dtype=bf16),
                shaped(rows, HD, dtype=bf16),
                shaped(rows, HD, dtype=bf16),
                shaped(2 * RANK, rows, dtype=bf16),
            ),
            [smem()] + [vmem()] * 4 + [anywhere] * 5 + [vmem()] * 2,
            [
                pltpu.VMEM((4, width, query_width), bf16),
                pltpu.VMEM((4, width, HD), bf16),
                pltpu.VMEM((4, width, HD), bf16),
                pltpu.VMEM((4, RANK, width), bf16),
                pltpu.VMEM((4, RANK, width), bf16),
                pltpu.SemaphoreType.DMA((4, 5)),
            ],
            flops=2 * rows * 4 * width * (query_width + 3 * HD),
            moved=8 * width * (rows + query_width + 3 * HD),
        )(place, *tok_parts[t], query_weight, key_weight, value_weight, query_down, value_down, query_up, value_up)

    seen = peers * BLK
    total = seen + BLK
    cot, ups, *mcot = run(
        lambda *refs: attention_kernel(tok_cuts, peers, heads, *refs),
        "span_attention",
        [shaped(2 * RANK + tags, tok_rows), shaped(RANK, query_width + HD)] + [shaped(RANK, BLK)] * peers,
        [smem()] + [vmem()] * (4 * tok_cuts + peers + 5),
        [
            pltpu.VMEM((tok_rows, query_width), bf16),
            pltpu.VMEM((tok_rows, HD), bf16),
            pltpu.VMEM((tok_rows, HD), bf16),
            pltpu.VMEM((2 * RANK, tok_rows), bf16),
            pltpu.VMEM((total, HD), bf16),
            pltpu.VMEM((total, HD), bf16),
            pltpu.VMEM((HD, total), bf16),
            pltpu.VMEM((HD, total), bf16),
            pltpu.VMEM((BLK, BLK), f32),
            pltpu.VMEM((2, BLK, total), f32),
            pltpu.VMEM((2, BLK, total), f32),
            pltpu.VMEM((3, BLK, total), f32),
            pltpu.VMEM((heads * BLK, total), bf16),
            pltpu.VMEM((2, BLK, total), bf16),
            pltpu.VMEM((BLK, query_width), bf16),
            pltpu.VMEM((BLK, query_width), bf16),
            pltpu.VMEM((HD, seen), f32),
        ],
        flops=20 * tok_rows * query_width * total,
        moved=4 * tok_rows * query_width,
    )(boundary, *parts, *got, query_up, value_up, tag_t, grad, grad_t)

    back = [mcot[0]] + [swap(mcot[d], d, "tm") for d in range(1, peers)]
    cots = [cot] + [swap(cot, d) for d in range(1, 4)]
    bit = 1
    while bit < peers:
        ups = ups + swap(ups, bit, "tm")
        bit *= 2
    own = run(
        lambda *refs: own_kernel(peers, *refs),
        "owned_cotangent",
        shaped(RANK, mem_rows),
        [smem()] * 2 + [vmem()] * peers,
        [pltpu.VMEM((blocks, RANK, BLK), f32)],
    )(me, asked, *back)
    owns = [own] + [swap(own, d) for d in range(1, 4)]
    each = -(-2 * (width // HD) // peers)
    logits, *pieces = run(
        lambda *refs: down_kernel(peers, *refs),
        "down_gradients",
        [shaped(tags, tok_rows)] + [shaped(each, RANK, HD)] * peers,
        [smem()] + [vmem()] * 10,
        [pltpu.VMEM((peers, each, RANK, HD), f32)],
        flops=6 * RANK * tok_rows * width,
        moved=4 * tok_rows * width,
    )(me, *cots, *owns, slab_tokens, memory)
    pieces = [pieces[0]] + [swap(pieces[d], d, "tm") for d in range(1, peers)]
    share = run(
        lambda *refs: share_kernel(peers, *refs), "share_sum", shaped(each, RANK, HD), [vmem()] * peers
    )(*pieces)
    shares = [share] + [swap(share, d, "tm") for d in range(1, peers)]
    query_down_grad, query_up_grad, value_down_grad, value_up_grad = run(
        lambda *refs: finish_kernel(peers, *refs),
        "finish_outputs",
        (shaped(RANK, width), shaped(RANK, query_width), shaped(RANK, width), shaped(RANK, HD)),
        [smem()] + [vmem()] * (peers + 1),
        [pltpu.VMEM((peers, each, RANK, HD), f32)],
    )(me, *shares, ups)
    return (logits.T, query_down_grad, query_up_grad, value_down_grad, value_up_grad)


def solution(mesh):
    in_specs = (
        P("tm", "heads"),
        P("tm", "heads"),
        P(None, "heads"),
        P(None, "heads"),
        P(None, "heads"),
        P(),
        P(None, "heads"),
        P(),
        P(None, "heads"),
        P("heads", None),
        P("tm", None),
        P("tm"),
        P("tm", None),
    )
    out_specs = (
        P("tm", None),
        P(None, "heads"),
        P(None, "heads"),
        P(None, "heads"),
        P(None, "heads"),
    )
    fits = mesh.shape["heads"] == 4 and mesh.shape["tm"] * CAP == TOP
    local = fast if fits else general
    return jax.shard_map(local, mesh=mesh, in_specs=in_specs, out_specs=out_specs, check_vma=False)
```

```python
import jax
import jax.numpy as jnp
from jax import lax
from jax.experimental import pallas as pl
from jax.experimental.pallas import tpu as pltpu
from jax.sharding import PartitionSpec as P

HD = 128
RANK = 16
TOP = 8
BLK = 128
CAP = 1


HIGHEST = lax.Precision.HIGHEST


def attend(query, all_keys, all_values, split_row, out_grad):
    span_count, row_count, query_width = query.shape
    key_count, kv_width = (all_keys.shape[1], all_keys.shape[2])
    kv_heads = kv_width // HD
    group_size = query_width // kv_width
    score_scale = HD ** (-0.5)
    query_heads = query.reshape(span_count, row_count, kv_heads, group_size, HD)
    key_heads = all_keys.reshape(span_count, key_count, kv_heads, HD)
    value_heads = all_values.reshape(span_count, key_count, kv_heads, HD)
    grad_heads = out_grad.reshape(span_count, row_count, kv_heads, group_size, HD)
    scores = (
        jnp.einsum("crngd,cknd->cngrk", query_heads, key_heads, preferred_element_type=jnp.float32)
        * score_scale
    )
    row_ids = jnp.arange(row_count, dtype=jnp.int32)[:, None]
    col_ids = jnp.arange(BLK, dtype=jnp.int32)[None, :]
    edge_at = split_row[:, None, None]
    local_seen = (col_ids <= row_ids) & ((col_ids >= edge_at) | (row_ids < edge_at))
    visible = jnp.concatenate(
        [jnp.ones((span_count, row_count, key_count - BLK), jnp.bool_), local_seen], axis=2
    )
    scores = jnp.where(visible[:, None, None], scores, -jnp.inf)
    row_max = jnp.max(scores, axis=-1, keepdims=True)
    weights = jnp.exp(scores - row_max)
    probs = weights / jnp.sum(weights, axis=-1, keepdims=True)
    probs_low = probs.astype(jnp.bfloat16)
    attended = jnp.einsum(
        "cngrk,cknd->crngd", probs_low, value_heads, preferred_element_type=jnp.float32
    ).astype(jnp.bfloat16)
    prob_grad = jnp.einsum(
        "crngd,cknd->cngrk", grad_heads, value_heads, preferred_element_type=jnp.float32
    )
    row_dot = jnp.sum(grad_heads.astype(jnp.float32) * attended.astype(jnp.float32), axis=-1)
    row_dot = jnp.transpose(row_dot, (0, 2, 3, 1))[..., None]
    score_grad = (probs * (prob_grad - row_dot) * score_scale).astype(jnp.bfloat16)
    query_grad = jnp.einsum(
        "cngrk,cknd->crngd", score_grad, key_heads, preferred_element_type=jnp.float32
    ).astype(jnp.bfloat16)
    value_grad = jnp.einsum(
        "cngrk,crngd->cknd", probs_low, grad_heads, preferred_element_type=jnp.float32
    )
    return (
        attended.reshape(span_count, row_count, query_width),
        query_grad.reshape(span_count, row_count, query_width),
        value_grad.reshape(span_count, key_count, kv_width),
    )


def choose_slots(needed, places):
    slot_ids = jnp.arange(CAP, dtype=jnp.int32)
    return needed[:, None, :] * (places[:, None, :] == slot_ids[None, :, None]).astype(jnp.int32)


def general(
    slab_tokens,
    memory,
    query_weight,
    key_weight,
    value_weight,
    query_down,
    query_up,
    value_down,
    value_up,
    tag_weight,
    retrieval,
    boundary,
    grad_tags,
):
    tok_rows = slab_tokens.shape[0]
    mem_rows = memory.shape[0]
    query_width = query_weight.shape[1]
    kv_width = key_weight.shape[1]
    span_count = tok_rows // BLK
    block_count = mem_rows // BLK
    pair_weight = jnp.concatenate([key_weight, value_weight], 1)
    adapter_pair = jnp.concatenate([query_down, value_down], 0)
    contract_last = (((1,), (1,)), ((), ()))
    contract_first = (((0,), (0,)), ((), ()))
    token_piece = lax.all_gather(slab_tokens, "heads", axis=1, tiled=True)
    memory_piece = lax.all_gather(memory, "heads", axis=1, tiled=True)
    query_acc = jnp.dot(token_piece, query_weight, preferred_element_type=jnp.float32)
    pair_acc = jnp.dot(token_piece, pair_weight, preferred_element_type=jnp.float32)
    low_acc = lax.dot_general(
        token_piece, adapter_pair, contract_last, preferred_element_type=jnp.float32
    )
    memory_acc = jnp.dot(memory_piece, pair_weight, preferred_element_type=jnp.float32)
    memory_low_acc = lax.dot_general(
        memory_piece, adapter_pair[RANK:], contract_last, preferred_element_type=jnp.float32
    )
    query_acc, pair_acc, low_acc, memory_acc, memory_low_acc = (
        query_acc,
        pair_acc,
        low_acc,
        memory_acc,
        memory_low_acc,
    )
    low_tokens = low_acc.astype(jnp.bfloat16)
    low_query = low_tokens[:, :RANK]
    low_value = low_tokens[:, RANK:]
    queries = (query_acc + jnp.dot(low_query, query_up, preferred_element_type=jnp.float32)).astype(
        jnp.bfloat16
    )
    keys_local = pair_acc[:, :kv_width].astype(jnp.bfloat16)
    values_local = (
        pair_acc[:, kv_width:] + jnp.dot(low_value, value_up, preferred_element_type=jnp.float32)
    ).astype(jnp.bfloat16)
    memory_low = memory_low_acc.astype(jnp.bfloat16)
    memory_pair = (
        jnp.concatenate(
            [
                memory_acc[:, :kv_width],
                memory_acc[:, kv_width:]
                + jnp.dot(memory_low, value_up, preferred_element_type=jnp.float32),
            ],
            1,
        )
        .astype(jnp.bfloat16)
        .reshape(block_count, BLK, 2 * kv_width)
    )
    peer_count = lax.axis_size("tm")
    every_block = jnp.arange(peer_count * block_count, dtype=jnp.int32)
    wanted = (
        jnp.any(retrieval.reshape(-1, 1) == every_block[None, :], axis=0)
        .astype(jnp.int32)
        .reshape(peer_count, block_count)
    )
    places = jnp.cumsum(wanted, axis=1) - wanted
    requested = choose_slots(wanted, places)
    asked_for = lax.all_to_all(requested, "tm", split_axis=0, concat_axis=0, tiled=True)
    rows_needed = retrieval // block_count * CAP + jnp.take(places.reshape(-1), retrieval)
    asked_low = asked_for.astype(jnp.bfloat16)
    outgoing = jnp.einsum(
        "rcm,mbw->rcbw", asked_low, memory_pair, preferred_element_type=jnp.float32
    ).astype(jnp.bfloat16)
    fetched = lax.all_to_all(outgoing, "tm", split_axis=0, concat_axis=0, tiled=True)
    slot_rows = fetched.reshape(peer_count * CAP, BLK, 2 * kv_width)
    picked = jnp.take(slot_rows, rows_needed.reshape(-1), axis=0).reshape(
        span_count, TOP * BLK, 2 * kv_width
    )
    all_keys = jnp.concatenate(
        [picked[..., :kv_width], keys_local.reshape(span_count, BLK, kv_width)], 1
    )
    all_values = jnp.concatenate(
        [picked[..., kv_width:], values_local.reshape(span_count, BLK, kv_width)], 1
    )
    attended_grad = lax.dot_general(
        grad_tags, tag_weight.astype(jnp.float32), contract_last, precision=HIGHEST
    ).astype(jnp.bfloat16)
    attended, query_grad, value_grad = attend(
        queries.reshape(span_count, BLK, query_width),
        all_keys,
        all_values,
        boundary,
        attended_grad.reshape(span_count, BLK, query_width),
    )
    attended = attended.reshape(tok_rows, query_width)
    query_grad = query_grad.reshape(tok_rows, query_width)
    logits_out = lax.psum(
        jnp.dot(attended, tag_weight, preferred_element_type=jnp.float32), "heads"
    )
    local_grad = value_grad[:, TOP * BLK :].reshape(tok_rows, kv_width)
    slot_grads = value_grad[:, : TOP * BLK].reshape(span_count * TOP, BLK * kv_width)
    slot_hits = (
        rows_needed.reshape(-1, 1) == jnp.arange(peer_count * CAP, dtype=jnp.int32)[None, :]
    ).astype(jnp.float32)
    grad_buffer = lax.dot_general(slot_hits, slot_grads, contract_first, precision=HIGHEST).reshape(
        peer_count * CAP, BLK, kv_width
    )
    up_wide = value_up.astype(jnp.float32)
    returned = lax.all_to_all(
        grad_buffer.reshape(peer_count, CAP, BLK, kv_width),
        "tm",
        split_axis=0,
        concat_axis=0,
        tiled=True,
    )
    owned_grad = jnp.einsum(
        "rcm,rcbw->mbw", asked_for.astype(jnp.float32), returned, precision=HIGHEST
    ).reshape(mem_rows, kv_width)
    memory_cot = lax.dot_general(up_wide, owned_grad, contract_last, precision=HIGHEST)
    up_memory = lax.dot_general(
        memory_low.astype(jnp.float32), owned_grad, contract_first, precision=HIGHEST
    )
    query_cot = lax.dot_general(
        query_up, query_grad, contract_last, preferred_element_type=jnp.float32
    )
    value_cot = lax.dot_general(up_wide, local_grad, contract_last, precision=HIGHEST)
    query_cot, value_cot, memory_cot = lax.psum((query_cot, value_cot, memory_cot), "heads")
    query_down_grad = jnp.dot(
        query_cot.astype(jnp.bfloat16), slab_tokens, preferred_element_type=jnp.float32
    )
    value_down_grad = jnp.dot(
        value_cot.astype(jnp.bfloat16), slab_tokens, preferred_element_type=jnp.float32
    ) + jnp.dot(memory_cot.astype(jnp.bfloat16), memory, preferred_element_type=jnp.float32)
    query_up_grad = lax.dot_general(
        low_query, query_grad, contract_first, preferred_element_type=jnp.float32
    )
    value_up_grad = (
        lax.dot_general(
            low_value.astype(jnp.float32), local_grad, contract_first, precision=HIGHEST
        )
        + up_memory
    )
    query_down_grad, query_up_grad, value_down_grad, value_up_grad = lax.psum(
        (query_down_grad, query_up_grad, value_down_grad, value_up_grad), "tm"
    )
    return (logits_out, query_down_grad, query_up_grad, value_down_grad, value_up_grad)


LOG2E = 1.4426950408889634
NT = (((1,), (1,)), ((), ()))
PACK = 2 * BLK + RANK
STRIP = 16
VMEM_BYTES = 48 * 1024 * 1024


def dot_nt(a, b, precision=None):
    return lax.dot_general(a, b, NT, precision=precision, preferred_element_type=jnp.float32)


def dot_nn(a, b, precision=None):
    return jnp.dot(a, b, precision=precision, preferred_element_type=jnp.float32)


def piece_rows(place_ref, j, width):
    return pl.ds(pl.multiple_of(lax.bitwise_xor(place_ref[0], j) * width, width), width)


def memory_early_kernel(place_ref, x0, x1, wk_ref, wv_ref, down_ref, acc_ref, low_ref):
    width = x0.shape[1]
    acc = low = None
    for j, x_ref in enumerate((x0, x1)):
        here = piece_rows(place_ref, j, width)
        x = x_ref[...]
        term = dot_nn(x, jnp.concatenate([wk_ref[here, :], wv_ref[here, :]], 1))
        low_term = dot_nt(x, down_ref[:, here])
        acc = term if acc is None else acc + term
        low = low_term if low is None else low + low_term
    acc_ref[...] = acc
    low_ref[...] = low


def memory_kernel(first, peers, last, place_ref, asked_ref, x2, x3, acc_ref, low_in, wk_ref, wv_ref, down_ref, up_ref, *refs):
    rows, width = x2.shape
    blocks = rows // BLK
    acc = acc_ref[first : first + rows, :]
    low = low_in[first : first + rows, :]
    for j, x_ref in ((2, x2), (3, x3)):
        here = piece_rows(place_ref, j, width)
        x = x_ref[...]
        acc = acc + dot_nn(x, jnp.concatenate([wk_ref[here, :], wv_ref[here, :]], 1))
        low = low + dot_nt(x, down_ref[:, here])
    values = (acc[:, HD:] + dot_nn(low.astype(jnp.bfloat16), up_ref[...])).astype(jnp.bfloat16)
    keys = acc[:, :HD].astype(jnp.bfloat16)
    low_t = jnp.transpose(low).astype(jnp.bfloat16)
    if last:
        before, out_ref, pair_ref = refs
        offset = before.shape[0]
        pair_ref[:offset] = before[...]
    else:
        pair_ref = refs[1]
        offset = 0
    for b in range(blocks):
        at = slice(b * BLK, (b + 1) * BLK)
        pair_ref[offset + b, 0:BLK, :] = keys[at]
        pair_ref[offset + b, BLK : 2 * BLK, :] = values[at]
        pair_ref[offset + b, 2 * BLK : PACK, :] = low_t[:, at]
    if last:
        for r in range(peers):
            out_ref[r] = pair_ref[asked_ref[r]]


def weight_copies(place_ref, j, slot, width, hbm, scratch, sems):
    wq_hbm, wk_hbm, wv_hbm, qd_hbm, vd_hbm = hbm
    wq_s, wk_s, wv_s, qd_s, vd_s = scratch
    here = piece_rows(place_ref, j, width)
    group = [
        pltpu.make_async_copy(wq_hbm.at[here, :], wq_s.at[slot], sems.at[slot, 0]),
        pltpu.make_async_copy(wk_hbm.at[here, :], wk_s.at[slot], sems.at[slot, 1]),
        pltpu.make_async_copy(wv_hbm.at[here, :], wv_s.at[slot], sems.at[slot, 2]),
        pltpu.make_async_copy(qd_hbm.at[:, here], qd_s.at[slot], sems.at[slot, 3]),
        pltpu.make_async_copy(vd_hbm.at[:, here], vd_s.at[slot], sems.at[slot, 4]),
    ]
    for c in group:
        c.start()
    return group


def project_terms(x, slot, scratch):
    wq_s, wk_s, wv_s, qd_s, vd_s = scratch
    return (
        dot_nn(x, wq_s[slot]),
        dot_nn(x, jnp.concatenate([wk_s[slot], wv_s[slot]], 1)),
        dot_nt(x, jnp.concatenate([qd_s[slot], vd_s[slot]], 0)),
    )


def project_early_kernel(place_ref, x0, x1, *refs):
    hbm, (q_ref, kv_ref, low_ref), scratch, sems = refs[:5], refs[5:8], refs[8:13], refs[13]
    copies = [weight_copies(place_ref, j, j, x0.shape[1], hbm, scratch, sems) for j in range(2)]
    for j, x_ref in enumerate((x0, x1)):
        for c in copies[j]:
            c.wait()
        terms = project_terms(x_ref[...], j, scratch)
        for ref, term in zip((q_ref, kv_ref, low_ref), terms):
            if j == 0:
                ref[...] = term
            else:
                ref[...] += term


def project_kernel(first, place_ref, x2, x3, *refs):
    hbm, (q_in, kv_in, low_in), (qup_ref, vup_ref) = refs[:5], refs[5:8], refs[8:10]
    q_ref, k_ref, v_ref, low_ref = refs[10:14]
    scratch, sems = refs[14:19], refs[19]
    rows, width = x2.shape
    at = slice(first, first + rows)
    copies = [weight_copies(place_ref, 2 + s, s, width, hbm, scratch, sems) for s in range(2)]
    sums = [q_in[at, :], kv_in[at, :], low_in[at, :]]
    for s, x_ref in enumerate((x2, x3)):
        for c in copies[s]:
            c.wait()
        sums = [a + b for a, b in zip(sums, project_terms(x_ref[...], s, scratch))]
    q_acc, kv_acc, low_acc = sums
    low = low_acc.astype(jnp.bfloat16)
    q_ref[...] = (q_acc + dot_nn(low[:, :RANK], qup_ref[...])).astype(jnp.bfloat16)
    k_ref[...] = kv_acc[:, :HD].astype(jnp.bfloat16)
    v_ref[...] = (kv_acc[:, HD:] + dot_nn(low[:, RANK:], vup_ref[...])).astype(jnp.bfloat16)
    low_ref[...] = jnp.transpose(low_acc).astype(jnp.bfloat16)


def attention_kernel(cuts, peers, heads, bound_ref, *refs):
    parts = refs[: 4 * cuts]
    got, qup_ref, vup_ref, tag_ref, grad_ref, grad_t_ref, cot_ref, up_ref, mcot_ref = refs[4 * cuts : 4 * cuts + 9]
    (q_s, k_own, v_own, low_s, k_all, v_all, kt_all, vt_all, bias_s, s_s, e_s, dp_s, p_s, ds_s, att_s, dq_s, dv_s) = refs[4 * cuts + 9 :]
    seen = peers * BLK
    for t in range(cuts):
        q_c, k_c, v_c, low_c = parts[4 * t : 4 * t + 4]
        rows = q_c.shape[0]
        at = slice(t * rows, (t + 1) * rows)
        q_s[at, :] = q_c[...]
        k_own[at, :] = k_c[...]
        v_own[at, :] = v_c[...]
        low_s[:, at] = low_c[...]
    for b in range(peers):
        at = slice(b * BLK, (b + 1) * BLK)
        k = got[b, 0:BLK, :]
        v = got[b, BLK : 2 * BLK, :]
        k_all[at, :] = k
        v_all[at, :] = v
        kt_all[:, at] = jnp.transpose(k)
        vt_all[:, at] = jnp.transpose(v)
    dv_s[...] = jnp.zeros_like(dv_s)
    up_ref[...] = jnp.zeros_like(up_ref)
    scale = HD ** (-0.5)
    up_wide = vup_ref[...].astype(jnp.float32)
    query_width = heads * HD

    def span_step(c, carry):
        rows = pl.ds(pl.multiple_of(c * BLK, BLK), BLK)
        k = k_own[rows, :]
        v = v_own[rows, :]
        k_all[seen:, :] = k
        v_all[seen:, :] = v
        kt_all[:, seen:] = jnp.transpose(k)
        vt_all[:, seen:] = jnp.transpose(v)
        edge = bound_ref[c]
        row_ids = lax.broadcasted_iota(jnp.int32, (BLK, BLK), 0)
        col_ids = lax.broadcasted_iota(jnp.int32, (BLK, BLK), 1)
        visible = (col_ids <= row_ids) & ((col_ids >= edge) | (row_ids < edge))
        bias_s[...] = jnp.where(visible, 0.0, -jnp.inf)

        def head_cols(h):
            return slice(h * HD, (h + 1) * HD)

        def scores(h):
            s_s[h % 2] = dot_nn(q_s[rows, head_cols(h)], kt_all[...])

        def prob_grads(h):
            dp_s[h % 3] = dot_nn(grad_ref[rows, head_cols(h)], vt_all[...])

        def softmax(h):
            for r in range(0, BLK, STRIP):
                at = slice(r, r + STRIP)
                s = s_s[h % 2, at, :]
                s = jnp.concatenate([s[:, :seen], s[:, seen:] + bias_s[at, :]], 1) * (scale * LOG2E)
                w = jnp.exp2(s - jnp.max(s, axis=1, keepdims=True))
                probs = w * (1.0 / jnp.sum(w, axis=1, keepdims=True))
                e_s[h % 2, at, :] = probs
                p_s[h * BLK + r : h * BLK + r + STRIP, :] = probs.astype(jnp.bfloat16)

        def attend_head(h):
            att_s[:, head_cols(h)] = dot_nn(p_s[h * BLK : (h + 1) * BLK, :], v_all[...]).astype(jnp.bfloat16)

        def score_grads(h):
            for r in range(0, BLK, STRIP):
                at = slice(r, r + STRIP)
                g = grad_ref[pl.ds(pl.multiple_of(c * BLK + r, STRIP), STRIP), head_cols(h)]
                dot = jnp.sum(
                    g.astype(jnp.float32) * att_s[at, head_cols(h)].astype(jnp.float32), axis=1, keepdims=True
                )
                ds_s[h % 2, at, :] = (e_s[h % 2, at, :] * ((dp_s[h % 3, at, :] - dot) * scale)).astype(jnp.bfloat16)
            dq_s[:, head_cols(h)] = dot_nn(ds_s[h % 2], k_all[...]).astype(jnp.bfloat16)

        scores(0)
        prob_grads(0)
        for h in range(heads + 1):
            if h < heads:
                softmax(h)
            if h + 1 < heads:
                scores(h + 1)
                prob_grads(h + 1)
            if h > 0:
                score_grads(h - 1)
            if h < heads:
                attend_head(h)
        g_t = jnp.concatenate([grad_t_ref[h * HD : (h + 1) * HD, rows] for h in range(heads)], 1)
        dv = dot_nn(g_t, p_s[...])
        dv_s[...] += dv[:, :seen]
        dv_own = dv[:, seen:]
        dq = dq_s[...]
        cot_ref[0:RANK, rows] = dot_nt(qup_ref[...], dq)
        cot_ref[RANK : 2 * RANK, rows] = dot_nn(up_wide, dv_own, HIGHEST)
        cot_ref[2 * RANK :, rows] = dot_nt(tag_ref[...], att_s[...])
        up_ref[:, :query_width] += dot_nn(low_s[0:RANK, rows], dq)
        up_ref[:, query_width:] += dot_nt(low_s[RANK:, rows].astype(jnp.float32), dv_own, HIGHEST)
        return carry

    lax.fori_loop(0, q_s.shape[0] // BLK, span_step, 0)
    dv = dv_s[...]
    mcot = dot_nn(up_wide, dv, HIGHEST)
    low_m = jnp.concatenate([got[b, 2 * BLK : PACK, :] for b in range(peers)], 1).astype(jnp.float32)
    up_ref[:, query_width:] += dot_nt(low_m, dv, HIGHEST)
    for b in range(peers):
        mcot_ref[b] = mcot[:, b * BLK : (b + 1) * BLK]


def own_kernel(peers, asked_ref, back_ref, cot_ref, dep_ref, out_ref, sum_s):
    sum_s[...] = jnp.zeros_like(sum_s)
    for r in range(peers):
        block = asked_ref[r]
        sum_s[block] = sum_s[block] + back_ref[r]
    rows = cot_ref.shape[0]
    out_ref[:rows, :] = cot_ref[...]
    out_ref[rows:, :] = jnp.concatenate([sum_s[m] for m in range(sum_s.shape[0])], 1)


def down_kernel(c0, c1, c2, c3, slab_ref, memory_ref, dep_ref, logit_ref, out_ref):
    cot = (c0[...] + c1[...]) + (c2[...] + c3[...])
    tags = logit_ref.shape[0]
    logit_ref[...] = cot[2 * RANK : 2 * RANK + tags]
    low = cot.astype(jnp.bfloat16)
    both = dot_nn(low[: 2 * RANK], slab_ref[...])
    out_ref[:RANK, :] = both[:RANK]
    out_ref[RANK:, :] = both[RANK:] + dot_nn(low[2 * RANK + tags :], memory_ref[...])


def finish_kernel(d0, d1, u0, u1, query_down_ref, query_up_ref, value_down_ref, value_up_ref):
    down = d0[...] + d1[...]
    up = u0[...] + u1[...]
    query_width = query_up_ref.shape[1]
    query_down_ref[...] = down[:RANK]
    value_down_ref[...] = down[RANK:]
    query_up_ref[...] = up[:, :query_width]
    value_up_ref[...] = up[:, query_width:]


def swap(x, bit, axis="heads"):
    return lax.ppermute(x, axis, [(i, i ^ bit) for i in range(lax.axis_size(axis))])


def split_after(x, cuts, dep):
    rows = x.shape[0] // cuts

    def body(x_ref, dep_ref, *outs):
        for n in range(cuts):
            outs[n][...] = x_ref[n * rows : (n + 1) * rows, :]

    out_shape = [jax.ShapeDtypeStruct((rows, x.shape[1]), x.dtype)] * cuts
    return run(body, "split_rows", out_shape, [vmem(), anywhere()], moved=4 * x.size)(x, dep)


def after(x, dep):
    return pl.pallas_call(
        lambda x_ref, dep_ref, out_ref: None,
        out_shape=jax.ShapeDtypeStruct(x.shape, x.dtype),
        in_specs=[anywhere(), anywhere()],
        out_specs=anywhere(),
        input_output_aliases={0: 0},
        name="in_order",
    )(x, dep)


def anywhere():
    return pl.BlockSpec(memory_space=pl.ANY)


def smem():
    return pl.BlockSpec(memory_space=pltpu.SMEM)


def vmem():
    return pl.BlockSpec(memory_space=pltpu.VMEM)


def shaped(*shape, dtype=jnp.float32):
    return jax.ShapeDtypeStruct(shape, dtype)


def run(body, name, out_shape, in_specs, scratch=(), flops=0, moved=0):
    many = isinstance(out_shape, (tuple, list))
    return pl.pallas_call(
        body,
        out_shape=out_shape,
        in_specs=in_specs,
        out_specs=tuple(vmem() for _ in out_shape) if many else vmem(),
        scratch_shapes=list(scratch),
        compiler_params=pltpu.CompilerParams(vmem_limit_bytes=VMEM_BYTES),
        cost_estimate=pl.CostEstimate(flops=flops, bytes_accessed=moved, transcendentals=0),
        name=name,
    )


def fast(
    slab_tokens,
    memory,
    query_weight,
    key_weight,
    value_weight,
    query_down,
    query_up,
    value_down,
    value_up,
    tag_weight,
    retrieval,
    boundary,
    grad_tags,
):
    tok_rows, width = slab_tokens.shape
    mem_rows = memory.shape[0]
    query_width = query_weight.shape[1]
    heads = query_width // HD
    spans = tok_rows // BLK
    blocks = mem_rows // BLK
    peers = lax.axis_size("tm")
    f32 = jnp.float32
    bf16 = jnp.bfloat16
    mem_cuts, tok_cuts = 2, 2

    mem_far = [swap(m, 2) for m in jnp.split(memory, mem_cuts, 0)]
    mem_near = swap(memory, 1)
    tok_near = swap(slab_tokens, 1)
    tok_far = [swap(x, 2) for x in split_after(slab_tokens, tok_cuts, mem_far[0])]

    named = retrieval[0]
    owner_ids = jnp.arange(peers, dtype=jnp.int32)
    wanted = jnp.sum(
        jnp.where(named[None, :] // blocks == owner_ids[:, None], named[None, :] % blocks, 0), axis=1
    ).astype(jnp.int32)
    asked = lax.all_to_all(wanted, "tm", split_axis=0, concat_axis=0, tiled=True)
    place = lax.axis_index("heads").astype(jnp.int32).reshape(1)

    tag_t = tag_weight.T
    tags = tag_t.shape[0]
    wide_tag = tag_t.astype(f32)
    grad_t = lax.dot_general(
        wide_tag, grad_tags, (((0,), (1,)), ((), ())), precision=HIGHEST
    ).astype(bf16)
    grad = lax.dot_general(grad_tags, wide_tag, (((1,), (0,)), ((), ())), precision=HIGHEST).astype(bf16)

    mem_acc, mem_low = run(
        memory_early_kernel,
        "memory_near_half",
        (shaped(mem_rows, 2 * HD), shaped(mem_rows, RANK)),
        [smem()] + [vmem()] * 5,
        flops=2 * mem_rows * 2 * width * 3 * HD,
        moved=4 * mem_rows * width,
    )(place, memory, mem_near, key_weight, value_weight, value_down)
    rows = tok_rows // tok_cuts
    weights = (query_weight, key_weight, value_weight, query_down, value_down)
    weight_scratch = [
        pltpu.VMEM((2, width, query_width), bf16),
        pltpu.VMEM((2, width, HD), bf16),
        pltpu.VMEM((2, width, HD), bf16),
        pltpu.VMEM((2, RANK, width), bf16),
        pltpu.VMEM((2, RANK, width), bf16),
        pltpu.SemaphoreType.DMA((2, 5)),
    ]
    early = run(
        project_early_kernel,
        "project_near_half",
        (shaped(tok_rows, query_width), shaped(tok_rows, 2 * HD), shaped(tok_rows, 2 * RANK)),
        [smem()] + [vmem()] * 2 + [anywhere()] * 5,
        weight_scratch,
        flops=2 * tok_rows * 2 * width * (query_width + 3 * HD),
        moved=4 * width * (tok_rows + query_width + 3 * HD),
    )(place, slab_tokens, tok_near, *weights)
    mem_far = [mem_far[0]] + [after(m, early[2]) for m in mem_far[1:]]
    mem_cross = [swap(m, 1) for m in mem_far]
    cut_rows = mem_rows // mem_cuts
    before = []
    for t in range(mem_cuts):
        last = t == mem_cuts - 1
        args = [place, asked, mem_far[t], mem_cross[t], mem_acc, mem_low, key_weight, value_weight, value_down, value_up]
        if last:
            args.append(jnp.concatenate(before, 0) if len(before) > 1 else before[0])
            out_shape = shaped(peers, PACK, HD, dtype=bf16)
            scratch = [pltpu.VMEM((blocks, PACK, HD), bf16)]
        else:
            args.append(early[2])
            out_shape = shaped(cut_rows // BLK, PACK, HD, dtype=bf16)
            scratch = []
        result = run(
            lambda *refs, t=t, last=last: memory_kernel(t * cut_rows, peers, last, *refs),
            "memory_pairs",
            out_shape,
            [smem()] * 2 + [vmem()] * (len(args) - 3) + [vmem() if last else anywhere()],
            scratch,
            flops=2 * cut_rows * 2 * width * 3 * HD,
            moved=4 * cut_rows * width,
        )(*args)
        before.append(result)
    got = lax.all_to_all(before[-1], "tm", split_axis=0, concat_axis=0, tiled=True)

    tok_far = [after(x, before[-1]) for x in tok_far]
    tok_cross = [swap(x, 1) for x in tok_far]
    parts = []
    for t in range(tok_cuts):
        parts += run(
            lambda *refs, t=t: project_kernel(t * rows, *refs),
            "project_far_half",
            (
                shaped(rows, query_width, dtype=bf16),
                shaped(rows, HD, dtype=bf16),
                shaped(rows, HD, dtype=bf16),
                shaped(2 * RANK, rows, dtype=bf16),
            ),
            [smem()] + [vmem()] * 2 + [anywhere()] * 5 + [vmem()] * 5,
            weight_scratch,
            flops=2 * rows * 2 * width * (query_width + 3 * HD),
            moved=4 * width * (rows + query_width + 3 * HD),
        )(place, tok_far[t], tok_cross[t], *weights, *early, query_up, value_up)

    seen = peers * BLK
    total = seen + BLK
    cot, ups, mcot = run(
        lambda *refs: attention_kernel(tok_cuts, peers, heads, *refs),
        "span_attention",
        (shaped(2 * RANK + tags, tok_rows), shaped(RANK, query_width + HD), shaped(peers, RANK, BLK)),
        [smem()] + [vmem()] * (4 * tok_cuts + 6),
        [
            pltpu.VMEM((tok_rows, query_width), bf16),
            pltpu.VMEM((tok_rows, HD), bf16),
            pltpu.VMEM((tok_rows, HD), bf16),
            pltpu.VMEM((2 * RANK, tok_rows), bf16),
            pltpu.VMEM((total, HD), bf16),
            pltpu.VMEM((total, HD), bf16),
            pltpu.VMEM((HD, total), bf16),
            pltpu.VMEM((HD, total), bf16),
            pltpu.VMEM((BLK, BLK), f32),
            pltpu.VMEM((2, BLK, total), f32),
            pltpu.VMEM((2, BLK, total), f32),
            pltpu.VMEM((3, BLK, total), f32),
            pltpu.VMEM((heads * BLK, total), bf16),
            pltpu.VMEM((2, BLK, total), bf16),
            pltpu.VMEM((BLK, query_width), bf16),
            pltpu.VMEM((BLK, query_width), bf16),
            pltpu.VMEM((HD, seen), f32),
        ],
        flops=20 * tok_rows * query_width * total,
        moved=4 * tok_rows * query_width,
    )(boundary, *parts, got, query_up, value_up, tag_t, grad, grad_t)

    back = lax.all_to_all(mcot, "tm", split_axis=0, concat_axis=0, tiled=True)
    ups = ups + swap(ups, 1, "tm")
    cots = run(
        lambda *refs: own_kernel(peers, *refs),
        "owned_cotangent",
        shaped(cot.shape[0] + RANK, mem_rows),
        [smem()] + [vmem()] * 2 + [anywhere()],
        [pltpu.VMEM((blocks, RANK, BLK), f32)],
    )(asked, back, cot, ups)
    ups = ups + swap(ups, 2, "tm")
    cots = [cots] + [swap(cots, d) for d in range(1, 4)]
    logits, downs = run(
        down_kernel,
        "down_gradients",
        (shaped(tags, tok_rows), shaped(2 * RANK, width)),
        [vmem()] * 6 + [anywhere()],
        flops=6 * RANK * tok_rows * width,
        moved=4 * tok_rows * width,
    )(*cots, slab_tokens, memory, ups)
    for bit in (1, 2):
        downs = downs + swap(downs, bit, "tm")
    query_down_grad, query_up_grad, value_down_grad, value_up_grad = run(
        finish_kernel,
        "finish_outputs",
        (shaped(RANK, width), shaped(RANK, query_width), shaped(RANK, width), shaped(RANK, HD)),
        [vmem()] * 4,
    )(downs, swap(downs, 4, "tm"), ups, swap(ups, 4, "tm"))
    return (logits.T, query_down_grad, query_up_grad, value_down_grad, value_up_grad)


def solution(mesh):
    in_specs = (
        P("tm", "heads"),
        P("tm", "heads"),
        P(None, "heads"),
        P(None, "heads"),
        P(None, "heads"),
        P(),
        P(None, "heads"),
        P(),
        P(None, "heads"),
        P("heads", None),
        P("tm", None),
        P("tm"),
        P("tm", None),
    )
    out_specs = (
        P("tm", None),
        P(None, "heads"),
        P(None, "heads"),
        P(None, "heads"),
        P(None, "heads"),
    )
    fits = mesh.shape["heads"] == 4 and mesh.shape["tm"] == 8 == TOP * CAP
    local = fast if fits else general
    return jax.shard_map(local, mesh=mesh, in_specs=in_specs, out_specs=out_specs, check_vma=False)
```

```python
import jax
import jax.numpy as jnp
from jax import lax
from jax.experimental import pallas as pl
from jax.experimental.pallas import tpu as pltpu
from jax.sharding import PartitionSpec as P

HD = 128
RANK = 16
TOP = 8
BLK = 128
CAP = 1


HIGHEST = lax.Precision.HIGHEST


def attend(query, all_keys, all_values, split_row, out_grad):
    span_count, row_count, query_width = query.shape
    key_count, kv_width = (all_keys.shape[1], all_keys.shape[2])
    kv_heads = kv_width // HD
    group_size = query_width // kv_width
    score_scale = HD ** (-0.5)
    query_heads = query.reshape(span_count, row_count, kv_heads, group_size, HD)
    key_heads = all_keys.reshape(span_count, key_count, kv_heads, HD)
    value_heads = all_values.reshape(span_count, key_count, kv_heads, HD)
    grad_heads = out_grad.reshape(span_count, row_count, kv_heads, group_size, HD)
    scores = (
        jnp.einsum("crngd,cknd->cngrk", query_heads, key_heads, preferred_element_type=jnp.float32)
        * score_scale
    )
    row_ids = jnp.arange(row_count, dtype=jnp.int32)[:, None]
    col_ids = jnp.arange(BLK, dtype=jnp.int32)[None, :]
    edge_at = split_row[:, None, None]
    local_seen = (col_ids <= row_ids) & ((col_ids >= edge_at) | (row_ids < edge_at))
    visible = jnp.concatenate(
        [jnp.ones((span_count, row_count, key_count - BLK), jnp.bool_), local_seen], axis=2
    )
    scores = jnp.where(visible[:, None, None], scores, -jnp.inf)
    row_max = jnp.max(scores, axis=-1, keepdims=True)
    weights = jnp.exp(scores - row_max)
    probs = weights / jnp.sum(weights, axis=-1, keepdims=True)
    probs_low = probs.astype(jnp.bfloat16)
    attended = jnp.einsum(
        "cngrk,cknd->crngd", probs_low, value_heads, preferred_element_type=jnp.float32
    ).astype(jnp.bfloat16)
    prob_grad = jnp.einsum(
        "crngd,cknd->cngrk", grad_heads, value_heads, preferred_element_type=jnp.float32
    )
    row_dot = jnp.sum(grad_heads.astype(jnp.float32) * attended.astype(jnp.float32), axis=-1)
    row_dot = jnp.transpose(row_dot, (0, 2, 3, 1))[..., None]
    score_grad = (probs * (prob_grad - row_dot) * score_scale).astype(jnp.bfloat16)
    query_grad = jnp.einsum(
        "cngrk,cknd->crngd", score_grad, key_heads, preferred_element_type=jnp.float32
    ).astype(jnp.bfloat16)
    value_grad = jnp.einsum(
        "cngrk,crngd->cknd", probs_low, grad_heads, preferred_element_type=jnp.float32
    )
    return (
        attended.reshape(span_count, row_count, query_width),
        query_grad.reshape(span_count, row_count, query_width),
        value_grad.reshape(span_count, key_count, kv_width),
    )


def choose_slots(needed, places):
    slot_ids = jnp.arange(CAP, dtype=jnp.int32)
    return needed[:, None, :] * (places[:, None, :] == slot_ids[None, :, None]).astype(jnp.int32)


def general(
    slab_tokens,
    memory,
    query_weight,
    key_weight,
    value_weight,
    query_down,
    query_up,
    value_down,
    value_up,
    tag_weight,
    retrieval,
    boundary,
    grad_tags,
):
    tok_rows = slab_tokens.shape[0]
    mem_rows = memory.shape[0]
    query_width = query_weight.shape[1]
    kv_width = key_weight.shape[1]
    span_count = tok_rows // BLK
    block_count = mem_rows // BLK
    pair_weight = jnp.concatenate([key_weight, value_weight], 1)
    adapter_pair = jnp.concatenate([query_down, value_down], 0)
    contract_last = (((1,), (1,)), ((), ()))
    contract_first = (((0,), (0,)), ((), ()))
    token_piece = lax.all_gather(slab_tokens, "heads", axis=1, tiled=True)
    memory_piece = lax.all_gather(memory, "heads", axis=1, tiled=True)
    query_acc = jnp.dot(token_piece, query_weight, preferred_element_type=jnp.float32)
    pair_acc = jnp.dot(token_piece, pair_weight, preferred_element_type=jnp.float32)
    low_acc = lax.dot_general(
        token_piece, adapter_pair, contract_last, preferred_element_type=jnp.float32
    )
    memory_acc = jnp.dot(memory_piece, pair_weight, preferred_element_type=jnp.float32)
    memory_low_acc = lax.dot_general(
        memory_piece, adapter_pair[RANK:], contract_last, preferred_element_type=jnp.float32
    )
    query_acc, pair_acc, low_acc, memory_acc, memory_low_acc = (
        query_acc,
        pair_acc,
        low_acc,
        memory_acc,
        memory_low_acc,
    )
    low_tokens = low_acc.astype(jnp.bfloat16)
    low_query = low_tokens[:, :RANK]
    low_value = low_tokens[:, RANK:]
    queries = (query_acc + jnp.dot(low_query, query_up, preferred_element_type=jnp.float32)).astype(
        jnp.bfloat16
    )
    keys_local = pair_acc[:, :kv_width].astype(jnp.bfloat16)
    values_local = (
        pair_acc[:, kv_width:] + jnp.dot(low_value, value_up, preferred_element_type=jnp.float32)
    ).astype(jnp.bfloat16)
    memory_low = memory_low_acc.astype(jnp.bfloat16)
    memory_pair = (
        jnp.concatenate(
            [
                memory_acc[:, :kv_width],
                memory_acc[:, kv_width:]
                + jnp.dot(memory_low, value_up, preferred_element_type=jnp.float32),
            ],
            1,
        )
        .astype(jnp.bfloat16)
        .reshape(block_count, BLK, 2 * kv_width)
    )
    peer_count = lax.axis_size("tm")
    every_block = jnp.arange(peer_count * block_count, dtype=jnp.int32)
    wanted = (
        jnp.any(retrieval.reshape(-1, 1) == every_block[None, :], axis=0)
        .astype(jnp.int32)
        .reshape(peer_count, block_count)
    )
    places = jnp.cumsum(wanted, axis=1) - wanted
    requested = choose_slots(wanted, places)
    asked_for = lax.all_to_all(requested, "tm", split_axis=0, concat_axis=0, tiled=True)
    rows_needed = retrieval // block_count * CAP + jnp.take(places.reshape(-1), retrieval)
    asked_low = asked_for.astype(jnp.bfloat16)
    outgoing = jnp.einsum(
        "rcm,mbw->rcbw", asked_low, memory_pair, preferred_element_type=jnp.float32
    ).astype(jnp.bfloat16)
    fetched = lax.all_to_all(outgoing, "tm", split_axis=0, concat_axis=0, tiled=True)
    slot_rows = fetched.reshape(peer_count * CAP, BLK, 2 * kv_width)
    picked = jnp.take(slot_rows, rows_needed.reshape(-1), axis=0).reshape(
        span_count, TOP * BLK, 2 * kv_width
    )
    all_keys = jnp.concatenate(
        [picked[..., :kv_width], keys_local.reshape(span_count, BLK, kv_width)], 1
    )
    all_values = jnp.concatenate(
        [picked[..., kv_width:], values_local.reshape(span_count, BLK, kv_width)], 1
    )
    attended_grad = lax.dot_general(
        grad_tags, tag_weight.astype(jnp.float32), contract_last, precision=HIGHEST
    ).astype(jnp.bfloat16)
    attended, query_grad, value_grad = attend(
        queries.reshape(span_count, BLK, query_width),
        all_keys,
        all_values,
        boundary,
        attended_grad.reshape(span_count, BLK, query_width),
    )
    attended = attended.reshape(tok_rows, query_width)
    query_grad = query_grad.reshape(tok_rows, query_width)
    logits_out = lax.psum(
        jnp.dot(attended, tag_weight, preferred_element_type=jnp.float32), "heads"
    )
    local_grad = value_grad[:, TOP * BLK :].reshape(tok_rows, kv_width)
    slot_grads = value_grad[:, : TOP * BLK].reshape(span_count * TOP, BLK * kv_width)
    slot_hits = (
        rows_needed.reshape(-1, 1) == jnp.arange(peer_count * CAP, dtype=jnp.int32)[None, :]
    ).astype(jnp.float32)
    grad_buffer = lax.dot_general(slot_hits, slot_grads, contract_first, precision=HIGHEST).reshape(
        peer_count * CAP, BLK, kv_width
    )
    up_wide = value_up.astype(jnp.float32)
    returned = lax.all_to_all(
        grad_buffer.reshape(peer_count, CAP, BLK, kv_width),
        "tm",
        split_axis=0,
        concat_axis=0,
        tiled=True,
    )
    owned_grad = jnp.einsum(
        "rcm,rcbw->mbw", asked_for.astype(jnp.float32), returned, precision=HIGHEST
    ).reshape(mem_rows, kv_width)
    memory_cot = lax.dot_general(up_wide, owned_grad, contract_last, precision=HIGHEST)
    up_memory = lax.dot_general(
        memory_low.astype(jnp.float32), owned_grad, contract_first, precision=HIGHEST
    )
    query_cot = lax.dot_general(
        query_up, query_grad, contract_last, preferred_element_type=jnp.float32
    )
    value_cot = lax.dot_general(up_wide, local_grad, contract_last, precision=HIGHEST)
    query_cot, value_cot, memory_cot = lax.psum((query_cot, value_cot, memory_cot), "heads")
    query_down_grad = jnp.dot(
        query_cot.astype(jnp.bfloat16), slab_tokens, preferred_element_type=jnp.float32
    )
    value_down_grad = jnp.dot(
        value_cot.astype(jnp.bfloat16), slab_tokens, preferred_element_type=jnp.float32
    ) + jnp.dot(memory_cot.astype(jnp.bfloat16), memory, preferred_element_type=jnp.float32)
    query_up_grad = lax.dot_general(
        low_query, query_grad, contract_first, preferred_element_type=jnp.float32
    )
    value_up_grad = (
        lax.dot_general(
            low_value.astype(jnp.float32), local_grad, contract_first, precision=HIGHEST
        )
        + up_memory
    )
    query_down_grad, query_up_grad, value_down_grad, value_up_grad = lax.psum(
        (query_down_grad, query_up_grad, value_down_grad, value_up_grad), "tm"
    )
    return (logits_out, query_down_grad, query_up_grad, value_down_grad, value_up_grad)


LOG2E = 1.4426950408889634
NT = (((1,), (1,)), ((), ()))
PACK = 2 * BLK + RANK
STRIP = 16
PAIR = 2
MIB = 1024 * 1024


def dot_nt(a, b, precision=None):
    return lax.dot_general(a, b, NT, precision=precision, preferred_element_type=jnp.float32)


def dot_nn(a, b, precision=None):
    return jnp.dot(a, b, precision=precision, preferred_element_type=jnp.float32)


def piece_rows(place_ref, j, width):
    return pl.ds(pl.multiple_of(lax.bitwise_xor(place_ref[0], j) * width, width), width)


def memory_early_kernel(place_ref, x0, x1, wk_ref, wv_ref, down_ref, dep0, dep1, acc_ref, low_ref):
    width = x0.shape[1]
    acc = low = None
    for j, x_ref in enumerate((x0, x1)):
        here = piece_rows(place_ref, j, width)
        x = x_ref[...]
        term = dot_nn(x, jnp.concatenate([wk_ref[here, :], wv_ref[here, :]], 1))
        low_term = dot_nt(x, down_ref[:, here])
        acc = term if acc is None else acc + term
        low = low_term if low is None else low + low_term
    acc_ref[...] = acc
    low_ref[...] = low


def memory_kernel(first, peers, last, place_ref, asked_ref, x2, x3, acc_ref, low_in, wk_ref, wv_ref, down_ref, up_ref, *refs):
    rows, width = x2.shape
    blocks = rows // BLK
    acc = acc_ref[first : first + rows, :]
    low = low_in[first : first + rows, :]
    for j, x_ref in ((2, x2), (3, x3)):
        here = piece_rows(place_ref, j, width)
        x = x_ref[...]
        acc = acc + dot_nn(x, jnp.concatenate([wk_ref[here, :], wv_ref[here, :]], 1))
        low = low + dot_nt(x, down_ref[:, here])
    values = (acc[:, HD:] + dot_nn(low.astype(jnp.bfloat16), up_ref[...])).astype(jnp.bfloat16)
    keys = acc[:, :HD].astype(jnp.bfloat16)
    low_t = jnp.transpose(low).astype(jnp.bfloat16)
    if last:
        before, out_ref, pair_ref = refs
        offset = before.shape[0]
        pair_ref[:offset] = before[...]
    else:
        pair_ref = refs[1]
        offset = 0
    for b in range(blocks):
        at = slice(b * BLK, (b + 1) * BLK)
        pair_ref[offset + b, 0:BLK, :] = keys[at]
        pair_ref[offset + b, BLK : 2 * BLK, :] = values[at]
        pair_ref[offset + b, 2 * BLK : PACK, :] = low_t[:, at]
    if last:
        for r in range(peers):
            out_ref[r] = pair_ref[asked_ref[r]]


def project_terms(place_ref, j, x, weights):
    wq_ref, wk_ref, wv_ref, qd_ref, vd_ref = weights
    here = piece_rows(place_ref, j, x.shape[1])
    return (
        dot_nn(x, wq_ref[here, :]),
        dot_nn(x, jnp.concatenate([wk_ref[here, :], wv_ref[here, :]], 1)),
        dot_nt(x, jnp.concatenate([qd_ref[:, here], vd_ref[:, here]], 0)),
    )


def project_early_kernel(place_ref, x0, x1, *refs):
    weights, outs = refs[:5], refs[7:10]
    for j, x_ref in enumerate((x0, x1)):
        for ref, term in zip(outs, project_terms(place_ref, j, x_ref[...], weights)):
            if j == 0:
                ref[...] = term
            else:
                ref[...] += term


def project_kernel(first, place_ref, x2, x3, *refs):
    weights, (q_in, kv_in, low_in), (qup_ref, vup_ref) = refs[:5], refs[5:8], refs[8:10]
    q_ref, k_ref, v_ref, low_ref = refs[10:14]
    rows = x2.shape[0]
    at = slice(first, first + rows)
    sums = [q_in[at, :], kv_in[at, :], low_in[at, :]]
    for j, x_ref in ((2, x2), (3, x3)):
        sums = [a + b for a, b in zip(sums, project_terms(place_ref, j, x_ref[...], weights))]
    q_acc, kv_acc, low_acc = sums
    low = low_acc.astype(jnp.bfloat16)
    q_ref[...] = (q_acc + dot_nn(low[:, :RANK], qup_ref[...])).astype(jnp.bfloat16)
    k_ref[...] = kv_acc[:, :HD].astype(jnp.bfloat16)
    v_ref[...] = (kv_acc[:, HD:] + dot_nn(low[:, RANK:], vup_ref[...])).astype(jnp.bfloat16)
    low_ref[...] = jnp.transpose(low_acc).astype(jnp.bfloat16)


def attention_kernel(cuts, peers, heads, bound_ref, *refs):
    parts = refs[: 4 * cuts]
    got, qup_ref, vup_ref, tag_ref, grad_ref, grad_t_ref, cot_ref, up_ref, mcot_ref = refs[4 * cuts : 4 * cuts + 9]
    (q_s, k_own, v_own, low_s, k_all, v_all, kt_all, vt_all, kt_own, vt_own, bias_s, s_s, e_s, dp_s, p_s, ds_s, att_s, dq_s, dv_s) = refs[4 * cuts + 9 :]
    seen = peers * BLK
    for t in range(cuts):
        q_c, k_c, v_c, low_c = parts[4 * t : 4 * t + 4]
        rows = q_c.shape[0]
        at = slice(t * rows, (t + 1) * rows)
        q_s[at, :] = q_c[...]
        k_own[at, :] = k_c[...]
        v_own[at, :] = v_c[...]
        low_s[:, at] = low_c[...]
    for b in range(peers):
        at = slice(b * BLK, (b + 1) * BLK)
        k = got[b, 0:BLK, :]
        v = got[b, BLK : 2 * BLK, :]
        k_all[at, :] = k
        v_all[at, :] = v
        kt_all[:, at] = jnp.transpose(k)
        vt_all[:, at] = jnp.transpose(v)
    dv_s[...] = jnp.zeros_like(dv_s)
    up_ref[...] = jnp.zeros_like(up_ref)
    scale = HD ** (-0.5)
    up_wide = vup_ref[...].astype(jnp.float32)
    query_width = heads * HD

    def pair_step(c, carry):
        base = c * (PAIR * BLK)
        rows = pl.ds(pl.multiple_of(base, PAIR * BLK), PAIR * BLK)
        own_rows = [pl.ds(pl.multiple_of(base + b * BLK, BLK), BLK) for b in range(PAIR)]
        row_ids = lax.broadcasted_iota(jnp.int32, (BLK, BLK), 0)
        col_ids = lax.broadcasted_iota(jnp.int32, (BLK, BLK), 1)
        for b in range(PAIR):
            kt_own[:, b * BLK : (b + 1) * BLK] = jnp.transpose(k_own[own_rows[b], :])
            vt_own[:, b * BLK : (b + 1) * BLK] = jnp.transpose(v_own[own_rows[b], :])
            edge = bound_ref[c * PAIR + b]
            visible = (col_ids <= row_ids) & ((col_ids >= edge) | (row_ids < edge))
            bias_s[b * BLK : (b + 1) * BLK, :] = jnp.where(visible, 0.0, -jnp.inf)

        def head_cols(h):
            return slice(h * HD, (h + 1) * HD)

        def times_keys(out_ref, left_ref, h, all_t, own_t):
            out_ref[:, :seen] = dot_nn(left_ref[rows, head_cols(h)], all_t[...])
            for b in range(PAIR):
                at = slice(b * BLK, (b + 1) * BLK)
                out_ref[at, seen:] = dot_nn(left_ref[own_rows[b], head_cols(h)], own_t[:, at])

        def over_keys(left_ref, first, all_ref, own_ref):
            whole = dot_nn(left_ref[first : first + PAIR * BLK, :seen], all_ref[...])
            mine = [
                dot_nn(left_ref[first + b * BLK : first + (b + 1) * BLK, seen:], own_ref[own_rows[b], :])
                for b in range(PAIR)
            ]
            return (whole + jnp.concatenate(mine, 0)).astype(jnp.bfloat16)

        def scores(h):
            times_keys(s_s.at[h % 2], q_s, h, kt_all, kt_own)

        def prob_grads(h):
            times_keys(dp_s.at[h % 3], grad_ref, h, vt_all, vt_own)

        def softmax(h):
            for r in range(0, PAIR * BLK, STRIP):
                at = slice(r, r + STRIP)
                s = s_s[h % 2, at, :]
                s = jnp.concatenate([s[:, :seen], s[:, seen:] + bias_s[at, :]], 1) * (scale * LOG2E)
                w = jnp.exp2(s - jnp.max(s, axis=1, keepdims=True))
                probs = w * (1.0 / jnp.sum(w, axis=1, keepdims=True))
                e_s[h % 2, at, :] = probs
                first = h * PAIR * BLK + r
                p_s[first : first + STRIP, :] = probs.astype(jnp.bfloat16)

        def attend_head(h):
            att_s[:, head_cols(h)] = over_keys(p_s, h * PAIR * BLK, v_all, v_own)

        def score_grads(h):
            for r in range(0, PAIR * BLK, STRIP):
                at = slice(r, r + STRIP)
                g = grad_ref[pl.ds(pl.multiple_of(base + r, STRIP), STRIP), head_cols(h)]
                dot = jnp.sum(
                    g.astype(jnp.float32) * att_s[at, head_cols(h)].astype(jnp.float32), axis=1, keepdims=True
                )
                ds_s[h % 2, at, :] = (e_s[h % 2, at, :] * ((dp_s[h % 3, at, :] - dot) * scale)).astype(jnp.bfloat16)
            dq_s[:, head_cols(h)] = over_keys(ds_s.at[h % 2], 0, k_all, k_own)

        scores(0)
        prob_grads(0)
        for h in range(heads + 1):
            if h < heads:
                softmax(h)
            if h + 1 < heads:
                scores(h + 1)
                prob_grads(h + 1)
            if h > 0:
                score_grads(h - 1)
            if h < heads:
                attend_head(h)
        g_t = jnp.concatenate([grad_t_ref[h * HD : (h + 1) * HD, rows] for h in range(heads)], 1)
        dv_s[...] += dot_nn(g_t, p_s[:, :seen])
        dv_own = []
        for b in range(PAIR):
            g_b = jnp.concatenate([grad_t_ref[h * HD : (h + 1) * HD, own_rows[b]] for h in range(heads)], 1)
            starts = [(h * PAIR + b) * BLK for h in range(heads)]
            p_b = jnp.concatenate([p_s[n : n + BLK, seen:] for n in starts], 0)
            dv_own.append(dot_nn(g_b, p_b))
        dv_own = jnp.concatenate(dv_own, 1)
        dq = dq_s[...]
        cot_ref[0:RANK, rows] = dot_nt(qup_ref[...], dq)
        cot_ref[RANK : 2 * RANK, rows] = dot_nn(up_wide, dv_own, HIGHEST)
        cot_ref[2 * RANK :, rows] = dot_nt(tag_ref[...], att_s[...])
        up_ref[:, :query_width] += dot_nn(low_s[0:RANK, rows], dq)
        up_ref[:, query_width:] += dot_nt(low_s[RANK:, rows].astype(jnp.float32), dv_own, HIGHEST)
        return carry

    lax.fori_loop(0, q_s.shape[0] // (PAIR * BLK), pair_step, 0)
    dv = dv_s[...]
    mcot = dot_nn(up_wide, dv, HIGHEST)
    low_m = jnp.concatenate([got[b, 2 * BLK : PACK, :] for b in range(peers)], 1).astype(jnp.float32)
    up_ref[:, query_width:] += dot_nt(low_m, dv, HIGHEST)
    for b in range(peers):
        mcot_ref[b] = mcot[:, b * BLK : (b + 1) * BLK]


def own_kernel(peers, asked_ref, back_ref, out_ref, sum_s):
    sum_s[...] = jnp.zeros_like(sum_s)
    for r in range(peers):
        block = asked_ref[r]
        sum_s[block] = sum_s[block] + back_ref[r]
    out_ref[...] = jnp.concatenate([sum_s[m] for m in range(sum_s.shape[0])], 1)


def first_down_kernel(c0, c1, c2, c3, slab_ref, up_ref, dep_ref, logit_ref, query_ref, value_ref):
    cot = (c0[...] + c1[...]) + (c2[...] + c3[...])
    logit_ref[...] = cot[2 * RANK :]
    both = dot_nn(cot[: 2 * RANK].astype(jnp.bfloat16), slab_ref[...])
    width = both.shape[1]
    query_ref[:, :width] = both[:RANK]
    query_ref[:, width:] = up_ref[...]
    value_ref[...] = both[RANK:]


def second_down_kernel(c0, c1, c2, c3, memory_ref, value_ref, out_ref):
    cot = (c0[...] + c1[...]) + (c2[...] + c3[...])
    out_ref[...] = value_ref[...] + dot_nn(cot.astype(jnp.bfloat16), memory_ref[...])


def finish_kernel(q0, q1, v0, v1, query_down_ref, query_up_ref, value_down_ref, value_up_ref):
    query = q0[...] + q1[...]
    value_down_ref[...] = v0[...] + v1[...]
    at = 0
    for out_ref in (query_down_ref, query_up_ref, value_up_ref):
        out_ref[...] = query[:, at : at + out_ref.shape[1]]
        at += out_ref.shape[1]


def swap(x, bit, axis="heads"):
    return lax.ppermute(x, axis, [(i, i ^ bit) for i in range(lax.axis_size(axis))])


def split_after(x, cuts, *deps):
    rows = x.shape[0] // cuts

    def body(x_ref, *refs):
        for n in range(cuts):
            refs[len(deps) + n][...] = x_ref[n * rows : (n + 1) * rows, :]

    out_shape = [jax.ShapeDtypeStruct((rows, x.shape[1]), x.dtype)] * cuts
    return run(body, "split_rows", out_shape, [vmem()] + [anywhere()] * len(deps))(x, *deps)


def after(x, dep):
    return pl.pallas_call(
        lambda x_ref, dep_ref, out_ref: None,
        out_shape=jax.ShapeDtypeStruct(x.shape, x.dtype),
        in_specs=[anywhere(), anywhere()],
        out_specs=anywhere(),
        input_output_aliases={0: 0},
        name="in_order",
    )(x, dep)


def anywhere():
    return pl.BlockSpec(memory_space=pl.ANY)


def smem():
    return pl.BlockSpec(memory_space=pltpu.SMEM)


def vmem():
    return pl.BlockSpec(memory_space=pltpu.VMEM)


def shaped(*shape, dtype=jnp.float32):
    return jax.ShapeDtypeStruct(shape, dtype)


def run(body, name, out_shape, in_specs, scratch=(), flops=0, moved=0, room=8):
    many = isinstance(out_shape, (tuple, list))
    return pl.pallas_call(
        body,
        out_shape=out_shape,
        in_specs=in_specs,
        out_specs=tuple(vmem() for _ in out_shape) if many else vmem(),
        scratch_shapes=list(scratch),
        compiler_params=pltpu.CompilerParams(vmem_limit_bytes=room * MIB),
        cost_estimate=pl.CostEstimate(flops=flops, bytes_accessed=moved, transcendentals=0),
        name=name,
    )


def fast(
    slab_tokens,
    memory,
    query_weight,
    key_weight,
    value_weight,
    query_down,
    query_up,
    value_down,
    value_up,
    tag_weight,
    retrieval,
    boundary,
    grad_tags,
):
    tok_rows, width = slab_tokens.shape
    mem_rows = memory.shape[0]
    query_width = query_weight.shape[1]
    heads = query_width // HD
    spans = tok_rows // BLK
    blocks = mem_rows // BLK
    peers = lax.axis_size("tm")
    f32 = jnp.float32
    bf16 = jnp.bfloat16
    mem_cuts, tok_cuts = 2, 2

    named = retrieval[0]
    owner_ids = jnp.arange(peers, dtype=jnp.int32)
    wanted = jnp.sum(
        jnp.where(named[None, :] // blocks == owner_ids[:, None], named[None, :] % blocks, 0), axis=1
    ).astype(jnp.int32)
    asked = lax.all_to_all(wanted, "tm", split_axis=0, concat_axis=0, tiled=True)
    place = lax.axis_index("heads").astype(jnp.int32).reshape(1)

    tag_t = tag_weight.T
    tags = tag_t.shape[0]
    wide_tag = tag_t.astype(f32)
    grad_t = lax.dot_general(
        wide_tag, grad_tags, (((0,), (1,)), ((), ())), precision=HIGHEST
    ).astype(bf16)
    grad = lax.dot_general(grad_tags, wide_tag, (((1,), (0,)), ((), ())), precision=HIGHEST).astype(bf16)

    mem_split = split_after(memory, mem_cuts)
    mem_far = [swap(m, 2) for m in mem_split]
    mem_near = swap(memory, 1)
    tok_near = swap(slab_tokens, 1)
    mem_acc, mem_low = run(
        memory_early_kernel,
        "memory_near_half",
        (shaped(mem_rows, 2 * HD), shaped(mem_rows, RANK)),
        [smem()] + [vmem()] * 5 + [anywhere()] * 2,
        room=16,
    )(place, memory, mem_near, key_weight, value_weight, value_down, grad, grad_t)
    tok_split = split_after(slab_tokens, tok_cuts, mem_split[-1])
    tok_far = [swap(x, 2) for x in tok_split]

    rows = tok_rows // tok_cuts
    weights = (query_weight, key_weight, value_weight, query_down, value_down)
    early = run(
        project_early_kernel,
        "project_near_half",
        (shaped(tok_rows, query_width), shaped(tok_rows, 2 * HD), shaped(tok_rows, 2 * RANK)),
        [smem()] + [vmem()] * 7 + [anywhere()] * 2,
        room=16,
    )(place, slab_tokens, tok_near, *weights, mem_low, asked)
    mem_far = [mem_far[0]] + [after(m, early[2]) for m in mem_far[1:]]
    mem_cross = [swap(m, 1) for m in mem_far]
    cut_rows = mem_rows // mem_cuts
    before = []
    for t in range(mem_cuts):
        last = t == mem_cuts - 1
        args = [place, asked if last else place, mem_far[t], mem_cross[t], mem_acc, mem_low, key_weight, value_weight, value_down, value_up]
        if last:
            args.append(jnp.concatenate(before, 0) if len(before) > 1 else before[0])
            out_shape = shaped(peers, PACK, HD, dtype=bf16)
            scratch = [pltpu.VMEM((blocks, PACK, HD), bf16)]
        else:
            args.append(early[2])
            out_shape = shaped(cut_rows // BLK, PACK, HD, dtype=bf16)
            scratch = []
        result = run(
            lambda *refs, t=t, last=last: memory_kernel(t * cut_rows, peers, last, *refs),
            "memory_pairs",
            out_shape,
            [smem()] * 2 + [vmem()] * 8 + [vmem() if last else anywhere()],
            scratch,
            room=16,
        )(*args)
        before.append(result)
    got = lax.all_to_all(before[-1], "tm", split_axis=0, concat_axis=0, tiled=True)

    tok_far = [after(x, before[-1]) for x in tok_far]
    tok_cross = [swap(x, 1) for x in tok_far]
    parts = []
    for t in range(tok_cuts):
        parts += run(
            lambda *refs, t=t: project_kernel(t * rows, *refs),
            "project_far_half",
            (
                shaped(rows, query_width, dtype=bf16),
                shaped(rows, HD, dtype=bf16),
                shaped(rows, HD, dtype=bf16),
                shaped(2 * RANK, rows, dtype=bf16),
            ),
            [smem()] + [vmem()] * 12,
            flops=2 * rows * 2 * width * (query_width + 3 * HD),
            moved=4 * width * (rows + query_width + 3 * HD),
            room=16,
        )(place, tok_far[t], tok_cross[t], *weights, *early, query_up, value_up)

    seen = peers * BLK
    total = seen + BLK
    cot, ups, mcot = run(
        lambda *refs: attention_kernel(tok_cuts, peers, heads, *refs),
        "span_attention",
        (shaped(2 * RANK + tags, tok_rows), shaped(RANK, query_width + HD), shaped(peers, RANK, BLK)),
        [smem()] + [vmem()] * (4 * tok_cuts + 6),
        [
            pltpu.VMEM((tok_rows, query_width), bf16),
            pltpu.VMEM((tok_rows, HD), bf16),
            pltpu.VMEM((tok_rows, HD), bf16),
            pltpu.VMEM((2 * RANK, tok_rows), bf16),
            pltpu.VMEM((seen, HD), bf16),
            pltpu.VMEM((seen, HD), bf16),
            pltpu.VMEM((HD, seen), bf16),
            pltpu.VMEM((HD, seen), bf16),
            pltpu.VMEM((HD, PAIR * BLK), bf16),
            pltpu.VMEM((HD, PAIR * BLK), bf16),
            pltpu.VMEM((PAIR * BLK, BLK), f32),
            pltpu.VMEM((2, PAIR * BLK, total), f32),
            pltpu.VMEM((2, PAIR * BLK, total), f32),
            pltpu.VMEM((3, PAIR * BLK, total), f32),
            pltpu.VMEM((heads * PAIR * BLK, total), bf16),
            pltpu.VMEM((2, PAIR * BLK, total), bf16),
            pltpu.VMEM((PAIR * BLK, query_width), bf16),
            pltpu.VMEM((PAIR * BLK, query_width), bf16),
            pltpu.VMEM((HD, seen), f32),
        ],
        flops=20 * tok_rows * query_width * total,
        moved=4 * tok_rows * query_width,
        room=28,
    )(boundary, *parts, got, query_up, value_up, tag_t, grad, grad_t)

    back = lax.all_to_all(mcot, "tm", split_axis=0, concat_axis=0, tiled=True)
    cots = [cot] + [swap(cot, d) for d in range(1, 4)]
    own = run(
        lambda *refs: own_kernel(peers, *refs),
        "owned_cotangent",
        shaped(RANK, mem_rows),
        [smem()] + [vmem()],
        [pltpu.VMEM((blocks, RANK, BLK), f32)],
    )(asked, back)
    logits, query_sum, value_part = run(
        first_down_kernel,
        "first_down",
        (shaped(tags, tok_rows), shaped(RANK, width + ups.shape[1]), shaped(RANK, width)),
        [vmem()] * 6 + [anywhere()],
        flops=4 * RANK * tok_rows * width,
        moved=2 * tok_rows * width,
    )(*cots, slab_tokens, ups, own)
    owns = [own] + [swap(own, d) for d in range(1, 4)]
    value_sum = run(
        second_down_kernel,
        "second_down",
        shaped(RANK, width),
        [vmem()] * 6,
        flops=2 * RANK * mem_rows * width,
        moved=2 * mem_rows * width,
    )(*owns, memory, value_part)
    for bit in (1, 2):
        query_sum = query_sum + swap(query_sum, bit, "tm")
        value_sum = value_sum + swap(value_sum, bit, "tm")
    query_down_grad, query_up_grad, value_down_grad, value_up_grad = run(
        finish_kernel,
        "finish_outputs",
        (shaped(RANK, width), shaped(RANK, query_width), shaped(RANK, width), shaped(RANK, HD)),
        [vmem()] * 4,
    )(query_sum, swap(query_sum, 4, "tm"), value_sum, swap(value_sum, 4, "tm"))
    return (logits.T, query_down_grad, query_up_grad, value_down_grad, value_up_grad)


def solution(mesh):
    in_specs = (
        P("tm", "heads"),
        P("tm", "heads"),
        P(None, "heads"),
        P(None, "heads"),
        P(None, "heads"),
        P(),
        P(None, "heads"),
        P(),
        P(None, "heads"),
        P("heads", None),
        P("tm", None),
        P("tm"),
        P("tm", None),
    )
    out_specs = (
        P("tm", None),
        P(None, "heads"),
        P(None, "heads"),
        P(None, "heads"),
        P(None, "heads"),
    )
    fits = mesh.shape["heads"] == 4 and mesh.shape["tm"] == 8 == TOP * CAP
    local = fast if fits else general
    return jax.shard_map(local, mesh=mesh, in_specs=in_specs, out_specs=out_specs, check_vma=False)
```

```python
import jax
import jax.numpy as jnp
from jax import lax
from jax.experimental import pallas as pl
from jax.experimental.pallas import tpu as pltpu
from jax.sharding import PartitionSpec as P

HD = 128
RANK = 16
TOP = 8
BLK = 128
CAP = 1


HIGHEST = lax.Precision.HIGHEST


def attend(query, all_keys, all_values, split_row, out_grad):
    span_count, row_count, query_width = query.shape
    key_count, kv_width = (all_keys.shape[1], all_keys.shape[2])
    kv_heads = kv_width // HD
    group_size = query_width // kv_width
    score_scale = HD ** (-0.5)
    query_heads = query.reshape(span_count, row_count, kv_heads, group_size, HD)
    key_heads = all_keys.reshape(span_count, key_count, kv_heads, HD)
    value_heads = all_values.reshape(span_count, key_count, kv_heads, HD)
    grad_heads = out_grad.reshape(span_count, row_count, kv_heads, group_size, HD)
    scores = (
        jnp.einsum("crngd,cknd->cngrk", query_heads, key_heads, preferred_element_type=jnp.float32)
        * score_scale
    )
    row_ids = jnp.arange(row_count, dtype=jnp.int32)[:, None]
    col_ids = jnp.arange(BLK, dtype=jnp.int32)[None, :]
    edge_at = split_row[:, None, None]
    local_seen = (col_ids <= row_ids) & ((col_ids >= edge_at) | (row_ids < edge_at))
    visible = jnp.concatenate(
        [jnp.ones((span_count, row_count, key_count - BLK), jnp.bool_), local_seen], axis=2
    )
    scores = jnp.where(visible[:, None, None], scores, -jnp.inf)
    row_max = jnp.max(scores, axis=-1, keepdims=True)
    weights = jnp.exp(scores - row_max)
    probs = weights / jnp.sum(weights, axis=-1, keepdims=True)
    probs_low = probs.astype(jnp.bfloat16)
    attended = jnp.einsum(
        "cngrk,cknd->crngd", probs_low, value_heads, preferred_element_type=jnp.float32
    ).astype(jnp.bfloat16)
    prob_grad = jnp.einsum(
        "crngd,cknd->cngrk", grad_heads, value_heads, preferred_element_type=jnp.float32
    )
    row_dot = jnp.sum(grad_heads.astype(jnp.float32) * attended.astype(jnp.float32), axis=-1)
    row_dot = jnp.transpose(row_dot, (0, 2, 3, 1))[..., None]
    score_grad = (probs * (prob_grad - row_dot) * score_scale).astype(jnp.bfloat16)
    query_grad = jnp.einsum(
        "cngrk,cknd->crngd", score_grad, key_heads, preferred_element_type=jnp.float32
    ).astype(jnp.bfloat16)
    value_grad = jnp.einsum(
        "cngrk,crngd->cknd", probs_low, grad_heads, preferred_element_type=jnp.float32
    )
    return (
        attended.reshape(span_count, row_count, query_width),
        query_grad.reshape(span_count, row_count, query_width),
        value_grad.reshape(span_count, key_count, kv_width),
    )


def choose_slots(needed, places):
    slot_ids = jnp.arange(CAP, dtype=jnp.int32)
    return needed[:, None, :] * (places[:, None, :] == slot_ids[None, :, None]).astype(jnp.int32)


def general(
    slab_tokens,
    memory,
    query_weight,
    key_weight,
    value_weight,
    query_down,
    query_up,
    value_down,
    value_up,
    tag_weight,
    retrieval,
    boundary,
    grad_tags,
):
    tok_rows = slab_tokens.shape[0]
    mem_rows = memory.shape[0]
    query_width = query_weight.shape[1]
    kv_width = key_weight.shape[1]
    span_count = tok_rows // BLK
    block_count = mem_rows // BLK
    pair_weight = jnp.concatenate([key_weight, value_weight], 1)
    adapter_pair = jnp.concatenate([query_down, value_down], 0)
    contract_last = (((1,), (1,)), ((), ()))
    contract_first = (((0,), (0,)), ((), ()))
    token_piece = lax.all_gather(slab_tokens, "heads", axis=1, tiled=True)
    memory_piece = lax.all_gather(memory, "heads", axis=1, tiled=True)
    query_acc = jnp.dot(token_piece, query_weight, preferred_element_type=jnp.float32)
    pair_acc = jnp.dot(token_piece, pair_weight, preferred_element_type=jnp.float32)
    low_acc = lax.dot_general(
        token_piece, adapter_pair, contract_last, preferred_element_type=jnp.float32
    )
    memory_acc = jnp.dot(memory_piece, pair_weight, preferred_element_type=jnp.float32)
    memory_low_acc = lax.dot_general(
        memory_piece, adapter_pair[RANK:], contract_last, preferred_element_type=jnp.float32
    )
    query_acc, pair_acc, low_acc, memory_acc, memory_low_acc = (
        query_acc,
        pair_acc,
        low_acc,
        memory_acc,
        memory_low_acc,
    )
    low_tokens = low_acc.astype(jnp.bfloat16)
    low_query = low_tokens[:, :RANK]
    low_value = low_tokens[:, RANK:]
    queries = (query_acc + jnp.dot(low_query, query_up, preferred_element_type=jnp.float32)).astype(
        jnp.bfloat16
    )
    keys_local = pair_acc[:, :kv_width].astype(jnp.bfloat16)
    values_local = (
        pair_acc[:, kv_width:] + jnp.dot(low_value, value_up, preferred_element_type=jnp.float32)
    ).astype(jnp.bfloat16)
    memory_low = memory_low_acc.astype(jnp.bfloat16)
    memory_pair = (
        jnp.concatenate(
            [
                memory_acc[:, :kv_width],
                memory_acc[:, kv_width:]
                + jnp.dot(memory_low, value_up, preferred_element_type=jnp.float32),
            ],
            1,
        )
        .astype(jnp.bfloat16)
        .reshape(block_count, BLK, 2 * kv_width)
    )
    peer_count = lax.axis_size("tm")
    every_block = jnp.arange(peer_count * block_count, dtype=jnp.int32)
    wanted = (
        jnp.any(retrieval.reshape(-1, 1) == every_block[None, :], axis=0)
        .astype(jnp.int32)
        .reshape(peer_count, block_count)
    )
    places = jnp.cumsum(wanted, axis=1) - wanted
    requested = choose_slots(wanted, places)
    asked_for = lax.all_to_all(requested, "tm", split_axis=0, concat_axis=0, tiled=True)
    rows_needed = retrieval // block_count * CAP + jnp.take(places.reshape(-1), retrieval)
    asked_low = asked_for.astype(jnp.bfloat16)
    outgoing = jnp.einsum(
        "rcm,mbw->rcbw", asked_low, memory_pair, preferred_element_type=jnp.float32
    ).astype(jnp.bfloat16)
    fetched = lax.all_to_all(outgoing, "tm", split_axis=0, concat_axis=0, tiled=True)
    slot_rows = fetched.reshape(peer_count * CAP, BLK, 2 * kv_width)
    picked = jnp.take(slot_rows, rows_needed.reshape(-1), axis=0).reshape(
        span_count, TOP * BLK, 2 * kv_width
    )
    all_keys = jnp.concatenate(
        [picked[..., :kv_width], keys_local.reshape(span_count, BLK, kv_width)], 1
    )
    all_values = jnp.concatenate(
        [picked[..., kv_width:], values_local.reshape(span_count, BLK, kv_width)], 1
    )
    attended_grad = lax.dot_general(
        grad_tags, tag_weight.astype(jnp.float32), contract_last, precision=HIGHEST
    ).astype(jnp.bfloat16)
    attended, query_grad, value_grad = attend(
        queries.reshape(span_count, BLK, query_width),
        all_keys,
        all_values,
        boundary,
        attended_grad.reshape(span_count, BLK, query_width),
    )
    attended = attended.reshape(tok_rows, query_width)
    query_grad = query_grad.reshape(tok_rows, query_width)
    logits_out = lax.psum(
        jnp.dot(attended, tag_weight, preferred_element_type=jnp.float32), "heads"
    )
    local_grad = value_grad[:, TOP * BLK :].reshape(tok_rows, kv_width)
    slot_grads = value_grad[:, : TOP * BLK].reshape(span_count * TOP, BLK * kv_width)
    slot_hits = (
        rows_needed.reshape(-1, 1) == jnp.arange(peer_count * CAP, dtype=jnp.int32)[None, :]
    ).astype(jnp.float32)
    grad_buffer = lax.dot_general(slot_hits, slot_grads, contract_first, precision=HIGHEST).reshape(
        peer_count * CAP, BLK, kv_width
    )
    up_wide = value_up.astype(jnp.float32)
    returned = lax.all_to_all(
        grad_buffer.reshape(peer_count, CAP, BLK, kv_width),
        "tm",
        split_axis=0,
        concat_axis=0,
        tiled=True,
    )
    owned_grad = jnp.einsum(
        "rcm,rcbw->mbw", asked_for.astype(jnp.float32), returned, precision=HIGHEST
    ).reshape(mem_rows, kv_width)
    memory_cot = lax.dot_general(up_wide, owned_grad, contract_last, precision=HIGHEST)
    up_memory = lax.dot_general(
        memory_low.astype(jnp.float32), owned_grad, contract_first, precision=HIGHEST
    )
    query_cot = lax.dot_general(
        query_up, query_grad, contract_last, preferred_element_type=jnp.float32
    )
    value_cot = lax.dot_general(up_wide, local_grad, contract_last, precision=HIGHEST)
    query_cot, value_cot, memory_cot = lax.psum((query_cot, value_cot, memory_cot), "heads")
    query_down_grad = jnp.dot(
        query_cot.astype(jnp.bfloat16), slab_tokens, preferred_element_type=jnp.float32
    )
    value_down_grad = jnp.dot(
        value_cot.astype(jnp.bfloat16), slab_tokens, preferred_element_type=jnp.float32
    ) + jnp.dot(memory_cot.astype(jnp.bfloat16), memory, preferred_element_type=jnp.float32)
    query_up_grad = lax.dot_general(
        low_query, query_grad, contract_first, preferred_element_type=jnp.float32
    )
    value_up_grad = (
        lax.dot_general(
            low_value.astype(jnp.float32), local_grad, contract_first, precision=HIGHEST
        )
        + up_memory
    )
    query_down_grad, query_up_grad, value_down_grad, value_up_grad = lax.psum(
        (query_down_grad, query_up_grad, value_down_grad, value_up_grad), "tm"
    )
    return (logits_out, query_down_grad, query_up_grad, value_down_grad, value_up_grad)


LOG2E = 1.4426950408889634
NT = (((1,), (1,)), ((), ()))
PACK = 2 * BLK + RANK
STRIP = 16
PAIR = 2
MIB = 1024 * 1024
FLAG = jax.ShapeDtypeStruct((8, 128), jnp.float32)


def dot_nt(a, b, precision=None):
    return lax.dot_general(a, b, NT, precision=precision, preferred_element_type=jnp.float32)


def dot_nn(a, b, precision=None):
    return jnp.dot(a, b, precision=precision, preferred_element_type=jnp.float32)


def piece_rows(place_ref, j, width):
    return pl.ds(pl.multiple_of(lax.bitwise_xor(place_ref[0], j) * width, width), width)


def start_copies(pairs, sems, first=0):
    copies = [pltpu.make_async_copy(src, dst, sems.at[first + n]) for n, (src, dst) in enumerate(pairs)]
    for copy in copies:
        copy.start()
    return copies


def wait_all(copies):
    for copy in copies:
        copy.wait()


def memory_pieces(place_ref, js, xs, hbm, scratch, sems):
    x_s, wk_s, wv_s, down_s = scratch
    width = x_s.shape[2]
    groups = []
    for n, j in enumerate(js):
        here = piece_rows(place_ref, j, width)
        pairs = [
            (xs[n], x_s.at[n]),
            (hbm[0].at[here, :], wk_s.at[n]),
            (hbm[1].at[here, :], wv_s.at[n]),
            (hbm[2].at[:, here], down_s.at[n]),
        ]
        groups.append(start_copies(pairs, sems, 4 * n))
    return groups


def memory_terms(n, scratch):
    x_s, wk_s, wv_s, down_s = scratch
    x = x_s[n]
    return dot_nn(x, jnp.concatenate([wk_s[n], wv_s[n]], 1)), dot_nt(x, down_s[n])


def memory_early_kernel(place_ref, x0, x1, *refs):
    hbm, acc_ref, low_ref, flag_ref, scratch, sems = refs[:3], refs[4], refs[5], refs[6], refs[7:11], refs[11]
    flag_ref[...] = jnp.zeros_like(flag_ref)
    groups = memory_pieces(place_ref, (0, 1), (x0, x1), hbm, scratch, sems)
    for n in range(2):
        wait_all(groups[n])
        term, low_term = memory_terms(n, scratch)
        if n == 0:
            acc_ref[...] = term
            low_ref[...] = low_term
        else:
            acc_ref[...] += term
            low_ref[...] += low_term


def memory_kernel(first, peers, last, place_ref, asked_ref, x2, x3, acc_hbm, low_hbm, *refs):
    hbm, up_ref, other, out_ref, flag_ref = refs[:3], refs[3], refs[4], refs[5], refs[6]
    scratch, sems, acc_s, low_s, acc_sems = refs[7:11], refs[11], refs[12], refs[13], refs[14]
    at = pl.ds(first, x2.shape[0])
    sums = start_copies([(acc_hbm.at[at, :], acc_s), (low_hbm.at[at, :], low_s)], acc_sems)
    groups = memory_pieces(place_ref, (2, 3), (x2, x3), hbm, scratch, sems)
    flag_ref[...] = jnp.zeros_like(flag_ref)
    wait_all(sums)
    acc = acc_s[...]
    low = low_s[...]
    for n in range(2):
        wait_all(groups[n])
        term, low_term = memory_terms(n, scratch)
        acc = acc + term
        low = low + low_term
    values = (acc[:, HD:] + dot_nn(low.astype(jnp.bfloat16), up_ref[...])).astype(jnp.bfloat16)
    keys = acc[:, :HD].astype(jnp.bfloat16)
    low_t = jnp.transpose(low).astype(jnp.bfloat16)
    if last:
        pair_ref = refs[15]
        offset = other.shape[0]
        pair_ref[:offset] = other[...]
    else:
        pair_ref = out_ref
        offset = 0
    for b in range(acc.shape[0] // BLK):
        at = slice(b * BLK, (b + 1) * BLK)
        pair_ref[offset + b, 0:BLK, :] = keys[at]
        pair_ref[offset + b, BLK : 2 * BLK, :] = values[at]
        pair_ref[offset + b, 2 * BLK : PACK, :] = low_t[:, at]
    if last:
        for r in range(peers):
            out_ref[r] = pair_ref[asked_ref[r]]


WQ_CUTS = 4


def project_pieces(place_ref, js, xs, hbm, scratch, sems):
    wq_hbm, wk_hbm, wv_hbm, qd_hbm, vd_hbm = hbm
    x_s, wq_s, wk_s, wv_s, qd_s, vd_s = scratch
    width = x_s.shape[2]
    part = width // WQ_CUTS
    groups = []
    for n, j in enumerate(js):
        here = piece_rows(place_ref, j, width)
        start = lax.bitwise_xor(place_ref[0], j) * width
        pairs = [(xs[n], x_s.at[n])]
        for m in range(WQ_CUTS):
            rows = pl.ds(pl.multiple_of(start + m * part, part), part)
            pairs.append((wq_hbm.at[rows, :], wq_s.at[n, pl.ds(m * part, part), :]))
        pairs += [
            (wk_hbm.at[here, :], wk_s.at[n]),
            (wv_hbm.at[here, :], wv_s.at[n]),
            (qd_hbm.at[:, here], qd_s.at[n]),
            (vd_hbm.at[:, here], vd_s.at[n]),
        ]
        groups.append(start_copies(pairs, sems, len(pairs) * n))
    return groups


def project_terms(n, scratch):
    x_s, wq_s, wk_s, wv_s, qd_s, vd_s = scratch
    x = x_s[n]
    return (
        dot_nn(x, wq_s[n]),
        dot_nn(x, jnp.concatenate([wk_s[n], wv_s[n]], 1)),
        dot_nt(x, jnp.concatenate([qd_s[n], vd_s[n]], 0)),
    )


def project_early_kernel(place_ref, x0, x1, *refs):
    hbm, outs, flag_ref, scratch, sems = refs[:5], refs[7:10], refs[10], refs[11:17], refs[17]
    flag_ref[...] = jnp.zeros_like(flag_ref)
    groups = project_pieces(place_ref, (0, 1), (x0, x1), hbm, scratch, sems)
    for n in range(2):
        wait_all(groups[n])
        for ref, term in zip(outs, project_terms(n, scratch)):
            if n == 0:
                ref[...] = term
            else:
                ref[...] += term


def project_kernel(first, place_ref, x2, x3, *refs):
    hbm, early, (qup_ref, vup_ref) = refs[:5], refs[5:8], refs[8:10]
    q_ref, k_ref, v_ref, low_ref = refs[10:14]
    scratch, sems, sum_refs, sum_sems = refs[14:20], refs[20], refs[21:24], refs[24]
    groups = project_pieces(place_ref, (2, 3), (x2, x3), hbm, scratch, sems)
    at = pl.ds(first, x2.shape[0])
    loads = start_copies([(src.at[at, :], dst) for src, dst in zip(early, sum_refs)], sum_sems)
    for n in range(2):
        wait_all(groups[n])
        if n == 0:
            wait_all(loads)
            sums = [ref[...] for ref in sum_refs]
        sums = [a + b for a, b in zip(sums, project_terms(n, scratch))]
    q_acc, kv_acc, low_acc = sums
    low = low_acc.astype(jnp.bfloat16)
    q_ref[...] = (q_acc + dot_nn(low[:, :RANK], qup_ref[...])).astype(jnp.bfloat16)
    k_ref[...] = kv_acc[:, :HD].astype(jnp.bfloat16)
    v_ref[...] = (kv_acc[:, HD:] + dot_nn(low[:, RANK:], vup_ref[...])).astype(jnp.bfloat16)
    low_ref[...] = jnp.transpose(low_acc).astype(jnp.bfloat16)


def attention_kernel(cuts, peers, heads, bound_ref, *refs):
    parts = refs[: 4 * cuts]
    got, grad_hbm, grad_t_hbm, qup_ref, vup_ref, tag_ref, cot_ref, up_ref, mcot_ref = refs[4 * cuts : 4 * cuts + 9]
    (q_s, k_own, v_own, low_s, low_m_s, grad_ref, grad_t_ref, k_all, v_all, kt_all, vt_all, kt_own, vt_own, bias_s, s_s, e_s, dp_s,
     p_s, ds_s, att_s, dq_s, dv_s, sems) = refs[4 * cuts + 9 :]
    seen = peers * BLK
    pairs = []
    for b in range(peers):
        at = slice(b * BLK, (b + 1) * BLK)
        pairs.append((got.at[b, pl.ds(0, BLK), :], k_all.at[at, :]))
        pairs.append((got.at[b, pl.ds(BLK, BLK), :], v_all.at[at, :]))
        pairs.append((got.at[b, pl.ds(2 * BLK, RANK), :], low_m_s.at[b]))
    for t in range(cuts):
        q_c, k_c, v_c, low_c = parts[4 * t : 4 * t + 4]
        rows = q_c.shape[0]
        at = slice(t * rows, (t + 1) * rows)
        pairs += [(q_c, q_s.at[at, :]), (k_c, k_own.at[at, :]), (v_c, v_own.at[at, :]), (low_c, low_s.at[:, at])]
    pairs += [(grad_hbm, grad_ref), (grad_t_hbm, grad_t_ref)]
    copies = start_copies(pairs, sems)
    wait_all(copies[: 3 * peers])
    for b in range(peers):
        at = slice(b * BLK, (b + 1) * BLK)
        kt_all[:, at] = jnp.transpose(k_all[at, :])
        vt_all[:, at] = jnp.transpose(v_all[at, :])
    wait_all(copies[3 * peers :])
    dv_s[...] = jnp.zeros_like(dv_s)
    up_ref[...] = jnp.zeros_like(up_ref)
    scale = HD ** (-0.5)
    up_wide = vup_ref[...].astype(jnp.float32)
    query_width = heads * HD

    def pair_step(c, carry):
        base = c * (PAIR * BLK)
        rows = pl.ds(pl.multiple_of(base, PAIR * BLK), PAIR * BLK)
        own_rows = [pl.ds(pl.multiple_of(base + b * BLK, BLK), BLK) for b in range(PAIR)]
        row_ids = lax.broadcasted_iota(jnp.int32, (BLK, BLK), 0)
        col_ids = lax.broadcasted_iota(jnp.int32, (BLK, BLK), 1)
        for b in range(PAIR):
            kt_own[:, b * BLK : (b + 1) * BLK] = jnp.transpose(k_own[own_rows[b], :])
            vt_own[:, b * BLK : (b + 1) * BLK] = jnp.transpose(v_own[own_rows[b], :])
            edge = bound_ref[c * PAIR + b]
            visible = (col_ids <= row_ids) & ((col_ids >= edge) | (row_ids < edge))
            bias_s[b * BLK : (b + 1) * BLK, :] = jnp.where(visible, 0.0, -jnp.inf)

        def head_cols(h):
            return slice(h * HD, (h + 1) * HD)

        def times_keys(out_ref, left_ref, h, all_t, own_t):
            out_ref[:, :seen] = dot_nn(left_ref[rows, head_cols(h)], all_t[...])
            for b in range(PAIR):
                at = slice(b * BLK, (b + 1) * BLK)
                out_ref[at, seen:] = dot_nn(left_ref[own_rows[b], head_cols(h)], own_t[:, at])

        def over_keys(left_ref, first, all_ref, own_ref):
            whole = dot_nn(left_ref[first : first + PAIR * BLK, :seen], all_ref[...])
            mine = [
                dot_nn(left_ref[first + b * BLK : first + (b + 1) * BLK, seen:], own_ref[own_rows[b], :])
                for b in range(PAIR)
            ]
            return (whole + jnp.concatenate(mine, 0)).astype(jnp.bfloat16)

        def scores(h):
            times_keys(s_s.at[h % 2], q_s, h, kt_all, kt_own)

        def prob_grads(h):
            times_keys(dp_s.at[h % 3], grad_ref, h, vt_all, vt_own)

        def softmax(h):
            for r in range(0, PAIR * BLK, STRIP):
                at = slice(r, r + STRIP)
                s = s_s[h % 2, at, :]
                s = jnp.concatenate([s[:, :seen], s[:, seen:] + bias_s[at, :]], 1) * (scale * LOG2E)
                w = jnp.exp2(s - jnp.max(s, axis=1, keepdims=True))
                probs = w * (1.0 / jnp.sum(w, axis=1, keepdims=True))
                e_s[h % 2, at, :] = probs
                first = h * PAIR * BLK + r
                p_s[first : first + STRIP, :] = probs.astype(jnp.bfloat16)

        def attend_head(h):
            att_s[:, head_cols(h)] = over_keys(p_s, h * PAIR * BLK, v_all, v_own)

        def score_grads(h):
            for r in range(0, PAIR * BLK, STRIP):
                at = slice(r, r + STRIP)
                g = grad_ref[pl.ds(pl.multiple_of(base + r, STRIP), STRIP), head_cols(h)]
                dot = jnp.sum(
                    g.astype(jnp.float32) * att_s[at, head_cols(h)].astype(jnp.float32), axis=1, keepdims=True
                )
                ds_s[h % 2, at, :] = (e_s[h % 2, at, :] * ((dp_s[h % 3, at, :] - dot) * scale)).astype(jnp.bfloat16)
            dq_s[:, head_cols(h)] = over_keys(ds_s.at[h % 2], 0, k_all, k_own)

        scores(0)
        prob_grads(0)
        for h in range(heads + 1):
            if h < heads:
                softmax(h)
            if h + 1 < heads:
                scores(h + 1)
                prob_grads(h + 1)
            if h > 0:
                score_grads(h - 1)
            if h < heads:
                attend_head(h)
        g_t = jnp.concatenate([grad_t_ref[h * HD : (h + 1) * HD, rows] for h in range(heads)], 1)
        dv_s[...] += dot_nn(g_t, p_s[:, :seen])
        dv_own = []
        for b in range(PAIR):
            g_b = jnp.concatenate([grad_t_ref[h * HD : (h + 1) * HD, own_rows[b]] for h in range(heads)], 1)
            starts = [(h * PAIR + b) * BLK for h in range(heads)]
            p_b = jnp.concatenate([p_s[n : n + BLK, seen:] for n in starts], 0)
            dv_own.append(dot_nn(g_b, p_b))
        dv_own = jnp.concatenate(dv_own, 1)
        dq = dq_s[...]
        cot_ref[0:RANK, rows] = dot_nt(qup_ref[...], dq)
        cot_ref[RANK : 2 * RANK, rows] = dot_nn(up_wide, dv_own, HIGHEST)
        cot_ref[2 * RANK :, rows] = dot_nt(tag_ref[...], att_s[...])
        up_ref[:, :query_width] += dot_nn(low_s[0:RANK, rows], dq)
        up_ref[:, query_width:] += dot_nt(low_s[RANK:, rows].astype(jnp.float32), dv_own, HIGHEST)
        return carry

    lax.fori_loop(0, q_s.shape[0] // (PAIR * BLK), pair_step, 0)
    dv = dv_s[...]
    mcot = dot_nn(up_wide, dv, HIGHEST)
    low_m = jnp.concatenate([low_m_s[b] for b in range(peers)], 1).astype(jnp.float32)
    up_ref[:, query_width:] += dot_nt(low_m, dv, HIGHEST)
    for b in range(peers):
        mcot_ref[b] = mcot[:, b * BLK : (b + 1) * BLK]


def own_kernel(peers, asked_ref, back_ref, out_ref, sum_s):
    sum_s[...] = jnp.zeros_like(sum_s)
    for r in range(peers):
        block = asked_ref[r]
        sum_s[block] = sum_s[block] + back_ref[r]
    out_ref[...] = jnp.concatenate([sum_s[m] for m in range(sum_s.shape[0])], 1)


def first_down_kernel(c0, c1, c2, c3, slab_ref, up_ref, dep_ref, logit_ref, query_ref, value_ref):
    cot = (c0[...] + c1[...]) + (c2[...] + c3[...])
    logit_ref[...] = cot[2 * RANK :]
    both = dot_nn(cot[: 2 * RANK].astype(jnp.bfloat16), slab_ref[...])
    width = both.shape[1]
    query_ref[:, :width] = both[:RANK]
    query_ref[:, width:] = up_ref[...]
    value_ref[...] = both[RANK:]


def second_down_kernel(c0, c1, c2, c3, memory_ref, value_ref, out_ref):
    cot = (c0[...] + c1[...]) + (c2[...] + c3[...])
    out_ref[...] = value_ref[...] + dot_nn(cot.astype(jnp.bfloat16), memory_ref[...])


def finish_kernel(q0, q1, v0, v1, query_down_ref, query_up_ref, value_down_ref, value_up_ref):
    query = q0[...] + q1[...]
    value_down_ref[...] = v0[...] + v1[...]
    at = 0
    for out_ref in (query_down_ref, query_up_ref, value_up_ref):
        out_ref[...] = query[:, at : at + out_ref.shape[1]]
        at += out_ref.shape[1]


def swap(x, bit, axis="heads"):
    return lax.ppermute(x, axis, [(i, i ^ bit) for i in range(lax.axis_size(axis))])


def split_after(x, cuts, *deps):
    rows = x.shape[0] // cuts
    half = rows // 2

    def body(x_ref, *refs):
        outs, flag_ref, sems = refs[len(deps) : len(deps) + cuts], refs[len(deps) + cuts], refs[-1]
        pairs = [
            (x_ref.at[pl.ds(n * rows + m * half, half), :], outs[n].at[pl.ds(m * half, half), :])
            for n in range(cuts)
            for m in range(2)
        ]
        copies = start_copies(pairs, sems)
        flag_ref[...] = jnp.zeros_like(flag_ref)
        wait_all(copies)

    part = jax.ShapeDtypeStruct((rows, x.shape[1]), x.dtype)
    *parts, flag = pl.pallas_call(
        body,
        out_shape=[part] * cuts + [FLAG],
        in_specs=[hbm()] + [anywhere()] * len(deps),
        out_specs=[anywhere()] * cuts + [vmem()],
        scratch_shapes=[pltpu.SemaphoreType.DMA((2 * cuts,))],
        name="split_rows",
    )(x, *deps)
    return parts, flag


def grad_kernel(tag_ref, grad_tags_ref, grad_ref, grad_t_ref, flag_ref):
    first = (((0,), (0,)), ((), ()))
    tag = tag_ref[...].astype(jnp.float32)
    grad_tags = grad_tags_ref[...]
    f32 = jnp.float32
    grad_ref[...] = lax.dot_general(
        grad_tags, tag, first, precision=HIGHEST, preferred_element_type=f32
    ).astype(jnp.bfloat16)
    grad_t_ref[...] = lax.dot_general(
        tag, grad_tags, first, precision=HIGHEST, preferred_element_type=f32
    ).astype(jnp.bfloat16)
    flag_ref[...] = jnp.zeros_like(flag_ref)


def after(x, dep):
    return pl.pallas_call(
        lambda x_ref, dep_ref, out_ref: None,
        out_shape=jax.ShapeDtypeStruct(x.shape, x.dtype),
        in_specs=[anywhere(), anywhere()],
        out_specs=anywhere(),
        input_output_aliases={0: 0},
        name="in_order",
    )(x, dep)


def anywhere():
    return pl.BlockSpec(memory_space=pl.ANY)


def hbm():
    return pl.BlockSpec(memory_space=pltpu.HBM)


def smem():
    return pl.BlockSpec(memory_space=pltpu.SMEM)


def vmem():
    return pl.BlockSpec(memory_space=pltpu.VMEM)


def shaped(*shape, dtype=jnp.float32):
    return jax.ShapeDtypeStruct(shape, dtype)


def run(body, name, out_shape, in_specs, scratch=(), flops=0, moved=0, room=8):
    many = isinstance(out_shape, (tuple, list))
    return pl.pallas_call(
        body,
        out_shape=out_shape,
        in_specs=in_specs,
        out_specs=tuple(vmem() for _ in out_shape) if many else vmem(),
        scratch_shapes=list(scratch),
        compiler_params=pltpu.CompilerParams(vmem_limit_bytes=room * MIB),
        cost_estimate=pl.CostEstimate(flops=flops, bytes_accessed=moved, transcendentals=0),
        name=name,
    )


def fast(
    slab_tokens,
    memory,
    query_weight,
    key_weight,
    value_weight,
    query_down,
    query_up,
    value_down,
    value_up,
    tag_weight,
    retrieval,
    boundary,
    grad_tags,
):
    tok_rows, width = slab_tokens.shape
    mem_rows = memory.shape[0]
    query_width = query_weight.shape[1]
    heads = query_width // HD
    spans = tok_rows // BLK
    blocks = mem_rows // BLK
    peers = lax.axis_size("tm")
    f32 = jnp.float32
    bf16 = jnp.bfloat16
    mem_cuts, tok_cuts = 2, 2

    def memory_scratch(rows):
        return [
            pltpu.VMEM((2, rows, width), bf16),
            pltpu.VMEM((2, width, HD), bf16),
            pltpu.VMEM((2, width, HD), bf16),
            pltpu.VMEM((2, RANK, width), bf16),
            pltpu.SemaphoreType.DMA((8,)),
        ]

    def project_scratch(rows):
        return [
            pltpu.VMEM((2, rows, width), bf16),
            pltpu.VMEM((2, width, query_width), bf16),
            pltpu.VMEM((2, width, HD), bf16),
            pltpu.VMEM((2, width, HD), bf16),
            pltpu.VMEM((2, RANK, width), bf16),
            pltpu.VMEM((2, RANK, width), bf16),
            pltpu.SemaphoreType.DMA((2 * (WQ_CUTS + 5),)),
        ]

    named = retrieval[0]
    owner_ids = jnp.arange(peers, dtype=jnp.int32)
    wanted = jnp.sum(
        jnp.where(named[None, :] // blocks == owner_ids[:, None], named[None, :] % blocks, 0), axis=1
    ).astype(jnp.int32)
    place = lax.axis_index("heads").astype(jnp.int32).reshape(1)
    tag_t = tag_weight.T
    tags = tag_t.shape[0]

    mem_split, split_flag = split_after(memory, mem_cuts)
    mem_far = [swap(m, 2) for m in mem_split]
    mem_near = swap(memory, 1)
    tok_near = swap(slab_tokens, 1)
    grad, grad_t, grad_flag = run(
        grad_kernel,
        "attended_cotangent",
        (shaped(tok_rows, query_width, dtype=bf16), shaped(query_width, tok_rows, dtype=bf16), FLAG),
        [vmem()] * 2,
        room=10,
    )(tag_t, grad_tags.T)
    mem_acc, mem_low, mem_flag = run(
        memory_early_kernel,
        "memory_near_half",
        (shaped(mem_rows, 2 * HD), shaped(mem_rows, RANK), FLAG),
        [smem(), hbm(), anywhere()] + [hbm()] * 3 + [anywhere()],
        memory_scratch(mem_rows),
        room=14,
    )(place, memory, mem_near, key_weight, value_weight, value_down, grad_flag)
    asked = lax.all_to_all(after(wanted, mem_flag), "tm", split_axis=0, concat_axis=0, tiled=True)
    tok_split, _ = split_after(slab_tokens, tok_cuts, split_flag)
    tok_far = [swap(x, 2) for x in tok_split]

    rows = tok_rows // tok_cuts
    weights = (query_weight, key_weight, value_weight, query_down, value_down)
    *early, early_flag = run(
        project_early_kernel,
        "project_near_half",
        (shaped(tok_rows, query_width), shaped(tok_rows, 2 * HD), shaped(tok_rows, 2 * RANK), FLAG),
        [smem(), hbm(), anywhere()] + [hbm()] * 5 + [anywhere()] * 2,
        project_scratch(tok_rows),
        room=24,
    )(place, slab_tokens, tok_near, *weights, mem_flag, asked)
    mem_far = [mem_far[0]] + [after(m, early_flag) for m in mem_far[1:]]
    mem_cross = [swap(m, 1) for m in mem_far]
    cut_rows = mem_rows // mem_cuts
    before = []
    for t in range(mem_cuts):
        last = t == mem_cuts - 1
        scratch = memory_scratch(cut_rows) + [
            pltpu.VMEM((cut_rows, 2 * HD), f32),
            pltpu.VMEM((cut_rows, RANK), f32),
            pltpu.SemaphoreType.DMA((2,)),
        ]
        if last:
            other = jnp.concatenate(before, 0) if len(before) > 1 else before[0]
            out_shape = shaped(peers, PACK, HD, dtype=bf16)
            scratch.append(pltpu.VMEM((blocks, PACK, HD), bf16))
        else:
            other = early_flag
            out_shape = shaped(cut_rows // BLK, PACK, HD, dtype=bf16)
        result, pair_flag = run(
            lambda *refs, t=t, last=last: memory_kernel(t * cut_rows, peers, last, *refs),
            "memory_pairs",
            (out_shape, FLAG),
            [smem()] * 2 + [anywhere()] * 4 + [hbm()] * 3 + [vmem()] * 2,
            scratch,
            room=14,
        )(
            place, asked if last else place, mem_far[t], mem_cross[t], mem_acc, mem_low,
            key_weight, value_weight, value_down, value_up, other,
        )
        before.append(result)
    got = lax.all_to_all(before[-1], "tm", split_axis=0, concat_axis=0, tiled=True)

    tok_far = [after(x, pair_flag) for x in tok_far]
    tok_cross = [swap(x, 1) for x in tok_far]
    parts = []
    for t in range(tok_cuts):
        parts += run(
            lambda *refs, t=t: project_kernel(t * rows, *refs),
            "project_far_half",
            (
                shaped(rows, query_width, dtype=bf16),
                shaped(rows, HD, dtype=bf16),
                shaped(rows, HD, dtype=bf16),
                shaped(2 * RANK, rows, dtype=bf16),
            ),
            [smem()] + [anywhere()] * 2 + [hbm()] * 5 + [anywhere()] * 3 + [vmem()] * 2,
            project_scratch(rows)
            + [
                pltpu.VMEM((rows, query_width), f32),
                pltpu.VMEM((rows, 2 * HD), f32),
                pltpu.VMEM((rows, 2 * RANK), f32),
                pltpu.SemaphoreType.DMA((3,)),
            ],
            flops=2 * rows * 2 * width * (query_width + 3 * HD),
            moved=4 * width * (rows + query_width + 3 * HD),
            room=24,
        )(place, tok_far[t], tok_cross[t], *weights, *early, query_up, value_up)

    seen = peers * BLK
    total = seen + BLK
    cot, ups, mcot = run(
        lambda *refs: attention_kernel(tok_cuts, peers, heads, *refs),
        "span_attention",
        (shaped(2 * RANK + tags, tok_rows), shaped(RANK, query_width + HD), shaped(peers, RANK, BLK)),
        [smem()] + [anywhere()] * (4 * tok_cuts + 3) + [vmem()] * 3,
        [
            pltpu.VMEM((tok_rows, query_width), bf16),
            pltpu.VMEM((tok_rows, HD), bf16),
            pltpu.VMEM((tok_rows, HD), bf16),
            pltpu.VMEM((2 * RANK, tok_rows), bf16),
            pltpu.VMEM((peers, RANK, BLK), bf16),
            pltpu.VMEM((tok_rows, query_width), bf16),
            pltpu.VMEM((query_width, tok_rows), bf16),
            pltpu.VMEM((seen, HD), bf16),
            pltpu.VMEM((seen, HD), bf16),
            pltpu.VMEM((HD, seen), bf16),
            pltpu.VMEM((HD, seen), bf16),
            pltpu.VMEM((HD, PAIR * BLK), bf16),
            pltpu.VMEM((HD, PAIR * BLK), bf16),
            pltpu.VMEM((PAIR * BLK, BLK), f32),
            pltpu.VMEM((2, PAIR * BLK, total), f32),
            pltpu.VMEM((2, PAIR * BLK, total), f32),
            pltpu.VMEM((3, PAIR * BLK, total), f32),
            pltpu.VMEM((heads * PAIR * BLK, total), bf16),
            pltpu.VMEM((2, PAIR * BLK, total), bf16),
            pltpu.VMEM((PAIR * BLK, query_width), bf16),
            pltpu.VMEM((PAIR * BLK, query_width), bf16),
            pltpu.VMEM((HD, seen), f32),
            pltpu.SemaphoreType.DMA((3 * peers + 4 * tok_cuts + 2,)),
        ],
        flops=20 * tok_rows * query_width * total,
        moved=4 * tok_rows * query_width,
        room=34,
    )(boundary, *parts, got, grad, grad_t, query_up, value_up, tag_t)

    back = lax.all_to_all(mcot, "tm", split_axis=0, concat_axis=0, tiled=True)
    cots = [cot] + [swap(cot, d) for d in range(1, 4)]
    own = run(
        lambda *refs: own_kernel(peers, *refs),
        "owned_cotangent",
        shaped(RANK, mem_rows),
        [smem()] + [vmem()],
        [pltpu.VMEM((blocks, RANK, BLK), f32)],
    )(asked, back)
    logits, query_sum, value_part = run(
        first_down_kernel,
        "first_down",
        (shaped(tags, tok_rows), shaped(RANK, width + ups.shape[1]), shaped(RANK, width)),
        [vmem()] * 6 + [anywhere()],
        flops=4 * RANK * tok_rows * width,
        moved=2 * tok_rows * width,
    )(*cots, slab_tokens, ups, own)
    owns = [own] + [swap(own, d) for d in range(1, 4)]
    value_sum = run(
        second_down_kernel,
        "second_down",
        shaped(RANK, width),
        [vmem()] * 6,
        flops=2 * RANK * mem_rows * width,
        moved=2 * mem_rows * width,
    )(*owns, memory, value_part)
    for bit in (1, 2):
        query_sum = query_sum + swap(query_sum, bit, "tm")
        value_sum = value_sum + swap(value_sum, bit, "tm")
    query_down_grad, query_up_grad, value_down_grad, value_up_grad = run(
        finish_kernel,
        "finish_outputs",
        (shaped(RANK, width), shaped(RANK, query_width), shaped(RANK, width), shaped(RANK, HD)),
        [vmem()] * 4,
    )(query_sum, swap(query_sum, 4, "tm"), value_sum, swap(value_sum, 4, "tm"))
    return (logits.T, query_down_grad, query_up_grad, value_down_grad, value_up_grad)


def solution(mesh):
    in_specs = (
        P("tm", "heads"),
        P("tm", "heads"),
        P(None, "heads"),
        P(None, "heads"),
        P(None, "heads"),
        P(),
        P(None, "heads"),
        P(),
        P(None, "heads"),
        P("heads", None),
        P("tm", None),
        P("tm"),
        P("tm", None),
    )
    out_specs = (
        P("tm", None),
        P(None, "heads"),
        P(None, "heads"),
        P(None, "heads"),
        P(None, "heads"),
    )
    fits = mesh.shape["heads"] == 4 and mesh.shape["tm"] == 8 == TOP * CAP
    local = fast if fits else general
    return jax.shard_map(local, mesh=mesh, in_specs=in_specs, out_specs=out_specs, check_vma=False)
```

```python
import jax
import jax.numpy as jnp
from jax import lax
from jax.experimental import pallas as pl
from jax.experimental.pallas import tpu as pltpu
from jax.sharding import PartitionSpec as P

HD = 128
RANK = 16
TOP = 8
BLK = 128
CAP = 1


HIGHEST = lax.Precision.HIGHEST


def attend(query, all_keys, all_values, split_row, out_grad):
    span_count, row_count, query_width = query.shape
    key_count, kv_width = (all_keys.shape[1], all_keys.shape[2])
    kv_heads = kv_width // HD
    group_size = query_width // kv_width
    score_scale = HD ** (-0.5)
    query_heads = query.reshape(span_count, row_count, kv_heads, group_size, HD)
    key_heads = all_keys.reshape(span_count, key_count, kv_heads, HD)
    value_heads = all_values.reshape(span_count, key_count, kv_heads, HD)
    grad_heads = out_grad.reshape(span_count, row_count, kv_heads, group_size, HD)
    scores = (
        jnp.einsum("crngd,cknd->cngrk", query_heads, key_heads, preferred_element_type=jnp.float32)
        * score_scale
    )
    row_ids = jnp.arange(row_count, dtype=jnp.int32)[:, None]
    col_ids = jnp.arange(BLK, dtype=jnp.int32)[None, :]
    edge_at = split_row[:, None, None]
    local_seen = (col_ids <= row_ids) & ((col_ids >= edge_at) | (row_ids < edge_at))
    visible = jnp.concatenate(
        [jnp.ones((span_count, row_count, key_count - BLK), jnp.bool_), local_seen], axis=2
    )
    scores = jnp.where(visible[:, None, None], scores, -jnp.inf)
    row_max = jnp.max(scores, axis=-1, keepdims=True)
    weights = jnp.exp(scores - row_max)
    probs = weights / jnp.sum(weights, axis=-1, keepdims=True)
    probs_low = probs.astype(jnp.bfloat16)
    attended = jnp.einsum(
        "cngrk,cknd->crngd", probs_low, value_heads, preferred_element_type=jnp.float32
    ).astype(jnp.bfloat16)
    prob_grad = jnp.einsum(
        "crngd,cknd->cngrk", grad_heads, value_heads, preferred_element_type=jnp.float32
    )
    row_dot = jnp.sum(grad_heads.astype(jnp.float32) * attended.astype(jnp.float32), axis=-1)
    row_dot = jnp.transpose(row_dot, (0, 2, 3, 1))[..., None]
    score_grad = (probs * (prob_grad - row_dot) * score_scale).astype(jnp.bfloat16)
    query_grad = jnp.einsum(
        "cngrk,cknd->crngd", score_grad, key_heads, preferred_element_type=jnp.float32
    ).astype(jnp.bfloat16)
    value_grad = jnp.einsum(
        "cngrk,crngd->cknd", probs_low, grad_heads, preferred_element_type=jnp.float32
    )
    return (
        attended.reshape(span_count, row_count, query_width),
        query_grad.reshape(span_count, row_count, query_width),
        value_grad.reshape(span_count, key_count, kv_width),
    )


def choose_slots(needed, places):
    slot_ids = jnp.arange(CAP, dtype=jnp.int32)
    return needed[:, None, :] * (places[:, None, :] == slot_ids[None, :, None]).astype(jnp.int32)


def general(
    slab_tokens,
    memory,
    query_weight,
    key_weight,
    value_weight,
    query_down,
    query_up,
    value_down,
    value_up,
    tag_weight,
    retrieval,
    boundary,
    grad_tags,
):
    tok_rows = slab_tokens.shape[0]
    mem_rows = memory.shape[0]
    query_width = query_weight.shape[1]
    kv_width = key_weight.shape[1]
    span_count = tok_rows // BLK
    block_count = mem_rows // BLK
    pair_weight = jnp.concatenate([key_weight, value_weight], 1)
    adapter_pair = jnp.concatenate([query_down, value_down], 0)
    contract_last = (((1,), (1,)), ((), ()))
    contract_first = (((0,), (0,)), ((), ()))
    token_piece = lax.all_gather(slab_tokens, "heads", axis=1, tiled=True)
    memory_piece = lax.all_gather(memory, "heads", axis=1, tiled=True)
    query_acc = jnp.dot(token_piece, query_weight, preferred_element_type=jnp.float32)
    pair_acc = jnp.dot(token_piece, pair_weight, preferred_element_type=jnp.float32)
    low_acc = lax.dot_general(
        token_piece, adapter_pair, contract_last, preferred_element_type=jnp.float32
    )
    memory_acc = jnp.dot(memory_piece, pair_weight, preferred_element_type=jnp.float32)
    memory_low_acc = lax.dot_general(
        memory_piece, adapter_pair[RANK:], contract_last, preferred_element_type=jnp.float32
    )
    query_acc, pair_acc, low_acc, memory_acc, memory_low_acc = (
        query_acc,
        pair_acc,
        low_acc,
        memory_acc,
        memory_low_acc,
    )
    low_tokens = low_acc.astype(jnp.bfloat16)
    low_query = low_tokens[:, :RANK]
    low_value = low_tokens[:, RANK:]
    queries = (query_acc + jnp.dot(low_query, query_up, preferred_element_type=jnp.float32)).astype(
        jnp.bfloat16
    )
    keys_local = pair_acc[:, :kv_width].astype(jnp.bfloat16)
    values_local = (
        pair_acc[:, kv_width:] + jnp.dot(low_value, value_up, preferred_element_type=jnp.float32)
    ).astype(jnp.bfloat16)
    memory_low = memory_low_acc.astype(jnp.bfloat16)
    memory_pair = (
        jnp.concatenate(
            [
                memory_acc[:, :kv_width],
                memory_acc[:, kv_width:]
                + jnp.dot(memory_low, value_up, preferred_element_type=jnp.float32),
            ],
            1,
        )
        .astype(jnp.bfloat16)
        .reshape(block_count, BLK, 2 * kv_width)
    )
    peer_count = lax.axis_size("tm")
    every_block = jnp.arange(peer_count * block_count, dtype=jnp.int32)
    wanted = (
        jnp.any(retrieval.reshape(-1, 1) == every_block[None, :], axis=0)
        .astype(jnp.int32)
        .reshape(peer_count, block_count)
    )
    places = jnp.cumsum(wanted, axis=1) - wanted
    requested = choose_slots(wanted, places)
    asked_for = lax.all_to_all(requested, "tm", split_axis=0, concat_axis=0, tiled=True)
    rows_needed = retrieval // block_count * CAP + jnp.take(places.reshape(-1), retrieval)
    asked_low = asked_for.astype(jnp.bfloat16)
    outgoing = jnp.einsum(
        "rcm,mbw->rcbw", asked_low, memory_pair, preferred_element_type=jnp.float32
    ).astype(jnp.bfloat16)
    fetched = lax.all_to_all(outgoing, "tm", split_axis=0, concat_axis=0, tiled=True)
    slot_rows = fetched.reshape(peer_count * CAP, BLK, 2 * kv_width)
    picked = jnp.take(slot_rows, rows_needed.reshape(-1), axis=0).reshape(
        span_count, TOP * BLK, 2 * kv_width
    )
    all_keys = jnp.concatenate(
        [picked[..., :kv_width], keys_local.reshape(span_count, BLK, kv_width)], 1
    )
    all_values = jnp.concatenate(
        [picked[..., kv_width:], values_local.reshape(span_count, BLK, kv_width)], 1
    )
    attended_grad = lax.dot_general(
        grad_tags, tag_weight.astype(jnp.float32), contract_last, precision=HIGHEST
    ).astype(jnp.bfloat16)
    attended, query_grad, value_grad = attend(
        queries.reshape(span_count, BLK, query_width),
        all_keys,
        all_values,
        boundary,
        attended_grad.reshape(span_count, BLK, query_width),
    )
    attended = attended.reshape(tok_rows, query_width)
    query_grad = query_grad.reshape(tok_rows, query_width)
    logits_out = lax.psum(
        jnp.dot(attended, tag_weight, preferred_element_type=jnp.float32), "heads"
    )
    local_grad = value_grad[:, TOP * BLK :].reshape(tok_rows, kv_width)
    slot_grads = value_grad[:, : TOP * BLK].reshape(span_count * TOP, BLK * kv_width)
    slot_hits = (
        rows_needed.reshape(-1, 1) == jnp.arange(peer_count * CAP, dtype=jnp.int32)[None, :]
    ).astype(jnp.float32)
    grad_buffer = lax.dot_general(slot_hits, slot_grads, contract_first, precision=HIGHEST).reshape(
        peer_count * CAP, BLK, kv_width
    )
    up_wide = value_up.astype(jnp.float32)
    returned = lax.all_to_all(
        grad_buffer.reshape(peer_count, CAP, BLK, kv_width),
        "tm",
        split_axis=0,
        concat_axis=0,
        tiled=True,
    )
    owned_grad = jnp.einsum(
        "rcm,rcbw->mbw", asked_for.astype(jnp.float32), returned, precision=HIGHEST
    ).reshape(mem_rows, kv_width)
    memory_cot = lax.dot_general(up_wide, owned_grad, contract_last, precision=HIGHEST)
    up_memory = lax.dot_general(
        memory_low.astype(jnp.float32), owned_grad, contract_first, precision=HIGHEST
    )
    query_cot = lax.dot_general(
        query_up, query_grad, contract_last, preferred_element_type=jnp.float32
    )
    value_cot = lax.dot_general(up_wide, local_grad, contract_last, precision=HIGHEST)
    query_cot, value_cot, memory_cot = lax.psum((query_cot, value_cot, memory_cot), "heads")
    query_down_grad = jnp.dot(
        query_cot.astype(jnp.bfloat16), slab_tokens, preferred_element_type=jnp.float32
    )
    value_down_grad = jnp.dot(
        value_cot.astype(jnp.bfloat16), slab_tokens, preferred_element_type=jnp.float32
    ) + jnp.dot(memory_cot.astype(jnp.bfloat16), memory, preferred_element_type=jnp.float32)
    query_up_grad = lax.dot_general(
        low_query, query_grad, contract_first, preferred_element_type=jnp.float32
    )
    value_up_grad = (
        lax.dot_general(
            low_value.astype(jnp.float32), local_grad, contract_first, precision=HIGHEST
        )
        + up_memory
    )
    query_down_grad, query_up_grad, value_down_grad, value_up_grad = lax.psum(
        (query_down_grad, query_up_grad, value_down_grad, value_up_grad), "tm"
    )
    return (logits_out, query_down_grad, query_up_grad, value_down_grad, value_up_grad)


LOG2E = 1.4426950408889634
NT = (((1,), (1,)), ((), ()))
PACK = 2 * BLK + RANK
STRIP = 16
PAIR = 2
MIB = 1024 * 1024
ROOM = 60


def dot_nt(a, b, precision=None):
    return lax.dot_general(a, b, NT, precision=precision, preferred_element_type=jnp.float32)


def dot_nn(a, b, precision=None):
    return jnp.dot(a, b, precision=precision, preferred_element_type=jnp.float32)


def piece_rows(place_ref, j, width):
    return pl.ds(pl.multiple_of(lax.bitwise_xor(place_ref[0], j) * width, width), width)


def start_copies(pairs, sems, first=0):
    copies = [pltpu.make_async_copy(src, dst, sems.at[first + n]) for n, (src, dst) in enumerate(pairs)]
    for copy in copies:
        copy.start()
    return copies


def wait_all(copies):
    for copy in copies:
        copy.wait()


def memory_pieces(place_ref, js, xs, hbm, scratch, sems):
    x_s, wk_s, wv_s, down_s = scratch
    width = x_s.shape[2]
    groups = []
    for n, j in enumerate(js):
        here = piece_rows(place_ref, j, width)
        pairs = [
            (xs[n], x_s.at[n]),
            (hbm[0].at[here, :], wk_s.at[n]),
            (hbm[1].at[here, :], wv_s.at[n]),
            (hbm[2].at[:, here], down_s.at[n]),
        ]
        groups.append(start_copies(pairs, sems, 4 * n))
    return groups


def memory_terms(n, scratch):
    x_s, wk_s, wv_s, down_s = scratch
    x = x_s[n]
    return dot_nn(x, jnp.concatenate([wk_s[n], wv_s[n]], 1)), dot_nt(x, down_s[n])


def memory_early_kernel(blocks, place_ref, named_ref, x0, x1, *refs):
    hbm, acc_ref, low_ref, wanted_ref, scratch, sems = refs[:3], refs[3], refs[4], refs[5], refs[6:10], refs[10]
    groups = memory_pieces(place_ref, (0, 1), (x0, x1), hbm, scratch, sems)
    for slot in range(TOP):
        block = named_ref[0, slot]
        wanted_ref[lax.div(block, blocks)] = lax.rem(block, blocks)
    for n in range(2):
        wait_all(groups[n])
        term, low_term = memory_terms(n, scratch)
        if n == 0:
            acc_ref[...] = term
            low_ref[...] = low_term
        else:
            acc_ref[...] += term
            low_ref[...] += low_term


def memory_kernel(peers, place_ref, asked_ref, x2, x3, acc_hbm, low_hbm, *refs):
    hbm, up_ref, out_ref = refs[:3], refs[3], refs[4]
    scratch, sems, acc_s, low_s, acc_sems, pair_ref = refs[5:9], refs[9], refs[10], refs[11], refs[12], refs[13]
    sums = start_copies([(acc_hbm, acc_s), (low_hbm, low_s)], acc_sems)
    groups = memory_pieces(place_ref, (2, 3), (x2, x3), hbm, scratch, sems)
    wait_all(sums)
    acc = acc_s[...]
    low = low_s[...]
    for n in range(2):
        wait_all(groups[n])
        term, low_term = memory_terms(n, scratch)
        acc = acc + term
        low = low + low_term
    values = (acc[:, HD:] + dot_nn(low.astype(jnp.bfloat16), up_ref[...])).astype(jnp.bfloat16)
    keys = acc[:, :HD].astype(jnp.bfloat16)
    low_t = jnp.transpose(low).astype(jnp.bfloat16)
    for b in range(acc.shape[0] // BLK):
        at = slice(b * BLK, (b + 1) * BLK)
        pair_ref[b, 0:BLK, :] = keys[at]
        pair_ref[b, BLK : 2 * BLK, :] = values[at]
        pair_ref[b, 2 * BLK : PACK, :] = low_t[:, at]
    for r in range(peers):
        out_ref[r] = pair_ref[asked_ref[r]]


WQ_CUTS = 4


def project_pieces(place_ref, js, xs, hbm, scratch, sems):
    wq_hbm, wk_hbm, wv_hbm, qd_hbm, vd_hbm = hbm
    x_s, wq_s, wk_s, wv_s, qd_s, vd_s = scratch
    width = x_s.shape[2]
    part = width // WQ_CUTS
    groups = []
    for n, j in enumerate(js):
        here = piece_rows(place_ref, j, width)
        start = lax.bitwise_xor(place_ref[0], j) * width
        pairs = [(xs[n], x_s.at[n])]
        for m in range(WQ_CUTS):
            rows = pl.ds(pl.multiple_of(start + m * part, part), part)
            pairs.append((wq_hbm.at[rows, :], wq_s.at[n, pl.ds(m * part, part), :]))
        pairs += [
            (wk_hbm.at[here, :], wk_s.at[n]),
            (wv_hbm.at[here, :], wv_s.at[n]),
            (qd_hbm.at[:, here], qd_s.at[n]),
            (vd_hbm.at[:, here], vd_s.at[n]),
        ]
        groups.append(start_copies(pairs, sems, len(pairs) * n))
    return groups


def project_terms(n, scratch):
    x_s, wq_s, wk_s, wv_s, qd_s, vd_s = scratch
    x = x_s[n]
    return (
        dot_nn(x, wq_s[n]),
        dot_nn(x, jnp.concatenate([wk_s[n], wv_s[n]], 1)),
        dot_nt(x, jnp.concatenate([qd_s[n], vd_s[n]], 0)),
    )


def project_early_kernel(place_ref, x0, x1, *refs):
    hbm, (tag_ref, tags_t_ref), outs, (grad_ref, grad_t_ref) = refs[:5], refs[5:7], refs[8:11], refs[11:13]
    scratch, sems = refs[13:19], refs[19]
    groups = project_pieces(place_ref, (0, 1), (x0, x1), hbm, scratch, sems)
    first = (((0,), (0,)), ((), ()))
    tag = tag_ref[...].astype(jnp.float32)
    tags_t = tags_t_ref[...]
    f32 = jnp.float32
    grad_ref[...] = lax.dot_general(
        tags_t, tag, first, precision=HIGHEST, preferred_element_type=f32
    ).astype(jnp.bfloat16)
    grad_t_ref[...] = lax.dot_general(
        tag, tags_t, first, precision=HIGHEST, preferred_element_type=f32
    ).astype(jnp.bfloat16)
    for n in range(2):
        wait_all(groups[n])
        for ref, term in zip(outs, project_terms(n, scratch)):
            if n == 0:
                ref[...] = term
            else:
                ref[...] += term


def attention_kernel(peers, heads, place_ref, bound_ref, x3, x2, *refs):
    hbm, early, got, grad_hbm, grad_t_hbm = refs[:5], refs[5:8], refs[8], refs[9], refs[10]
    qup_ref, vup_ref, tag_ref, cot_ref, up_ref, mcot_ref = refs[11:17]
    scratch, sems, sum_refs = refs[17:23], refs[23], refs[24:27]
    (q_s, k_own, v_own, low_s, low_m_s, grad_ref, grad_t_ref, k_all, v_all, kt_all, vt_all, kt_own, vt_own, bias_s, s_s, e_s, dp_s,
     p_s, ds_s, att_s, dq_s, dv_s, more_sems) = refs[27:]
    seen = peers * BLK
    groups = project_pieces(place_ref, (3, 2), (x3, x2), hbm, scratch, sems)
    pairs = list(zip(early, sum_refs))
    for b in range(peers):
        at = slice(b * BLK, (b + 1) * BLK)
        pairs.append((got.at[b, pl.ds(0, BLK), :], k_all.at[at, :]))
        pairs.append((got.at[b, pl.ds(BLK, BLK), :], v_all.at[at, :]))
        pairs.append((got.at[b, pl.ds(2 * BLK, RANK), :], low_m_s.at[b]))
    pairs += [(grad_hbm, grad_ref), (grad_t_hbm, grad_t_ref)]
    copies = start_copies(pairs, more_sems)
    wait_all(groups[0])
    for ref, term in zip(sum_refs, project_terms(0, scratch)):
        if ref is sum_refs[0]:
            wait_all(copies[:3])
        ref[...] += term
    wait_all(groups[1])
    q_acc, kv_acc, low_acc = [ref[...] + term for ref, term in zip(sum_refs, project_terms(1, scratch))]
    low = low_acc.astype(jnp.bfloat16)
    q_s[...] = (q_acc + dot_nn(low[:, :RANK], qup_ref[...])).astype(jnp.bfloat16)
    k_own[...] = kv_acc[:, :HD].astype(jnp.bfloat16)
    v_own[...] = (kv_acc[:, HD:] + dot_nn(low[:, RANK:], vup_ref[...])).astype(jnp.bfloat16)
    low_s[...] = jnp.transpose(low_acc).astype(jnp.bfloat16)
    wait_all(copies[3:])
    for b in range(peers):
        at = slice(b * BLK, (b + 1) * BLK)
        kt_all[:, at] = jnp.transpose(k_all[at, :])
        vt_all[:, at] = jnp.transpose(v_all[at, :])
    dv_s[...] = jnp.zeros_like(dv_s)
    up_ref[...] = jnp.zeros_like(up_ref)
    scale = HD ** (-0.5)
    up_wide = vup_ref[...].astype(jnp.float32)
    query_width = heads * HD

    def pair_step(c, carry):
        base = c * (PAIR * BLK)
        rows = pl.ds(pl.multiple_of(base, PAIR * BLK), PAIR * BLK)
        own_rows = [pl.ds(pl.multiple_of(base + b * BLK, BLK), BLK) for b in range(PAIR)]
        row_ids = lax.broadcasted_iota(jnp.int32, (BLK, BLK), 0)
        col_ids = lax.broadcasted_iota(jnp.int32, (BLK, BLK), 1)
        for b in range(PAIR):
            kt_own[:, b * BLK : (b + 1) * BLK] = jnp.transpose(k_own[own_rows[b], :])
            vt_own[:, b * BLK : (b + 1) * BLK] = jnp.transpose(v_own[own_rows[b], :])
            edge = bound_ref[c * PAIR + b]
            visible = (col_ids <= row_ids) & ((col_ids >= edge) | (row_ids < edge))
            bias_s[b * BLK : (b + 1) * BLK, :] = jnp.where(visible, 0.0, -jnp.inf)

        def head_cols(h):
            return slice(h * HD, (h + 1) * HD)

        def times_keys(out_ref, left_ref, h, all_t, own_t):
            out_ref[:, :seen] = dot_nn(left_ref[rows, head_cols(h)], all_t[...])
            for b in range(PAIR):
                at = slice(b * BLK, (b + 1) * BLK)
                out_ref[at, seen:] = dot_nn(left_ref[own_rows[b], head_cols(h)], own_t[:, at])

        def over_keys(left_ref, first, all_ref, own_ref):
            whole = dot_nn(left_ref[first : first + PAIR * BLK, :seen], all_ref[...])
            mine = [
                dot_nn(left_ref[first + b * BLK : first + (b + 1) * BLK, seen:], own_ref[own_rows[b], :])
                for b in range(PAIR)
            ]
            return (whole + jnp.concatenate(mine, 0)).astype(jnp.bfloat16)

        def scores(h):
            times_keys(s_s.at[h % 2], q_s, h, kt_all, kt_own)

        def prob_grads(h):
            times_keys(dp_s.at[h % 3], grad_ref, h, vt_all, vt_own)

        def softmax(h):
            for r in range(0, PAIR * BLK, STRIP):
                at = slice(r, r + STRIP)
                s = s_s[h % 2, at, :]
                s = jnp.concatenate([s[:, :seen], s[:, seen:] + bias_s[at, :]], 1) * (scale * LOG2E)
                w = jnp.exp2(s - jnp.max(s, axis=1, keepdims=True))
                probs = w * (1.0 / jnp.sum(w, axis=1, keepdims=True))
                e_s[h % 2, at, :] = probs
                first = h * PAIR * BLK + r
                p_s[first : first + STRIP, :] = probs.astype(jnp.bfloat16)

        def attend_head(h):
            att_s[:, head_cols(h)] = over_keys(p_s, h * PAIR * BLK, v_all, v_own)

        def score_grads(h):
            for r in range(0, PAIR * BLK, STRIP):
                at = slice(r, r + STRIP)
                g = grad_ref[pl.ds(pl.multiple_of(base + r, STRIP), STRIP), head_cols(h)]
                dot = jnp.sum(
                    g.astype(jnp.float32) * att_s[at, head_cols(h)].astype(jnp.float32), axis=1, keepdims=True
                )
                ds_s[h % 2, at, :] = (e_s[h % 2, at, :] * ((dp_s[h % 3, at, :] - dot) * scale)).astype(jnp.bfloat16)
            dq_s[:, head_cols(h)] = over_keys(ds_s.at[h % 2], 0, k_all, k_own)

        scores(0)
        prob_grads(0)
        for h in range(heads + 1):
            if h < heads:
                softmax(h)
            if h + 1 < heads:
                scores(h + 1)
                prob_grads(h + 1)
            if h > 0:
                score_grads(h - 1)
            if h < heads:
                attend_head(h)
        g_t = jnp.concatenate([grad_t_ref[h * HD : (h + 1) * HD, rows] for h in range(heads)], 1)
        dv_s[...] += dot_nn(g_t, p_s[:, :seen])
        dv_own = []
        for b in range(PAIR):
            g_b = jnp.concatenate([grad_t_ref[h * HD : (h + 1) * HD, own_rows[b]] for h in range(heads)], 1)
            starts = [(h * PAIR + b) * BLK for h in range(heads)]
            p_b = jnp.concatenate([p_s[n : n + BLK, seen:] for n in starts], 0)
            dv_own.append(dot_nn(g_b, p_b))
        dv_own = jnp.concatenate(dv_own, 1)
        dq = dq_s[...]
        cot_ref[0:RANK, rows] = dot_nt(qup_ref[...], dq)
        cot_ref[RANK : 2 * RANK, rows] = dot_nn(up_wide, dv_own, HIGHEST)
        cot_ref[2 * RANK :, rows] = dot_nt(tag_ref[...], att_s[...])
        up_ref[:, :query_width] += dot_nn(low_s[0:RANK, rows], dq)
        up_ref[:, query_width:] += dot_nt(low_s[RANK:, rows].astype(jnp.float32), dv_own, HIGHEST)
        return carry

    lax.fori_loop(0, q_s.shape[0] // (PAIR * BLK), pair_step, 0)
    dv = dv_s[...]
    mcot = dot_nn(up_wide, dv, HIGHEST)
    low_m = jnp.concatenate([low_m_s[b] for b in range(peers)], 1).astype(jnp.float32)
    up_ref[:, query_width:] += dot_nt(low_m, dv, HIGHEST)
    for b in range(peers):
        mcot_ref[b] = mcot[:, b * BLK : (b + 1) * BLK]


def own_kernel(peers, asked_ref, back_ref, out_ref, sum_s):
    sum_s[...] = jnp.zeros_like(sum_s)
    for r in range(peers):
        block = asked_ref[r]
        sum_s[block] = sum_s[block] + back_ref[r]
    out_ref[...] = jnp.concatenate([sum_s[m] for m in range(sum_s.shape[0])], 1)


def first_down_kernel(c0, c1, c2, c3, slab_ref, up_ref, dep_ref, logit_ref, query_ref, value_ref):
    cot = (c0[...] + c1[...]) + (c2[...] + c3[...])
    logit_ref[...] = cot[2 * RANK :]
    both = dot_nn(cot[: 2 * RANK].astype(jnp.bfloat16), slab_ref[...])
    width = both.shape[1]
    query_ref[:, :width] = both[:RANK]
    query_ref[:, width:] = up_ref[...]
    value_ref[...] = both[RANK:]


def second_down_kernel(c0, c1, c2, c3, memory_ref, value_ref, out_ref):
    cot = (c0[...] + c1[...]) + (c2[...] + c3[...])
    out_ref[...] = value_ref[...] + dot_nn(cot.astype(jnp.bfloat16), memory_ref[...])


def finish_kernel(*refs):
    query, value = [
        (ref[0][...].astype(jnp.float32) + ref[1][...].astype(jnp.float32))
        + (ref[2][...].astype(jnp.float32) + ref[3][...].astype(jnp.float32))
        for ref in (refs[:4], refs[4:8])
    ]
    query_down_ref, query_up_ref, value_down_ref, value_up_ref = refs[8:]
    value_down_ref[...] = value
    at = 0
    for out_ref in (query_down_ref, query_up_ref, value_up_ref):
        out_ref[...] = query[:, at : at + out_ref.shape[1]]
        at += out_ref.shape[1]


def swap(x, bit, axis="heads"):
    return lax.ppermute(x, axis, [(i, i ^ bit) for i in range(lax.axis_size(axis))])


def after(x, dep):
    return pl.pallas_call(
        lambda x_ref, dep_ref, out_ref: None,
        out_shape=jax.ShapeDtypeStruct(x.shape, x.dtype),
        in_specs=[anywhere(), anywhere()],
        out_specs=anywhere(),
        input_output_aliases={0: 0},
        name="in_order",
    )(x, dep)


def anywhere():
    return pl.BlockSpec(memory_space=pl.ANY)


def smem():
    return pl.BlockSpec(memory_space=pltpu.SMEM)


def vmem():
    return pl.BlockSpec(memory_space=pltpu.VMEM)


def shaped(*shape, dtype=jnp.float32):
    return jax.ShapeDtypeStruct(shape, dtype)


def run(body, name, out_shape, in_specs, scratch=(), flops=0, moved=0, room=ROOM, out_specs=None):
    many = isinstance(out_shape, (tuple, list))
    return pl.pallas_call(
        body,
        out_shape=out_shape,
        in_specs=in_specs,
        out_specs=out_specs or (tuple(vmem() for _ in out_shape) if many else vmem()),
        scratch_shapes=list(scratch),
        compiler_params=pltpu.CompilerParams(vmem_limit_bytes=room * MIB),
        cost_estimate=pl.CostEstimate(flops=flops, bytes_accessed=moved, transcendentals=0),
        name=name,
    )


def fast(
    slab_tokens,
    memory,
    query_weight,
    key_weight,
    value_weight,
    query_down,
    query_up,
    value_down,
    value_up,
    tag_weight,
    retrieval,
    boundary,
    grad_tags,
):
    tok_rows, width = slab_tokens.shape
    mem_rows = memory.shape[0]
    query_width = query_weight.shape[1]
    heads = query_width // HD
    spans = tok_rows // BLK
    blocks = mem_rows // BLK
    peers = lax.axis_size("tm")
    f32 = jnp.float32
    bf16 = jnp.bfloat16

    def memory_scratch(rows):
        return [
            pltpu.VMEM((2, rows, width), bf16),
            pltpu.VMEM((2, width, HD), bf16),
            pltpu.VMEM((2, width, HD), bf16),
            pltpu.VMEM((2, RANK, width), bf16),
            pltpu.SemaphoreType.DMA((8,)),
        ]

    def project_scratch(rows):
        return [
            pltpu.VMEM((2, rows, width), bf16),
            pltpu.VMEM((2, width, query_width), bf16),
            pltpu.VMEM((2, width, HD), bf16),
            pltpu.VMEM((2, width, HD), bf16),
            pltpu.VMEM((2, RANK, width), bf16),
            pltpu.VMEM((2, RANK, width), bf16),
            pltpu.SemaphoreType.DMA((2 * (WQ_CUTS + 5),)),
        ]

    place = lax.axis_index("heads").astype(jnp.int32).reshape(1)
    tag_t = tag_weight.T
    tags = tag_t.shape[0]
    mem_far = swap(memory, 2)
    mem_near = swap(memory, 1)
    tok_near = swap(slab_tokens, 1)
    tok_far = swap(tok_near, 2)
    mem_acc, mem_low, wanted = run(
        lambda *refs: memory_early_kernel(blocks, *refs),
        "memory_near_half",
        (shaped(mem_rows, 2 * HD), shaped(mem_rows, RANK), shaped(peers, dtype=jnp.int32)),
        [smem()] * 2 + [anywhere()] * 5,
        memory_scratch(mem_rows),
        out_specs=(vmem(), vmem(), smem()),
    )(place, retrieval, memory, mem_near, key_weight, value_weight, value_down)
    asked = lax.all_to_all(wanted, "tm", split_axis=0, concat_axis=0, tiled=True)
    weights = (query_weight, key_weight, value_weight, query_down, value_down)
    *early, grad, grad_t = run(
        project_early_kernel,
        "project_near_half",
        (
            shaped(tok_rows, query_width),
            shaped(tok_rows, 2 * HD),
            shaped(tok_rows, 2 * RANK),
            shaped(tok_rows, query_width, dtype=bf16),
            shaped(query_width, tok_rows, dtype=bf16),
        ),
        [smem()] + [anywhere()] * 7 + [vmem()] * 2 + [smem()],
        project_scratch(tok_rows),
    )(place, slab_tokens, tok_near, *weights, tag_t, grad_tags.T, wanted)
    mem_far = after(mem_far, early[2])
    mem_cross = swap(mem_far, 1)
    pairs = run(
        lambda *refs: memory_kernel(peers, *refs),
        "memory_pairs",
        shaped(peers, PACK, HD, dtype=bf16),
        [smem()] * 2 + [anywhere()] * 7 + [vmem()],
        memory_scratch(mem_rows)
        + [
            pltpu.VMEM((mem_rows, 2 * HD), f32),
            pltpu.VMEM((mem_rows, RANK), f32),
            pltpu.SemaphoreType.DMA((2,)),
            pltpu.VMEM((blocks, PACK, HD), bf16),
        ],
    )(place, asked, mem_far, mem_cross, mem_acc, mem_low, key_weight, value_weight, value_down, value_up)
    got = lax.all_to_all(pairs, "tm", split_axis=0, concat_axis=0, tiled=True)
    tok_far = after(tok_far, pairs)
    tok_cross = swap(tok_far, 1)

    seen = peers * BLK
    total = seen + BLK
    cot, ups, mcot = run(
        lambda *refs: attention_kernel(peers, heads, *refs),
        "span_attention",
        (shaped(2 * RANK + tags, tok_rows), shaped(RANK, query_width + HD), shaped(peers, RANK, BLK)),
        [smem()] * 2 + [anywhere()] * 13 + [vmem()] * 3,
        project_scratch(tok_rows)
        + [
            pltpu.VMEM((tok_rows, query_width), f32),
            pltpu.VMEM((tok_rows, 2 * HD), f32),
            pltpu.VMEM((tok_rows, 2 * RANK), f32),
            pltpu.VMEM((tok_rows, query_width), bf16),
            pltpu.VMEM((tok_rows, HD), bf16),
            pltpu.VMEM((tok_rows, HD), bf16),
            pltpu.VMEM((2 * RANK, tok_rows), bf16),
            pltpu.VMEM((peers, RANK, BLK), bf16),
            pltpu.VMEM((tok_rows, query_width), bf16),
            pltpu.VMEM((query_width, tok_rows), bf16),
            pltpu.VMEM((seen, HD), bf16),
            pltpu.VMEM((seen, HD), bf16),
            pltpu.VMEM((HD, seen), bf16),
            pltpu.VMEM((HD, seen), bf16),
            pltpu.VMEM((HD, PAIR * BLK), bf16),
            pltpu.VMEM((HD, PAIR * BLK), bf16),
            pltpu.VMEM((PAIR * BLK, BLK), f32),
            pltpu.VMEM((2, PAIR * BLK, total), f32),
            pltpu.VMEM((2, PAIR * BLK, total), f32),
            pltpu.VMEM((3, PAIR * BLK, total), f32),
            pltpu.VMEM((heads * PAIR * BLK, total), bf16),
            pltpu.VMEM((2, PAIR * BLK, total), bf16),
            pltpu.VMEM((PAIR * BLK, query_width), bf16),
            pltpu.VMEM((PAIR * BLK, query_width), bf16),
            pltpu.VMEM((HD, seen), f32),
            pltpu.SemaphoreType.DMA((3 * peers + 5,)),
        ],
        flops=20 * tok_rows * query_width * total,
        moved=4 * tok_rows * query_width,
    )(place, boundary, tok_far, tok_cross, *weights, *early, got, grad, grad_t, query_up, value_up, tag_t)

    back = lax.all_to_all(mcot, "tm", split_axis=0, concat_axis=0, tiled=True)
    cots = [cot] + [swap(cot, d) for d in range(1, 4)]
    own = run(
        lambda *refs: own_kernel(peers, *refs),
        "owned_cotangent",
        shaped(RANK, mem_rows),
        [smem()] + [vmem()],
        [pltpu.VMEM((blocks, RANK, BLK), f32)],
        room=8,
    )(asked, back)
    logits, query_sum, value_part = run(
        first_down_kernel,
        "first_down",
        (shaped(tags, tok_rows), shaped(RANK, width + ups.shape[1]), shaped(RANK, width)),
        [vmem()] * 6 + [anywhere()],
        flops=4 * RANK * tok_rows * width,
        moved=2 * tok_rows * width,
        room=8,
    )(*cots, slab_tokens, ups, own)
    owns = [own] + [swap(own, d) for d in range(1, 4)]
    value_sum = run(
        second_down_kernel,
        "second_down",
        shaped(RANK, width),
        [vmem()] * 6,
        flops=2 * RANK * mem_rows * width,
        moved=2 * mem_rows * width,
        room=8,
    )(*owns, memory, value_part)
    sums = []
    for part in (query_sum, value_sum):
        part = (part + swap(part, 1, "tm")).astype(bf16)
        sums += [part] + [swap(part, bit, "tm") for bit in (2, 4, 6)]
    query_down_grad, query_up_grad, value_down_grad, value_up_grad = run(
        finish_kernel,
        "finish_outputs",
        (shaped(RANK, width), shaped(RANK, query_width), shaped(RANK, width), shaped(RANK, HD)),
        [vmem()] * 8,
        room=8,
    )(*sums)
    return (logits.T, query_down_grad, query_up_grad, value_down_grad, value_up_grad)


def solution(mesh):
    in_specs = (
        P("tm", "heads"),
        P("tm", "heads"),
        P(None, "heads"),
        P(None, "heads"),
        P(None, "heads"),
        P(),
        P(None, "heads"),
        P(),
        P(None, "heads"),
        P("heads", None),
        P("tm", None),
        P("tm"),
        P("tm", None),
    )
    out_specs = (
        P("tm", None),
        P(None, "heads"),
        P(None, "heads"),
        P(None, "heads"),
        P(None, "heads"),
    )
    fits = mesh.shape["heads"] == 4 and mesh.shape["tm"] == 8 == TOP * CAP
    local = fast if fits else general
    return jax.shard_map(local, mesh=mesh, in_specs=in_specs, out_specs=out_specs, check_vma=False)
```

```python
import jax
import jax.numpy as jnp
from jax import lax
from jax.experimental import pallas as pl
from jax.experimental.pallas import tpu as pltpu
from jax.sharding import PartitionSpec as P

HD = 128
RANK = 16
TOP = 8
BLK = 128
CAP = 1


HIGHEST = lax.Precision.HIGHEST


def attend(query, all_keys, all_values, split_row, out_grad):
    span_count, row_count, query_width = query.shape
    key_count, kv_width = (all_keys.shape[1], all_keys.shape[2])
    kv_heads = kv_width // HD
    group_size = query_width // kv_width
    score_scale = HD ** (-0.5)
    query_heads = query.reshape(span_count, row_count, kv_heads, group_size, HD)
    key_heads = all_keys.reshape(span_count, key_count, kv_heads, HD)
    value_heads = all_values.reshape(span_count, key_count, kv_heads, HD)
    grad_heads = out_grad.reshape(span_count, row_count, kv_heads, group_size, HD)
    scores = (
        jnp.einsum("crngd,cknd->cngrk", query_heads, key_heads, preferred_element_type=jnp.float32)
        * score_scale
    )
    row_ids = jnp.arange(row_count, dtype=jnp.int32)[:, None]
    col_ids = jnp.arange(BLK, dtype=jnp.int32)[None, :]
    edge_at = split_row[:, None, None]
    local_seen = (col_ids <= row_ids) & ((col_ids >= edge_at) | (row_ids < edge_at))
    visible = jnp.concatenate(
        [jnp.ones((span_count, row_count, key_count - BLK), jnp.bool_), local_seen], axis=2
    )
    scores = jnp.where(visible[:, None, None], scores, -jnp.inf)
    row_max = jnp.max(scores, axis=-1, keepdims=True)
    weights = jnp.exp(scores - row_max)
    probs = weights / jnp.sum(weights, axis=-1, keepdims=True)
    probs_low = probs.astype(jnp.bfloat16)
    attended = jnp.einsum(
        "cngrk,cknd->crngd", probs_low, value_heads, preferred_element_type=jnp.float32
    ).astype(jnp.bfloat16)
    prob_grad = jnp.einsum(
        "crngd,cknd->cngrk", grad_heads, value_heads, preferred_element_type=jnp.float32
    )
    row_dot = jnp.sum(grad_heads.astype(jnp.float32) * attended.astype(jnp.float32), axis=-1)
    row_dot = jnp.transpose(row_dot, (0, 2, 3, 1))[..., None]
    score_grad = (probs * (prob_grad - row_dot) * score_scale).astype(jnp.bfloat16)
    query_grad = jnp.einsum(
        "cngrk,cknd->crngd", score_grad, key_heads, preferred_element_type=jnp.float32
    ).astype(jnp.bfloat16)
    value_grad = jnp.einsum(
        "cngrk,crngd->cknd", probs_low, grad_heads, preferred_element_type=jnp.float32
    )
    return (
        attended.reshape(span_count, row_count, query_width),
        query_grad.reshape(span_count, row_count, query_width),
        value_grad.reshape(span_count, key_count, kv_width),
    )


def choose_slots(needed, places):
    slot_ids = jnp.arange(CAP, dtype=jnp.int32)
    return needed[:, None, :] * (places[:, None, :] == slot_ids[None, :, None]).astype(jnp.int32)


def general(
    slab_tokens,
    memory,
    query_weight,
    key_weight,
    value_weight,
    query_down,
    query_up,
    value_down,
    value_up,
    tag_weight,
    retrieval,
    boundary,
    grad_tags,
):
    tok_rows = slab_tokens.shape[0]
    mem_rows = memory.shape[0]
    query_width = query_weight.shape[1]
    kv_width = key_weight.shape[1]
    span_count = tok_rows // BLK
    block_count = mem_rows // BLK
    pair_weight = jnp.concatenate([key_weight, value_weight], 1)
    adapter_pair = jnp.concatenate([query_down, value_down], 0)
    contract_last = (((1,), (1,)), ((), ()))
    contract_first = (((0,), (0,)), ((), ()))
    token_piece = lax.all_gather(slab_tokens, "heads", axis=1, tiled=True)
    memory_piece = lax.all_gather(memory, "heads", axis=1, tiled=True)
    query_acc = jnp.dot(token_piece, query_weight, preferred_element_type=jnp.float32)
    pair_acc = jnp.dot(token_piece, pair_weight, preferred_element_type=jnp.float32)
    low_acc = lax.dot_general(
        token_piece, adapter_pair, contract_last, preferred_element_type=jnp.float32
    )
    memory_acc = jnp.dot(memory_piece, pair_weight, preferred_element_type=jnp.float32)
    memory_low_acc = lax.dot_general(
        memory_piece, adapter_pair[RANK:], contract_last, preferred_element_type=jnp.float32
    )
    query_acc, pair_acc, low_acc, memory_acc, memory_low_acc = (
        query_acc,
        pair_acc,
        low_acc,
        memory_acc,
        memory_low_acc,
    )
    low_tokens = low_acc.astype(jnp.bfloat16)
    low_query = low_tokens[:, :RANK]
    low_value = low_tokens[:, RANK:]
    queries = (query_acc + jnp.dot(low_query, query_up, preferred_element_type=jnp.float32)).astype(
        jnp.bfloat16
    )
    keys_local = pair_acc[:, :kv_width].astype(jnp.bfloat16)
    values_local = (
        pair_acc[:, kv_width:] + jnp.dot(low_value, value_up, preferred_element_type=jnp.float32)
    ).astype(jnp.bfloat16)
    memory_low = memory_low_acc.astype(jnp.bfloat16)
    memory_pair = (
        jnp.concatenate(
            [
                memory_acc[:, :kv_width],
                memory_acc[:, kv_width:]
                + jnp.dot(memory_low, value_up, preferred_element_type=jnp.float32),
            ],
            1,
        )
        .astype(jnp.bfloat16)
        .reshape(block_count, BLK, 2 * kv_width)
    )
    peer_count = lax.axis_size("tm")
    every_block = jnp.arange(peer_count * block_count, dtype=jnp.int32)
    wanted = (
        jnp.any(retrieval.reshape(-1, 1) == every_block[None, :], axis=0)
        .astype(jnp.int32)
        .reshape(peer_count, block_count)
    )
    places = jnp.cumsum(wanted, axis=1) - wanted
    requested = choose_slots(wanted, places)
    asked_for = lax.all_to_all(requested, "tm", split_axis=0, concat_axis=0, tiled=True)
    rows_needed = retrieval // block_count * CAP + jnp.take(places.reshape(-1), retrieval)
    asked_low = asked_for.astype(jnp.bfloat16)
    outgoing = jnp.einsum(
        "rcm,mbw->rcbw", asked_low, memory_pair, preferred_element_type=jnp.float32
    ).astype(jnp.bfloat16)
    fetched = lax.all_to_all(outgoing, "tm", split_axis=0, concat_axis=0, tiled=True)
    slot_rows = fetched.reshape(peer_count * CAP, BLK, 2 * kv_width)
    picked = jnp.take(slot_rows, rows_needed.reshape(-1), axis=0).reshape(
        span_count, TOP * BLK, 2 * kv_width
    )
    all_keys = jnp.concatenate(
        [picked[..., :kv_width], keys_local.reshape(span_count, BLK, kv_width)], 1
    )
    all_values = jnp.concatenate(
        [picked[..., kv_width:], values_local.reshape(span_count, BLK, kv_width)], 1
    )
    attended_grad = lax.dot_general(
        grad_tags, tag_weight.astype(jnp.float32), contract_last, precision=HIGHEST
    ).astype(jnp.bfloat16)
    attended, query_grad, value_grad = attend(
        queries.reshape(span_count, BLK, query_width),
        all_keys,
        all_values,
        boundary,
        attended_grad.reshape(span_count, BLK, query_width),
    )
    attended = attended.reshape(tok_rows, query_width)
    query_grad = query_grad.reshape(tok_rows, query_width)
    logits_out = lax.psum(
        jnp.dot(attended, tag_weight, preferred_element_type=jnp.float32), "heads"
    )
    local_grad = value_grad[:, TOP * BLK :].reshape(tok_rows, kv_width)
    slot_grads = value_grad[:, : TOP * BLK].reshape(span_count * TOP, BLK * kv_width)
    slot_hits = (
        rows_needed.reshape(-1, 1) == jnp.arange(peer_count * CAP, dtype=jnp.int32)[None, :]
    ).astype(jnp.float32)
    grad_buffer = lax.dot_general(slot_hits, slot_grads, contract_first, precision=HIGHEST).reshape(
        peer_count * CAP, BLK, kv_width
    )
    up_wide = value_up.astype(jnp.float32)
    returned = lax.all_to_all(
        grad_buffer.reshape(peer_count, CAP, BLK, kv_width),
        "tm",
        split_axis=0,
        concat_axis=0,
        tiled=True,
    )
    owned_grad = jnp.einsum(
        "rcm,rcbw->mbw", asked_for.astype(jnp.float32), returned, precision=HIGHEST
    ).reshape(mem_rows, kv_width)
    memory_cot = lax.dot_general(up_wide, owned_grad, contract_last, precision=HIGHEST)
    up_memory = lax.dot_general(
        memory_low.astype(jnp.float32), owned_grad, contract_first, precision=HIGHEST
    )
    query_cot = lax.dot_general(
        query_up, query_grad, contract_last, preferred_element_type=jnp.float32
    )
    value_cot = lax.dot_general(up_wide, local_grad, contract_last, precision=HIGHEST)
    query_cot, value_cot, memory_cot = lax.psum((query_cot, value_cot, memory_cot), "heads")
    query_down_grad = jnp.dot(
        query_cot.astype(jnp.bfloat16), slab_tokens, preferred_element_type=jnp.float32
    )
    value_down_grad = jnp.dot(
        value_cot.astype(jnp.bfloat16), slab_tokens, preferred_element_type=jnp.float32
    ) + jnp.dot(memory_cot.astype(jnp.bfloat16), memory, preferred_element_type=jnp.float32)
    query_up_grad = lax.dot_general(
        low_query, query_grad, contract_first, preferred_element_type=jnp.float32
    )
    value_up_grad = (
        lax.dot_general(
            low_value.astype(jnp.float32), local_grad, contract_first, precision=HIGHEST
        )
        + up_memory
    )
    query_down_grad, query_up_grad, value_down_grad, value_up_grad = lax.psum(
        (query_down_grad, query_up_grad, value_down_grad, value_up_grad), "tm"
    )
    return (logits_out, query_down_grad, query_up_grad, value_down_grad, value_up_grad)


LOG2E = 1.4426950408889634
NT = (((1,), (1,)), ((), ()))
PACK = 2 * BLK + RANK
STRIP = 16
PAIR = 2
MIB = 1024 * 1024
ROOM = 63


def dot_nt(a, b, precision=None):
    return lax.dot_general(a, b, NT, precision=precision, preferred_element_type=jnp.float32)


def dot_nn(a, b, precision=None):
    return jnp.dot(a, b, precision=precision, preferred_element_type=jnp.float32)


def piece_rows(place_ref, j, width):
    return pl.ds(pl.multiple_of(lax.bitwise_xor(place_ref[0], j) * width, width), width)


def start_copies(pairs, sems, first=0):
    copies = [pltpu.make_async_copy(src, dst, sems.at[first + n]) for n, (src, dst) in enumerate(pairs)]
    for copy in copies:
        copy.start()
    return copies


def wait_all(copies):
    for copy in copies:
        copy.wait()


def memory_pieces(place_ref, js, xs, hbm, scratch, sems):
    x_s, wk_s, wv_s, down_s = scratch
    width = x_s.shape[2]
    groups = []
    for n, j in enumerate(js):
        here = piece_rows(place_ref, j, width)
        pairs = [
            (xs[n], x_s.at[n]),
            (hbm[0].at[here, :], wk_s.at[n]),
            (hbm[1].at[here, :], wv_s.at[n]),
            (hbm[2].at[:, here], down_s.at[n]),
        ]
        groups.append(start_copies(pairs, sems, 4 * n))
    return groups


def memory_terms(n, scratch):
    x_s, wk_s, wv_s, down_s = scratch
    x = x_s[n]
    return dot_nn(x, jnp.concatenate([wk_s[n], wv_s[n]], 1)), dot_nt(x, down_s[n])


def memory_early_kernel(blocks, place_ref, named_ref, x0, x1, *refs):
    hbm, acc_ref, low_ref, wanted_ref, scratch, sems = refs[:3], refs[3], refs[4], refs[5], refs[6:10], refs[10]
    groups = memory_pieces(place_ref, (0, 1), (x0, x1), hbm, scratch, sems)
    for slot in range(TOP):
        block = named_ref[0, slot]
        wanted_ref[lax.div(block, blocks)] = lax.rem(block, blocks)
    for n in range(2):
        wait_all(groups[n])
        term, low_term = memory_terms(n, scratch)
        if n == 0:
            acc_ref[...] = term
            low_ref[...] = low_term
        else:
            acc_ref[...] += term
            low_ref[...] += low_term


def memory_middle_kernel(place_ref, x2, acc_hbm, low_hbm, *refs):
    hbm, acc_ref, low_ref, scratch, sems = refs[:3], refs[3], refs[4], refs[5:9], refs[9]
    acc_s, low_s, acc_sems = refs[10:13]
    groups = memory_pieces(place_ref, (2,), (x2,), hbm, scratch, sems)
    sums = start_copies([(acc_hbm, acc_s), (low_hbm, low_s)], acc_sems)
    wait_all(groups[0])
    term, low_term = memory_terms(0, scratch)
    wait_all(sums)
    acc_ref[...] = acc_s[...] + term
    low_ref[...] = low_s[...] + low_term


def memory_kernel(peers, place_ref, asked_ref, x3, acc_hbm, low_hbm, *refs):
    hbm, up_ref, out_ref = refs[:3], refs[3], refs[4]
    scratch, sems, acc_s, low_s, acc_sems, pair_ref = refs[5:9], refs[9], refs[10], refs[11], refs[12], refs[13]
    groups = memory_pieces(place_ref, (3,), (x3,), hbm, scratch, sems)
    sums = start_copies([(acc_hbm, acc_s), (low_hbm, low_s)], acc_sems)
    wait_all(groups[0])
    term, low_term = memory_terms(0, scratch)
    wait_all(sums)
    acc = acc_s[...] + term
    low = low_s[...] + low_term
    values = (acc[:, HD:] + dot_nn(low.astype(jnp.bfloat16), up_ref[...])).astype(jnp.bfloat16)
    keys = acc[:, :HD].astype(jnp.bfloat16)
    low_t = jnp.transpose(low).astype(jnp.bfloat16)
    for b in range(acc.shape[0] // BLK):
        at = slice(b * BLK, (b + 1) * BLK)
        pair_ref[b, 0:BLK, :] = keys[at]
        pair_ref[b, BLK : 2 * BLK, :] = values[at]
        pair_ref[b, 2 * BLK : PACK, :] = low_t[:, at]
    for r in range(peers):
        out_ref[r] = pair_ref[asked_ref[r]]


WQ_CUTS = 4


def project_pieces(place_ref, js, xs, hbm, scratch, sems):
    wq_hbm, wk_hbm, wv_hbm, qd_hbm, vd_hbm = hbm
    x_s, wq_s, wk_s, wv_s, qd_s, vd_s = scratch
    width = x_s.shape[2]
    part = width // WQ_CUTS
    groups = []
    for n, j in enumerate(js):
        here = piece_rows(place_ref, j, width)
        start = lax.bitwise_xor(place_ref[0], j) * width
        pairs = [(xs[n], x_s.at[n])]
        for m in range(WQ_CUTS):
            rows = pl.ds(pl.multiple_of(start + m * part, part), part)
            pairs.append((wq_hbm.at[rows, :], wq_s.at[n, pl.ds(m * part, part), :]))
        pairs += [
            (wk_hbm.at[here, :], wk_s.at[n]),
            (wv_hbm.at[here, :], wv_s.at[n]),
            (qd_hbm.at[:, here], qd_s.at[n]),
            (vd_hbm.at[:, here], vd_s.at[n]),
        ]
        groups.append(start_copies(pairs, sems, len(pairs) * n))
    return groups


def project_terms(n, scratch):
    x_s, wq_s, wk_s, wv_s, qd_s, vd_s = scratch
    x = x_s[n]
    return (
        dot_nn(x, wq_s[n]),
        dot_nn(x, jnp.concatenate([wk_s[n], wv_s[n]], 1)),
        dot_nt(x, jnp.concatenate([qd_s[n], vd_s[n]], 0)),
    )


def project_early_kernel(place_ref, x0, x1, *refs):
    hbm, (tag_ref, tags_t_ref), outs, (grad_ref, grad_t_ref) = refs[:5], refs[5:7], refs[8:11], refs[11:13]
    scratch, sems = refs[13:19], refs[19]
    groups = project_pieces(place_ref, (0, 1), (x0, x1), hbm, scratch, sems)
    first = (((0,), (0,)), ((), ()))
    tag = tag_ref[...].astype(jnp.float32)
    tags_t = tags_t_ref[...]
    f32 = jnp.float32
    grad_ref[...] = lax.dot_general(
        tags_t, tag, first, precision=HIGHEST, preferred_element_type=f32
    ).astype(jnp.bfloat16)
    grad_t_ref[...] = lax.dot_general(
        tag, tags_t, first, precision=HIGHEST, preferred_element_type=f32
    ).astype(jnp.bfloat16)
    for n in range(2):
        wait_all(groups[n])
        for ref, term in zip(outs, project_terms(n, scratch)):
            if n == 0:
                ref[...] = term
            else:
                ref[...] += term


def project_middle_kernel(place_ref, x3, *refs):
    hbm, early, outs, scratch, sems = refs[:5], refs[5:8], refs[8:11], refs[11:17], refs[17]
    sum_refs, sum_sems = refs[18:21], refs[21]
    groups = project_pieces(place_ref, (3,), (x3,), hbm, scratch, sems)
    loads = start_copies(list(zip(early, sum_refs)), sum_sems)
    wait_all(groups[0])
    terms = project_terms(0, scratch)
    wait_all(loads)
    for out, ref, term in zip(outs, sum_refs, terms):
        out[...] = ref[...] + term


def attention_kernel(peers, heads, place_ref, bound_ref, x2, *refs):
    hbm, early, got, grad_hbm, grad_t_hbm = refs[:5], refs[5:8], refs[8], refs[9], refs[10]
    qup_ref, vup_ref, tag_ref, cot_ref, up_ref, mcot_ref = refs[11:17]
    scratch, sems, sum_refs = refs[17:23], refs[23], refs[24:27]
    (q_s, k_own, v_own, low_s, low_m_s, grad_ref, grad_t_ref, k_all, v_all, kt_all, vt_all, kt_own, vt_own, bias_s, s_s, dp_s,
     p_s, ds_s, att_s, dq_s, dv_s, more_sems) = refs[27:]
    seen = peers * BLK
    groups = project_pieces(place_ref, (2,), (x2,), hbm, scratch, sems)
    pairs = list(zip(early, sum_refs))
    for b in range(peers):
        at = slice(b * BLK, (b + 1) * BLK)
        pairs.append((got.at[b, pl.ds(0, BLK), :], k_all.at[at, :]))
        pairs.append((got.at[b, pl.ds(BLK, BLK), :], v_all.at[at, :]))
        pairs.append((got.at[b, pl.ds(2 * BLK, RANK), :], low_m_s.at[b]))
    pairs += [(grad_hbm, grad_ref), (grad_t_hbm, grad_t_ref)]
    copies = start_copies(pairs, more_sems)
    wait_all(groups[0])
    wait_all(copies[:3])
    q_acc, kv_acc, low_acc = [ref[...] + term for ref, term in zip(sum_refs, project_terms(0, scratch))]
    low = low_acc.astype(jnp.bfloat16)
    q_s[...] = (q_acc + dot_nn(low[:, :RANK], qup_ref[...])).astype(jnp.bfloat16)
    k_own[...] = kv_acc[:, :HD].astype(jnp.bfloat16)
    v_own[...] = (kv_acc[:, HD:] + dot_nn(low[:, RANK:], vup_ref[...])).astype(jnp.bfloat16)
    low_s[...] = jnp.transpose(low_acc).astype(jnp.bfloat16)
    wait_all(copies[3:])
    for b in range(peers):
        at = slice(b * BLK, (b + 1) * BLK)
        kt_all[:, at] = jnp.transpose(k_all[at, :])
        vt_all[:, at] = jnp.transpose(v_all[at, :])
    dv_s[...] = jnp.zeros_like(dv_s)
    up_ref[...] = jnp.zeros_like(up_ref)
    scale = HD ** (-0.5)
    up_wide = vup_ref[...].astype(jnp.float32)
    query_width = heads * HD

    def pair_step(c, carry):
        base = c * (PAIR * BLK)
        rows = pl.ds(pl.multiple_of(base, PAIR * BLK), PAIR * BLK)
        own_rows = [pl.ds(pl.multiple_of(base + b * BLK, BLK), BLK) for b in range(PAIR)]
        row_ids = lax.broadcasted_iota(jnp.int32, (BLK, BLK), 0)
        col_ids = lax.broadcasted_iota(jnp.int32, (BLK, BLK), 1)
        for b in range(PAIR):
            kt_own[:, b * BLK : (b + 1) * BLK] = jnp.transpose(k_own[own_rows[b], :])
            vt_own[:, b * BLK : (b + 1) * BLK] = jnp.transpose(v_own[own_rows[b], :])
            edge = bound_ref[c * PAIR + b]
            visible = (col_ids <= row_ids) & ((col_ids >= edge) | (row_ids < edge))
            bias_s[b * BLK : (b + 1) * BLK, :] = jnp.where(visible, 0.0, -jnp.inf)

        def head_cols(h):
            return slice(h * HD, (h + 1) * HD)

        def times_keys(out_ref, left_ref, h, all_t, own_t):
            out_ref[:, :seen] = dot_nn(left_ref[rows, head_cols(h)], all_t[...])
            for b in range(PAIR):
                at = slice(b * BLK, (b + 1) * BLK)
                out_ref[at, seen:] = dot_nn(left_ref[own_rows[b], head_cols(h)], own_t[:, at])

        def over_keys(left_ref, first, all_ref, own_ref):
            whole = dot_nn(left_ref[first : first + PAIR * BLK, :seen], all_ref[...])
            mine = [
                dot_nn(left_ref[first + b * BLK : first + (b + 1) * BLK, seen:], own_ref[own_rows[b], :])
                for b in range(PAIR)
            ]
            return (whole + jnp.concatenate(mine, 0)).astype(jnp.bfloat16)

        def scores(h):
            times_keys(s_s.at[h % 2], q_s, h, kt_all, kt_own)

        def prob_grads(h):
            times_keys(dp_s.at[h % 2], grad_ref, h, vt_all, vt_own)

        def strips(h):
            for r in range(0, PAIR * BLK, STRIP):
                at = slice(r, r + STRIP)
                s = s_s[h % 2, at, :]
                s = jnp.concatenate([s[:, :seen], s[:, seen:] + bias_s[at, :]], 1) * (scale * LOG2E)
                w = jnp.exp2(s - jnp.max(s, axis=1, keepdims=True))
                probs = w * (1.0 / jnp.sum(w, axis=1, keepdims=True))
                probs_low = probs.astype(jnp.bfloat16)
                first = h * PAIR * BLK + r
                p_s[first : first + STRIP, :] = probs_low
                dp = dp_s[h % 2, at, :]
                dot = jnp.sum(probs_low.astype(jnp.float32) * dp, axis=1, keepdims=True)
                ds_s[h % 2, at, :] = (probs * ((dp - dot) * scale)).astype(jnp.bfloat16)

        def finish_head(h):
            att_s[:, head_cols(h)] = over_keys(p_s, h * PAIR * BLK, v_all, v_own)
            dq_s[:, head_cols(h)] = over_keys(ds_s.at[h % 2], 0, k_all, k_own)

        scores(0)
        prob_grads(0)
        for h in range(heads + 1):
            if h + 1 < heads:
                scores(h + 1)
                prob_grads(h + 1)
            if h < heads:
                strips(h)
            if h > 0:
                finish_head(h - 1)
        g_t = jnp.concatenate([grad_t_ref[h * HD : (h + 1) * HD, rows] for h in range(heads)], 1)
        dv_s[...] += dot_nn(g_t, p_s[:, :seen])
        dv_own = []
        for b in range(PAIR):
            g_b = jnp.concatenate([grad_t_ref[h * HD : (h + 1) * HD, own_rows[b]] for h in range(heads)], 1)
            starts = [(h * PAIR + b) * BLK for h in range(heads)]
            p_b = jnp.concatenate([p_s[n : n + BLK, seen:] for n in starts], 0)
            dv_own.append(dot_nn(g_b, p_b))
        dv_own = jnp.concatenate(dv_own, 1)
        dq = dq_s[...]
        cot_ref[0:RANK, rows] = dot_nt(qup_ref[...], dq)
        cot_ref[RANK : 2 * RANK, rows] = dot_nn(up_wide, dv_own, HIGHEST)
        cot_ref[2 * RANK :, rows] = dot_nt(tag_ref[...], att_s[...])
        up_ref[:, :query_width] += dot_nn(low_s[0:RANK, rows], dq)
        up_ref[:, query_width:] += dot_nt(low_s[RANK:, rows].astype(jnp.float32), dv_own, HIGHEST)
        return carry

    lax.fori_loop(0, q_s.shape[0] // (PAIR * BLK), pair_step, 0)
    dv = dv_s[...]
    mcot = dot_nn(up_wide, dv, HIGHEST)
    low_m = jnp.concatenate([low_m_s[b] for b in range(peers)], 1).astype(jnp.float32)
    up_ref[:, query_width:] += dot_nt(low_m, dv, HIGHEST)
    for b in range(peers):
        mcot_ref[b] = mcot[:, b * BLK : (b + 1) * BLK]


def own_kernel(peers, asked_ref, back_ref, out_ref, sum_s):
    sum_s[...] = jnp.zeros_like(sum_s)
    for r in range(peers):
        block = asked_ref[r]
        sum_s[block] = sum_s[block] + back_ref[r]
    out_ref[...] = jnp.concatenate([sum_s[m] for m in range(sum_s.shape[0])], 1)


def first_down_kernel(c0, c1, c2, c3, slab_ref, up_ref, logit_ref, query_ref, value_ref):
    cot = (c0[...] + c1[...]) + (c2[...] + c3[...])
    logit_ref[...] = cot[2 * RANK :]
    both = dot_nn(cot[: 2 * RANK].astype(jnp.bfloat16), slab_ref[...])
    width = both.shape[1]
    query_ref[:, :width] = both[:RANK]
    query_ref[:, width:] = up_ref[...]
    value_ref[...] = both[RANK:]


def second_down_kernel(c0, c1, c2, c3, memory_ref, value_ref, out_ref):
    cot = (c0[...] + c1[...]) + (c2[...] + c3[...])
    out_ref[...] = value_ref[...] + dot_nn(cot.astype(jnp.bfloat16), memory_ref[...])


def finish_kernel(*refs):
    query, value = [
        (ref[0][...].astype(jnp.float32) + ref[1][...].astype(jnp.float32))
        + (ref[2][...].astype(jnp.float32) + ref[3][...].astype(jnp.float32))
        for ref in (refs[:4], refs[4:8])
    ]
    query_down_ref, query_up_ref, value_down_ref, value_up_ref = refs[8:]
    value_down_ref[...] = value
    at = 0
    for out_ref in (query_down_ref, query_up_ref, value_up_ref):
        out_ref[...] = query[:, at : at + out_ref.shape[1]]
        at += out_ref.shape[1]


def swap(x, bit, axis="heads"):
    return lax.ppermute(x, axis, [(i, i ^ bit) for i in range(lax.axis_size(axis))])


def after(x, *deps):
    return pl.pallas_call(
        lambda *refs: None,
        out_shape=jax.ShapeDtypeStruct(x.shape, x.dtype),
        in_specs=[anywhere()] * (1 + len(deps)),
        out_specs=anywhere(),
        input_output_aliases={0: 0},
        name="in_order",
    )(x, *deps)


def anywhere():
    return pl.BlockSpec(memory_space=pl.ANY)


def smem():
    return pl.BlockSpec(memory_space=pltpu.SMEM)


def vmem():
    return pl.BlockSpec(memory_space=pltpu.VMEM)


def shaped(*shape, dtype=jnp.float32):
    return jax.ShapeDtypeStruct(shape, dtype)


def run(body, name, out_shape, in_specs, scratch=(), flops=0, moved=0, room=ROOM, out_specs=None):
    many = isinstance(out_shape, (tuple, list))
    return pl.pallas_call(
        body,
        out_shape=out_shape,
        in_specs=in_specs,
        out_specs=out_specs or (tuple(vmem() for _ in out_shape) if many else vmem()),
        scratch_shapes=list(scratch),
        compiler_params=pltpu.CompilerParams(vmem_limit_bytes=room * MIB),
        cost_estimate=pl.CostEstimate(flops=flops, bytes_accessed=moved, transcendentals=0),
        name=name,
    )


def fast(
    slab_tokens,
    memory,
    query_weight,
    key_weight,
    value_weight,
    query_down,
    query_up,
    value_down,
    value_up,
    tag_weight,
    retrieval,
    boundary,
    grad_tags,
):
    tok_rows, width = slab_tokens.shape
    mem_rows = memory.shape[0]
    query_width = query_weight.shape[1]
    heads = query_width // HD
    spans = tok_rows // BLK
    blocks = mem_rows // BLK
    peers = lax.axis_size("tm")
    f32 = jnp.float32
    bf16 = jnp.bfloat16

    def memory_scratch(count):
        return [
            pltpu.VMEM((count, mem_rows, width), bf16),
            pltpu.VMEM((count, width, HD), bf16),
            pltpu.VMEM((count, width, HD), bf16),
            pltpu.VMEM((count, RANK, width), bf16),
            pltpu.SemaphoreType.DMA((4 * count,)),
        ]

    def project_scratch(count):
        return [
            pltpu.VMEM((count, tok_rows, width), bf16),
            pltpu.VMEM((count, width, query_width), bf16),
            pltpu.VMEM((count, width, HD), bf16),
            pltpu.VMEM((count, width, HD), bf16),
            pltpu.VMEM((count, RANK, width), bf16),
            pltpu.VMEM((count, RANK, width), bf16),
            pltpu.SemaphoreType.DMA((count * (WQ_CUTS + 5),)),
        ]

    memory_sums = [
        pltpu.VMEM((mem_rows, 2 * HD), f32),
        pltpu.VMEM((mem_rows, RANK), f32),
        pltpu.SemaphoreType.DMA((2,)),
    ]
    project_sums = [
        pltpu.VMEM((tok_rows, query_width), f32),
        pltpu.VMEM((tok_rows, 2 * HD), f32),
        pltpu.VMEM((tok_rows, 2 * RANK), f32),
    ]

    place = lax.axis_index("heads").astype(jnp.int32).reshape(1)
    tag_t = tag_weight.T
    tags = tag_t.shape[0]
    mem_far = swap(memory, 2)
    mem_near = swap(memory, 1)
    tok_near = swap(slab_tokens, 1)
    tok_far = swap(tok_near, 2)
    mem_acc, mem_low, wanted = run(
        lambda *refs: memory_early_kernel(blocks, *refs),
        "memory_near_half",
        (shaped(mem_rows, 2 * HD), shaped(mem_rows, RANK), shaped(peers, dtype=jnp.int32)),
        [smem()] * 2 + [anywhere()] * 5,
        memory_scratch(2),
        out_specs=(vmem(), vmem(), smem()),
    )(place, retrieval, memory, mem_near, key_weight, value_weight, value_down)
    asked = lax.all_to_all(wanted, "tm", split_axis=0, concat_axis=0, tiled=True)
    weights = (query_weight, key_weight, value_weight, query_down, value_down)
    *early, grad, grad_t = run(
        project_early_kernel,
        "project_near_half",
        (
            shaped(tok_rows, query_width),
            shaped(tok_rows, 2 * HD),
            shaped(tok_rows, 2 * RANK),
            shaped(tok_rows, query_width, dtype=bf16),
            shaped(query_width, tok_rows, dtype=bf16),
        ),
        [smem()] + [anywhere()] * 7 + [vmem()] * 2 + [smem()],
        project_scratch(2),
    )(place, slab_tokens, tok_near, *weights, tag_t, grad_tags.T, wanted)
    mem_far = after(mem_far, early[2], asked)
    mem_cross = swap(mem_far, 1)
    mem_weights = (key_weight, value_weight, value_down)
    mem_acc, mem_low = run(
        memory_middle_kernel,
        "memory_far_quarter",
        (shaped(mem_rows, 2 * HD), shaped(mem_rows, RANK)),
        [smem()] + [anywhere()] * 6,
        memory_scratch(1) + memory_sums,
    )(place, mem_far, mem_acc, mem_low, *mem_weights)
    pairs = run(
        lambda *refs: memory_kernel(peers, *refs),
        "memory_pairs",
        shaped(peers, PACK, HD, dtype=bf16),
        [smem()] * 2 + [anywhere()] * 6 + [vmem()],
        memory_scratch(1) + memory_sums + [pltpu.VMEM((blocks, PACK, HD), bf16)],
    )(place, asked, mem_cross, mem_acc, mem_low, *mem_weights, value_up)
    got = lax.all_to_all(pairs, "tm", split_axis=0, concat_axis=0, tiled=True)
    tok_far = after(tok_far, pairs)
    tok_cross = swap(tok_far, 1)
    early = run(
        project_middle_kernel,
        "project_far_quarter",
        (shaped(tok_rows, query_width), shaped(tok_rows, 2 * HD), shaped(tok_rows, 2 * RANK)),
        [smem()] + [anywhere()] * 9,
        project_scratch(1) + project_sums + [pltpu.SemaphoreType.DMA((3,))],
    )(place, tok_far, *weights, *early)

    seen = peers * BLK
    total = seen + BLK
    cot, ups, mcot = run(
        lambda *refs: attention_kernel(peers, heads, *refs),
        "span_attention",
        (shaped(2 * RANK + tags, tok_rows), shaped(RANK, query_width + HD), shaped(peers, RANK, BLK)),
        [smem()] * 2 + [anywhere()] * 12 + [vmem()] * 3,
        project_scratch(1)
        + project_sums
        + [
            pltpu.VMEM((tok_rows, query_width), bf16),
            pltpu.VMEM((tok_rows, HD), bf16),
            pltpu.VMEM((tok_rows, HD), bf16),
            pltpu.VMEM((2 * RANK, tok_rows), bf16),
            pltpu.VMEM((peers, RANK, BLK), bf16),
            pltpu.VMEM((tok_rows, query_width), bf16),
            pltpu.VMEM((query_width, tok_rows), bf16),
            pltpu.VMEM((seen, HD), bf16),
            pltpu.VMEM((seen, HD), bf16),
            pltpu.VMEM((HD, seen), bf16),
            pltpu.VMEM((HD, seen), bf16),
            pltpu.VMEM((HD, PAIR * BLK), bf16),
            pltpu.VMEM((HD, PAIR * BLK), bf16),
            pltpu.VMEM((PAIR * BLK, BLK), f32),
            pltpu.VMEM((2, PAIR * BLK, total), f32),
            pltpu.VMEM((2, PAIR * BLK, total), f32),
            pltpu.VMEM((heads * PAIR * BLK, total), bf16),
            pltpu.VMEM((2, PAIR * BLK, total), bf16),
            pltpu.VMEM((PAIR * BLK, query_width), bf16),
            pltpu.VMEM((PAIR * BLK, query_width), bf16),
            pltpu.VMEM((HD, seen), f32),
            pltpu.SemaphoreType.DMA((3 * peers + 5,)),
        ],
        flops=20 * tok_rows * query_width * total,
        moved=4 * tok_rows * query_width,
    )(place, boundary, tok_cross, *weights, *early, got, grad, grad_t, query_up, value_up, tag_t)

    back = lax.all_to_all(mcot, "tm", split_axis=0, concat_axis=0, tiled=True)
    cots = [cot] + [swap(cot, d) for d in range(1, 4)]
    own = run(
        lambda *refs: own_kernel(peers, *refs),
        "owned_cotangent",
        shaped(RANK, mem_rows),
        [smem()] + [vmem()],
        [pltpu.VMEM((blocks, RANK, BLK), f32)],
        room=8,
    )(asked, back)
    logits, query_sum, value_part = run(
        first_down_kernel,
        "first_down",
        (shaped(tags, tok_rows), shaped(RANK, width + ups.shape[1]), shaped(RANK, width)),
        [vmem()] * 6,
        flops=4 * RANK * tok_rows * width,
        moved=2 * tok_rows * width,
        room=8,
    )(*cots, slab_tokens, ups)
    owns = [own] + [swap(own, d) for d in range(1, 4)]
    value_sum = run(
        second_down_kernel,
        "second_down",
        shaped(RANK, width),
        [vmem()] * 6,
        flops=2 * RANK * mem_rows * width,
        moved=2 * mem_rows * width,
        room=8,
    )(*owns, memory, value_part)
    sums = []
    for part in (query_sum, value_sum):
        part = (part + swap(part, 1, "tm")).astype(bf16)
        sums += [part] + [swap(part, bit, "tm") for bit in (2, 4, 6)]
    query_down_grad, query_up_grad, value_down_grad, value_up_grad = run(
        finish_kernel,
        "finish_outputs",
        (shaped(RANK, width), shaped(RANK, query_width), shaped(RANK, width), shaped(RANK, HD)),
        [vmem()] * 8,
        room=8,
    )(*sums)
    return (logits.T, query_down_grad, query_up_grad, value_down_grad, value_up_grad)


def solution(mesh):
    in_specs = (
        P("tm", "heads"),
        P("tm", "heads"),
        P(None, "heads"),
        P(None, "heads"),
        P(None, "heads"),
        P(),
        P(None, "heads"),
        P(),
        P(None, "heads"),
        P("heads", None),
        P("tm", None),
        P("tm"),
        P("tm", None),
    )
    out_specs = (
        P("tm", None),
        P(None, "heads"),
        P(None, "heads"),
        P(None, "heads"),
        P(None, "heads"),
    )
    fits = mesh.shape["heads"] == 4 and mesh.shape["tm"] == 8 == TOP * CAP
    local = fast if fits else general
    return jax.shard_map(local, mesh=mesh, in_specs=in_specs, out_specs=out_specs, check_vma=False)
```

```python
import jax
import jax.numpy as jnp
from jax import lax
from jax.experimental import pallas as pl
from jax.experimental.pallas import tpu as pltpu
from jax.sharding import PartitionSpec as P

HD = 128
RANK = 16
TOP = 8
BLK = 128
CAP = 1


HIGHEST = lax.Precision.HIGHEST


def attend(query, all_keys, all_values, split_row, out_grad):
    span_count, row_count, query_width = query.shape
    key_count, kv_width = (all_keys.shape[1], all_keys.shape[2])
    kv_heads = kv_width // HD
    group_size = query_width // kv_width
    score_scale = HD ** (-0.5)
    query_heads = query.reshape(span_count, row_count, kv_heads, group_size, HD)
    key_heads = all_keys.reshape(span_count, key_count, kv_heads, HD)
    value_heads = all_values.reshape(span_count, key_count, kv_heads, HD)
    grad_heads = out_grad.reshape(span_count, row_count, kv_heads, group_size, HD)
    scores = (
        jnp.einsum("crngd,cknd->cngrk", query_heads, key_heads, preferred_element_type=jnp.float32)
        * score_scale
    )
    row_ids = jnp.arange(row_count, dtype=jnp.int32)[:, None]
    col_ids = jnp.arange(BLK, dtype=jnp.int32)[None, :]
    edge_at = split_row[:, None, None]
    local_seen = (col_ids <= row_ids) & ((col_ids >= edge_at) | (row_ids < edge_at))
    visible = jnp.concatenate(
        [jnp.ones((span_count, row_count, key_count - BLK), jnp.bool_), local_seen], axis=2
    )
    scores = jnp.where(visible[:, None, None], scores, -jnp.inf)
    row_max = jnp.max(scores, axis=-1, keepdims=True)
    weights = jnp.exp(scores - row_max)
    probs = weights / jnp.sum(weights, axis=-1, keepdims=True)
    probs_low = probs.astype(jnp.bfloat16)
    attended = jnp.einsum(
        "cngrk,cknd->crngd", probs_low, value_heads, preferred_element_type=jnp.float32
    ).astype(jnp.bfloat16)
    prob_grad = jnp.einsum(
        "crngd,cknd->cngrk", grad_heads, value_heads, preferred_element_type=jnp.float32
    )
    row_dot = jnp.sum(grad_heads.astype(jnp.float32) * attended.astype(jnp.float32), axis=-1)
    row_dot = jnp.transpose(row_dot, (0, 2, 3, 1))[..., None]
    score_grad = (probs * (prob_grad - row_dot) * score_scale).astype(jnp.bfloat16)
    query_grad = jnp.einsum(
        "cngrk,cknd->crngd", score_grad, key_heads, preferred_element_type=jnp.float32
    ).astype(jnp.bfloat16)
    value_grad = jnp.einsum(
        "cngrk,crngd->cknd", probs_low, grad_heads, preferred_element_type=jnp.float32
    )
    return (
        attended.reshape(span_count, row_count, query_width),
        query_grad.reshape(span_count, row_count, query_width),
        value_grad.reshape(span_count, key_count, kv_width),
    )


def choose_slots(needed, places):
    slot_ids = jnp.arange(CAP, dtype=jnp.int32)
    return needed[:, None, :] * (places[:, None, :] == slot_ids[None, :, None]).astype(jnp.int32)


def general(
    slab_tokens,
    memory,
    query_weight,
    key_weight,
    value_weight,
    query_down,
    query_up,
    value_down,
    value_up,
    tag_weight,
    retrieval,
    boundary,
    grad_tags,
):
    tok_rows = slab_tokens.shape[0]
    mem_rows = memory.shape[0]
    query_width = query_weight.shape[1]
    kv_width = key_weight.shape[1]
    span_count = tok_rows // BLK
    block_count = mem_rows // BLK
    pair_weight = jnp.concatenate([key_weight, value_weight], 1)
    adapter_pair = jnp.concatenate([query_down, value_down], 0)
    contract_last = (((1,), (1,)), ((), ()))
    contract_first = (((0,), (0,)), ((), ()))
    token_piece = lax.all_gather(slab_tokens, "heads", axis=1, tiled=True)
    memory_piece = lax.all_gather(memory, "heads", axis=1, tiled=True)
    query_acc = jnp.dot(token_piece, query_weight, preferred_element_type=jnp.float32)
    pair_acc = jnp.dot(token_piece, pair_weight, preferred_element_type=jnp.float32)
    low_acc = lax.dot_general(
        token_piece, adapter_pair, contract_last, preferred_element_type=jnp.float32
    )
    memory_acc = jnp.dot(memory_piece, pair_weight, preferred_element_type=jnp.float32)
    memory_low_acc = lax.dot_general(
        memory_piece, adapter_pair[RANK:], contract_last, preferred_element_type=jnp.float32
    )
    query_acc, pair_acc, low_acc, memory_acc, memory_low_acc = (
        query_acc,
        pair_acc,
        low_acc,
        memory_acc,
        memory_low_acc,
    )
    low_tokens = low_acc.astype(jnp.bfloat16)
    low_query = low_tokens[:, :RANK]
    low_value = low_tokens[:, RANK:]
    queries = (query_acc + jnp.dot(low_query, query_up, preferred_element_type=jnp.float32)).astype(
        jnp.bfloat16
    )
    keys_local = pair_acc[:, :kv_width].astype(jnp.bfloat16)
    values_local = (
        pair_acc[:, kv_width:] + jnp.dot(low_value, value_up, preferred_element_type=jnp.float32)
    ).astype(jnp.bfloat16)
    memory_low = memory_low_acc.astype(jnp.bfloat16)
    memory_pair = (
        jnp.concatenate(
            [
                memory_acc[:, :kv_width],
                memory_acc[:, kv_width:]
                + jnp.dot(memory_low, value_up, preferred_element_type=jnp.float32),
            ],
            1,
        )
        .astype(jnp.bfloat16)
        .reshape(block_count, BLK, 2 * kv_width)
    )
    peer_count = lax.axis_size("tm")
    every_block = jnp.arange(peer_count * block_count, dtype=jnp.int32)
    wanted = (
        jnp.any(retrieval.reshape(-1, 1) == every_block[None, :], axis=0)
        .astype(jnp.int32)
        .reshape(peer_count, block_count)
    )
    places = jnp.cumsum(wanted, axis=1) - wanted
    requested = choose_slots(wanted, places)
    asked_for = lax.all_to_all(requested, "tm", split_axis=0, concat_axis=0, tiled=True)
    rows_needed = retrieval // block_count * CAP + jnp.take(places.reshape(-1), retrieval)
    asked_low = asked_for.astype(jnp.bfloat16)
    outgoing = jnp.einsum(
        "rcm,mbw->rcbw", asked_low, memory_pair, preferred_element_type=jnp.float32
    ).astype(jnp.bfloat16)
    fetched = lax.all_to_all(outgoing, "tm", split_axis=0, concat_axis=0, tiled=True)
    slot_rows = fetched.reshape(peer_count * CAP, BLK, 2 * kv_width)
    picked = jnp.take(slot_rows, rows_needed.reshape(-1), axis=0).reshape(
        span_count, TOP * BLK, 2 * kv_width
    )
    all_keys = jnp.concatenate(
        [picked[..., :kv_width], keys_local.reshape(span_count, BLK, kv_width)], 1
    )
    all_values = jnp.concatenate(
        [picked[..., kv_width:], values_local.reshape(span_count, BLK, kv_width)], 1
    )
    attended_grad = lax.dot_general(
        grad_tags, tag_weight.astype(jnp.float32), contract_last, precision=HIGHEST
    ).astype(jnp.bfloat16)
    attended, query_grad, value_grad = attend(
        queries.reshape(span_count, BLK, query_width),
        all_keys,
        all_values,
        boundary,
        attended_grad.reshape(span_count, BLK, query_width),
    )
    attended = attended.reshape(tok_rows, query_width)
    query_grad = query_grad.reshape(tok_rows, query_width)
    logits_out = lax.psum(
        jnp.dot(attended, tag_weight, preferred_element_type=jnp.float32), "heads"
    )
    local_grad = value_grad[:, TOP * BLK :].reshape(tok_rows, kv_width)
    slot_grads = value_grad[:, : TOP * BLK].reshape(span_count * TOP, BLK * kv_width)
    slot_hits = (
        rows_needed.reshape(-1, 1) == jnp.arange(peer_count * CAP, dtype=jnp.int32)[None, :]
    ).astype(jnp.float32)
    grad_buffer = lax.dot_general(slot_hits, slot_grads, contract_first, precision=HIGHEST).reshape(
        peer_count * CAP, BLK, kv_width
    )
    up_wide = value_up.astype(jnp.float32)
    returned = lax.all_to_all(
        grad_buffer.reshape(peer_count, CAP, BLK, kv_width),
        "tm",
        split_axis=0,
        concat_axis=0,
        tiled=True,
    )
    owned_grad = jnp.einsum(
        "rcm,rcbw->mbw", asked_for.astype(jnp.float32), returned, precision=HIGHEST
    ).reshape(mem_rows, kv_width)
    memory_cot = lax.dot_general(up_wide, owned_grad, contract_last, precision=HIGHEST)
    up_memory = lax.dot_general(
        memory_low.astype(jnp.float32), owned_grad, contract_first, precision=HIGHEST
    )
    query_cot = lax.dot_general(
        query_up, query_grad, contract_last, preferred_element_type=jnp.float32
    )
    value_cot = lax.dot_general(up_wide, local_grad, contract_last, precision=HIGHEST)
    query_cot, value_cot, memory_cot = lax.psum((query_cot, value_cot, memory_cot), "heads")
    query_down_grad = jnp.dot(
        query_cot.astype(jnp.bfloat16), slab_tokens, preferred_element_type=jnp.float32
    )
    value_down_grad = jnp.dot(
        value_cot.astype(jnp.bfloat16), slab_tokens, preferred_element_type=jnp.float32
    ) + jnp.dot(memory_cot.astype(jnp.bfloat16), memory, preferred_element_type=jnp.float32)
    query_up_grad = lax.dot_general(
        low_query, query_grad, contract_first, preferred_element_type=jnp.float32
    )
    value_up_grad = (
        lax.dot_general(
            low_value.astype(jnp.float32), local_grad, contract_first, precision=HIGHEST
        )
        + up_memory
    )
    query_down_grad, query_up_grad, value_down_grad, value_up_grad = lax.psum(
        (query_down_grad, query_up_grad, value_down_grad, value_up_grad), "tm"
    )
    return (logits_out, query_down_grad, query_up_grad, value_down_grad, value_up_grad)


LOG2E = 1.4426950408889634
NT = (((1,), (1,)), ((), ()))
PACK = 2 * BLK + RANK
STRIP = 16
PAIR = 2
MIB = 1024 * 1024
FLAG = jax.ShapeDtypeStruct((1,), jnp.int32)
ROOM = 63


def dot_nt(a, b, precision=None):
    return lax.dot_general(a, b, NT, precision=precision, preferred_element_type=jnp.float32)


def dot_nn(a, b, precision=None):
    return jnp.dot(a, b, precision=precision, preferred_element_type=jnp.float32)


def piece_rows(place_ref, j, width):
    return pl.ds(pl.multiple_of(lax.bitwise_xor(place_ref[0], j) * width, width), width)


def start_copies(pairs, sems, first=0):
    copies = [pltpu.make_async_copy(src, dst, sems.at[first + n]) for n, (src, dst) in enumerate(pairs)]
    for copy in copies:
        copy.start()
    return copies


def in_parts(src, dst, parts=4):
    step = dst.shape[0] // parts
    return [(src.at[pl.ds(n * step, step), :], dst.at[pl.ds(n * step, step), :]) for n in range(parts)]


def wait_all(copies):
    for copy in copies:
        copy.wait()


def memory_pieces(place_ref, js, xs, hbm, scratch, sems):
    x_s, wk_s, wv_s, down_s = scratch
    width = x_s.shape[2]
    groups = []
    for n, j in enumerate(js):
        here = piece_rows(place_ref, j, width)
        pairs = in_parts(xs[n], x_s.at[n]) + [
            (hbm[0].at[here, :], wk_s.at[n]),
            (hbm[1].at[here, :], wv_s.at[n]),
            (hbm[2].at[:, here], down_s.at[n]),
        ]
        groups.append(start_copies(pairs, sems, 7 * n))
    return groups


def memory_terms(n, scratch):
    x_s, wk_s, wv_s, down_s = scratch
    x = x_s[n]
    return dot_nn(x, jnp.concatenate([wk_s[n], wv_s[n]], 1)), dot_nt(x, down_s[n])


def memory_early_kernel(blocks, place_ref, named_ref, x0, x1, *refs):
    hbm, acc_ref, low_ref, wanted_ref, scratch, sems = refs[:3], refs[3], refs[4], refs[5], refs[6:10], refs[10]
    groups = memory_pieces(place_ref, (0, 1), (x0, x1), hbm, scratch, sems)
    for slot in range(TOP):
        block = named_ref[0, slot]
        wanted_ref[lax.div(block, blocks)] = lax.rem(block, blocks)
    for n in range(2):
        wait_all(groups[n])
        term, low_term = memory_terms(n, scratch)
        if n == 0:
            acc_ref[...] = term
            low_ref[...] = low_term
        else:
            acc_ref[...] += term
            low_ref[...] += low_term


def memory_middle_kernel(place_ref, x2, acc_hbm, low_hbm, *refs):
    hbm, acc_ref, low_ref, scratch, sems = refs[:3], refs[3], refs[4], refs[5:9], refs[9]
    acc_s, low_s, acc_sems = refs[10:13]
    groups = memory_pieces(place_ref, (2,), (x2,), hbm, scratch, sems)
    sums = start_copies([(acc_hbm, acc_s), (low_hbm, low_s)], acc_sems)
    wait_all(groups[0])
    term, low_term = memory_terms(0, scratch)
    wait_all(sums)
    acc_ref[...] = acc_s[...] + term
    low_ref[...] = low_s[...] + low_term


def memory_kernel(peers, place_ref, asked_ref, x3, acc_hbm, low_hbm, *refs):
    hbm, up_ref, out_ref, flag_ref = refs[:3], refs[3], refs[4], refs[5]
    scratch, sems, acc_s, low_s, acc_sems, pair_ref = refs[6:10], refs[10], refs[11], refs[12], refs[13], refs[14]
    flag_ref[0] = 0
    groups = memory_pieces(place_ref, (3,), (x3,), hbm, scratch, sems)
    sums = start_copies([(acc_hbm, acc_s), (low_hbm, low_s)], acc_sems)
    wait_all(groups[0])
    term, low_term = memory_terms(0, scratch)
    wait_all(sums)
    acc = acc_s[...] + term
    low = low_s[...] + low_term
    values = (acc[:, HD:] + dot_nn(low.astype(jnp.bfloat16), up_ref[...])).astype(jnp.bfloat16)
    keys = acc[:, :HD].astype(jnp.bfloat16)
    low_t = jnp.transpose(low).astype(jnp.bfloat16)
    for b in range(acc.shape[0] // BLK):
        at = slice(b * BLK, (b + 1) * BLK)
        pair_ref[b, 0:BLK, :] = keys[at]
        pair_ref[b, BLK : 2 * BLK, :] = values[at]
        pair_ref[b, 2 * BLK : PACK, :] = low_t[:, at]
    for r in range(peers):
        out_ref[r] = pair_ref[asked_ref[r]]


WQ_CUTS = 4


def project_pieces(place_ref, js, xs, hbm, scratch, sems):
    wq_hbm, wk_hbm, wv_hbm, qd_hbm, vd_hbm = hbm
    x_s, wq_s, wk_s, wv_s, qd_s, vd_s = scratch
    width = x_s.shape[2]
    part = width // WQ_CUTS
    groups = []
    for n, j in enumerate(js):
        here = piece_rows(place_ref, j, width)
        start = lax.bitwise_xor(place_ref[0], j) * width
        pairs = in_parts(xs[n], x_s.at[n])
        for m in range(WQ_CUTS):
            rows = pl.ds(pl.multiple_of(start + m * part, part), part)
            pairs.append((wq_hbm.at[rows, :], wq_s.at[n, pl.ds(m * part, part), :]))
        pairs += [
            (wk_hbm.at[here, :], wk_s.at[n]),
            (wv_hbm.at[here, :], wv_s.at[n]),
            (qd_hbm.at[:, here], qd_s.at[n]),
            (vd_hbm.at[:, here], vd_s.at[n]),
        ]
        groups.append(start_copies(pairs, sems, len(pairs) * n))
    return groups


def project_terms(n, scratch):
    x_s, wq_s, wk_s, wv_s, qd_s, vd_s = scratch
    x = x_s[n]
    return (
        dot_nn(x, wq_s[n]),
        dot_nn(x, jnp.concatenate([wk_s[n], wv_s[n]], 1)),
        dot_nt(x, jnp.concatenate([qd_s[n], vd_s[n]], 0)),
    )


def project_early_kernel(place_ref, x0, x1, *refs):
    hbm, outs, flag_ref, scratch, sems = refs[:5], refs[6:9], refs[9], refs[10:16], refs[16]
    flag_ref[0] = 0
    groups = project_pieces(place_ref, (0, 1), (x0, x1), hbm, scratch, sems)
    for n in range(2):
        wait_all(groups[n])
        for ref, term in zip(outs, project_terms(n, scratch)):
            if n == 0:
                ref[...] = term
            else:
                ref[...] += term


def grad_kernel(tag_ref, tags_t_ref, dep_ref, grad_ref, grad_t_ref, flag_ref):
    flag_ref[0] = 0
    first = (((0,), (0,)), ((), ()))
    tag = tag_ref[...].astype(jnp.float32)
    tags_t = tags_t_ref[...]
    f32 = jnp.float32
    grad_ref[...] = lax.dot_general(
        tags_t, tag, first, precision=HIGHEST, preferred_element_type=f32
    ).astype(jnp.bfloat16)
    grad_t_ref[...] = lax.dot_general(
        tag, tags_t, first, precision=HIGHEST, preferred_element_type=f32
    ).astype(jnp.bfloat16)


def project_middle_kernel(place_ref, x3, *refs):
    hbm, early, outs, scratch, sems = refs[:5], refs[5:8], refs[8:11], refs[11:17], refs[17]
    sum_refs, sum_sems = refs[18:21], refs[21]
    groups = project_pieces(place_ref, (3,), (x3,), hbm, scratch, sems)
    loads = start_copies(in_parts(early[0], sum_refs[0]) + list(zip(early[1:], sum_refs[1:])), sum_sems)
    wait_all(groups[0])
    terms = project_terms(0, scratch)
    wait_all(loads)
    for out, ref, term in zip(outs, sum_refs, terms):
        out[...] = ref[...] + term


def attention_kernel(peers, heads, place_ref, me_ref, bound_ref, x2, *refs):
    hbm, early, got, grad_hbm, grad_t_hbm = refs[:5], refs[5:8], refs[8], refs[9], refs[10]
    qup_ref, vup_ref, tag_ref, cot_ref, up_ref, same_ref, other_ref = refs[11:18]
    scratch, sems, sum_refs = refs[18:24], refs[24], refs[25:28]
    (q_s, k_own, v_own, low_s, low_m_s, grad_ref, grad_t_ref, k_all, v_all, kt_all, vt_all, kt_own, vt_own, bias_s, s_s, dp_s,
     p_s, ds_s, att_s, dq_s, dv_s, mcot_s, more_sems) = refs[28:]
    seen = peers * BLK
    groups = project_pieces(place_ref, (2,), (x2,), hbm, scratch, sems)
    pairs = in_parts(early[0], sum_refs[0]) + list(zip(early[1:], sum_refs[1:]))
    for b in range(peers):
        at = slice(b * BLK, (b + 1) * BLK)
        pairs.append((got.at[b, pl.ds(0, BLK), :], k_all.at[at, :]))
        pairs.append((got.at[b, pl.ds(BLK, BLK), :], v_all.at[at, :]))
        pairs.append((got.at[b, pl.ds(2 * BLK, RANK), :], low_m_s.at[b]))
    pairs += in_parts(grad_hbm, grad_ref) + in_parts(grad_t_hbm, grad_t_ref)
    copies = start_copies(pairs, more_sems)
    wait_all(groups[0])
    wait_all(copies[:6])
    q_acc, kv_acc, low_acc = [ref[...] + term for ref, term in zip(sum_refs, project_terms(0, scratch))]
    low = low_acc.astype(jnp.bfloat16)
    q_s[...] = (q_acc + dot_nn(low[:, :RANK], qup_ref[...])).astype(jnp.bfloat16)
    k_own[...] = kv_acc[:, :HD].astype(jnp.bfloat16)
    v_own[...] = (kv_acc[:, HD:] + dot_nn(low[:, RANK:], vup_ref[...])).astype(jnp.bfloat16)
    low_s[...] = jnp.transpose(low_acc).astype(jnp.bfloat16)
    wait_all(copies[6:])
    for b in range(peers):
        at = slice(b * BLK, (b + 1) * BLK)
        kt_all[:, at] = jnp.transpose(k_all[at, :])
        vt_all[:, at] = jnp.transpose(v_all[at, :])
    dv_s[...] = jnp.zeros_like(dv_s)
    up_ref[...] = jnp.zeros_like(up_ref)
    scale = HD ** (-0.5)
    up_wide = vup_ref[...].astype(jnp.float32)
    query_width = heads * HD

    def pair_step(c, carry):
        base = c * (PAIR * BLK)
        rows = pl.ds(pl.multiple_of(base, PAIR * BLK), PAIR * BLK)
        own_rows = [pl.ds(pl.multiple_of(base + b * BLK, BLK), BLK) for b in range(PAIR)]
        row_ids = lax.broadcasted_iota(jnp.int32, (BLK, BLK), 0)
        col_ids = lax.broadcasted_iota(jnp.int32, (BLK, BLK), 1)
        for b in range(PAIR):
            kt_own[:, b * BLK : (b + 1) * BLK] = jnp.transpose(k_own[own_rows[b], :])
            vt_own[:, b * BLK : (b + 1) * BLK] = jnp.transpose(v_own[own_rows[b], :])
            edge = bound_ref[c * PAIR + b]
            visible = (col_ids <= row_ids) & ((col_ids >= edge) | (row_ids < edge))
            bias_s[b * BLK : (b + 1) * BLK, :] = jnp.where(visible, 0.0, -jnp.inf)

        def head_cols(h):
            return slice(h * HD, (h + 1) * HD)

        def times_keys(out_ref, left_ref, h, all_t, own_t):
            out_ref[:, :seen] = dot_nn(left_ref[rows, head_cols(h)], all_t[...])
            for b in range(PAIR):
                at = slice(b * BLK, (b + 1) * BLK)
                out_ref[at, seen:] = dot_nn(left_ref[own_rows[b], head_cols(h)], own_t[:, at])

        def over_keys(left_ref, first, all_ref, own_ref):
            whole = dot_nn(left_ref[first : first + PAIR * BLK, :seen], all_ref[...])
            mine = [
                dot_nn(left_ref[first + b * BLK : first + (b + 1) * BLK, seen:], own_ref[own_rows[b], :])
                for b in range(PAIR)
            ]
            return (whole + jnp.concatenate(mine, 0)).astype(jnp.bfloat16)

        def scores(h):
            times_keys(s_s.at[h % 2], q_s, h, kt_all, kt_own)

        def prob_grads(h):
            times_keys(dp_s.at[h % 2], grad_ref, h, vt_all, vt_own)

        def strips(h):
            for r in range(0, PAIR * BLK, STRIP):
                at = slice(r, r + STRIP)
                s = s_s[h % 2, at, :]
                s = jnp.concatenate([s[:, :seen], s[:, seen:] + bias_s[at, :]], 1) * (scale * LOG2E)
                w = jnp.exp2(s - jnp.max(s, axis=1, keepdims=True))
                probs = w * (1.0 / jnp.sum(w, axis=1, keepdims=True))
                probs_low = probs.astype(jnp.bfloat16)
                first = h * PAIR * BLK + r
                p_s[first : first + STRIP, :] = probs_low
                dp = dp_s[h % 2, at, :]
                dot = jnp.sum(probs_low.astype(jnp.float32) * dp, axis=1, keepdims=True)
                ds_s[h % 2, at, :] = (probs * ((dp - dot) * scale)).astype(jnp.bfloat16)

        def finish_head(h):
            att_s[:, head_cols(h)] = over_keys(p_s, h * PAIR * BLK, v_all, v_own)
            dq_s[:, head_cols(h)] = over_keys(ds_s.at[h % 2], 0, k_all, k_own)

        scores(0)
        prob_grads(0)
        for h in range(heads + 1):
            if h + 1 < heads:
                scores(h + 1)
                prob_grads(h + 1)
            if h < heads:
                strips(h)
            if h > 0:
                finish_head(h - 1)
        g_t = jnp.concatenate([grad_t_ref[h * HD : (h + 1) * HD, rows] for h in range(heads)], 1)
        dv_s[...] += dot_nn(g_t, p_s[:, :seen])
        dv_own = []
        for b in range(PAIR):
            g_b = jnp.concatenate([grad_t_ref[h * HD : (h + 1) * HD, own_rows[b]] for h in range(heads)], 1)
            starts = [(h * PAIR + b) * BLK for h in range(heads)]
            p_b = jnp.concatenate([p_s[n : n + BLK, seen:] for n in starts], 0)
            dv_own.append(dot_nn(g_b, p_b))
        dv_own = jnp.concatenate(dv_own, 1)
        dq = dq_s[...]
        cot_ref[0:RANK, rows] = dot_nt(qup_ref[...], dq)
        cot_ref[RANK : 2 * RANK, rows] = dot_nn(up_wide, dv_own, HIGHEST)
        cot_ref[2 * RANK :, rows] = dot_nt(tag_ref[...], att_s[...])
        up_ref[:, :query_width] += dot_nn(low_s[0:RANK, rows], dq)
        up_ref[:, query_width:] += dot_nt(low_s[RANK:, rows].astype(jnp.float32), dv_own, HIGHEST)
        return carry

    lax.fori_loop(0, q_s.shape[0] // (PAIR * BLK), pair_step, 0)
    dv = dv_s[...]
    mcot = dot_nn(up_wide, dv, HIGHEST)
    low_m = jnp.concatenate([low_m_s[b] for b in range(peers)], 1).astype(jnp.float32)
    up_ref[:, query_width:] += dot_nt(low_m, dv, HIGHEST)
    for b in range(peers):
        mcot_s[b] = mcot[:, b * BLK : (b + 1) * BLK]
    for n in range(peers // 2):
        same_ref[n] = mcot_s[lax.bitwise_xor(me_ref[0], 2 * n)]
        other_ref[n] = mcot_s[lax.bitwise_xor(me_ref[0], 2 * n + 1)]


def mix_kernel(same_ref, other_ref, *outs):
    for n, out in enumerate(outs):
        out[0] = same_ref[n]
        out[1] = other_ref[n]


def first_down_kernel(steps, me_ref, asked_ref, *refs):
    pieces, cots, slab_ref, up_ref = refs[:steps], refs[steps : steps + 4], refs[steps + 4], refs[steps + 5]
    logit_ref, query_ref, value_ref, own_ref, sum_s = refs[steps + 6 :]
    sum_s[...] = jnp.zeros_like(sum_s)
    for n, piece in enumerate(pieces):
        for side in range(2):
            block = asked_ref[lax.bitwise_xor(me_ref[0], 2 * n + side)]
            sum_s[block] = sum_s[block] + piece[side]
    own_ref[...] = jnp.concatenate([sum_s[m] for m in range(sum_s.shape[0])], 1)
    cot = (cots[0][...] + cots[1][...]) + (cots[2][...] + cots[3][...])
    logit_ref[...] = cot[2 * RANK :]
    both = dot_nn(cot[: 2 * RANK].astype(jnp.bfloat16), slab_ref[...])
    width = both.shape[1]
    query_ref[:, :width] = both[:RANK]
    query_ref[:, width:] = up_ref[...]
    value_ref[...] = both[RANK:]


def second_down_kernel(c0, c1, c2, c3, memory_ref, value_ref, out_ref):
    cot = (c0[...] + c1[...]) + (c2[...] + c3[...])
    out_ref[...] = value_ref[...] + dot_nn(cot.astype(jnp.bfloat16), memory_ref[...])


def finish_kernel(*refs):
    query, value = [
        (ref[0][...].astype(jnp.float32) + ref[1][...].astype(jnp.float32))
        + (ref[2][...].astype(jnp.float32) + ref[3][...].astype(jnp.float32))
        for ref in (refs[:4], refs[4:8])
    ]
    query_down_ref, query_up_ref, value_down_ref, value_up_ref = refs[8:]
    value_down_ref[...] = value
    at = 0
    for out_ref in (query_down_ref, query_up_ref, value_up_ref):
        out_ref[...] = query[:, at : at + out_ref.shape[1]]
        at += out_ref.shape[1]


def swap(x, bit, axis="heads"):
    return lax.ppermute(x, axis, [(i, i ^ bit) for i in range(lax.axis_size(axis))])


def after(x, *flags):
    return pl.pallas_call(
        lambda *refs: None,
        out_shape=jax.ShapeDtypeStruct(x.shape, x.dtype),
        in_specs=[anywhere()] + [smem()] * len(flags),
        out_specs=anywhere(),
        input_output_aliases={0: 0},
        name="in_order",
    )(x, *flags)


def anywhere():
    return pl.BlockSpec(memory_space=pl.ANY)


def smem():
    return pl.BlockSpec(memory_space=pltpu.SMEM)


def vmem():
    return pl.BlockSpec(memory_space=pltpu.VMEM)


def shaped(*shape, dtype=jnp.float32):
    return jax.ShapeDtypeStruct(shape, dtype)


def run(body, name, out_shape, in_specs, scratch=(), flops=0, moved=0, room=ROOM, out_specs=None):
    many = isinstance(out_shape, (tuple, list))
    return pl.pallas_call(
        body,
        out_shape=out_shape,
        in_specs=in_specs,
        out_specs=out_specs or (tuple(vmem() for _ in out_shape) if many else vmem()),
        scratch_shapes=list(scratch),
        compiler_params=pltpu.CompilerParams(vmem_limit_bytes=room * MIB),
        cost_estimate=pl.CostEstimate(flops=flops, bytes_accessed=moved, transcendentals=0),
        name=name,
    )


def fast(
    slab_tokens,
    memory,
    query_weight,
    key_weight,
    value_weight,
    query_down,
    query_up,
    value_down,
    value_up,
    tag_weight,
    retrieval,
    boundary,
    grad_tags,
):
    tok_rows, width = slab_tokens.shape
    mem_rows = memory.shape[0]
    query_width = query_weight.shape[1]
    heads = query_width // HD
    spans = tok_rows // BLK
    blocks = mem_rows // BLK
    peers = lax.axis_size("tm")
    f32 = jnp.float32
    bf16 = jnp.bfloat16

    def memory_scratch(count):
        return [
            pltpu.VMEM((count, mem_rows, width), bf16),
            pltpu.VMEM((count, width, HD), bf16),
            pltpu.VMEM((count, width, HD), bf16),
            pltpu.VMEM((count, RANK, width), bf16),
            pltpu.SemaphoreType.DMA((7 * count,)),
        ]

    def project_scratch(count):
        return [
            pltpu.VMEM((count, tok_rows, width), bf16),
            pltpu.VMEM((count, width, query_width), bf16),
            pltpu.VMEM((count, width, HD), bf16),
            pltpu.VMEM((count, width, HD), bf16),
            pltpu.VMEM((count, RANK, width), bf16),
            pltpu.VMEM((count, RANK, width), bf16),
            pltpu.SemaphoreType.DMA((count * (WQ_CUTS + 8),)),
        ]

    memory_sums = [
        pltpu.VMEM((mem_rows, 2 * HD), f32),
        pltpu.VMEM((mem_rows, RANK), f32),
        pltpu.SemaphoreType.DMA((2,)),
    ]
    project_sums = [
        pltpu.VMEM((tok_rows, query_width), f32),
        pltpu.VMEM((tok_rows, 2 * HD), f32),
        pltpu.VMEM((tok_rows, 2 * RANK), f32),
    ]

    place = lax.axis_index("heads").astype(jnp.int32).reshape(1)
    me = lax.axis_index("tm").astype(jnp.int32).reshape(1)
    tag_t = tag_weight.T
    tags = tag_t.shape[0]
    mem_far = swap(memory, 2)
    mem_near = swap(memory, 1)
    tok_near = swap(slab_tokens, 1)
    tok_far = swap(tok_near, 2)
    mem_acc, mem_low, wanted = run(
        lambda *refs: memory_early_kernel(blocks, *refs),
        "memory_near_half",
        (shaped(mem_rows, 2 * HD), shaped(mem_rows, RANK), shaped(peers, dtype=jnp.int32)),
        [smem()] * 2 + [anywhere()] * 5,
        memory_scratch(2),
        out_specs=(vmem(), vmem(), smem()),
    )(place, retrieval, memory, mem_near, key_weight, value_weight, value_down)
    asked = lax.all_to_all(wanted, "tm", split_axis=0, concat_axis=0, tiled=True)
    weights = (query_weight, key_weight, value_weight, query_down, value_down)
    *early, near_flag = run(
        project_early_kernel,
        "project_near_half",
        (shaped(tok_rows, query_width), shaped(tok_rows, 2 * HD), shaped(tok_rows, 2 * RANK), FLAG),
        [smem()] + [anywhere()] * 7 + [smem()],
        project_scratch(2),
        out_specs=(vmem(), vmem(), vmem(), smem()),
    )(place, slab_tokens, tok_near, *weights, wanted)
    mem_far = after(mem_far, near_flag, asked)
    mem_cross = swap(mem_far, 1)
    mem_weights = (key_weight, value_weight, value_down)
    mem_acc, mem_low = run(
        memory_middle_kernel,
        "memory_far_quarter",
        (shaped(mem_rows, 2 * HD), shaped(mem_rows, RANK)),
        [smem()] + [anywhere()] * 6,
        memory_scratch(1) + memory_sums,
    )(place, mem_far, mem_acc, mem_low, *mem_weights)
    pairs, pair_flag = run(
        lambda *refs: memory_kernel(peers, *refs),
        "memory_pairs",
        (shaped(peers, PACK, HD, dtype=bf16), FLAG),
        [smem()] * 2 + [anywhere()] * 6 + [vmem()],
        memory_scratch(1) + memory_sums + [pltpu.VMEM((blocks, PACK, HD), bf16)],
        out_specs=(vmem(), smem()),
    )(place, asked, mem_cross, mem_acc, mem_low, *mem_weights, value_up)
    got = lax.all_to_all(pairs, "tm", split_axis=0, concat_axis=0, tiled=True)
    grad, grad_t, grad_flag = run(
        grad_kernel,
        "attended_cotangent",
        (shaped(tok_rows, query_width, dtype=bf16), shaped(query_width, tok_rows, dtype=bf16), FLAG),
        [vmem()] * 2 + [smem()],
        out_specs=(vmem(), vmem(), smem()),
    )(tag_t, grad_tags.T, pair_flag)
    tok_far = after(tok_far, grad_flag)
    tok_cross = swap(tok_far, 1)
    early = run(
        project_middle_kernel,
        "project_far_quarter",
        (shaped(tok_rows, query_width), shaped(tok_rows, 2 * HD), shaped(tok_rows, 2 * RANK)),
        [smem()] + [anywhere()] * 9,
        project_scratch(1) + project_sums + [pltpu.SemaphoreType.DMA((6,))],
    )(place, tok_far, *weights, *early)

    seen = peers * BLK
    total = seen + BLK
    cot, ups, same, other = run(
        lambda *refs: attention_kernel(peers, heads, *refs),
        "span_attention",
        (shaped(2 * RANK + tags, tok_rows), shaped(RANK, query_width + HD))
        + (shaped(peers // 2, RANK, BLK),) * 2,
        [smem()] * 3 + [anywhere()] * 12 + [vmem()] * 3,
        project_scratch(1)
        + project_sums
        + [
            pltpu.VMEM((tok_rows, query_width), bf16),
            pltpu.VMEM((tok_rows, HD), bf16),
            pltpu.VMEM((tok_rows, HD), bf16),
            pltpu.VMEM((2 * RANK, tok_rows), bf16),
            pltpu.VMEM((peers, RANK, BLK), bf16),
            pltpu.VMEM((tok_rows, query_width), bf16),
            pltpu.VMEM((query_width, tok_rows), bf16),
            pltpu.VMEM((seen, HD), bf16),
            pltpu.VMEM((seen, HD), bf16),
            pltpu.VMEM((HD, seen), bf16),
            pltpu.VMEM((HD, seen), bf16),
            pltpu.VMEM((HD, PAIR * BLK), bf16),
            pltpu.VMEM((HD, PAIR * BLK), bf16),
            pltpu.VMEM((PAIR * BLK, BLK), f32),
            pltpu.VMEM((2, PAIR * BLK, total), f32),
            pltpu.VMEM((2, PAIR * BLK, total), f32),
            pltpu.VMEM((heads * PAIR * BLK, total), bf16),
            pltpu.VMEM((2, PAIR * BLK, total), bf16),
            pltpu.VMEM((PAIR * BLK, query_width), bf16),
            pltpu.VMEM((PAIR * BLK, query_width), bf16),
            pltpu.VMEM((HD, seen), f32),
            pltpu.VMEM((peers, RANK, BLK), f32),
            pltpu.SemaphoreType.DMA((3 * peers + 14,)),
        ],
        flops=20 * tok_rows * query_width * total,
        moved=4 * tok_rows * query_width,
    )(place, me, boundary, tok_cross, *weights, *early, got, grad, grad_t, query_up, value_up, tag_t)

    steps = peers // 2
    mixed = run(
        mix_kernel,
        "both_sides",
        (shaped(2, RANK, BLK),) * steps,
        [vmem()] * 2,
        room=8,
    )(same, swap(other, 1, "tm"))
    back = [mixed[0]] + [swap(mixed[n], 2 * n, "tm") for n in range(1, steps)]
    cots = [cot] + [swap(cot, d) for d in range(1, 4)]
    logits, query_sum, value_part, own = run(
        lambda *refs: first_down_kernel(steps, *refs),
        "first_down",
        (
            shaped(tags, tok_rows),
            shaped(RANK, width + ups.shape[1]),
            shaped(RANK, width),
            shaped(RANK, mem_rows),
        ),
        [smem()] * 2 + [vmem()] * (steps + 6),
        [pltpu.VMEM((blocks, RANK, BLK), f32)],
        room=8,
    )(me, asked, *back, *cots, slab_tokens, ups)
    owns = [own] + [swap(own, d) for d in range(1, 4)]
    value_sum = run(
        second_down_kernel,
        "second_down",
        shaped(RANK, width),
        [vmem()] * 6,
        flops=2 * RANK * mem_rows * width,
        moved=2 * mem_rows * width,
        room=8,
    )(*owns, memory, value_part)
    sums = []
    for part in (query_sum, value_sum):
        part = (part + swap(part, 1, "tm")).astype(bf16)
        sums += [part] + [swap(part, bit, "tm") for bit in (2, 4, 6)]
    query_down_grad, query_up_grad, value_down_grad, value_up_grad = run(
        finish_kernel,
        "finish_outputs",
        (shaped(RANK, width), shaped(RANK, query_width), shaped(RANK, width), shaped(RANK, HD)),
        [vmem()] * 8,
        room=8,
    )(*sums)
    return (logits.T, query_down_grad, query_up_grad, value_down_grad, value_up_grad)


def solution(mesh):
    in_specs = (
        P("tm", "heads"),
        P("tm", "heads"),
        P(None, "heads"),
        P(None, "heads"),
        P(None, "heads"),
        P(),
        P(None, "heads"),
        P(),
        P(None, "heads"),
        P("heads", None),
        P("tm", None),
        P("tm"),
        P("tm", None),
    )
    out_specs = (
        P("tm", None),
        P(None, "heads"),
        P(None, "heads"),
        P(None, "heads"),
        P(None, "heads"),
    )
    fits = mesh.shape["heads"] == 4 and mesh.shape["tm"] == 8 == TOP * CAP
    local = fast if fits else general
    return jax.shard_map(local, mesh=mesh, in_specs=in_specs, out_specs=out_specs, check_vma=False)
```

```python
import jax
import jax.numpy as jnp
from jax import lax
from jax.experimental import pallas as pl
from jax.experimental.pallas import tpu as pltpu
from jax.sharding import PartitionSpec as P

HD = 128
RANK = 16
TOP = 8
BLK = 128
CAP = 1


HIGHEST = lax.Precision.HIGHEST


def attend(query, all_keys, all_values, split_row, out_grad):
    span_count, row_count, query_width = query.shape
    key_count, kv_width = (all_keys.shape[1], all_keys.shape[2])
    kv_heads = kv_width // HD
    group_size = query_width // kv_width
    score_scale = HD ** (-0.5)
    query_heads = query.reshape(span_count, row_count, kv_heads, group_size, HD)
    key_heads = all_keys.reshape(span_count, key_count, kv_heads, HD)
    value_heads = all_values.reshape(span_count, key_count, kv_heads, HD)
    grad_heads = out_grad.reshape(span_count, row_count, kv_heads, group_size, HD)
    scores = (
        jnp.einsum("crngd,cknd->cngrk", query_heads, key_heads, preferred_element_type=jnp.float32)
        * score_scale
    )
    row_ids = jnp.arange(row_count, dtype=jnp.int32)[:, None]
    col_ids = jnp.arange(BLK, dtype=jnp.int32)[None, :]
    edge_at = split_row[:, None, None]
    local_seen = (col_ids <= row_ids) & ((col_ids >= edge_at) | (row_ids < edge_at))
    visible = jnp.concatenate(
        [jnp.ones((span_count, row_count, key_count - BLK), jnp.bool_), local_seen], axis=2
    )
    scores = jnp.where(visible[:, None, None], scores, -jnp.inf)
    row_max = jnp.max(scores, axis=-1, keepdims=True)
    weights = jnp.exp(scores - row_max)
    probs = weights / jnp.sum(weights, axis=-1, keepdims=True)
    probs_low = probs.astype(jnp.bfloat16)
    attended = jnp.einsum(
        "cngrk,cknd->crngd", probs_low, value_heads, preferred_element_type=jnp.float32
    ).astype(jnp.bfloat16)
    prob_grad = jnp.einsum(
        "crngd,cknd->cngrk", grad_heads, value_heads, preferred_element_type=jnp.float32
    )
    row_dot = jnp.sum(grad_heads.astype(jnp.float32) * attended.astype(jnp.float32), axis=-1)
    row_dot = jnp.transpose(row_dot, (0, 2, 3, 1))[..., None]
    score_grad = (probs * (prob_grad - row_dot) * score_scale).astype(jnp.bfloat16)
    query_grad = jnp.einsum(
        "cngrk,cknd->crngd", score_grad, key_heads, preferred_element_type=jnp.float32
    ).astype(jnp.bfloat16)
    value_grad = jnp.einsum(
        "cngrk,crngd->cknd", probs_low, grad_heads, preferred_element_type=jnp.float32
    )
    return (
        attended.reshape(span_count, row_count, query_width),
        query_grad.reshape(span_count, row_count, query_width),
        value_grad.reshape(span_count, key_count, kv_width),
    )


def choose_slots(needed, places):
    slot_ids = jnp.arange(CAP, dtype=jnp.int32)
    return needed[:, None, :] * (places[:, None, :] == slot_ids[None, :, None]).astype(jnp.int32)


def general(
    slab_tokens,
    memory,
    query_weight,
    key_weight,
    value_weight,
    query_down,
    query_up,
    value_down,
    value_up,
    tag_weight,
    retrieval,
    boundary,
    grad_tags,
):
    tok_rows = slab_tokens.shape[0]
    mem_rows = memory.shape[0]
    query_width = query_weight.shape[1]
    kv_width = key_weight.shape[1]
    span_count = tok_rows // BLK
    block_count = mem_rows // BLK
    pair_weight = jnp.concatenate([key_weight, value_weight], 1)
    adapter_pair = jnp.concatenate([query_down, value_down], 0)
    contract_last = (((1,), (1,)), ((), ()))
    contract_first = (((0,), (0,)), ((), ()))
    token_piece = lax.all_gather(slab_tokens, "heads", axis=1, tiled=True)
    memory_piece = lax.all_gather(memory, "heads", axis=1, tiled=True)
    query_acc = jnp.dot(token_piece, query_weight, preferred_element_type=jnp.float32)
    pair_acc = jnp.dot(token_piece, pair_weight, preferred_element_type=jnp.float32)
    low_acc = lax.dot_general(
        token_piece, adapter_pair, contract_last, preferred_element_type=jnp.float32
    )
    memory_acc = jnp.dot(memory_piece, pair_weight, preferred_element_type=jnp.float32)
    memory_low_acc = lax.dot_general(
        memory_piece, adapter_pair[RANK:], contract_last, preferred_element_type=jnp.float32
    )
    query_acc, pair_acc, low_acc, memory_acc, memory_low_acc = (
        query_acc,
        pair_acc,
        low_acc,
        memory_acc,
        memory_low_acc,
    )
    low_tokens = low_acc.astype(jnp.bfloat16)
    low_query = low_tokens[:, :RANK]
    low_value = low_tokens[:, RANK:]
    queries = (query_acc + jnp.dot(low_query, query_up, preferred_element_type=jnp.float32)).astype(
        jnp.bfloat16
    )
    keys_local = pair_acc[:, :kv_width].astype(jnp.bfloat16)
    values_local = (
        pair_acc[:, kv_width:] + jnp.dot(low_value, value_up, preferred_element_type=jnp.float32)
    ).astype(jnp.bfloat16)
    memory_low = memory_low_acc.astype(jnp.bfloat16)
    memory_pair = (
        jnp.concatenate(
            [
                memory_acc[:, :kv_width],
                memory_acc[:, kv_width:]
                + jnp.dot(memory_low, value_up, preferred_element_type=jnp.float32),
            ],
            1,
        )
        .astype(jnp.bfloat16)
        .reshape(block_count, BLK, 2 * kv_width)
    )
    peer_count = lax.axis_size("tm")
    every_block = jnp.arange(peer_count * block_count, dtype=jnp.int32)
    wanted = (
        jnp.any(retrieval.reshape(-1, 1) == every_block[None, :], axis=0)
        .astype(jnp.int32)
        .reshape(peer_count, block_count)
    )
    places = jnp.cumsum(wanted, axis=1) - wanted
    requested = choose_slots(wanted, places)
    asked_for = lax.all_to_all(requested, "tm", split_axis=0, concat_axis=0, tiled=True)
    rows_needed = retrieval // block_count * CAP + jnp.take(places.reshape(-1), retrieval)
    asked_low = asked_for.astype(jnp.bfloat16)
    outgoing = jnp.einsum(
        "rcm,mbw->rcbw", asked_low, memory_pair, preferred_element_type=jnp.float32
    ).astype(jnp.bfloat16)
    fetched = lax.all_to_all(outgoing, "tm", split_axis=0, concat_axis=0, tiled=True)
    slot_rows = fetched.reshape(peer_count * CAP, BLK, 2 * kv_width)
    picked = jnp.take(slot_rows, rows_needed.reshape(-1), axis=0).reshape(
        span_count, TOP * BLK, 2 * kv_width
    )
    all_keys = jnp.concatenate(
        [picked[..., :kv_width], keys_local.reshape(span_count, BLK, kv_width)], 1
    )
    all_values = jnp.concatenate(
        [picked[..., kv_width:], values_local.reshape(span_count, BLK, kv_width)], 1
    )
    attended_grad = lax.dot_general(
        grad_tags, tag_weight.astype(jnp.float32), contract_last, precision=HIGHEST
    ).astype(jnp.bfloat16)
    attended, query_grad, value_grad = attend(
        queries.reshape(span_count, BLK, query_width),
        all_keys,
        all_values,
        boundary,
        attended_grad.reshape(span_count, BLK, query_width),
    )
    attended = attended.reshape(tok_rows, query_width)
    query_grad = query_grad.reshape(tok_rows, query_width)
    logits_out = lax.psum(
        jnp.dot(attended, tag_weight, preferred_element_type=jnp.float32), "heads"
    )
    local_grad = value_grad[:, TOP * BLK :].reshape(tok_rows, kv_width)
    slot_grads = value_grad[:, : TOP * BLK].reshape(span_count * TOP, BLK * kv_width)
    slot_hits = (
        rows_needed.reshape(-1, 1) == jnp.arange(peer_count * CAP, dtype=jnp.int32)[None, :]
    ).astype(jnp.float32)
    grad_buffer = lax.dot_general(slot_hits, slot_grads, contract_first, precision=HIGHEST).reshape(
        peer_count * CAP, BLK, kv_width
    )
    up_wide = value_up.astype(jnp.float32)
    returned = lax.all_to_all(
        grad_buffer.reshape(peer_count, CAP, BLK, kv_width),
        "tm",
        split_axis=0,
        concat_axis=0,
        tiled=True,
    )
    owned_grad = jnp.einsum(
        "rcm,rcbw->mbw", asked_for.astype(jnp.float32), returned, precision=HIGHEST
    ).reshape(mem_rows, kv_width)
    memory_cot = lax.dot_general(up_wide, owned_grad, contract_last, precision=HIGHEST)
    up_memory = lax.dot_general(
        memory_low.astype(jnp.float32), owned_grad, contract_first, precision=HIGHEST
    )
    query_cot = lax.dot_general(
        query_up, query_grad, contract_last, preferred_element_type=jnp.float32
    )
    value_cot = lax.dot_general(up_wide, local_grad, contract_last, precision=HIGHEST)
    query_cot, value_cot, memory_cot = lax.psum((query_cot, value_cot, memory_cot), "heads")
    query_down_grad = jnp.dot(
        query_cot.astype(jnp.bfloat16), slab_tokens, preferred_element_type=jnp.float32
    )
    value_down_grad = jnp.dot(
        value_cot.astype(jnp.bfloat16), slab_tokens, preferred_element_type=jnp.float32
    ) + jnp.dot(memory_cot.astype(jnp.bfloat16), memory, preferred_element_type=jnp.float32)
    query_up_grad = lax.dot_general(
        low_query, query_grad, contract_first, preferred_element_type=jnp.float32
    )
    value_up_grad = (
        lax.dot_general(
            low_value.astype(jnp.float32), local_grad, contract_first, precision=HIGHEST
        )
        + up_memory
    )
    query_down_grad, query_up_grad, value_down_grad, value_up_grad = lax.psum(
        (query_down_grad, query_up_grad, value_down_grad, value_up_grad), "tm"
    )
    return (logits_out, query_down_grad, query_up_grad, value_down_grad, value_up_grad)


LOG2E = 1.4426950408889634
NT = (((1,), (1,)), ((), ()))
PACK = 2 * BLK + RANK
STRIP = 16
PAIR = 2
MIB = 1024 * 1024
ROOM = 63.5


def dot_nt(a, b, precision=None):
    return lax.dot_general(a, b, NT, precision=precision, preferred_element_type=jnp.float32)


def dot_nn(a, b, precision=None):
    return jnp.dot(a, b, precision=precision, preferred_element_type=jnp.float32)


def piece_rows(place_ref, j, width):
    return pl.ds(pl.multiple_of(lax.bitwise_xor(place_ref[0], j) * width, width), width)


def start_copies(pairs, sems, first=0):
    copies = [pltpu.make_async_copy(src, dst, sems.at[first + n]) for n, (src, dst) in enumerate(pairs)]
    for copy in copies:
        copy.start()
    return copies


def wait_all(copies):
    for copy in copies:
        copy.wait()


def memory_pieces(place_ref, js, xs, hbm, scratch, sems):
    x_s, wk_s, wv_s, down_s = scratch
    width = x_s.shape[2]
    groups = []
    for n, j in enumerate(js):
        here = piece_rows(place_ref, j, width)
        pairs = [
            (xs[n], x_s.at[n]),
            (hbm[0].at[here, :], wk_s.at[n]),
            (hbm[1].at[here, :], wv_s.at[n]),
            (hbm[2].at[:, here], down_s.at[n]),
        ]
        groups.append(start_copies(pairs, sems, 4 * n))
    return groups


def memory_terms(n, scratch):
    x_s, wk_s, wv_s, down_s = scratch
    x = x_s[n]
    return dot_nn(x, jnp.concatenate([wk_s[n], wv_s[n]], 1)), dot_nt(x, down_s[n])


def memory_early_kernel(blocks, place_ref, named_ref, x0, x1, *refs):
    hbm, acc_ref, low_ref, wanted_ref, scratch, sems = refs[:3], refs[3], refs[4], refs[5], refs[6:10], refs[10]
    groups = memory_pieces(place_ref, (0, 1), (x0, x1), hbm, scratch, sems)
    for slot in range(TOP):
        block = named_ref[0, slot]
        wanted_ref[lax.div(block, blocks)] = lax.rem(block, blocks)
    for n in range(2):
        wait_all(groups[n])
        term, low_term = memory_terms(n, scratch)
        if n == 0:
            acc_ref[...] = term
            low_ref[...] = low_term
        else:
            acc_ref[...] += term
            low_ref[...] += low_term


def memory_middle_kernel(place_ref, x2, acc_hbm, low_hbm, *refs):
    hbm, acc_ref, low_ref, scratch, sems = refs[:3], refs[3], refs[4], refs[5:9], refs[9]
    acc_s, low_s, acc_sems = refs[10:13]
    groups = memory_pieces(place_ref, (2,), (x2,), hbm, scratch, sems)
    sums = start_copies([(acc_hbm, acc_s), (low_hbm, low_s)], acc_sems)
    wait_all(groups[0])
    term, low_term = memory_terms(0, scratch)
    wait_all(sums)
    acc_ref[...] = acc_s[...] + term
    low_ref[...] = low_s[...] + low_term


def memory_kernel(peers, place_ref, asked_ref, x3, acc_hbm, low_hbm, *refs):
    hbm, up_ref, out_ref = refs[:3], refs[3], refs[4]
    scratch, sems, acc_s, low_s, acc_sems, pair_ref = refs[5:9], refs[9], refs[10], refs[11], refs[12], refs[13]
    groups = memory_pieces(place_ref, (3,), (x3,), hbm, scratch, sems)
    sums = start_copies([(acc_hbm, acc_s), (low_hbm, low_s)], acc_sems)
    wait_all(groups[0])
    term, low_term = memory_terms(0, scratch)
    wait_all(sums)
    acc = acc_s[...] + term
    low = low_s[...] + low_term
    values = (acc[:, HD:] + dot_nn(low.astype(jnp.bfloat16), up_ref[...])).astype(jnp.bfloat16)
    keys = acc[:, :HD].astype(jnp.bfloat16)
    low_t = jnp.transpose(low).astype(jnp.bfloat16)
    for b in range(acc.shape[0] // BLK):
        at = slice(b * BLK, (b + 1) * BLK)
        pair_ref[b, 0:BLK, :] = keys[at]
        pair_ref[b, BLK : 2 * BLK, :] = values[at]
        pair_ref[b, 2 * BLK : PACK, :] = low_t[:, at]
    for r in range(peers):
        out_ref[r] = pair_ref[asked_ref[r]]


WQ_CUTS = 4


def project_pieces(place_ref, js, xs, hbm, scratch, sems):
    wq_hbm, wk_hbm, wv_hbm, qd_hbm, vd_hbm = hbm
    x_s, wq_s, wk_s, wv_s, qd_s, vd_s = scratch
    width = x_s.shape[2]
    part = width // WQ_CUTS
    groups = []
    for n, j in enumerate(js):
        here = piece_rows(place_ref, j, width)
        start = lax.bitwise_xor(place_ref[0], j) * width
        pairs = [(xs[n], x_s.at[n])]
        for m in range(WQ_CUTS):
            rows = pl.ds(pl.multiple_of(start + m * part, part), part)
            pairs.append((wq_hbm.at[rows, :], wq_s.at[n, pl.ds(m * part, part), :]))
        pairs += [
            (wk_hbm.at[here, :], wk_s.at[n]),
            (wv_hbm.at[here, :], wv_s.at[n]),
            (qd_hbm.at[:, here], qd_s.at[n]),
            (vd_hbm.at[:, here], vd_s.at[n]),
        ]
        groups.append(start_copies(pairs, sems, len(pairs) * n))
    return groups


def project_terms(n, scratch):
    x_s, wq_s, wk_s, wv_s, qd_s, vd_s = scratch
    x = x_s[n]
    return (
        dot_nn(x, wq_s[n]),
        dot_nn(x, jnp.concatenate([wk_s[n], wv_s[n]], 1)),
        dot_nt(x, jnp.concatenate([qd_s[n], vd_s[n]], 0)),
    )


def project_early_kernel(place_ref, x0, x1, *refs):
    hbm, (tag_ref, tags_t_ref), outs, (grad_ref, grad_t_ref) = refs[:5], refs[5:7], refs[8:11], refs[11:13]
    scratch, sems = refs[13:19], refs[19]
    groups = project_pieces(place_ref, (0, 1), (x0, x1), hbm, scratch, sems)
    first = (((0,), (0,)), ((), ()))
    tag = tag_ref[...].astype(jnp.float32)
    tags_t = tags_t_ref[...]
    f32 = jnp.float32
    grad_ref[...] = lax.dot_general(
        tags_t, tag, first, precision=HIGHEST, preferred_element_type=f32
    ).astype(jnp.bfloat16)
    grad_t_ref[...] = lax.dot_general(
        tag, tags_t, first, precision=HIGHEST, preferred_element_type=f32
    ).astype(jnp.bfloat16)
    for n in range(2):
        wait_all(groups[n])
        for ref, term in zip(outs, project_terms(n, scratch)):
            if n == 0:
                ref[...] = term
            else:
                ref[...] += term


def project_far_kernel(place_ref, x3, x2, *refs):
    hbm, early, (qup_ref, vup_ref), (q_ref, k_ref, v_ref, low_ref) = refs[:5], refs[5:8], refs[8:10], refs[10:14]
    scratch, sems, sum_refs, sum_sems = refs[14:20], refs[20], refs[21:24], refs[24]
    groups = project_pieces(place_ref, (3, 2), (x3, x2), hbm, scratch, sems)
    loads = start_copies(list(zip(early, sum_refs)), sum_sems)
    wait_all(groups[0])
    terms = project_terms(0, scratch)
    wait_all(loads)
    for ref, term in zip(sum_refs, terms):
        ref[...] += term
    wait_all(groups[1])
    q_acc, kv_acc, low_acc = [ref[...] + term for ref, term in zip(sum_refs, project_terms(1, scratch))]
    low = low_acc.astype(jnp.bfloat16)
    q_ref[...] = (q_acc + dot_nn(low[:, :RANK], qup_ref[...])).astype(jnp.bfloat16)
    k_ref[...] = kv_acc[:, :HD].astype(jnp.bfloat16)
    v_ref[...] = (kv_acc[:, HD:] + dot_nn(low[:, RANK:], vup_ref[...])).astype(jnp.bfloat16)
    low_ref[...] = jnp.transpose(low_acc).astype(jnp.bfloat16)


def attention_kernel(peers, heads, bound_ref, *refs):
    parts, got, grad_hbm, grad_t_hbm = refs[:4], refs[4], refs[5], refs[6]
    qup_ref, vup_ref, tag_ref, cot_ref, up_ref, mcot_ref = refs[7:13]
    (q_s, k_own, v_own, low_s, low_m_s, grad_ref, grad_t_ref, k_all, v_all, kt_all, vt_all, kt_own, vt_own, bias_s, s_s, dp_s,
     p_s, ds_s, att_s, dq_s, dv_s, more_sems) = refs[13:]
    seen = peers * BLK
    pairs = []
    for b in range(peers):
        at = slice(b * BLK, (b + 1) * BLK)
        pairs.append((got.at[b, pl.ds(0, BLK), :], k_all.at[at, :]))
        pairs.append((got.at[b, pl.ds(BLK, BLK), :], v_all.at[at, :]))
        pairs.append((got.at[b, pl.ds(2 * BLK, RANK), :], low_m_s.at[b]))
    pairs += list(zip(parts, (q_s, k_own, v_own, low_s))) + [(grad_hbm, grad_ref), (grad_t_hbm, grad_t_ref)]
    copies = start_copies(pairs, more_sems)
    wait_all(copies[: 3 * peers])
    for b in range(peers):
        at = slice(b * BLK, (b + 1) * BLK)
        kt_all[:, at] = jnp.transpose(k_all[at, :])
        vt_all[:, at] = jnp.transpose(v_all[at, :])
    wait_all(copies[3 * peers :])
    dv_s[...] = jnp.zeros_like(dv_s)
    up_ref[...] = jnp.zeros_like(up_ref)
    scale = HD ** (-0.5)
    up_wide = vup_ref[...].astype(jnp.float32)
    query_width = heads * HD

    def pair_step(c, carry):
        base = c * (PAIR * BLK)
        rows = pl.ds(pl.multiple_of(base, PAIR * BLK), PAIR * BLK)
        own_rows = [pl.ds(pl.multiple_of(base + b * BLK, BLK), BLK) for b in range(PAIR)]
        row_ids = lax.broadcasted_iota(jnp.int32, (BLK, BLK), 0)
        col_ids = lax.broadcasted_iota(jnp.int32, (BLK, BLK), 1)
        for b in range(PAIR):
            kt_own[:, b * BLK : (b + 1) * BLK] = jnp.transpose(k_own[own_rows[b], :])
            vt_own[:, b * BLK : (b + 1) * BLK] = jnp.transpose(v_own[own_rows[b], :])
            edge = bound_ref[c * PAIR + b]
            visible = (col_ids <= row_ids) & ((col_ids >= edge) | (row_ids < edge))
            bias_s[b * BLK : (b + 1) * BLK, :] = jnp.where(visible, 0.0, -jnp.inf)

        def head_cols(h):
            return slice(h * HD, (h + 1) * HD)

        def times_keys(out_ref, left_ref, h, all_t, own_t):
            out_ref[:, :seen] = dot_nn(left_ref[rows, head_cols(h)], all_t[...])
            for b in range(PAIR):
                at = slice(b * BLK, (b + 1) * BLK)
                out_ref[at, seen:] = dot_nn(left_ref[own_rows[b], head_cols(h)], own_t[:, at])

        def over_keys(left_ref, first, all_ref, own_ref):
            whole = dot_nn(left_ref[first : first + PAIR * BLK, :seen], all_ref[...])
            mine = [
                dot_nn(left_ref[first + b * BLK : first + (b + 1) * BLK, seen:], own_ref[own_rows[b], :])
                for b in range(PAIR)
            ]
            return (whole + jnp.concatenate(mine, 0)).astype(jnp.bfloat16)

        def scores(h):
            times_keys(s_s.at[h % 2], q_s, h, kt_all, kt_own)

        def prob_grads(h):
            times_keys(dp_s.at[h % 2], grad_ref, h, vt_all, vt_own)

        def strips(h):
            for r in range(0, PAIR * BLK, STRIP):
                at = slice(r, r + STRIP)
                s = s_s[h % 2, at, :]
                s = jnp.concatenate([s[:, :seen], s[:, seen:] + bias_s[at, :]], 1) * (scale * LOG2E)
                w = jnp.exp2(s - jnp.max(s, axis=1, keepdims=True))
                probs = w * (1.0 / jnp.sum(w, axis=1, keepdims=True))
                probs_low = probs.astype(jnp.bfloat16)
                first = h * PAIR * BLK + r
                p_s[first : first + STRIP, :] = probs_low
                dp = dp_s[h % 2, at, :]
                dot = jnp.sum(probs_low.astype(jnp.float32) * dp, axis=1, keepdims=True)
                ds_s[h % 2, at, :] = (probs * ((dp - dot) * scale)).astype(jnp.bfloat16)

        def finish_head(h):
            att_s[:, head_cols(h)] = over_keys(p_s, h * PAIR * BLK, v_all, v_own)
            dq_s[:, head_cols(h)] = over_keys(ds_s.at[h % 2], 0, k_all, k_own)

        scores(0)
        prob_grads(0)
        for h in range(heads + 1):
            if h + 1 < heads:
                scores(h + 1)
                prob_grads(h + 1)
            if h < heads:
                strips(h)
            if h > 0:
                finish_head(h - 1)
        g_t = jnp.concatenate([grad_t_ref[h * HD : (h + 1) * HD, rows] for h in range(heads)], 1)
        dv_s[...] += dot_nn(g_t, p_s[:, :seen])
        dv_own = []
        for b in range(PAIR):
            g_b = jnp.concatenate([grad_t_ref[h * HD : (h + 1) * HD, own_rows[b]] for h in range(heads)], 1)
            starts = [(h * PAIR + b) * BLK for h in range(heads)]
            p_b = jnp.concatenate([p_s[n : n + BLK, seen:] for n in starts], 0)
            dv_own.append(dot_nn(g_b, p_b))
        dv_own = jnp.concatenate(dv_own, 1)
        dq = dq_s[...]
        cot_ref[0:RANK, rows] = dot_nt(qup_ref[...], dq)
        cot_ref[RANK : 2 * RANK, rows] = dot_nn(up_wide, dv_own, HIGHEST)
        cot_ref[2 * RANK :, rows] = dot_nt(tag_ref[...], att_s[...])
        up_ref[:, :query_width] += dot_nn(low_s[0:RANK, rows], dq)
        up_ref[:, query_width:] += dot_nt(low_s[RANK:, rows].astype(jnp.float32), dv_own, HIGHEST)
        return carry

    lax.fori_loop(0, q_s.shape[0] // (PAIR * BLK), pair_step, 0)
    dv = dv_s[...]
    mcot = dot_nn(up_wide, dv, HIGHEST)
    low_m = jnp.concatenate([low_m_s[b] for b in range(peers)], 1).astype(jnp.float32)
    up_ref[:, query_width:] += dot_nt(low_m, dv, HIGHEST)
    for b in range(peers):
        mcot_ref[b] = mcot[:, b * BLK : (b + 1) * BLK]


def first_down_kernel(peers, asked_ref, back_ref, c0, c1, c2, c3, slab_ref, up_ref, logit_ref, query_ref, value_ref, own_ref, sum_s):
    sum_s[...] = jnp.zeros_like(sum_s)
    for r in range(peers):
        block = asked_ref[r]
        sum_s[block] = sum_s[block] + back_ref[r]
    own_ref[...] = jnp.concatenate([sum_s[m] for m in range(sum_s.shape[0])], 1)
    cot = (c0[...] + c1[...]) + (c2[...] + c3[...])
    logit_ref[...] = cot[2 * RANK :]
    both = dot_nn(cot[: 2 * RANK].astype(jnp.bfloat16), slab_ref[...])
    width = both.shape[1]
    query_ref[:, :width] = both[:RANK]
    query_ref[:, width:] = up_ref[...]
    value_ref[...] = both[RANK:]


def second_down_kernel(c0, c1, c2, c3, memory_ref, value_ref, out_ref):
    cot = (c0[...] + c1[...]) + (c2[...] + c3[...])
    out_ref[...] = value_ref[...] + dot_nn(cot.astype(jnp.bfloat16), memory_ref[...])


def finish_kernel(*refs):
    query, value = [
        (ref[0][...].astype(jnp.float32) + ref[1][...].astype(jnp.float32))
        + (ref[2][...].astype(jnp.float32) + ref[3][...].astype(jnp.float32))
        for ref in (refs[:4], refs[4:8])
    ]
    query_down_ref, query_up_ref, value_down_ref, value_up_ref = refs[8:]
    value_down_ref[...] = value
    at = 0
    for out_ref in (query_down_ref, query_up_ref, value_up_ref):
        out_ref[...] = query[:, at : at + out_ref.shape[1]]
        at += out_ref.shape[1]


def swap(x, bit, axis="heads"):
    return lax.ppermute(x, axis, [(i, i ^ bit) for i in range(lax.axis_size(axis))])


def after(x, *deps):
    return pl.pallas_call(
        lambda *refs: None,
        out_shape=jax.ShapeDtypeStruct(x.shape, x.dtype),
        in_specs=[anywhere()] * (1 + len(deps)),
        out_specs=anywhere(),
        input_output_aliases={0: 0},
        name="in_order",
    )(x, *deps)


def anywhere():
    return pl.BlockSpec(memory_space=pl.ANY)


def smem():
    return pl.BlockSpec(memory_space=pltpu.SMEM)


def vmem():
    return pl.BlockSpec(memory_space=pltpu.VMEM)


def shaped(*shape, dtype=jnp.float32):
    return jax.ShapeDtypeStruct(shape, dtype)


def run(body, name, out_shape, in_specs, scratch=(), flops=0, moved=0, room=ROOM, out_specs=None):
    many = isinstance(out_shape, (tuple, list))
    return pl.pallas_call(
        body,
        out_shape=out_shape,
        in_specs=in_specs,
        out_specs=out_specs or (tuple(vmem() for _ in out_shape) if many else vmem()),
        scratch_shapes=list(scratch),
        compiler_params=pltpu.CompilerParams(vmem_limit_bytes=int(room * MIB)),
        cost_estimate=pl.CostEstimate(flops=flops, bytes_accessed=moved, transcendentals=0),
        name=name,
    )


def fast(
    slab_tokens,
    memory,
    query_weight,
    key_weight,
    value_weight,
    query_down,
    query_up,
    value_down,
    value_up,
    tag_weight,
    retrieval,
    boundary,
    grad_tags,
):
    tok_rows, width = slab_tokens.shape
    mem_rows = memory.shape[0]
    query_width = query_weight.shape[1]
    heads = query_width // HD
    spans = tok_rows // BLK
    blocks = mem_rows // BLK
    peers = lax.axis_size("tm")
    f32 = jnp.float32
    bf16 = jnp.bfloat16

    def memory_scratch(count):
        return [
            pltpu.VMEM((count, mem_rows, width), bf16),
            pltpu.VMEM((count, width, HD), bf16),
            pltpu.VMEM((count, width, HD), bf16),
            pltpu.VMEM((count, RANK, width), bf16),
            pltpu.SemaphoreType.DMA((4 * count,)),
        ]

    def project_scratch(count):
        return [
            pltpu.VMEM((count, tok_rows, width), bf16),
            pltpu.VMEM((count, width, query_width), bf16),
            pltpu.VMEM((count, width, HD), bf16),
            pltpu.VMEM((count, width, HD), bf16),
            pltpu.VMEM((count, RANK, width), bf16),
            pltpu.VMEM((count, RANK, width), bf16),
            pltpu.SemaphoreType.DMA((count * (WQ_CUTS + 5),)),
        ]

    memory_sums = [
        pltpu.VMEM((mem_rows, 2 * HD), f32),
        pltpu.VMEM((mem_rows, RANK), f32),
        pltpu.SemaphoreType.DMA((2,)),
    ]
    project_sums = [
        pltpu.VMEM((tok_rows, query_width), f32),
        pltpu.VMEM((tok_rows, 2 * HD), f32),
        pltpu.VMEM((tok_rows, 2 * RANK), f32),
    ]

    place = lax.axis_index("heads").astype(jnp.int32).reshape(1)
    tag_t = tag_weight.T
    tags = tag_t.shape[0]
    mem_far = swap(memory, 2)
    mem_near = swap(memory, 1)
    tok_near = swap(slab_tokens, 1)
    tok_far = swap(tok_near, 2)
    mem_acc, mem_low, wanted = run(
        lambda *refs: memory_early_kernel(blocks, *refs),
        "memory_near_half",
        (shaped(mem_rows, 2 * HD), shaped(mem_rows, RANK), shaped(peers, dtype=jnp.int32)),
        [smem()] * 2 + [anywhere()] * 5,
        memory_scratch(2),
        out_specs=(vmem(), vmem(), smem()),
    )(place, retrieval, memory, mem_near, key_weight, value_weight, value_down)
    asked = lax.all_to_all(wanted, "tm", split_axis=0, concat_axis=0, tiled=True)
    weights = (query_weight, key_weight, value_weight, query_down, value_down)
    mem_far = after(mem_far, asked)
    mem_cross = swap(mem_far, 1)
    mem_weights = (key_weight, value_weight, value_down)
    mem_acc, mem_low = run(
        memory_middle_kernel,
        "memory_far_quarter",
        (shaped(mem_rows, 2 * HD), shaped(mem_rows, RANK)),
        [smem()] + [anywhere()] * 6,
        memory_scratch(1) + memory_sums,
    )(place, mem_far, mem_acc, mem_low, *mem_weights)
    pairs = run(
        lambda *refs: memory_kernel(peers, *refs),
        "memory_pairs",
        shaped(peers, PACK, HD, dtype=bf16),
        [smem()] * 2 + [anywhere()] * 6 + [vmem()],
        memory_scratch(1) + memory_sums + [pltpu.VMEM((blocks, PACK, HD), bf16)],
    )(place, asked, mem_cross, mem_acc, mem_low, *mem_weights, value_up)
    got = lax.all_to_all(pairs, "tm", split_axis=0, concat_axis=0, tiled=True)
    *early, grad, grad_t = run(
        project_early_kernel,
        "project_near_half",
        (
            shaped(tok_rows, query_width),
            shaped(tok_rows, 2 * HD),
            shaped(tok_rows, 2 * RANK),
            shaped(tok_rows, query_width, dtype=bf16),
            shaped(query_width, tok_rows, dtype=bf16),
        ),
        [smem()] + [anywhere()] * 7 + [vmem()] * 2 + [anywhere()],
        project_scratch(2),
    )(place, slab_tokens, tok_near, *weights, tag_t, grad_tags.T, pairs)
    tok_far = after(tok_far, early[2])
    tok_cross = swap(tok_far, 1)
    parts = run(
        project_far_kernel,
        "project_far_half",
        (
            shaped(tok_rows, query_width, dtype=bf16),
            shaped(tok_rows, HD, dtype=bf16),
            shaped(tok_rows, HD, dtype=bf16),
            shaped(2 * RANK, tok_rows, dtype=bf16),
        ),
        [smem()] + [anywhere()] * 10 + [vmem()] * 2,
        project_scratch(2) + project_sums + [pltpu.SemaphoreType.DMA((3,))],
    )(place, tok_far, tok_cross, *weights, *early, query_up, value_up)

    seen = peers * BLK
    total = seen + BLK
    cot, ups, mcot = run(
        lambda *refs: attention_kernel(peers, heads, *refs),
        "span_attention",
        (shaped(2 * RANK + tags, tok_rows), shaped(RANK, query_width + HD), shaped(peers, RANK, BLK)),
        [smem()] + [anywhere()] * 7 + [vmem()] * 3,
        [
            pltpu.VMEM((tok_rows, query_width), bf16),
            pltpu.VMEM((tok_rows, HD), bf16),
            pltpu.VMEM((tok_rows, HD), bf16),
            pltpu.VMEM((2 * RANK, tok_rows), bf16),
            pltpu.VMEM((peers, RANK, BLK), bf16),
            pltpu.VMEM((tok_rows, query_width), bf16),
            pltpu.VMEM((query_width, tok_rows), bf16),
            pltpu.VMEM((seen, HD), bf16),
            pltpu.VMEM((seen, HD), bf16),
            pltpu.VMEM((HD, seen), bf16),
            pltpu.VMEM((HD, seen), bf16),
            pltpu.VMEM((HD, PAIR * BLK), bf16),
            pltpu.VMEM((HD, PAIR * BLK), bf16),
            pltpu.VMEM((PAIR * BLK, BLK), f32),
            pltpu.VMEM((2, PAIR * BLK, total), f32),
            pltpu.VMEM((2, PAIR * BLK, total), f32),
            pltpu.VMEM((heads * PAIR * BLK, total), bf16),
            pltpu.VMEM((2, PAIR * BLK, total), bf16),
            pltpu.VMEM((PAIR * BLK, query_width), bf16),
            pltpu.VMEM((PAIR * BLK, query_width), bf16),
            pltpu.VMEM((HD, seen), f32),
            pltpu.SemaphoreType.DMA((3 * peers + 6,)),
        ],
        flops=20 * tok_rows * query_width * total,
        moved=4 * tok_rows * query_width,
        room=60,
    )(boundary, *parts, got, grad, grad_t, query_up, value_up, tag_t)

    back = lax.all_to_all(mcot, "tm", split_axis=0, concat_axis=0, tiled=True)
    cots = [cot] + [swap(cot, d) for d in range(1, 4)]
    logits, query_sum, value_part, own = run(
        lambda *refs: first_down_kernel(peers, *refs),
        "first_down",
        (
            shaped(tags, tok_rows),
            shaped(RANK, width + ups.shape[1]),
            shaped(RANK, width),
            shaped(RANK, mem_rows),
        ),
        [smem()] + [vmem()] * 7,
        [pltpu.VMEM((blocks, RANK, BLK), f32)],
        room=8,
    )(asked, back, *cots, slab_tokens, ups)
    owns = [own] + [swap(own, d) for d in range(1, 4)]
    value_sum = run(
        second_down_kernel,
        "second_down",
        shaped(RANK, width),
        [vmem()] * 6,
        flops=2 * RANK * mem_rows * width,
        moved=2 * mem_rows * width,
        room=8,
    )(*owns, memory, value_part)
    sums = []
    for part in (query_sum, value_sum):
        part = (part + swap(part, 1, "tm")).astype(bf16)
        sums += [part] + [swap(part, bit, "tm") for bit in (2, 4, 6)]
    query_down_grad, query_up_grad, value_down_grad, value_up_grad = run(
        finish_kernel,
        "finish_outputs",
        (shaped(RANK, width), shaped(RANK, query_width), shaped(RANK, width), shaped(RANK, HD)),
        [vmem()] * 8,
        room=8,
    )(*sums)
    return (logits.T, query_down_grad, query_up_grad, value_down_grad, value_up_grad)


def solution(mesh):
    in_specs = (
        P("tm", "heads"),
        P("tm", "heads"),
        P(None, "heads"),
        P(None, "heads"),
        P(None, "heads"),
        P(),
        P(None, "heads"),
        P(),
        P(None, "heads"),
        P("heads", None),
        P("tm", None),
        P("tm"),
        P("tm", None),
    )
    out_specs = (
        P("tm", None),
        P(None, "heads"),
        P(None, "heads"),
        P(None, "heads"),
        P(None, "heads"),
    )
    fits = mesh.shape["heads"] == 4 and mesh.shape["tm"] == 8 == TOP * CAP
    local = fast if fits else general
    return jax.shard_map(local, mesh=mesh, in_specs=in_specs, out_specs=out_specs, check_vma=False)
```

```python
import jax
import jax.numpy as jnp
from jax import lax
from jax.experimental import pallas as pl
from jax.experimental.pallas import tpu as pltpu
from jax.sharding import PartitionSpec as P

HD = 128
RANK = 16
TOP = 8
BLK = 128
CAP = 1


HIGHEST = lax.Precision.HIGHEST


def attend(query, all_keys, all_values, split_row, out_grad):
    span_count, row_count, query_width = query.shape
    key_count, kv_width = (all_keys.shape[1], all_keys.shape[2])
    kv_heads = kv_width // HD
    group_size = query_width // kv_width
    score_scale = HD ** (-0.5)
    query_heads = query.reshape(span_count, row_count, kv_heads, group_size, HD)
    key_heads = all_keys.reshape(span_count, key_count, kv_heads, HD)
    value_heads = all_values.reshape(span_count, key_count, kv_heads, HD)
    grad_heads = out_grad.reshape(span_count, row_count, kv_heads, group_size, HD)
    scores = (
        jnp.einsum("crngd,cknd->cngrk", query_heads, key_heads, preferred_element_type=jnp.float32)
        * score_scale
    )
    row_ids = jnp.arange(row_count, dtype=jnp.int32)[:, None]
    col_ids = jnp.arange(BLK, dtype=jnp.int32)[None, :]
    edge_at = split_row[:, None, None]
    local_seen = (col_ids <= row_ids) & ((col_ids >= edge_at) | (row_ids < edge_at))
    visible = jnp.concatenate(
        [jnp.ones((span_count, row_count, key_count - BLK), jnp.bool_), local_seen], axis=2
    )
    scores = jnp.where(visible[:, None, None], scores, -jnp.inf)
    row_max = jnp.max(scores, axis=-1, keepdims=True)
    weights = jnp.exp(scores - row_max)
    probs = weights / jnp.sum(weights, axis=-1, keepdims=True)
    probs_low = probs.astype(jnp.bfloat16)
    attended = jnp.einsum(
        "cngrk,cknd->crngd", probs_low, value_heads, preferred_element_type=jnp.float32
    ).astype(jnp.bfloat16)
    prob_grad = jnp.einsum(
        "crngd,cknd->cngrk", grad_heads, value_heads, preferred_element_type=jnp.float32
    )
    row_dot = jnp.sum(grad_heads.astype(jnp.float32) * attended.astype(jnp.float32), axis=-1)
    row_dot = jnp.transpose(row_dot, (0, 2, 3, 1))[..., None]
    score_grad = (probs * (prob_grad - row_dot) * score_scale).astype(jnp.bfloat16)
    query_grad = jnp.einsum(
        "cngrk,cknd->crngd", score_grad, key_heads, preferred_element_type=jnp.float32
    ).astype(jnp.bfloat16)
    value_grad = jnp.einsum(
        "cngrk,crngd->cknd", probs_low, grad_heads, preferred_element_type=jnp.float32
    )
    return (
        attended.reshape(span_count, row_count, query_width),
        query_grad.reshape(span_count, row_count, query_width),
        value_grad.reshape(span_count, key_count, kv_width),
    )


def choose_slots(needed, places):
    slot_ids = jnp.arange(CAP, dtype=jnp.int32)
    return needed[:, None, :] * (places[:, None, :] == slot_ids[None, :, None]).astype(jnp.int32)


def general(
    slab_tokens,
    memory,
    query_weight,
    key_weight,
    value_weight,
    query_down,
    query_up,
    value_down,
    value_up,
    tag_weight,
    retrieval,
    boundary,
    grad_tags,
):
    tok_rows = slab_tokens.shape[0]
    mem_rows = memory.shape[0]
    query_width = query_weight.shape[1]
    kv_width = key_weight.shape[1]
    span_count = tok_rows // BLK
    block_count = mem_rows // BLK
    pair_weight = jnp.concatenate([key_weight, value_weight], 1)
    adapter_pair = jnp.concatenate([query_down, value_down], 0)
    contract_last = (((1,), (1,)), ((), ()))
    contract_first = (((0,), (0,)), ((), ()))
    token_piece = lax.all_gather(slab_tokens, "heads", axis=1, tiled=True)
    memory_piece = lax.all_gather(memory, "heads", axis=1, tiled=True)
    query_acc = jnp.dot(token_piece, query_weight, preferred_element_type=jnp.float32)
    pair_acc = jnp.dot(token_piece, pair_weight, preferred_element_type=jnp.float32)
    low_acc = lax.dot_general(
        token_piece, adapter_pair, contract_last, preferred_element_type=jnp.float32
    )
    memory_acc = jnp.dot(memory_piece, pair_weight, preferred_element_type=jnp.float32)
    memory_low_acc = lax.dot_general(
        memory_piece, adapter_pair[RANK:], contract_last, preferred_element_type=jnp.float32
    )
    query_acc, pair_acc, low_acc, memory_acc, memory_low_acc = (
        query_acc,
        pair_acc,
        low_acc,
        memory_acc,
        memory_low_acc,
    )
    low_tokens = low_acc.astype(jnp.bfloat16)
    low_query = low_tokens[:, :RANK]
    low_value = low_tokens[:, RANK:]
    queries = (query_acc + jnp.dot(low_query, query_up, preferred_element_type=jnp.float32)).astype(
        jnp.bfloat16
    )
    keys_local = pair_acc[:, :kv_width].astype(jnp.bfloat16)
    values_local = (
        pair_acc[:, kv_width:] + jnp.dot(low_value, value_up, preferred_element_type=jnp.float32)
    ).astype(jnp.bfloat16)
    memory_low = memory_low_acc.astype(jnp.bfloat16)
    memory_pair = (
        jnp.concatenate(
            [
                memory_acc[:, :kv_width],
                memory_acc[:, kv_width:]
                + jnp.dot(memory_low, value_up, preferred_element_type=jnp.float32),
            ],
            1,
        )
        .astype(jnp.bfloat16)
        .reshape(block_count, BLK, 2 * kv_width)
    )
    peer_count = lax.axis_size("tm")
    every_block = jnp.arange(peer_count * block_count, dtype=jnp.int32)
    wanted = (
        jnp.any(retrieval.reshape(-1, 1) == every_block[None, :], axis=0)
        .astype(jnp.int32)
        .reshape(peer_count, block_count)
    )
    places = jnp.cumsum(wanted, axis=1) - wanted
    requested = choose_slots(wanted, places)
    asked_for = lax.all_to_all(requested, "tm", split_axis=0, concat_axis=0, tiled=True)
    rows_needed = retrieval // block_count * CAP + jnp.take(places.reshape(-1), retrieval)
    asked_low = asked_for.astype(jnp.bfloat16)
    outgoing = jnp.einsum(
        "rcm,mbw->rcbw", asked_low, memory_pair, preferred_element_type=jnp.float32
    ).astype(jnp.bfloat16)
    fetched = lax.all_to_all(outgoing, "tm", split_axis=0, concat_axis=0, tiled=True)
    slot_rows = fetched.reshape(peer_count * CAP, BLK, 2 * kv_width)
    picked = jnp.take(slot_rows, rows_needed.reshape(-1), axis=0).reshape(
        span_count, TOP * BLK, 2 * kv_width
    )
    all_keys = jnp.concatenate(
        [picked[..., :kv_width], keys_local.reshape(span_count, BLK, kv_width)], 1
    )
    all_values = jnp.concatenate(
        [picked[..., kv_width:], values_local.reshape(span_count, BLK, kv_width)], 1
    )
    attended_grad = lax.dot_general(
        grad_tags, tag_weight.astype(jnp.float32), contract_last, precision=HIGHEST
    ).astype(jnp.bfloat16)
    attended, query_grad, value_grad = attend(
        queries.reshape(span_count, BLK, query_width),
        all_keys,
        all_values,
        boundary,
        attended_grad.reshape(span_count, BLK, query_width),
    )
    attended = attended.reshape(tok_rows, query_width)
    query_grad = query_grad.reshape(tok_rows, query_width)
    logits_out = lax.psum(
        jnp.dot(attended, tag_weight, preferred_element_type=jnp.float32), "heads"
    )
    local_grad = value_grad[:, TOP * BLK :].reshape(tok_rows, kv_width)
    slot_grads = value_grad[:, : TOP * BLK].reshape(span_count * TOP, BLK * kv_width)
    slot_hits = (
        rows_needed.reshape(-1, 1) == jnp.arange(peer_count * CAP, dtype=jnp.int32)[None, :]
    ).astype(jnp.float32)
    grad_buffer = lax.dot_general(slot_hits, slot_grads, contract_first, precision=HIGHEST).reshape(
        peer_count * CAP, BLK, kv_width
    )
    up_wide = value_up.astype(jnp.float32)
    returned = lax.all_to_all(
        grad_buffer.reshape(peer_count, CAP, BLK, kv_width),
        "tm",
        split_axis=0,
        concat_axis=0,
        tiled=True,
    )
    owned_grad = jnp.einsum(
        "rcm,rcbw->mbw", asked_for.astype(jnp.float32), returned, precision=HIGHEST
    ).reshape(mem_rows, kv_width)
    memory_cot = lax.dot_general(up_wide, owned_grad, contract_last, precision=HIGHEST)
    up_memory = lax.dot_general(
        memory_low.astype(jnp.float32), owned_grad, contract_first, precision=HIGHEST
    )
    query_cot = lax.dot_general(
        query_up, query_grad, contract_last, preferred_element_type=jnp.float32
    )
    value_cot = lax.dot_general(up_wide, local_grad, contract_last, precision=HIGHEST)
    query_cot, value_cot, memory_cot = lax.psum((query_cot, value_cot, memory_cot), "heads")
    query_down_grad = jnp.dot(
        query_cot.astype(jnp.bfloat16), slab_tokens, preferred_element_type=jnp.float32
    )
    value_down_grad = jnp.dot(
        value_cot.astype(jnp.bfloat16), slab_tokens, preferred_element_type=jnp.float32
    ) + jnp.dot(memory_cot.astype(jnp.bfloat16), memory, preferred_element_type=jnp.float32)
    query_up_grad = lax.dot_general(
        low_query, query_grad, contract_first, preferred_element_type=jnp.float32
    )
    value_up_grad = (
        lax.dot_general(
            low_value.astype(jnp.float32), local_grad, contract_first, precision=HIGHEST
        )
        + up_memory
    )
    query_down_grad, query_up_grad, value_down_grad, value_up_grad = lax.psum(
        (query_down_grad, query_up_grad, value_down_grad, value_up_grad), "tm"
    )
    return (logits_out, query_down_grad, query_up_grad, value_down_grad, value_up_grad)


LOG2E = 1.4426950408889634
NT = (((1,), (1,)), ((), ()))
PACK = 2 * BLK + RANK
STRIP = 16
PAIR = 2
MIB = 1024 * 1024
ROOM = 63.5


def dot_nt(a, b, precision=None):
    return lax.dot_general(a, b, NT, precision=precision, preferred_element_type=jnp.float32)


def dot_nn(a, b, precision=None):
    return jnp.dot(a, b, precision=precision, preferred_element_type=jnp.float32)


def piece_rows(place_ref, j, width):
    return pl.ds(pl.multiple_of(lax.bitwise_xor(place_ref[0], j) * width, width), width)


def start_copies(pairs, sems, first=0):
    copies = [pltpu.make_async_copy(src, dst, sems.at[first + n]) for n, (src, dst) in enumerate(pairs)]
    for copy in copies:
        copy.start()
    return copies


def wait_all(copies):
    for copy in copies:
        copy.wait()


def memory_pieces(place_ref, js, xs, hbm, scratch, sems):
    x_s, wk_s, wv_s, down_s = scratch
    width = x_s.shape[2]
    groups = []
    for n, j in enumerate(js):
        here = piece_rows(place_ref, j, width)
        pairs = [
            (xs[n], x_s.at[n]),
            (hbm[0].at[here, :], wk_s.at[n]),
            (hbm[1].at[here, :], wv_s.at[n]),
            (hbm[2].at[:, here], down_s.at[n]),
        ]
        groups.append(start_copies(pairs, sems, 4 * n))
    return groups


def memory_terms(n, scratch):
    x_s, wk_s, wv_s, down_s = scratch
    x = x_s[n]
    return dot_nn(x, jnp.concatenate([wk_s[n], wv_s[n]], 1)), dot_nt(x, down_s[n])


def wanted_kernel(blocks, named_ref, dep_ref, wanted_ref):
    for slot in range(TOP):
        block = named_ref[0, slot]
        wanted_ref[lax.div(block, blocks)] = lax.rem(block, blocks)


def memory_early_kernel(place_ref, x0, x1, *refs):
    hbm, acc_ref, low_ref, scratch, sems = refs[:3], refs[4], refs[5], refs[6:10], refs[10]
    groups = memory_pieces(place_ref, (0, 1), (x0, x1), hbm, scratch, sems)
    for n in range(2):
        wait_all(groups[n])
        term, low_term = memory_terms(n, scratch)
        if n == 0:
            acc_ref[...] = term
            low_ref[...] = low_term
        else:
            acc_ref[...] += term
            low_ref[...] += low_term


def memory_kernel(first, peers, place_ref, asked_ref, x2, x3, acc_hbm, low_hbm, *refs):
    hbm, up_ref, before, out_ref = refs[:3], refs[3], refs[4], refs[5]
    scratch, sems, acc_s, low_s, acc_sems = refs[6:10], refs[10], refs[11], refs[12], refs[13]
    groups = memory_pieces(place_ref, (2, 3), (x2, x3), hbm, scratch, sems)
    at = pl.ds(first, x2.shape[0])
    pairs = [(acc_hbm.at[at, :], acc_s), (low_hbm.at[at, :], low_s)]
    if first:
        pair_ref = refs[14]
        offset = before.shape[0]
        pairs.append((before, pair_ref.at[pl.ds(0, offset)]))
    else:
        pair_ref = out_ref
        offset = 0
    sums = start_copies(pairs, acc_sems)
    terms = []
    for n in range(2):
        wait_all(groups[n])
        terms.append(memory_terms(n, scratch))
    wait_all(sums)
    acc = acc_s[...] + terms[0][0] + terms[1][0]
    low = low_s[...] + terms[0][1] + terms[1][1]
    values = (acc[:, HD:] + dot_nn(low.astype(jnp.bfloat16), up_ref[...])).astype(jnp.bfloat16)
    keys = acc[:, :HD].astype(jnp.bfloat16)
    low_t = jnp.transpose(low).astype(jnp.bfloat16)
    for b in range(acc.shape[0] // BLK):
        at = slice(b * BLK, (b + 1) * BLK)
        pair_ref[offset + b, 0:BLK, :] = keys[at]
        pair_ref[offset + b, BLK : 2 * BLK, :] = values[at]
        pair_ref[offset + b, 2 * BLK : PACK, :] = low_t[:, at]
    if first:
        for r in range(peers):
            out_ref[r] = pair_ref[asked_ref[r]]


WQ_CUTS = 4


def project_pieces(place_ref, js, xs, hbm, scratch, sems):
    wq_hbm, wk_hbm, wv_hbm, qd_hbm, vd_hbm = hbm
    x_s, wq_s, wk_s, wv_s, qd_s, vd_s = scratch
    width = x_s.shape[2]
    part = width // WQ_CUTS
    groups = []
    for n, j in enumerate(js):
        here = piece_rows(place_ref, j, width)
        start = lax.bitwise_xor(place_ref[0], j) * width
        pairs = [(xs[n], x_s.at[n])]
        for m in range(WQ_CUTS):
            rows = pl.ds(pl.multiple_of(start + m * part, part), part)
            pairs.append((wq_hbm.at[rows, :], wq_s.at[n, pl.ds(m * part, part), :]))
        pairs += [
            (wk_hbm.at[here, :], wk_s.at[n]),
            (wv_hbm.at[here, :], wv_s.at[n]),
            (qd_hbm.at[:, here], qd_s.at[n]),
            (vd_hbm.at[:, here], vd_s.at[n]),
        ]
        groups.append(start_copies(pairs, sems, len(pairs) * n))
    return groups


def project_terms(n, scratch):
    x_s, wq_s, wk_s, wv_s, qd_s, vd_s = scratch
    x = x_s[n]
    return (
        dot_nn(x, wq_s[n]),
        dot_nn(x, jnp.concatenate([wk_s[n], wv_s[n]], 1)),
        dot_nt(x, jnp.concatenate([qd_s[n], vd_s[n]], 0)),
    )


def project_early_kernel(place_ref, x0, x1, *refs):
    hbm, (tag_ref, tags_t_ref), outs, (grad_ref, grad_t_ref) = refs[:5], refs[5:7], refs[8:11], refs[11:13]
    scratch, sems = refs[13:19], refs[19]
    groups = project_pieces(place_ref, (0, 1), (x0, x1), hbm, scratch, sems)
    first = (((0,), (0,)), ((), ()))
    tag = tag_ref[...].astype(jnp.float32)
    tags_t = tags_t_ref[...]
    f32 = jnp.float32
    grad_ref[...] = lax.dot_general(
        tags_t, tag, first, precision=HIGHEST, preferred_element_type=f32
    ).astype(jnp.bfloat16)
    grad_t_ref[...] = lax.dot_general(
        tag, tags_t, first, precision=HIGHEST, preferred_element_type=f32
    ).astype(jnp.bfloat16)
    for n in range(2):
        wait_all(groups[n])
        for ref, term in zip(outs, project_terms(n, scratch)):
            if n == 0:
                ref[...] = term
            else:
                ref[...] += term


def project_far_kernel(place_ref, x3, x2, *refs):
    hbm, early, (qup_ref, vup_ref), (q_ref, k_ref, v_ref, low_ref) = refs[:5], refs[5:8], refs[8:10], refs[10:14]
    scratch, sems, sum_refs, sum_sems = refs[14:20], refs[20], refs[21:24], refs[24]
    groups = project_pieces(place_ref, (3, 2), (x3, x2), hbm, scratch, sems)
    loads = start_copies(list(zip(early, sum_refs)), sum_sems)
    wait_all(groups[0])
    terms = project_terms(0, scratch)
    wait_all(loads)
    for ref, term in zip(sum_refs, terms):
        ref[...] += term
    wait_all(groups[1])
    q_acc, kv_acc, low_acc = [ref[...] + term for ref, term in zip(sum_refs, project_terms(1, scratch))]
    low = low_acc.astype(jnp.bfloat16)
    q_ref[...] = (q_acc + dot_nn(low[:, :RANK], qup_ref[...])).astype(jnp.bfloat16)
    k_ref[...] = kv_acc[:, :HD].astype(jnp.bfloat16)
    v_ref[...] = (kv_acc[:, HD:] + dot_nn(low[:, RANK:], vup_ref[...])).astype(jnp.bfloat16)
    low_ref[...] = jnp.transpose(low_acc).astype(jnp.bfloat16)


def attention_kernel(peers, heads, bound_ref, *refs):
    parts, got, grad_hbm, grad_t_hbm = refs[:4], refs[4], refs[5], refs[6]
    qup_ref, vup_ref, tag_ref, cot_ref, up_ref, mcot_ref = refs[7:13]
    (q_s, k_own, v_own, low_s, low_m_s, grad_ref, grad_t_ref, k_all, v_all, kt_all, vt_all, kt_own, vt_own, bias_s, s_s, dp_s,
     p_s, ds_s, att_s, dq_s, dv_s, more_sems) = refs[13:]
    seen = peers * BLK
    pairs = []
    for b in range(peers):
        at = slice(b * BLK, (b + 1) * BLK)
        pairs.append((got.at[b, pl.ds(0, BLK), :], k_all.at[at, :]))
        pairs.append((got.at[b, pl.ds(BLK, BLK), :], v_all.at[at, :]))
        pairs.append((got.at[b, pl.ds(2 * BLK, RANK), :], low_m_s.at[b]))
    pairs += list(zip(parts, (q_s, k_own, v_own, low_s))) + [(grad_hbm, grad_ref), (grad_t_hbm, grad_t_ref)]
    copies = start_copies(pairs, more_sems)
    wait_all(copies[: 3 * peers])
    for b in range(peers):
        at = slice(b * BLK, (b + 1) * BLK)
        kt_all[:, at] = jnp.transpose(k_all[at, :])
        vt_all[:, at] = jnp.transpose(v_all[at, :])
    wait_all(copies[3 * peers :])
    dv_s[...] = jnp.zeros_like(dv_s)
    up_ref[...] = jnp.zeros_like(up_ref)
    scale = HD ** (-0.5)
    up_wide = vup_ref[...].astype(jnp.float32)
    query_width = heads * HD

    def pair_step(c, carry):
        base = c * (PAIR * BLK)
        rows = pl.ds(pl.multiple_of(base, PAIR * BLK), PAIR * BLK)
        own_rows = [pl.ds(pl.multiple_of(base + b * BLK, BLK), BLK) for b in range(PAIR)]
        row_ids = lax.broadcasted_iota(jnp.int32, (BLK, BLK), 0)
        col_ids = lax.broadcasted_iota(jnp.int32, (BLK, BLK), 1)
        for b in range(PAIR):
            kt_own[:, b * BLK : (b + 1) * BLK] = jnp.transpose(k_own[own_rows[b], :])
            vt_own[:, b * BLK : (b + 1) * BLK] = jnp.transpose(v_own[own_rows[b], :])
            edge = bound_ref[c * PAIR + b]
            visible = (col_ids <= row_ids) & ((col_ids >= edge) | (row_ids < edge))
            bias_s[b * BLK : (b + 1) * BLK, :] = jnp.where(visible, 0.0, -jnp.inf)

        def head_cols(h):
            return slice(h * HD, (h + 1) * HD)

        def times_keys(out_ref, left_ref, h, all_t, own_t):
            out_ref[:, :seen] = dot_nn(left_ref[rows, head_cols(h)], all_t[...])
            for b in range(PAIR):
                at = slice(b * BLK, (b + 1) * BLK)
                out_ref[at, seen:] = dot_nn(left_ref[own_rows[b], head_cols(h)], own_t[:, at])

        def over_keys(left_ref, first, all_ref, own_ref):
            whole = dot_nn(left_ref[first : first + PAIR * BLK, :seen], all_ref[...])
            mine = [
                dot_nn(left_ref[first + b * BLK : first + (b + 1) * BLK, seen:], own_ref[own_rows[b], :])
                for b in range(PAIR)
            ]
            return (whole + jnp.concatenate(mine, 0)).astype(jnp.bfloat16)

        def scores(h):
            times_keys(s_s.at[h % 2], q_s, h, kt_all, kt_own)

        def prob_grads(h):
            times_keys(dp_s.at[h % 2], grad_ref, h, vt_all, vt_own)

        def strips(h):
            for r in range(0, PAIR * BLK, STRIP):
                at = slice(r, r + STRIP)
                s = s_s[h % 2, at, :]
                s = jnp.concatenate([s[:, :seen], s[:, seen:] + bias_s[at, :]], 1) * (scale * LOG2E)
                w = jnp.exp2(s - jnp.max(s, axis=1, keepdims=True))
                probs = w * (1.0 / jnp.sum(w, axis=1, keepdims=True))
                probs_low = probs.astype(jnp.bfloat16)
                first = h * PAIR * BLK + r
                p_s[first : first + STRIP, :] = probs_low
                dp = dp_s[h % 2, at, :]
                dot = jnp.sum(probs_low.astype(jnp.float32) * dp, axis=1, keepdims=True)
                ds_s[h % 2, at, :] = (probs * ((dp - dot) * scale)).astype(jnp.bfloat16)

        def finish_head(h):
            att_s[:, head_cols(h)] = over_keys(p_s, h * PAIR * BLK, v_all, v_own)
            dq_s[:, head_cols(h)] = over_keys(ds_s.at[h % 2], 0, k_all, k_own)

        scores(0)
        prob_grads(0)
        for h in range(heads + 1):
            if h + 1 < heads:
                scores(h + 1)
                prob_grads(h + 1)
            if h < heads:
                strips(h)
            if h > 0:
                finish_head(h - 1)
        g_t = jnp.concatenate([grad_t_ref[h * HD : (h + 1) * HD, rows] for h in range(heads)], 1)
        dv_s[...] += dot_nn(g_t, p_s[:, :seen])
        dv_own = []
        for b in range(PAIR):
            g_b = jnp.concatenate([grad_t_ref[h * HD : (h + 1) * HD, own_rows[b]] for h in range(heads)], 1)
            starts = [(h * PAIR + b) * BLK for h in range(heads)]
            p_b = jnp.concatenate([p_s[n : n + BLK, seen:] for n in starts], 0)
            dv_own.append(dot_nn(g_b, p_b))
        dv_own = jnp.concatenate(dv_own, 1)
        dq = dq_s[...]
        cot_ref[0:RANK, rows] = dot_nt(qup_ref[...], dq)
        cot_ref[RANK : 2 * RANK, rows] = dot_nn(up_wide, dv_own, HIGHEST)
        cot_ref[2 * RANK :, rows] = dot_nt(tag_ref[...], att_s[...])
        up_ref[:, :query_width] += dot_nn(low_s[0:RANK, rows], dq)
        up_ref[:, query_width:] += dot_nt(low_s[RANK:, rows].astype(jnp.float32), dv_own, HIGHEST)
        return carry

    lax.fori_loop(0, q_s.shape[0] // (PAIR * BLK), pair_step, 0)
    dv = dv_s[...]
    mcot = dot_nn(up_wide, dv, HIGHEST)
    low_m = jnp.concatenate([low_m_s[b] for b in range(peers)], 1).astype(jnp.float32)
    up_ref[:, query_width:] += dot_nt(low_m, dv, HIGHEST)
    for b in range(peers):
        mcot_ref[b] = mcot[:, b * BLK : (b + 1) * BLK]


def first_down_kernel(peers, asked_ref, back_ref, c0, c1, c2, c3, slab_ref, up_ref, logit_ref, query_ref, value_ref, own_ref, sum_s):
    sum_s[...] = jnp.zeros_like(sum_s)
    for r in range(peers):
        block = asked_ref[r]
        sum_s[block] = sum_s[block] + back_ref[r]
    own_ref[...] = jnp.concatenate([sum_s[m] for m in range(sum_s.shape[0])], 1)
    cot = (c0[...] + c1[...]) + (c2[...] + c3[...])
    logit_ref[...] = cot[2 * RANK :]
    both = dot_nn(cot[: 2 * RANK].astype(jnp.bfloat16), slab_ref[...])
    width = both.shape[1]
    query_ref[:, :width] = both[:RANK]
    query_ref[:, width:] = up_ref[...]
    value_ref[...] = both[RANK:]


def second_down_kernel(c0, c1, c2, c3, memory_ref, value_ref, out_ref):
    cot = (c0[...] + c1[...]) + (c2[...] + c3[...])
    out_ref[...] = value_ref[...] + dot_nn(cot.astype(jnp.bfloat16), memory_ref[...])


def finish_kernel(*refs):
    query, value = [
        (ref[0][...].astype(jnp.float32) + ref[1][...].astype(jnp.float32))
        + (ref[2][...].astype(jnp.float32) + ref[3][...].astype(jnp.float32))
        for ref in (refs[:4], refs[4:8])
    ]
    query_down_ref, query_up_ref, value_down_ref, value_up_ref = refs[8:]
    value_down_ref[...] = value
    at = 0
    for out_ref in (query_down_ref, query_up_ref, value_up_ref):
        out_ref[...] = query[:, at : at + out_ref.shape[1]]
        at += out_ref.shape[1]


def swap(x, bit, axis="heads"):
    return lax.ppermute(x, axis, [(i, i ^ bit) for i in range(lax.axis_size(axis))])


def after(x, *deps):
    return pl.pallas_call(
        lambda *refs: None,
        out_shape=jax.ShapeDtypeStruct(x.shape, x.dtype),
        in_specs=[anywhere()] * (1 + len(deps)),
        out_specs=anywhere(),
        input_output_aliases={0: 0},
        name="in_order",
    )(x, *deps)


def anywhere():
    return pl.BlockSpec(memory_space=pl.ANY)


def smem():
    return pl.BlockSpec(memory_space=pltpu.SMEM)


def vmem():
    return pl.BlockSpec(memory_space=pltpu.VMEM)


def shaped(*shape, dtype=jnp.float32):
    return jax.ShapeDtypeStruct(shape, dtype)


def run(body, name, out_shape, in_specs, scratch=(), flops=0, moved=0, room=ROOM, out_specs=None):
    many = isinstance(out_shape, (tuple, list))
    return pl.pallas_call(
        body,
        out_shape=out_shape,
        in_specs=in_specs,
        out_specs=out_specs or (tuple(vmem() for _ in out_shape) if many else vmem()),
        scratch_shapes=list(scratch),
        compiler_params=pltpu.CompilerParams(vmem_limit_bytes=int(room * MIB)),
        cost_estimate=pl.CostEstimate(flops=flops, bytes_accessed=moved, transcendentals=0),
        name=name,
    )


def fast(
    slab_tokens,
    memory,
    query_weight,
    key_weight,
    value_weight,
    query_down,
    query_up,
    value_down,
    value_up,
    tag_weight,
    retrieval,
    boundary,
    grad_tags,
):
    tok_rows, width = slab_tokens.shape
    mem_rows = memory.shape[0]
    query_width = query_weight.shape[1]
    heads = query_width // HD
    spans = tok_rows // BLK
    blocks = mem_rows // BLK
    peers = lax.axis_size("tm")
    f32 = jnp.float32
    bf16 = jnp.bfloat16

    def memory_scratch(count, rows):
        return [
            pltpu.VMEM((count, rows, width), bf16),
            pltpu.VMEM((count, width, HD), bf16),
            pltpu.VMEM((count, width, HD), bf16),
            pltpu.VMEM((count, RANK, width), bf16),
            pltpu.SemaphoreType.DMA((4 * count,)),
        ]

    def project_scratch(count):
        return [
            pltpu.VMEM((count, tok_rows, width), bf16),
            pltpu.VMEM((count, width, query_width), bf16),
            pltpu.VMEM((count, width, HD), bf16),
            pltpu.VMEM((count, width, HD), bf16),
            pltpu.VMEM((count, RANK, width), bf16),
            pltpu.VMEM((count, RANK, width), bf16),
            pltpu.SemaphoreType.DMA((count * (WQ_CUTS + 5),)),
        ]

    project_sums = [
        pltpu.VMEM((tok_rows, query_width), f32),
        pltpu.VMEM((tok_rows, 2 * HD), f32),
        pltpu.VMEM((tok_rows, 2 * RANK), f32),
    ]

    place = lax.axis_index("heads").astype(jnp.int32).reshape(1)
    tag_t = tag_weight.T
    tags = tag_t.shape[0]
    cut_rows = mem_rows // 2
    mem_far = [swap(m, 2) for m in jnp.split(memory, 2, 0)]
    mem_near = swap(memory, 1)
    tok_near = swap(slab_tokens, 1)
    tok_far = swap(tok_near, 2)
    wanted = run(
        lambda *refs: wanted_kernel(blocks, *refs),
        "wanted_blocks",
        shaped(peers, dtype=jnp.int32),
        [smem(), anywhere()],
        out_specs=smem(),
    )(retrieval, mem_near)
    asked = lax.all_to_all(wanted, "tm", split_axis=0, concat_axis=0, tiled=True)
    weights = (query_weight, key_weight, value_weight, query_down, value_down)
    mem_weights = (key_weight, value_weight, value_down)
    mem_acc, mem_low = run(
        memory_early_kernel,
        "memory_near_half",
        (shaped(mem_rows, 2 * HD), shaped(mem_rows, RANK)),
        [smem()] + [anywhere()] * 5 + [smem()],
        memory_scratch(2, mem_rows),
    )(place, memory, mem_near, *mem_weights, wanted)
    before = mem_low
    for t in range(2):
        if t == 0:
            far = after(mem_far[0], asked, mem_low)
            out_shape = shaped(blocks // 2, PACK, HD, dtype=bf16)
            extra = []
        else:
            far = mem_far[1]
            out_shape = shaped(peers, PACK, HD, dtype=bf16)
            extra = [pltpu.VMEM((blocks, PACK, HD), bf16)]
        before = run(
            lambda *refs, t=t: memory_kernel(t * cut_rows, peers, *refs),
            "memory_pairs",
            out_shape,
            [smem()] * 2 + [anywhere()] * 7 + [vmem(), anywhere()],
            memory_scratch(2, cut_rows)
            + [
                pltpu.VMEM((cut_rows, 2 * HD), f32),
                pltpu.VMEM((cut_rows, RANK), f32),
                pltpu.SemaphoreType.DMA((3,)),
            ]
            + extra,
        )(place, asked, far, swap(far, 1), mem_acc, mem_low, *mem_weights, value_up, before)
    pairs = before
    got = lax.all_to_all(pairs, "tm", split_axis=0, concat_axis=0, tiled=True)
    *early, grad, grad_t = run(
        project_early_kernel,
        "project_near_half",
        (
            shaped(tok_rows, query_width),
            shaped(tok_rows, 2 * HD),
            shaped(tok_rows, 2 * RANK),
            shaped(tok_rows, query_width, dtype=bf16),
            shaped(query_width, tok_rows, dtype=bf16),
        ),
        [smem()] + [anywhere()] * 7 + [vmem()] * 2 + [anywhere()],
        project_scratch(2),
    )(place, slab_tokens, tok_near, *weights, tag_t, grad_tags.T, pairs)
    tok_far = after(tok_far, early[2])
    tok_cross = swap(tok_far, 1)
    parts = run(
        project_far_kernel,
        "project_far_half",
        (
            shaped(tok_rows, query_width, dtype=bf16),
            shaped(tok_rows, HD, dtype=bf16),
            shaped(tok_rows, HD, dtype=bf16),
            shaped(2 * RANK, tok_rows, dtype=bf16),
        ),
        [smem()] + [anywhere()] * 10 + [vmem()] * 2,
        project_scratch(2) + project_sums + [pltpu.SemaphoreType.DMA((3,))],
    )(place, tok_far, tok_cross, *weights, *early, query_up, value_up)

    seen = peers * BLK
    total = seen + BLK
    cot, ups, mcot = run(
        lambda *refs: attention_kernel(peers, heads, *refs),
        "span_attention",
        (shaped(2 * RANK + tags, tok_rows), shaped(RANK, query_width + HD), shaped(peers, RANK, BLK)),
        [smem()] + [anywhere()] * 7 + [vmem()] * 3,
        [
            pltpu.VMEM((tok_rows, query_width), bf16),
            pltpu.VMEM((tok_rows, HD), bf16),
            pltpu.VMEM((tok_rows, HD), bf16),
            pltpu.VMEM((2 * RANK, tok_rows), bf16),
            pltpu.VMEM((peers, RANK, BLK), bf16),
            pltpu.VMEM((tok_rows, query_width), bf16),
            pltpu.VMEM((query_width, tok_rows), bf16),
            pltpu.VMEM((seen, HD), bf16),
            pltpu.VMEM((seen, HD), bf16),
            pltpu.VMEM((HD, seen), bf16),
            pltpu.VMEM((HD, seen), bf16),
            pltpu.VMEM((HD, PAIR * BLK), bf16),
            pltpu.VMEM((HD, PAIR * BLK), bf16),
            pltpu.VMEM((PAIR * BLK, BLK), f32),
            pltpu.VMEM((2, PAIR * BLK, total), f32),
            pltpu.VMEM((2, PAIR * BLK, total), f32),
            pltpu.VMEM((heads * PAIR * BLK, total), bf16),
            pltpu.VMEM((2, PAIR * BLK, total), bf16),
            pltpu.VMEM((PAIR * BLK, query_width), bf16),
            pltpu.VMEM((PAIR * BLK, query_width), bf16),
            pltpu.VMEM((HD, seen), f32),
            pltpu.SemaphoreType.DMA((3 * peers + 6,)),
        ],
        flops=20 * tok_rows * query_width * total,
        moved=4 * tok_rows * query_width,
        room=60,
    )(boundary, *parts, got, grad, grad_t, query_up, value_up, tag_t)

    back = lax.all_to_all(mcot, "tm", split_axis=0, concat_axis=0, tiled=True)
    cots = [cot] + [swap(cot, d) for d in range(1, 4)]
    logits, query_sum, value_part, own = run(
        lambda *refs: first_down_kernel(peers, *refs),
        "first_down",
        (
            shaped(tags, tok_rows),
            shaped(RANK, width + ups.shape[1]),
            shaped(RANK, width),
            shaped(RANK, mem_rows),
        ),
        [smem()] + [vmem()] * 7,
        [pltpu.VMEM((blocks, RANK, BLK), f32)],
        room=8,
    )(asked, back, *cots, slab_tokens, ups)
    owns = [own] + [swap(own, d) for d in range(1, 4)]
    value_sum = run(
        second_down_kernel,
        "second_down",
        shaped(RANK, width),
        [vmem()] * 6,
        flops=2 * RANK * mem_rows * width,
        moved=2 * mem_rows * width,
        room=8,
    )(*owns, memory, value_part)
    sums = []
    for part in (query_sum, value_sum):
        part = (part + swap(part, 1, "tm")).astype(bf16)
        sums += [part] + [swap(part, bit, "tm") for bit in (2, 4, 6)]
    query_down_grad, query_up_grad, value_down_grad, value_up_grad = run(
        finish_kernel,
        "finish_outputs",
        (shaped(RANK, width), shaped(RANK, query_width), shaped(RANK, width), shaped(RANK, HD)),
        [vmem()] * 8,
        room=8,
    )(*sums)
    return (logits.T, query_down_grad, query_up_grad, value_down_grad, value_up_grad)


def solution(mesh):
    in_specs = (
        P("tm", "heads"),
        P("tm", "heads"),
        P(None, "heads"),
        P(None, "heads"),
        P(None, "heads"),
        P(),
        P(None, "heads"),
        P(),
        P(None, "heads"),
        P("heads", None),
        P("tm", None),
        P("tm"),
        P("tm", None),
    )
    out_specs = (
        P("tm", None),
        P(None, "heads"),
        P(None, "heads"),
        P(None, "heads"),
        P(None, "heads"),
    )
    fits = mesh.shape["heads"] == 4 and mesh.shape["tm"] == 8 == TOP * CAP
    local = fast if fits else general
    return jax.shard_map(local, mesh=mesh, in_specs=in_specs, out_specs=out_specs, check_vma=False)
```

```python
import jax
import jax.numpy as jnp
from jax import lax
from jax.experimental import pallas as pl
from jax.experimental.pallas import tpu as pltpu
from jax.sharding import PartitionSpec as P

HD = 128
RANK = 16
TOP = 8
BLK = 128
CAP = 1


HIGHEST = lax.Precision.HIGHEST


def attend(query, all_keys, all_values, split_row, out_grad):
    span_count, row_count, query_width = query.shape
    key_count, kv_width = (all_keys.shape[1], all_keys.shape[2])
    kv_heads = kv_width // HD
    group_size = query_width // kv_width
    score_scale = HD ** (-0.5)
    query_heads = query.reshape(span_count, row_count, kv_heads, group_size, HD)
    key_heads = all_keys.reshape(span_count, key_count, kv_heads, HD)
    value_heads = all_values.reshape(span_count, key_count, kv_heads, HD)
    grad_heads = out_grad.reshape(span_count, row_count, kv_heads, group_size, HD)
    scores = (
        jnp.einsum("crngd,cknd->cngrk", query_heads, key_heads, preferred_element_type=jnp.float32)
        * score_scale
    )
    row_ids = jnp.arange(row_count, dtype=jnp.int32)[:, None]
    col_ids = jnp.arange(BLK, dtype=jnp.int32)[None, :]
    edge_at = split_row[:, None, None]
    local_seen = (col_ids <= row_ids) & ((col_ids >= edge_at) | (row_ids < edge_at))
    visible = jnp.concatenate(
        [jnp.ones((span_count, row_count, key_count - BLK), jnp.bool_), local_seen], axis=2
    )
    scores = jnp.where(visible[:, None, None], scores, -jnp.inf)
    row_max = jnp.max(scores, axis=-1, keepdims=True)
    weights = jnp.exp(scores - row_max)
    probs = weights / jnp.sum(weights, axis=-1, keepdims=True)
    probs_low = probs.astype(jnp.bfloat16)
    attended = jnp.einsum(
        "cngrk,cknd->crngd", probs_low, value_heads, preferred_element_type=jnp.float32
    ).astype(jnp.bfloat16)
    prob_grad = jnp.einsum(
        "crngd,cknd->cngrk", grad_heads, value_heads, preferred_element_type=jnp.float32
    )
    row_dot = jnp.sum(grad_heads.astype(jnp.float32) * attended.astype(jnp.float32), axis=-1)
    row_dot = jnp.transpose(row_dot, (0, 2, 3, 1))[..., None]
    score_grad = (probs * (prob_grad - row_dot) * score_scale).astype(jnp.bfloat16)
    query_grad = jnp.einsum(
        "cngrk,cknd->crngd", score_grad, key_heads, preferred_element_type=jnp.float32
    ).astype(jnp.bfloat16)
    value_grad = jnp.einsum(
        "cngrk,crngd->cknd", probs_low, grad_heads, preferred_element_type=jnp.float32
    )
    return (
        attended.reshape(span_count, row_count, query_width),
        query_grad.reshape(span_count, row_count, query_width),
        value_grad.reshape(span_count, key_count, kv_width),
    )


def choose_slots(needed, places):
    slot_ids = jnp.arange(CAP, dtype=jnp.int32)
    return needed[:, None, :] * (places[:, None, :] == slot_ids[None, :, None]).astype(jnp.int32)


def general(
    slab_tokens,
    memory,
    query_weight,
    key_weight,
    value_weight,
    query_down,
    query_up,
    value_down,
    value_up,
    tag_weight,
    retrieval,
    boundary,
    grad_tags,
):
    tok_rows = slab_tokens.shape[0]
    mem_rows = memory.shape[0]
    query_width = query_weight.shape[1]
    kv_width = key_weight.shape[1]
    span_count = tok_rows // BLK
    block_count = mem_rows // BLK
    pair_weight = jnp.concatenate([key_weight, value_weight], 1)
    adapter_pair = jnp.concatenate([query_down, value_down], 0)
    contract_last = (((1,), (1,)), ((), ()))
    contract_first = (((0,), (0,)), ((), ()))
    token_piece = lax.all_gather(slab_tokens, "heads", axis=1, tiled=True)
    memory_piece = lax.all_gather(memory, "heads", axis=1, tiled=True)
    query_acc = jnp.dot(token_piece, query_weight, preferred_element_type=jnp.float32)
    pair_acc = jnp.dot(token_piece, pair_weight, preferred_element_type=jnp.float32)
    low_acc = lax.dot_general(
        token_piece, adapter_pair, contract_last, preferred_element_type=jnp.float32
    )
    memory_acc = jnp.dot(memory_piece, pair_weight, preferred_element_type=jnp.float32)
    memory_low_acc = lax.dot_general(
        memory_piece, adapter_pair[RANK:], contract_last, preferred_element_type=jnp.float32
    )
    query_acc, pair_acc, low_acc, memory_acc, memory_low_acc = (
        query_acc,
        pair_acc,
        low_acc,
        memory_acc,
        memory_low_acc,
    )
    low_tokens = low_acc.astype(jnp.bfloat16)
    low_query = low_tokens[:, :RANK]
    low_value = low_tokens[:, RANK:]
    queries = (query_acc + jnp.dot(low_query, query_up, preferred_element_type=jnp.float32)).astype(
        jnp.bfloat16
    )
    keys_local = pair_acc[:, :kv_width].astype(jnp.bfloat16)
    values_local = (
        pair_acc[:, kv_width:] + jnp.dot(low_value, value_up, preferred_element_type=jnp.float32)
    ).astype(jnp.bfloat16)
    memory_low = memory_low_acc.astype(jnp.bfloat16)
    memory_pair = (
        jnp.concatenate(
            [
                memory_acc[:, :kv_width],
                memory_acc[:, kv_width:]
                + jnp.dot(memory_low, value_up, preferred_element_type=jnp.float32),
            ],
            1,
        )
        .astype(jnp.bfloat16)
        .reshape(block_count, BLK, 2 * kv_width)
    )
    peer_count = lax.axis_size("tm")
    every_block = jnp.arange(peer_count * block_count, dtype=jnp.int32)
    wanted = (
        jnp.any(retrieval.reshape(-1, 1) == every_block[None, :], axis=0)
        .astype(jnp.int32)
        .reshape(peer_count, block_count)
    )
    places = jnp.cumsum(wanted, axis=1) - wanted
    requested = choose_slots(wanted, places)
    asked_for = lax.all_to_all(requested, "tm", split_axis=0, concat_axis=0, tiled=True)
    rows_needed = retrieval // block_count * CAP + jnp.take(places.reshape(-1), retrieval)
    asked_low = asked_for.astype(jnp.bfloat16)
    outgoing = jnp.einsum(
        "rcm,mbw->rcbw", asked_low, memory_pair, preferred_element_type=jnp.float32
    ).astype(jnp.bfloat16)
    fetched = lax.all_to_all(outgoing, "tm", split_axis=0, concat_axis=0, tiled=True)
    slot_rows = fetched.reshape(peer_count * CAP, BLK, 2 * kv_width)
    picked = jnp.take(slot_rows, rows_needed.reshape(-1), axis=0).reshape(
        span_count, TOP * BLK, 2 * kv_width
    )
    all_keys = jnp.concatenate(
        [picked[..., :kv_width], keys_local.reshape(span_count, BLK, kv_width)], 1
    )
    all_values = jnp.concatenate(
        [picked[..., kv_width:], values_local.reshape(span_count, BLK, kv_width)], 1
    )
    attended_grad = lax.dot_general(
        grad_tags, tag_weight.astype(jnp.float32), contract_last, precision=HIGHEST
    ).astype(jnp.bfloat16)
    attended, query_grad, value_grad = attend(
        queries.reshape(span_count, BLK, query_width),
        all_keys,
        all_values,
        boundary,
        attended_grad.reshape(span_count, BLK, query_width),
    )
    attended = attended.reshape(tok_rows, query_width)
    query_grad = query_grad.reshape(tok_rows, query_width)
    logits_out = lax.psum(
        jnp.dot(attended, tag_weight, preferred_element_type=jnp.float32), "heads"
    )
    local_grad = value_grad[:, TOP * BLK :].reshape(tok_rows, kv_width)
    slot_grads = value_grad[:, : TOP * BLK].reshape(span_count * TOP, BLK * kv_width)
    slot_hits = (
        rows_needed.reshape(-1, 1) == jnp.arange(peer_count * CAP, dtype=jnp.int32)[None, :]
    ).astype(jnp.float32)
    grad_buffer = lax.dot_general(slot_hits, slot_grads, contract_first, precision=HIGHEST).reshape(
        peer_count * CAP, BLK, kv_width
    )
    up_wide = value_up.astype(jnp.float32)
    returned = lax.all_to_all(
        grad_buffer.reshape(peer_count, CAP, BLK, kv_width),
        "tm",
        split_axis=0,
        concat_axis=0,
        tiled=True,
    )
    owned_grad = jnp.einsum(
        "rcm,rcbw->mbw", asked_for.astype(jnp.float32), returned, precision=HIGHEST
    ).reshape(mem_rows, kv_width)
    memory_cot = lax.dot_general(up_wide, owned_grad, contract_last, precision=HIGHEST)
    up_memory = lax.dot_general(
        memory_low.astype(jnp.float32), owned_grad, contract_first, precision=HIGHEST
    )
    query_cot = lax.dot_general(
        query_up, query_grad, contract_last, preferred_element_type=jnp.float32
    )
    value_cot = lax.dot_general(up_wide, local_grad, contract_last, precision=HIGHEST)
    query_cot, value_cot, memory_cot = lax.psum((query_cot, value_cot, memory_cot), "heads")
    query_down_grad = jnp.dot(
        query_cot.astype(jnp.bfloat16), slab_tokens, preferred_element_type=jnp.float32
    )
    value_down_grad = jnp.dot(
        value_cot.astype(jnp.bfloat16), slab_tokens, preferred_element_type=jnp.float32
    ) + jnp.dot(memory_cot.astype(jnp.bfloat16), memory, preferred_element_type=jnp.float32)
    query_up_grad = lax.dot_general(
        low_query, query_grad, contract_first, preferred_element_type=jnp.float32
    )
    value_up_grad = (
        lax.dot_general(
            low_value.astype(jnp.float32), local_grad, contract_first, precision=HIGHEST
        )
        + up_memory
    )
    query_down_grad, query_up_grad, value_down_grad, value_up_grad = lax.psum(
        (query_down_grad, query_up_grad, value_down_grad, value_up_grad), "tm"
    )
    return (logits_out, query_down_grad, query_up_grad, value_down_grad, value_up_grad)


LOG2E = 1.4426950408889634
NT = (((1,), (1,)), ((), ()))
PACK = 2 * BLK + RANK
STRIP = 16
PAIR = 2
MIB = 1024 * 1024
ROOM = 63.5


def dot_nt(a, b, precision=None):
    return lax.dot_general(a, b, NT, precision=precision, preferred_element_type=jnp.float32)


def dot_nn(a, b, precision=None):
    return jnp.dot(a, b, precision=precision, preferred_element_type=jnp.float32)


def piece_rows(place_ref, j, width):
    return pl.ds(pl.multiple_of(lax.bitwise_xor(place_ref[0], j) * width, width), width)


def start_copies(pairs, sems, first=0):
    copies = [pltpu.make_async_copy(src, dst, sems.at[first + n]) for n, (src, dst) in enumerate(pairs)]
    for copy in copies:
        copy.start()
    return copies


def wait_all(copies):
    for copy in copies:
        copy.wait()


def memory_pieces(place_ref, js, xs, hbm, scratch, sems):
    x_s, wk_s, wv_s, down_s = scratch
    width = x_s.shape[2]
    groups = []
    for n, j in enumerate(js):
        here = piece_rows(place_ref, j, width)
        pairs = [
            (xs[n], x_s.at[n]),
            (hbm[0].at[here, :], wk_s.at[n]),
            (hbm[1].at[here, :], wv_s.at[n]),
            (hbm[2].at[:, here], down_s.at[n]),
        ]
        groups.append(start_copies(pairs, sems, 4 * n))
    return groups


def memory_terms(n, scratch):
    x_s, wk_s, wv_s, down_s = scratch
    x = x_s[n]
    return dot_nn(x, jnp.concatenate([wk_s[n], wv_s[n]], 1)), dot_nt(x, down_s[n])


def memory_early_kernel(blocks, place_ref, named_ref, x0, x1, *refs):
    hbm, acc_ref, low_ref, wanted_ref, scratch, sems = refs[:3], refs[3], refs[4], refs[5], refs[6:10], refs[10]
    groups = memory_pieces(place_ref, (0, 1), (x0, x1), hbm, scratch, sems)
    for slot in range(TOP):
        block = named_ref[0, slot]
        wanted_ref[lax.div(block, blocks)] = lax.rem(block, blocks)
    for n in range(2):
        wait_all(groups[n])
        term, low_term = memory_terms(n, scratch)
        if n == 0:
            acc_ref[...] = term
            low_ref[...] = low_term
        else:
            acc_ref[...] += term
            low_ref[...] += low_term


def memory_middle_kernel(place_ref, x2, acc_hbm, low_hbm, *refs):
    hbm, acc_ref, low_ref, scratch, sems = refs[:3], refs[3], refs[4], refs[5:9], refs[9]
    acc_s, low_s, acc_sems = refs[10:13]
    groups = memory_pieces(place_ref, (2,), (x2,), hbm, scratch, sems)
    sums = start_copies([(acc_hbm, acc_s), (low_hbm, low_s)], acc_sems)
    wait_all(groups[0])
    term, low_term = memory_terms(0, scratch)
    wait_all(sums)
    acc_ref[...] = acc_s[...] + term
    low_ref[...] = low_s[...] + low_term


def memory_kernel(peers, place_ref, asked_ref, x3, acc_hbm, low_hbm, *refs):
    hbm, up_ref, out_ref = refs[:3], refs[3], refs[4]
    scratch, sems, acc_s, low_s, acc_sems, pair_ref = refs[5:9], refs[9], refs[10], refs[11], refs[12], refs[13]
    groups = memory_pieces(place_ref, (3,), (x3,), hbm, scratch, sems)
    sums = start_copies([(acc_hbm, acc_s), (low_hbm, low_s)], acc_sems)
    wait_all(groups[0])
    term, low_term = memory_terms(0, scratch)
    wait_all(sums)
    acc = acc_s[...] + term
    low = low_s[...] + low_term
    values = (acc[:, HD:] + dot_nn(low.astype(jnp.bfloat16), up_ref[...])).astype(jnp.bfloat16)
    keys = acc[:, :HD].astype(jnp.bfloat16)
    low_t = jnp.transpose(low).astype(jnp.bfloat16)
    for b in range(acc.shape[0] // BLK):
        at = slice(b * BLK, (b + 1) * BLK)
        pair_ref[b, 0:BLK, :] = keys[at]
        pair_ref[b, BLK : 2 * BLK, :] = values[at]
        pair_ref[b, 2 * BLK : PACK, :] = low_t[:, at]
    for r in range(peers):
        out_ref[r] = pair_ref[asked_ref[r]]


WQ_CUTS = 4


def project_pieces(place_ref, js, xs, hbm, scratch, sems):
    wq_hbm, wk_hbm, wv_hbm, qd_hbm, vd_hbm = hbm
    x_s, wq_s, wk_s, wv_s, qd_s, vd_s = scratch
    width = x_s.shape[2]
    part = width // WQ_CUTS
    groups = []
    for n, j in enumerate(js):
        here = piece_rows(place_ref, j, width)
        start = lax.bitwise_xor(place_ref[0], j) * width
        pairs = [(xs[n], x_s.at[n])]
        for m in range(WQ_CUTS):
            rows = pl.ds(pl.multiple_of(start + m * part, part), part)
            pairs.append((wq_hbm.at[rows, :], wq_s.at[n, pl.ds(m * part, part), :]))
        pairs += [
            (wk_hbm.at[here, :], wk_s.at[n]),
            (wv_hbm.at[here, :], wv_s.at[n]),
            (qd_hbm.at[:, here], qd_s.at[n]),
            (vd_hbm.at[:, here], vd_s.at[n]),
        ]
        groups.append(start_copies(pairs, sems, len(pairs) * n))
    return groups


def project_terms(n, scratch):
    x_s, wq_s, wk_s, wv_s, qd_s, vd_s = scratch
    x = x_s[n]
    return (
        dot_nn(x, wq_s[n]),
        dot_nn(x, jnp.concatenate([wk_s[n], wv_s[n]], 1)),
        dot_nt(x, jnp.concatenate([qd_s[n], vd_s[n]], 0)),
    )


def project_early_kernel(place_ref, x0, x1, *refs):
    hbm, (tag_ref, tags_t_ref), outs, (grad_ref, grad_t_ref) = refs[:5], refs[5:7], refs[8:11], refs[11:13]
    scratch, sems = refs[13:19], refs[19]
    groups = project_pieces(place_ref, (0, 1), (x0, x1), hbm, scratch, sems)
    first = (((0,), (0,)), ((), ()))
    tag = tag_ref[...].astype(jnp.float32)
    tags_t = tags_t_ref[...]
    f32 = jnp.float32
    grad_ref[...] = lax.dot_general(
        tags_t, tag, first, precision=HIGHEST, preferred_element_type=f32
    ).astype(jnp.bfloat16)
    grad_t_ref[...] = lax.dot_general(
        tag, tags_t, first, precision=HIGHEST, preferred_element_type=f32
    ).astype(jnp.bfloat16)
    for n in range(2):
        wait_all(groups[n])
        for ref, term in zip(outs, project_terms(n, scratch)):
            if n == 0:
                ref[...] = term
            else:
                ref[...] += term


def project_far_kernel(place_ref, x3, x2, *refs):
    hbm, early, (qup_ref, vup_ref), (q_ref, k_ref, v_ref, low_ref) = refs[:5], refs[5:8], refs[8:10], refs[10:14]
    scratch, sems, sum_refs, sum_sems = refs[14:20], refs[20], refs[21:24], refs[24]
    groups = project_pieces(place_ref, (3, 2), (x3, x2), hbm, scratch, sems)
    loads = start_copies(list(zip(early, sum_refs)), sum_sems)
    wait_all(groups[0])
    terms = project_terms(0, scratch)
    wait_all(loads)
    for ref, term in zip(sum_refs, terms):
        ref[...] += term
    wait_all(groups[1])
    q_acc, kv_acc, low_acc = [ref[...] + term for ref, term in zip(sum_refs, project_terms(1, scratch))]
    low = low_acc.astype(jnp.bfloat16)
    q_ref[...] = (q_acc + dot_nn(low[:, :RANK], qup_ref[...])).astype(jnp.bfloat16)
    k_ref[...] = kv_acc[:, :HD].astype(jnp.bfloat16)
    v_ref[...] = (kv_acc[:, HD:] + dot_nn(low[:, RANK:], vup_ref[...])).astype(jnp.bfloat16)
    low_ref[...] = jnp.transpose(low_acc).astype(jnp.bfloat16)


def attention_kernel(peers, heads, bound_ref, *refs):
    parts, got, grad_hbm, grad_t_hbm = refs[:4], refs[4], refs[5], refs[6]
    qup_ref, vup_ref, tag_ref, cot_ref, up_ref, mcot_ref = refs[7:13]
    (q_s, k_own, v_own, low_s, low_m_s, grad_ref, grad_t_ref, k_all, v_all, kt_all, vt_all, kt_own, vt_own, bias_s, s_s, dp_s,
     p_s, ds_s, att_s, dq_s, dv_s, more_sems) = refs[13:]
    seen = peers * BLK
    pairs = []
    for b in range(peers):
        at = slice(b * BLK, (b + 1) * BLK)
        pairs.append((got.at[b, pl.ds(0, BLK), :], k_all.at[at, :]))
        pairs.append((got.at[b, pl.ds(BLK, BLK), :], v_all.at[at, :]))
        pairs.append((got.at[b, pl.ds(2 * BLK, RANK), :], low_m_s.at[b]))
    pairs += list(zip(parts, (q_s, k_own, v_own, low_s))) + [(grad_hbm, grad_ref), (grad_t_hbm, grad_t_ref)]
    copies = start_copies(pairs, more_sems)
    wait_all(copies[: 3 * peers])
    for b in range(peers):
        at = slice(b * BLK, (b + 1) * BLK)
        kt_all[:, at] = jnp.transpose(k_all[at, :])
        vt_all[:, at] = jnp.transpose(v_all[at, :])
    wait_all(copies[3 * peers :])
    dv_s[...] = jnp.zeros_like(dv_s)
    up_ref[...] = jnp.zeros_like(up_ref)
    scale = HD ** (-0.5)
    up_wide = vup_ref[...].astype(jnp.float32)
    query_width = heads * HD

    def pair_step(c, carry):
        base = c * (PAIR * BLK)
        rows = pl.ds(pl.multiple_of(base, PAIR * BLK), PAIR * BLK)
        own_rows = [pl.ds(pl.multiple_of(base + b * BLK, BLK), BLK) for b in range(PAIR)]
        row_ids = lax.broadcasted_iota(jnp.int32, (BLK, BLK), 0)
        col_ids = lax.broadcasted_iota(jnp.int32, (BLK, BLK), 1)
        for b in range(PAIR):
            kt_own[:, b * BLK : (b + 1) * BLK] = jnp.transpose(k_own[own_rows[b], :])
            vt_own[:, b * BLK : (b + 1) * BLK] = jnp.transpose(v_own[own_rows[b], :])
            edge = bound_ref[c * PAIR + b]
            visible = (col_ids <= row_ids) & ((col_ids >= edge) | (row_ids < edge))
            bias_s[b * BLK : (b + 1) * BLK, :] = jnp.where(visible, 0.0, -jnp.inf)

        def head_cols(h):
            return slice(h * HD, (h + 1) * HD)

        def times_keys(out_ref, left_ref, h, all_t, own_t):
            out_ref[:, :seen] = dot_nn(left_ref[rows, head_cols(h)], all_t[...])
            for b in range(PAIR):
                at = slice(b * BLK, (b + 1) * BLK)
                out_ref[at, seen:] = dot_nn(left_ref[own_rows[b], head_cols(h)], own_t[:, at])

        def over_keys(right_ref, first, all_t, own_t):
            whole = dot_nt(all_t[...], right_ref[first : first + PAIR * BLK, :seen])
            mine = [
                dot_nt(own_t[:, b * BLK : (b + 1) * BLK], right_ref[first + b * BLK : first + (b + 1) * BLK, seen:])
                for b in range(PAIR)
            ]
            return (whole + jnp.concatenate(mine, 1)).astype(jnp.bfloat16)

        def scores(h):
            times_keys(s_s.at[h % 2], q_s, h, kt_all, kt_own)

        def prob_grads(h):
            times_keys(dp_s.at[h % 2], grad_ref, h, vt_all, vt_own)

        def strips(h):
            for r in range(0, PAIR * BLK, STRIP):
                at = slice(r, r + STRIP)
                s = s_s[h % 2, at, :]
                s = jnp.concatenate([s[:, :seen], s[:, seen:] + bias_s[at, :]], 1) * (scale * LOG2E)
                w = jnp.exp2(s - jnp.max(s, axis=1, keepdims=True))
                probs = w * (1.0 / jnp.sum(w, axis=1, keepdims=True))
                probs_low = probs.astype(jnp.bfloat16)
                first = h * PAIR * BLK + r
                p_s[first : first + STRIP, :] = probs_low
                dp = dp_s[h % 2, at, :]
                dot = jnp.sum(probs_low.astype(jnp.float32) * dp, axis=1, keepdims=True)
                ds_s[h % 2, at, :] = (probs * ((dp - dot) * scale)).astype(jnp.bfloat16)

        def finish_head(h):
            att_s[head_cols(h), :] = over_keys(p_s, h * PAIR * BLK, vt_all, vt_own)
            dq_s[head_cols(h), :] = over_keys(ds_s.at[h % 2], 0, kt_all, kt_own)

        scores(0)
        prob_grads(0)
        for h in range(heads + 1):
            if h + 1 < heads:
                scores(h + 1)
                prob_grads(h + 1)
            if h < heads:
                strips(h)
            if h > 0:
                finish_head(h - 1)
        g_t = jnp.concatenate([grad_t_ref[h * HD : (h + 1) * HD, rows] for h in range(heads)], 1)
        dv_s[...] += dot_nn(g_t, p_s[:, :seen])
        dv_own = []
        for b in range(PAIR):
            g_b = jnp.concatenate([grad_t_ref[h * HD : (h + 1) * HD, own_rows[b]] for h in range(heads)], 1)
            starts = [(h * PAIR + b) * BLK for h in range(heads)]
            p_b = jnp.concatenate([p_s[n : n + BLK, seen:] for n in starts], 0)
            dv_own.append(dot_nn(g_b, p_b))
        dv_own = jnp.concatenate(dv_own, 1)
        dq = dq_s[...]
        cot_ref[0:RANK, rows] = dot_nn(qup_ref[...], dq)
        cot_ref[RANK : 2 * RANK, rows] = dot_nn(up_wide, dv_own, HIGHEST)
        cot_ref[2 * RANK :, rows] = dot_nn(tag_ref[...], att_s[...])
        up_ref[:, :query_width] += dot_nt(low_s[0:RANK, rows], dq)
        up_ref[:, query_width:] += dot_nt(low_s[RANK:, rows].astype(jnp.float32), dv_own, HIGHEST)
        return carry

    lax.fori_loop(0, q_s.shape[0] // (PAIR * BLK), pair_step, 0)
    dv = dv_s[...]
    mcot = dot_nn(up_wide, dv, HIGHEST)
    low_m = jnp.concatenate([low_m_s[b] for b in range(peers)], 1).astype(jnp.float32)
    up_ref[:, query_width:] += dot_nt(low_m, dv, HIGHEST)
    for b in range(peers):
        mcot_ref[b] = mcot[:, b * BLK : (b + 1) * BLK]


def first_down_kernel(peers, asked_ref, back_ref, c0, c1, c2, c3, slab_ref, up_ref, logit_ref, query_ref, value_ref, own_ref, sum_s):
    sum_s[...] = jnp.zeros_like(sum_s)
    for r in range(peers):
        block = asked_ref[r]
        sum_s[block] = sum_s[block] + back_ref[r]
    own_ref[...] = jnp.concatenate([sum_s[m] for m in range(sum_s.shape[0])], 1)
    cot = (c0[...] + c1[...]) + (c2[...] + c3[...])
    logit_ref[...] = cot[2 * RANK :]
    both = dot_nn(cot[: 2 * RANK].astype(jnp.bfloat16), slab_ref[...])
    width = both.shape[1]
    query_ref[:, :width] = both[:RANK]
    query_ref[:, width:] = up_ref[...]
    value_ref[...] = both[RANK:]


def second_down_kernel(c0, c1, c2, c3, memory_ref, value_ref, out_ref):
    cot = (c0[...] + c1[...]) + (c2[...] + c3[...])
    out_ref[...] = value_ref[...] + dot_nn(cot.astype(jnp.bfloat16), memory_ref[...])


def finish_kernel(*refs):
    query, value = [
        (ref[0][...].astype(jnp.float32) + ref[1][...].astype(jnp.float32))
        + (ref[2][...].astype(jnp.float32) + ref[3][...].astype(jnp.float32))
        for ref in (refs[:4], refs[4:8])
    ]
    query_down_ref, query_up_ref, value_down_ref, value_up_ref = refs[8:]
    value_down_ref[...] = value
    at = 0
    for out_ref in (query_down_ref, query_up_ref, value_up_ref):
        out_ref[...] = query[:, at : at + out_ref.shape[1]]
        at += out_ref.shape[1]


def swap(x, bit, axis="heads"):
    return lax.ppermute(x, axis, [(i, i ^ bit) for i in range(lax.axis_size(axis))])


def after(x, *deps):
    return pl.pallas_call(
        lambda *refs: None,
        out_shape=jax.ShapeDtypeStruct(x.shape, x.dtype),
        in_specs=[anywhere()] * (1 + len(deps)),
        out_specs=anywhere(),
        input_output_aliases={0: 0},
        name="in_order",
    )(x, *deps)


def anywhere():
    return pl.BlockSpec(memory_space=pl.ANY)


def smem():
    return pl.BlockSpec(memory_space=pltpu.SMEM)


def vmem():
    return pl.BlockSpec(memory_space=pltpu.VMEM)


def shaped(*shape, dtype=jnp.float32):
    return jax.ShapeDtypeStruct(shape, dtype)


def run(body, name, out_shape, in_specs, scratch=(), flops=0, moved=0, room=ROOM, out_specs=None):
    many = isinstance(out_shape, (tuple, list))
    return pl.pallas_call(
        body,
        out_shape=out_shape,
        in_specs=in_specs,
        out_specs=out_specs or (tuple(vmem() for _ in out_shape) if many else vmem()),
        scratch_shapes=list(scratch),
        compiler_params=pltpu.CompilerParams(vmem_limit_bytes=int(room * MIB)),
        cost_estimate=pl.CostEstimate(flops=flops, bytes_accessed=moved, transcendentals=0),
        name=name,
    )


def fast(
    slab_tokens,
    memory,
    query_weight,
    key_weight,
    value_weight,
    query_down,
    query_up,
    value_down,
    value_up,
    tag_weight,
    retrieval,
    boundary,
    grad_tags,
):
    tok_rows, width = slab_tokens.shape
    mem_rows = memory.shape[0]
    query_width = query_weight.shape[1]
    heads = query_width // HD
    spans = tok_rows // BLK
    blocks = mem_rows // BLK
    peers = lax.axis_size("tm")
    f32 = jnp.float32
    bf16 = jnp.bfloat16

    def memory_scratch(count):
        return [
            pltpu.VMEM((count, mem_rows, width), bf16),
            pltpu.VMEM((count, width, HD), bf16),
            pltpu.VMEM((count, width, HD), bf16),
            pltpu.VMEM((count, RANK, width), bf16),
            pltpu.SemaphoreType.DMA((4 * count,)),
        ]

    def project_scratch(count):
        return [
            pltpu.VMEM((count, tok_rows, width), bf16),
            pltpu.VMEM((count, width, query_width), bf16),
            pltpu.VMEM((count, width, HD), bf16),
            pltpu.VMEM((count, width, HD), bf16),
            pltpu.VMEM((count, RANK, width), bf16),
            pltpu.VMEM((count, RANK, width), bf16),
            pltpu.SemaphoreType.DMA((count * (WQ_CUTS + 5),)),
        ]

    memory_sums = [
        pltpu.VMEM((mem_rows, 2 * HD), f32),
        pltpu.VMEM((mem_rows, RANK), f32),
        pltpu.SemaphoreType.DMA((2,)),
    ]
    project_sums = [
        pltpu.VMEM((tok_rows, query_width), f32),
        pltpu.VMEM((tok_rows, 2 * HD), f32),
        pltpu.VMEM((tok_rows, 2 * RANK), f32),
    ]

    place = lax.axis_index("heads").astype(jnp.int32).reshape(1)
    tag_t = tag_weight.T
    tags = tag_t.shape[0]
    mem_far = swap(memory, 2)
    mem_near = swap(memory, 1)
    tok_near = swap(slab_tokens, 1)
    tok_far = swap(tok_near, 2)
    mem_acc, mem_low, wanted = run(
        lambda *refs: memory_early_kernel(blocks, *refs),
        "memory_near_half",
        (shaped(mem_rows, 2 * HD), shaped(mem_rows, RANK), shaped(peers, dtype=jnp.int32)),
        [smem()] * 2 + [anywhere()] * 5,
        memory_scratch(2),
        out_specs=(vmem(), vmem(), smem()),
    )(place, retrieval, memory, mem_near, key_weight, value_weight, value_down)
    asked = lax.all_to_all(wanted, "tm", split_axis=0, concat_axis=0, tiled=True)
    weights = (query_weight, key_weight, value_weight, query_down, value_down)
    mem_far = after(mem_far, asked)
    mem_cross = swap(mem_far, 1)
    mem_weights = (key_weight, value_weight, value_down)
    mem_acc, mem_low = run(
        memory_middle_kernel,
        "memory_far_quarter",
        (shaped(mem_rows, 2 * HD), shaped(mem_rows, RANK)),
        [smem()] + [anywhere()] * 6,
        memory_scratch(1) + memory_sums,
    )(place, mem_far, mem_acc, mem_low, *mem_weights)
    pairs = run(
        lambda *refs: memory_kernel(peers, *refs),
        "memory_pairs",
        shaped(peers, PACK, HD, dtype=bf16),
        [smem()] * 2 + [anywhere()] * 6 + [vmem()],
        memory_scratch(1) + memory_sums + [pltpu.VMEM((blocks, PACK, HD), bf16)],
    )(place, asked, mem_cross, mem_acc, mem_low, *mem_weights, value_up)
    got = lax.all_to_all(pairs, "tm", split_axis=0, concat_axis=0, tiled=True)
    *early, grad, grad_t = run(
        project_early_kernel,
        "project_near_half",
        (
            shaped(tok_rows, query_width),
            shaped(tok_rows, 2 * HD),
            shaped(tok_rows, 2 * RANK),
            shaped(tok_rows, query_width, dtype=bf16),
            shaped(query_width, tok_rows, dtype=bf16),
        ),
        [smem()] + [anywhere()] * 7 + [vmem()] * 2 + [anywhere()],
        project_scratch(2),
    )(place, slab_tokens, tok_near, *weights, tag_t, grad_tags.T, pairs)
    tok_far = after(tok_far, early[2])
    tok_cross = swap(tok_far, 1)
    parts = run(
        project_far_kernel,
        "project_far_half",
        (
            shaped(tok_rows, query_width, dtype=bf16),
            shaped(tok_rows, HD, dtype=bf16),
            shaped(tok_rows, HD, dtype=bf16),
            shaped(2 * RANK, tok_rows, dtype=bf16),
        ),
        [smem()] + [anywhere()] * 10 + [vmem()] * 2,
        project_scratch(2) + project_sums + [pltpu.SemaphoreType.DMA((3,))],
    )(place, tok_far, tok_cross, *weights, *early, query_up, value_up)

    seen = peers * BLK
    total = seen + BLK
    cot, ups, mcot = run(
        lambda *refs: attention_kernel(peers, heads, *refs),
        "span_attention",
        (shaped(2 * RANK + tags, tok_rows), shaped(RANK, query_width + HD), shaped(peers, RANK, BLK)),
        [smem()] + [anywhere()] * 7 + [vmem()] * 3,
        [
            pltpu.VMEM((tok_rows, query_width), bf16),
            pltpu.VMEM((tok_rows, HD), bf16),
            pltpu.VMEM((tok_rows, HD), bf16),
            pltpu.VMEM((2 * RANK, tok_rows), bf16),
            pltpu.VMEM((peers, RANK, BLK), bf16),
            pltpu.VMEM((tok_rows, query_width), bf16),
            pltpu.VMEM((query_width, tok_rows), bf16),
            pltpu.VMEM((seen, HD), bf16),
            pltpu.VMEM((seen, HD), bf16),
            pltpu.VMEM((HD, seen), bf16),
            pltpu.VMEM((HD, seen), bf16),
            pltpu.VMEM((HD, PAIR * BLK), bf16),
            pltpu.VMEM((HD, PAIR * BLK), bf16),
            pltpu.VMEM((PAIR * BLK, BLK), f32),
            pltpu.VMEM((2, PAIR * BLK, total), f32),
            pltpu.VMEM((2, PAIR * BLK, total), f32),
            pltpu.VMEM((heads * PAIR * BLK, total), bf16),
            pltpu.VMEM((2, PAIR * BLK, total), bf16),
            pltpu.VMEM((query_width, PAIR * BLK), bf16),
            pltpu.VMEM((query_width, PAIR * BLK), bf16),
            pltpu.VMEM((HD, seen), f32),
            pltpu.SemaphoreType.DMA((3 * peers + 6,)),
        ],
        flops=20 * tok_rows * query_width * total,
        moved=4 * tok_rows * query_width,
        room=60,
    )(boundary, *parts, got, grad, grad_t, query_up, value_up, tag_t)

    back = lax.all_to_all(mcot, "tm", split_axis=0, concat_axis=0, tiled=True)
    cots = [cot] + [swap(cot, d) for d in range(1, 4)]
    logits, query_sum, value_part, own = run(
        lambda *refs: first_down_kernel(peers, *refs),
        "first_down",
        (
            shaped(tags, tok_rows),
            shaped(RANK, width + ups.shape[1]),
            shaped(RANK, width),
            shaped(RANK, mem_rows),
        ),
        [smem()] + [vmem()] * 7,
        [pltpu.VMEM((blocks, RANK, BLK), f32)],
        room=8,
    )(asked, back, *cots, slab_tokens, ups)
    owns = [own] + [swap(own, d) for d in range(1, 4)]
    value_sum = run(
        second_down_kernel,
        "second_down",
        shaped(RANK, width),
        [vmem()] * 6,
        flops=2 * RANK * mem_rows * width,
        moved=2 * mem_rows * width,
        room=8,
    )(*owns, memory, value_part)
    sums = []
    for part in (query_sum, value_sum):
        part = (part + swap(part, 1, "tm")).astype(bf16)
        sums += [part] + [swap(part, bit, "tm") for bit in (2, 4, 6)]
    query_down_grad, query_up_grad, value_down_grad, value_up_grad = run(
        finish_kernel,
        "finish_outputs",
        (shaped(RANK, width), shaped(RANK, query_width), shaped(RANK, width), shaped(RANK, HD)),
        [vmem()] * 8,
        room=8,
    )(*sums)
    return (logits.T, query_down_grad, query_up_grad, value_down_grad, value_up_grad)


def solution(mesh):
    in_specs = (
        P("tm", "heads"),
        P("tm", "heads"),
        P(None, "heads"),
        P(None, "heads"),
        P(None, "heads"),
        P(),
        P(None, "heads"),
        P(),
        P(None, "heads"),
        P("heads", None),
        P("tm", None),
        P("tm"),
        P("tm", None),
    )
    out_specs = (
        P("tm", None),
        P(None, "heads"),
        P(None, "heads"),
        P(None, "heads"),
        P(None, "heads"),
    )
    fits = mesh.shape["heads"] == 4 and mesh.shape["tm"] == 8 == TOP * CAP
    local = fast if fits else general
    return jax.shard_map(local, mesh=mesh, in_specs=in_specs, out_specs=out_specs, check_vma=False)
```

```python
import jax
import jax.numpy as jnp
from jax import lax
from jax.experimental import pallas as pl
from jax.experimental.pallas import tpu as pltpu
from jax.sharding import PartitionSpec as P

HD = 128
RANK = 16
TOP = 8
BLK = 128
CAP = 1


HIGHEST = lax.Precision.HIGHEST


def attend(query, all_keys, all_values, split_row, out_grad):
    span_count, row_count, query_width = query.shape
    key_count, kv_width = (all_keys.shape[1], all_keys.shape[2])
    kv_heads = kv_width // HD
    group_size = query_width // kv_width
    score_scale = HD ** (-0.5)
    query_heads = query.reshape(span_count, row_count, kv_heads, group_size, HD)
    key_heads = all_keys.reshape(span_count, key_count, kv_heads, HD)
    value_heads = all_values.reshape(span_count, key_count, kv_heads, HD)
    grad_heads = out_grad.reshape(span_count, row_count, kv_heads, group_size, HD)
    scores = (
        jnp.einsum("crngd,cknd->cngrk", query_heads, key_heads, preferred_element_type=jnp.float32)
        * score_scale
    )
    row_ids = jnp.arange(row_count, dtype=jnp.int32)[:, None]
    col_ids = jnp.arange(BLK, dtype=jnp.int32)[None, :]
    edge_at = split_row[:, None, None]
    local_seen = (col_ids <= row_ids) & ((col_ids >= edge_at) | (row_ids < edge_at))
    visible = jnp.concatenate(
        [jnp.ones((span_count, row_count, key_count - BLK), jnp.bool_), local_seen], axis=2
    )
    scores = jnp.where(visible[:, None, None], scores, -jnp.inf)
    row_max = jnp.max(scores, axis=-1, keepdims=True)
    weights = jnp.exp(scores - row_max)
    probs = weights / jnp.sum(weights, axis=-1, keepdims=True)
    probs_low = probs.astype(jnp.bfloat16)
    attended = jnp.einsum(
        "cngrk,cknd->crngd", probs_low, value_heads, preferred_element_type=jnp.float32
    ).astype(jnp.bfloat16)
    prob_grad = jnp.einsum(
        "crngd,cknd->cngrk", grad_heads, value_heads, preferred_element_type=jnp.float32
    )
    row_dot = jnp.sum(grad_heads.astype(jnp.float32) * attended.astype(jnp.float32), axis=-1)
    row_dot = jnp.transpose(row_dot, (0, 2, 3, 1))[..., None]
    score_grad = (probs * (prob_grad - row_dot) * score_scale).astype(jnp.bfloat16)
    query_grad = jnp.einsum(
        "cngrk,cknd->crngd", score_grad, key_heads, preferred_element_type=jnp.float32
    ).astype(jnp.bfloat16)
    value_grad = jnp.einsum(
        "cngrk,crngd->cknd", probs_low, grad_heads, preferred_element_type=jnp.float32
    )
    return (
        attended.reshape(span_count, row_count, query_width),
        query_grad.reshape(span_count, row_count, query_width),
        value_grad.reshape(span_count, key_count, kv_width),
    )


def choose_slots(needed, places):
    slot_ids = jnp.arange(CAP, dtype=jnp.int32)
    return needed[:, None, :] * (places[:, None, :] == slot_ids[None, :, None]).astype(jnp.int32)


def general(
    slab_tokens,
    memory,
    query_weight,
    key_weight,
    value_weight,
    query_down,
    query_up,
    value_down,
    value_up,
    tag_weight,
    retrieval,
    boundary,
    grad_tags,
):
    tok_rows = slab_tokens.shape[0]
    mem_rows = memory.shape[0]
    query_width = query_weight.shape[1]
    kv_width = key_weight.shape[1]
    span_count = tok_rows // BLK
    block_count = mem_rows // BLK
    pair_weight = jnp.concatenate([key_weight, value_weight], 1)
    adapter_pair = jnp.concatenate([query_down, value_down], 0)
    contract_last = (((1,), (1,)), ((), ()))
    contract_first = (((0,), (0,)), ((), ()))
    token_piece = lax.all_gather(slab_tokens, "heads", axis=1, tiled=True)
    memory_piece = lax.all_gather(memory, "heads", axis=1, tiled=True)
    query_acc = jnp.dot(token_piece, query_weight, preferred_element_type=jnp.float32)
    pair_acc = jnp.dot(token_piece, pair_weight, preferred_element_type=jnp.float32)
    low_acc = lax.dot_general(
        token_piece, adapter_pair, contract_last, preferred_element_type=jnp.float32
    )
    memory_acc = jnp.dot(memory_piece, pair_weight, preferred_element_type=jnp.float32)
    memory_low_acc = lax.dot_general(
        memory_piece, adapter_pair[RANK:], contract_last, preferred_element_type=jnp.float32
    )
    query_acc, pair_acc, low_acc, memory_acc, memory_low_acc = (
        query_acc,
        pair_acc,
        low_acc,
        memory_acc,
        memory_low_acc,
    )
    low_tokens = low_acc.astype(jnp.bfloat16)
    low_query = low_tokens[:, :RANK]
    low_value = low_tokens[:, RANK:]
    queries = (query_acc + jnp.dot(low_query, query_up, preferred_element_type=jnp.float32)).astype(
        jnp.bfloat16
    )
    keys_local = pair_acc[:, :kv_width].astype(jnp.bfloat16)
    values_local = (
        pair_acc[:, kv_width:] + jnp.dot(low_value, value_up, preferred_element_type=jnp.float32)
    ).astype(jnp.bfloat16)
    memory_low = memory_low_acc.astype(jnp.bfloat16)
    memory_pair = (
        jnp.concatenate(
            [
                memory_acc[:, :kv_width],
                memory_acc[:, kv_width:]
                + jnp.dot(memory_low, value_up, preferred_element_type=jnp.float32),
            ],
            1,
        )
        .astype(jnp.bfloat16)
        .reshape(block_count, BLK, 2 * kv_width)
    )
    peer_count = lax.axis_size("tm")
    every_block = jnp.arange(peer_count * block_count, dtype=jnp.int32)
    wanted = (
        jnp.any(retrieval.reshape(-1, 1) == every_block[None, :], axis=0)
        .astype(jnp.int32)
        .reshape(peer_count, block_count)
    )
    places = jnp.cumsum(wanted, axis=1) - wanted
    requested = choose_slots(wanted, places)
    asked_for = lax.all_to_all(requested, "tm", split_axis=0, concat_axis=0, tiled=True)
    rows_needed = retrieval // block_count * CAP + jnp.take(places.reshape(-1), retrieval)
    asked_low = asked_for.astype(jnp.bfloat16)
    outgoing = jnp.einsum(
        "rcm,mbw->rcbw", asked_low, memory_pair, preferred_element_type=jnp.float32
    ).astype(jnp.bfloat16)
    fetched = lax.all_to_all(outgoing, "tm", split_axis=0, concat_axis=0, tiled=True)
    slot_rows = fetched.reshape(peer_count * CAP, BLK, 2 * kv_width)
    picked = jnp.take(slot_rows, rows_needed.reshape(-1), axis=0).reshape(
        span_count, TOP * BLK, 2 * kv_width
    )
    all_keys = jnp.concatenate(
        [picked[..., :kv_width], keys_local.reshape(span_count, BLK, kv_width)], 1
    )
    all_values = jnp.concatenate(
        [picked[..., kv_width:], values_local.reshape(span_count, BLK, kv_width)], 1
    )
    attended_grad = lax.dot_general(
        grad_tags, tag_weight.astype(jnp.float32), contract_last, precision=HIGHEST
    ).astype(jnp.bfloat16)
    attended, query_grad, value_grad = attend(
        queries.reshape(span_count, BLK, query_width),
        all_keys,
        all_values,
        boundary,
        attended_grad.reshape(span_count, BLK, query_width),
    )
    attended = attended.reshape(tok_rows, query_width)
    query_grad = query_grad.reshape(tok_rows, query_width)
    logits_out = lax.psum(
        jnp.dot(attended, tag_weight, preferred_element_type=jnp.float32), "heads"
    )
    local_grad = value_grad[:, TOP * BLK :].reshape(tok_rows, kv_width)
    slot_grads = value_grad[:, : TOP * BLK].reshape(span_count * TOP, BLK * kv_width)
    slot_hits = (
        rows_needed.reshape(-1, 1) == jnp.arange(peer_count * CAP, dtype=jnp.int32)[None, :]
    ).astype(jnp.float32)
    grad_buffer = lax.dot_general(slot_hits, slot_grads, contract_first, precision=HIGHEST).reshape(
        peer_count * CAP, BLK, kv_width
    )
    up_wide = value_up.astype(jnp.float32)
    returned = lax.all_to_all(
        grad_buffer.reshape(peer_count, CAP, BLK, kv_width),
        "tm",
        split_axis=0,
        concat_axis=0,
        tiled=True,
    )
    owned_grad = jnp.einsum(
        "rcm,rcbw->mbw", asked_for.astype(jnp.float32), returned, precision=HIGHEST
    ).reshape(mem_rows, kv_width)
    memory_cot = lax.dot_general(up_wide, owned_grad, contract_last, precision=HIGHEST)
    up_memory = lax.dot_general(
        memory_low.astype(jnp.float32), owned_grad, contract_first, precision=HIGHEST
    )
    query_cot = lax.dot_general(
        query_up, query_grad, contract_last, preferred_element_type=jnp.float32
    )
    value_cot = lax.dot_general(up_wide, local_grad, contract_last, precision=HIGHEST)
    query_cot, value_cot, memory_cot = lax.psum((query_cot, value_cot, memory_cot), "heads")
    query_down_grad = jnp.dot(
        query_cot.astype(jnp.bfloat16), slab_tokens, preferred_element_type=jnp.float32
    )
    value_down_grad = jnp.dot(
        value_cot.astype(jnp.bfloat16), slab_tokens, preferred_element_type=jnp.float32
    ) + jnp.dot(memory_cot.astype(jnp.bfloat16), memory, preferred_element_type=jnp.float32)
    query_up_grad = lax.dot_general(
        low_query, query_grad, contract_first, preferred_element_type=jnp.float32
    )
    value_up_grad = (
        lax.dot_general(
            low_value.astype(jnp.float32), local_grad, contract_first, precision=HIGHEST
        )
        + up_memory
    )
    query_down_grad, query_up_grad, value_down_grad, value_up_grad = lax.psum(
        (query_down_grad, query_up_grad, value_down_grad, value_up_grad), "tm"
    )
    return (logits_out, query_down_grad, query_up_grad, value_down_grad, value_up_grad)


LOG2E = 1.4426950408889634
NT = (((1,), (1,)), ((), ()))
PACK = 2 * BLK + RANK
STRIP = 16
PAIR = 2
MIB = 1024 * 1024
ROOM = 63.5


def dot_nt(a, b, precision=None):
    return lax.dot_general(a, b, NT, precision=precision, preferred_element_type=jnp.float32)


def dot_nn(a, b, precision=None):
    return jnp.dot(a, b, precision=precision, preferred_element_type=jnp.float32)


def piece_rows(place_ref, j, width):
    return pl.ds(pl.multiple_of(lax.bitwise_xor(place_ref[0], j) * width, width), width)


def start_copies(pairs, sems, first=0):
    copies = [pltpu.make_async_copy(src, dst, sems.at[first + n]) for n, (src, dst) in enumerate(pairs)]
    for copy in copies:
        copy.start()
    return copies


def wait_all(copies):
    for copy in copies:
        copy.wait()


def memory_pieces(place_ref, js, xs, hbm, scratch, sems):
    x_s, wk_s, wv_s, down_s = scratch
    width = x_s.shape[2]
    groups = []
    for n, j in enumerate(js):
        here = piece_rows(place_ref, j, width)
        pairs = [
            (xs[n], x_s.at[n]),
            (hbm[0].at[here, :], wk_s.at[n]),
            (hbm[1].at[here, :], wv_s.at[n]),
            (hbm[2].at[:, here], down_s.at[n]),
        ]
        groups.append(start_copies(pairs, sems, 4 * n))
    return groups


def memory_terms(n, scratch):
    x_s, wk_s, wv_s, down_s = scratch
    x = x_s[n]
    return dot_nn(x, jnp.concatenate([wk_s[n], wv_s[n]], 1)), dot_nt(x, down_s[n])


def memory_early_kernel(blocks, place_ref, named_ref, x0, x1, *refs):
    hbm, acc_ref, low_ref, wanted_ref, scratch, sems = refs[:3], refs[3], refs[4], refs[5], refs[6:10], refs[10]
    groups = memory_pieces(place_ref, (0, 1), (x0, x1), hbm, scratch, sems)
    for slot in range(TOP):
        block = named_ref[0, slot]
        wanted_ref[lax.div(block, blocks)] = lax.rem(block, blocks)
    for n in range(2):
        wait_all(groups[n])
        term, low_term = memory_terms(n, scratch)
        if n == 0:
            acc_ref[...] = term
            low_ref[...] = low_term
        else:
            acc_ref[...] += term
            low_ref[...] += low_term


def memory_middle_kernel(place_ref, x2, acc_hbm, low_hbm, *refs):
    hbm, acc_ref, low_ref, scratch, sems = refs[:3], refs[3], refs[4], refs[5:9], refs[9]
    acc_s, low_s, acc_sems = refs[10:13]
    groups = memory_pieces(place_ref, (2,), (x2,), hbm, scratch, sems)
    sums = start_copies([(acc_hbm, acc_s), (low_hbm, low_s)], acc_sems)
    wait_all(groups[0])
    term, low_term = memory_terms(0, scratch)
    wait_all(sums)
    acc_ref[...] = acc_s[...] + term
    low_ref[...] = low_s[...] + low_term


def memory_kernel(peers, place_ref, asked_ref, x3, acc_hbm, low_hbm, *refs):
    hbm, up_ref, out_ref = refs[:3], refs[3], refs[4]
    scratch, sems, acc_s, low_s, acc_sems, pair_ref = refs[5:9], refs[9], refs[10], refs[11], refs[12], refs[13]
    groups = memory_pieces(place_ref, (3,), (x3,), hbm, scratch, sems)
    sums = start_copies([(acc_hbm, acc_s), (low_hbm, low_s)], acc_sems)
    wait_all(groups[0])
    term, low_term = memory_terms(0, scratch)
    wait_all(sums)
    acc = acc_s[...] + term
    low = low_s[...] + low_term
    values = (acc[:, HD:] + dot_nn(low.astype(jnp.bfloat16), up_ref[...])).astype(jnp.bfloat16)
    keys = acc[:, :HD].astype(jnp.bfloat16)
    low_t = jnp.transpose(low).astype(jnp.bfloat16)
    for b in range(acc.shape[0] // BLK):
        at = slice(b * BLK, (b + 1) * BLK)
        pair_ref[b, 0:BLK, :] = keys[at]
        pair_ref[b, BLK : 2 * BLK, :] = values[at]
        pair_ref[b, 2 * BLK : PACK, :] = low_t[:, at]
    for r in range(peers):
        out_ref[r] = pair_ref[asked_ref[r]]


WQ_CUTS = 4


def project_pieces(place_ref, js, xs, hbm, scratch, sems):
    wq_hbm, wk_hbm, wv_hbm, qd_hbm, vd_hbm = hbm
    x_s, wq_s, wk_s, wv_s, qd_s, vd_s = scratch
    width = x_s.shape[2]
    part = width // WQ_CUTS
    groups = []
    for n, j in enumerate(js):
        here = piece_rows(place_ref, j, width)
        start = lax.bitwise_xor(place_ref[0], j) * width
        pairs = [(xs[n], x_s.at[n])]
        for m in range(WQ_CUTS):
            rows = pl.ds(pl.multiple_of(start + m * part, part), part)
            pairs.append((wq_hbm.at[rows, :], wq_s.at[n, pl.ds(m * part, part), :]))
        pairs += [
            (wk_hbm.at[here, :], wk_s.at[n]),
            (wv_hbm.at[here, :], wv_s.at[n]),
            (qd_hbm.at[:, here], qd_s.at[n]),
            (vd_hbm.at[:, here], vd_s.at[n]),
        ]
        groups.append(start_copies(pairs, sems, len(pairs) * n))
    return groups


def project_terms(n, scratch):
    x_s, wq_s, wk_s, wv_s, qd_s, vd_s = scratch
    x = x_s[n]
    return (
        dot_nn(x, wq_s[n]),
        dot_nn(x, jnp.concatenate([wk_s[n], wv_s[n]], 1)),
        dot_nt(x, jnp.concatenate([qd_s[n], vd_s[n]], 0)),
    )


def project_early_kernel(place_ref, x0, x1, *refs):
    hbm, (tag_ref, tags_t_ref), outs, grad_t_ref = refs[:5], refs[5:7], refs[8:11], refs[11]
    scratch, sems = refs[12:18], refs[18]
    groups = project_pieces(place_ref, (0, 1), (x0, x1), hbm, scratch, sems)
    first = (((0,), (0,)), ((), ()))
    tag = tag_ref[...].astype(jnp.float32)
    tags_t = tags_t_ref[...]
    f32 = jnp.float32
    grad_t_ref[...] = lax.dot_general(
        tag, tags_t, first, precision=HIGHEST, preferred_element_type=f32
    ).astype(jnp.bfloat16)
    for n in range(2):
        wait_all(groups[n])
        for ref, term in zip(outs, project_terms(n, scratch)):
            if n == 0:
                ref[...] = term
            else:
                ref[...] += term


def project_far_kernel(place_ref, x3, x2, *refs):
    hbm, early, (qup_ref, vup_ref), (q_ref, k_ref, v_ref, low_ref) = refs[:5], refs[5:8], refs[8:10], refs[10:14]
    scratch, sems, sum_refs, sum_sems = refs[14:20], refs[20], refs[21:24], refs[24]
    groups = project_pieces(place_ref, (3, 2), (x3, x2), hbm, scratch, sems)
    loads = start_copies(list(zip(early, sum_refs)), sum_sems)
    wait_all(groups[0])
    terms = project_terms(0, scratch)
    wait_all(loads)
    for ref, term in zip(sum_refs, terms):
        ref[...] += term
    wait_all(groups[1])
    q_acc, kv_acc, low_acc = [ref[...] + term for ref, term in zip(sum_refs, project_terms(1, scratch))]
    low = low_acc.astype(jnp.bfloat16)
    q_ref[...] = jnp.transpose((q_acc + dot_nn(low[:, :RANK], qup_ref[...])).astype(jnp.bfloat16))
    k_ref[...] = kv_acc[:, :HD].astype(jnp.bfloat16)
    v_ref[...] = (kv_acc[:, HD:] + dot_nn(low[:, RANK:], vup_ref[...])).astype(jnp.bfloat16)
    low_ref[...] = jnp.transpose(low_acc).astype(jnp.bfloat16)


def attention_kernel(peers, heads, bound_ref, *refs):
    parts, got, grad_t_hbm = refs[:4], refs[4], refs[5]
    qup_ref, vup_ref, tag_ref, cot_ref, up_ref, mcot_ref = refs[6:12]
    (q_s, k_own, v_own, low_s, low_m_s, grad_t_ref, k_all, v_all, kt_all, vt_all, kt_own, vt_own, bias_s, s_s, dp_s,
     p_s, ds_s, att_s, dq_s, dv_s, more_sems) = refs[12:]
    seen = peers * BLK
    total = seen + BLK
    pairs = []
    for b in range(peers):
        at = slice(b * BLK, (b + 1) * BLK)
        pairs.append((got.at[b, pl.ds(0, BLK), :], k_all.at[at, :]))
        pairs.append((got.at[b, pl.ds(BLK, BLK), :], v_all.at[at, :]))
        pairs.append((got.at[b, pl.ds(2 * BLK, RANK), :], low_m_s.at[b]))
    pairs += list(zip(parts, (q_s, k_own, v_own, low_s))) + [(grad_t_hbm, grad_t_ref)]
    copies = start_copies(pairs, more_sems)
    wait_all(copies[: 3 * peers])
    for b in range(peers):
        at = slice(b * BLK, (b + 1) * BLK)
        kt_all[:, at] = jnp.transpose(k_all[at, :])
        vt_all[:, at] = jnp.transpose(v_all[at, :])
    wait_all(copies[3 * peers :])
    dv_s[...] = jnp.zeros_like(dv_s)
    up_ref[...] = jnp.zeros_like(up_ref)
    scale = HD ** (-0.5)
    up_wide = vup_ref[...].astype(jnp.float32)
    query_width = heads * HD

    span = PAIR * BLK

    def pair_step(c, carry):
        base = c * span
        rows = pl.ds(pl.multiple_of(base, span), span)
        own_rows = [pl.ds(pl.multiple_of(base + b * BLK, BLK), BLK) for b in range(PAIR)]
        key_ids = lax.broadcasted_iota(jnp.int32, (BLK, BLK), 0)
        row_ids = lax.broadcasted_iota(jnp.int32, (BLK, BLK), 1)
        for b in range(PAIR):
            lanes = slice(b * BLK, (b + 1) * BLK)
            kt_own[:, lanes] = jnp.transpose(k_own[own_rows[b], :])
            vt_own[:, lanes] = jnp.transpose(v_own[own_rows[b], :])
            edge = bound_ref[c * PAIR + b]
            visible = (key_ids <= row_ids) & ((key_ids >= edge) | (row_ids < edge))
            bias_s[:, lanes] = jnp.where(visible, 0.0, -jnp.inf)

        def head_cols(h):
            return slice(h * HD, (h + 1) * HD)

        def times_keys(out_ref, right_ref, h, all_ref, own_ref):
            out_ref[:seen, :] = dot_nn(all_ref[...], right_ref[head_cols(h), rows])
            for b in range(PAIR):
                own = dot_nn(own_ref[own_rows[b], :], right_ref[head_cols(h), own_rows[b]])
                out_ref[seen:, b * BLK : (b + 1) * BLK] = own

        def over_keys(right, all_t, own_t):
            whole = dot_nn(all_t[...], right(slice(0, seen), slice(0, span)))
            mine = []
            for b in range(PAIR):
                lanes = slice(b * BLK, (b + 1) * BLK)
                mine.append(dot_nn(own_t[:, lanes], right(slice(seen, total), lanes)))
            return (whole + jnp.concatenate(mine, 1)).astype(jnp.bfloat16)

        def scores(h):
            times_keys(s_s.at[h % 2], q_s, h, k_all, k_own)

        def prob_grads(h):
            times_keys(dp_s.at[h % 2], grad_t_ref, h, v_all, v_own)

        def folded(op, x, before):
            part = op(x.reshape(BLK // 8, 8, BLK), axis=0)
            if before is None:
                return part
            return jnp.maximum(before, part) if op is jnp.max else before + part

        def passes(h, b):
            lanes = slice(b * BLK, (b + 1) * BLK)
            chunks = [slice(n, n + BLK) for n in range(0, total, BLK)]
            part = None
            for at in chunks:
                s = s_s[h % 2, at, lanes]
                if at.start == seen:
                    s = s + bias_s[:, lanes]
                    s_s[h % 2, at, lanes] = s
                part = folded(jnp.max, s, part)
            top = jnp.max(part, axis=0, keepdims=True) * (scale * LOG2E)
            part = None
            for at in chunks:
                w = jnp.exp2(s_s[h % 2, at, lanes] * (scale * LOG2E) - top)
                s_s[h % 2, at, lanes] = w
                part = folded(jnp.sum, w, part)
            inv = 1.0 / jnp.sum(part, axis=0, keepdims=True)
            part = None
            for at in chunks:
                probs_low = (s_s[h % 2, at, lanes] * inv).astype(jnp.bfloat16)
                p_s[at, h * span + b * BLK : h * span + (b + 1) * BLK] = probs_low
                part = folded(jnp.sum, probs_low.astype(jnp.float32) * dp_s[h % 2, at, lanes], part)
            dot = jnp.sum(part, axis=0, keepdims=True)
            inv = inv * scale
            for at in chunks:
                ds = (s_s[h % 2, at, lanes] * inv) * (dp_s[h % 2, at, lanes] - dot)
                ds_s[h % 2, at, lanes] = ds.astype(jnp.bfloat16)

        def finish_head(h):
            att_s[head_cols(h), :] = over_keys(
                lambda at, lanes: p_s[at, h * span + lanes.start : h * span + lanes.stop], vt_all, vt_own
            )
            dq_s[head_cols(h), :] = over_keys(lambda at, lanes: ds_s[h % 2, at, lanes], kt_all, kt_own)

        scores(0)
        prob_grads(0)
        for h in range(heads + 1):
            if h + 1 < heads:
                scores(h + 1)
                prob_grads(h + 1)
            if h < heads:
                for b in range(PAIR):
                    passes(h, b)
            if h > 0:
                finish_head(h - 1)
        g_t = jnp.concatenate([grad_t_ref[head_cols(h), rows] for h in range(heads)], 1)
        dv_s[...] += dot_nt(g_t, p_s[:seen, :])
        dv_own = []
        for b in range(PAIR):
            g_b = jnp.concatenate([grad_t_ref[head_cols(h), own_rows[b]] for h in range(heads)], 1)
            starts = [h * span + b * BLK for h in range(heads)]
            p_b = jnp.concatenate([p_s[seen:, n : n + BLK] for n in starts], 1)
            dv_own.append(dot_nt(g_b, p_b))
        dv_own = jnp.concatenate(dv_own, 1)
        dq = dq_s[...]
        cot_ref[0:RANK, rows] = dot_nn(qup_ref[...], dq)
        cot_ref[RANK : 2 * RANK, rows] = dot_nn(up_wide, dv_own, HIGHEST)
        cot_ref[2 * RANK :, rows] = dot_nn(tag_ref[...], att_s[...])
        up_ref[:, :query_width] += dot_nt(low_s[0:RANK, rows], dq)
        up_ref[:, query_width:] += dot_nt(low_s[RANK:, rows].astype(jnp.float32), dv_own, HIGHEST)
        return carry

    lax.fori_loop(0, q_s.shape[1] // span, pair_step, 0)
    dv = dv_s[...]
    mcot = dot_nn(up_wide, dv, HIGHEST)
    low_m = jnp.concatenate([low_m_s[b] for b in range(peers)], 1).astype(jnp.float32)
    up_ref[:, query_width:] += dot_nt(low_m, dv, HIGHEST)
    for b in range(peers):
        mcot_ref[b] = mcot[:, b * BLK : (b + 1) * BLK]


def first_down_kernel(peers, asked_ref, back_ref, c0, c1, c2, c3, slab_ref, up_ref, logit_ref, query_ref, value_ref, own_ref, sum_s):
    sum_s[...] = jnp.zeros_like(sum_s)
    for r in range(peers):
        block = asked_ref[r]
        sum_s[block] = sum_s[block] + back_ref[r]
    own_ref[...] = jnp.concatenate([sum_s[m] for m in range(sum_s.shape[0])], 1)
    cot = (c0[...] + c1[...]) + (c2[...] + c3[...])
    logit_ref[...] = cot[2 * RANK :]
    both = dot_nn(cot[: 2 * RANK].astype(jnp.bfloat16), slab_ref[...])
    width = both.shape[1]
    query_ref[:, :width] = both[:RANK]
    query_ref[:, width:] = up_ref[...]
    value_ref[...] = both[RANK:]


def second_down_kernel(c0, c1, c2, c3, memory_ref, value_ref, out_ref):
    cot = (c0[...] + c1[...]) + (c2[...] + c3[...])
    out_ref[...] = value_ref[...] + dot_nn(cot.astype(jnp.bfloat16), memory_ref[...])


def finish_kernel(*refs):
    query, value = [
        (ref[0][...].astype(jnp.float32) + ref[1][...].astype(jnp.float32))
        + (ref[2][...].astype(jnp.float32) + ref[3][...].astype(jnp.float32))
        for ref in (refs[:4], refs[4:8])
    ]
    query_down_ref, query_up_ref, value_down_ref, value_up_ref = refs[8:]
    value_down_ref[...] = value
    at = 0
    for out_ref in (query_down_ref, query_up_ref, value_up_ref):
        out_ref[...] = query[:, at : at + out_ref.shape[1]]
        at += out_ref.shape[1]


def swap(x, bit, axis="heads"):
    return lax.ppermute(x, axis, [(i, i ^ bit) for i in range(lax.axis_size(axis))])


def after(x, *deps):
    return pl.pallas_call(
        lambda *refs: None,
        out_shape=jax.ShapeDtypeStruct(x.shape, x.dtype),
        in_specs=[anywhere()] * (1 + len(deps)),
        out_specs=anywhere(),
        input_output_aliases={0: 0},
        name="in_order",
    )(x, *deps)


def anywhere():
    return pl.BlockSpec(memory_space=pl.ANY)


def smem():
    return pl.BlockSpec(memory_space=pltpu.SMEM)


def vmem():
    return pl.BlockSpec(memory_space=pltpu.VMEM)


def shaped(*shape, dtype=jnp.float32):
    return jax.ShapeDtypeStruct(shape, dtype)


def run(body, name, out_shape, in_specs, scratch=(), flops=0, moved=0, room=ROOM, out_specs=None):
    many = isinstance(out_shape, (tuple, list))
    return pl.pallas_call(
        body,
        out_shape=out_shape,
        in_specs=in_specs,
        out_specs=out_specs or (tuple(vmem() for _ in out_shape) if many else vmem()),
        scratch_shapes=list(scratch),
        compiler_params=pltpu.CompilerParams(vmem_limit_bytes=int(room * MIB)),
        cost_estimate=pl.CostEstimate(flops=flops, bytes_accessed=moved, transcendentals=0),
        name=name,
    )


def fast(
    slab_tokens,
    memory,
    query_weight,
    key_weight,
    value_weight,
    query_down,
    query_up,
    value_down,
    value_up,
    tag_weight,
    retrieval,
    boundary,
    grad_tags,
):
    tok_rows, width = slab_tokens.shape
    mem_rows = memory.shape[0]
    query_width = query_weight.shape[1]
    heads = query_width // HD
    spans = tok_rows // BLK
    blocks = mem_rows // BLK
    peers = lax.axis_size("tm")
    f32 = jnp.float32
    bf16 = jnp.bfloat16

    def memory_scratch(count):
        return [
            pltpu.VMEM((count, mem_rows, width), bf16),
            pltpu.VMEM((count, width, HD), bf16),
            pltpu.VMEM((count, width, HD), bf16),
            pltpu.VMEM((count, RANK, width), bf16),
            pltpu.SemaphoreType.DMA((4 * count,)),
        ]

    def project_scratch(count):
        return [
            pltpu.VMEM((count, tok_rows, width), bf16),
            pltpu.VMEM((count, width, query_width), bf16),
            pltpu.VMEM((count, width, HD), bf16),
            pltpu.VMEM((count, width, HD), bf16),
            pltpu.VMEM((count, RANK, width), bf16),
            pltpu.VMEM((count, RANK, width), bf16),
            pltpu.SemaphoreType.DMA((count * (WQ_CUTS + 5),)),
        ]

    memory_sums = [
        pltpu.VMEM((mem_rows, 2 * HD), f32),
        pltpu.VMEM((mem_rows, RANK), f32),
        pltpu.SemaphoreType.DMA((2,)),
    ]
    project_sums = [
        pltpu.VMEM((tok_rows, query_width), f32),
        pltpu.VMEM((tok_rows, 2 * HD), f32),
        pltpu.VMEM((tok_rows, 2 * RANK), f32),
    ]

    place = lax.axis_index("heads").astype(jnp.int32).reshape(1)
    tag_t = tag_weight.T
    tags = tag_t.shape[0]
    mem_far = swap(memory, 2)
    mem_near = swap(memory, 1)
    tok_near = swap(slab_tokens, 1)
    tok_far = swap(tok_near, 2)
    mem_acc, mem_low, wanted = run(
        lambda *refs: memory_early_kernel(blocks, *refs),
        "memory_near_half",
        (shaped(mem_rows, 2 * HD), shaped(mem_rows, RANK), shaped(peers, dtype=jnp.int32)),
        [smem()] * 2 + [anywhere()] * 5,
        memory_scratch(2),
        out_specs=(vmem(), vmem(), smem()),
    )(place, retrieval, memory, mem_near, key_weight, value_weight, value_down)
    asked = lax.all_to_all(wanted, "tm", split_axis=0, concat_axis=0, tiled=True)
    weights = (query_weight, key_weight, value_weight, query_down, value_down)
    mem_far = after(mem_far, asked)
    mem_cross = swap(mem_far, 1)
    mem_weights = (key_weight, value_weight, value_down)
    mem_acc, mem_low = run(
        memory_middle_kernel,
        "memory_far_quarter",
        (shaped(mem_rows, 2 * HD), shaped(mem_rows, RANK)),
        [smem()] + [anywhere()] * 6,
        memory_scratch(1) + memory_sums,
    )(place, mem_far, mem_acc, mem_low, *mem_weights)
    pairs = run(
        lambda *refs: memory_kernel(peers, *refs),
        "memory_pairs",
        shaped(peers, PACK, HD, dtype=bf16),
        [smem()] * 2 + [anywhere()] * 6 + [vmem()],
        memory_scratch(1) + memory_sums + [pltpu.VMEM((blocks, PACK, HD), bf16)],
    )(place, asked, mem_cross, mem_acc, mem_low, *mem_weights, value_up)
    got = lax.all_to_all(pairs, "tm", split_axis=0, concat_axis=0, tiled=True)
    *early, grad_t = run(
        project_early_kernel,
        "project_near_half",
        (
            shaped(tok_rows, query_width),
            shaped(tok_rows, 2 * HD),
            shaped(tok_rows, 2 * RANK),
            shaped(query_width, tok_rows, dtype=bf16),
        ),
        [smem()] + [anywhere()] * 7 + [vmem()] * 2 + [anywhere()],
        project_scratch(2),
    )(place, slab_tokens, tok_near, *weights, tag_t, grad_tags.T, pairs)
    tok_far = after(tok_far, early[2])
    tok_cross = swap(tok_far, 1)
    parts = run(
        project_far_kernel,
        "project_far_half",
        (
            shaped(query_width, tok_rows, dtype=bf16),
            shaped(tok_rows, HD, dtype=bf16),
            shaped(tok_rows, HD, dtype=bf16),
            shaped(2 * RANK, tok_rows, dtype=bf16),
        ),
        [smem()] + [anywhere()] * 10 + [vmem()] * 2,
        project_scratch(2) + project_sums + [pltpu.SemaphoreType.DMA((3,))],
    )(place, tok_far, tok_cross, *weights, *early, query_up, value_up)

    seen = peers * BLK
    total = seen + BLK
    cot, ups, mcot = run(
        lambda *refs: attention_kernel(peers, heads, *refs),
        "span_attention",
        (shaped(2 * RANK + tags, tok_rows), shaped(RANK, query_width + HD), shaped(peers, RANK, BLK)),
        [smem()] + [anywhere()] * 6 + [vmem()] * 3,
        [
            pltpu.VMEM((query_width, tok_rows), bf16),
            pltpu.VMEM((tok_rows, HD), bf16),
            pltpu.VMEM((tok_rows, HD), bf16),
            pltpu.VMEM((2 * RANK, tok_rows), bf16),
            pltpu.VMEM((peers, RANK, BLK), bf16),
            pltpu.VMEM((query_width, tok_rows), bf16),
            pltpu.VMEM((seen, HD), bf16),
            pltpu.VMEM((seen, HD), bf16),
            pltpu.VMEM((HD, seen), bf16),
            pltpu.VMEM((HD, seen), bf16),
            pltpu.VMEM((HD, PAIR * BLK), bf16),
            pltpu.VMEM((HD, PAIR * BLK), bf16),
            pltpu.VMEM((BLK, PAIR * BLK), f32),
            pltpu.VMEM((2, total, PAIR * BLK), f32),
            pltpu.VMEM((2, total, PAIR * BLK), f32),
            pltpu.VMEM((total, heads * PAIR * BLK), bf16),
            pltpu.VMEM((2, total, PAIR * BLK), bf16),
            pltpu.VMEM((query_width, PAIR * BLK), bf16),
            pltpu.VMEM((query_width, PAIR * BLK), bf16),
            pltpu.VMEM((HD, seen), f32),
            pltpu.SemaphoreType.DMA((3 * peers + 5,)),
        ],
        flops=20 * tok_rows * query_width * total,
        moved=4 * tok_rows * query_width,
        room=60,
    )(boundary, *parts, got, grad_t, query_up, value_up, tag_t)

    back = lax.all_to_all(mcot, "tm", split_axis=0, concat_axis=0, tiled=True)
    cots = [cot] + [swap(cot, d) for d in range(1, 4)]
    logits, query_sum, value_part, own = run(
        lambda *refs: first_down_kernel(peers, *refs),
        "first_down",
        (
            shaped(tags, tok_rows),
            shaped(RANK, width + ups.shape[1]),
            shaped(RANK, width),
            shaped(RANK, mem_rows),
        ),
        [smem()] + [vmem()] * 7,
        [pltpu.VMEM((blocks, RANK, BLK), f32)],
        room=8,
    )(asked, back, *cots, slab_tokens, ups)
    owns = [own] + [swap(own, d) for d in range(1, 4)]
    value_sum = run(
        second_down_kernel,
        "second_down",
        shaped(RANK, width),
        [vmem()] * 6,
        flops=2 * RANK * mem_rows * width,
        moved=2 * mem_rows * width,
        room=8,
    )(*owns, memory, value_part)
    sums = []
    for part in (query_sum, value_sum):
        part = (part + swap(part, 1, "tm")).astype(bf16)
        sums += [part] + [swap(part, bit, "tm") for bit in (2, 4, 6)]
    query_down_grad, query_up_grad, value_down_grad, value_up_grad = run(
        finish_kernel,
        "finish_outputs",
        (shaped(RANK, width), shaped(RANK, query_width), shaped(RANK, width), shaped(RANK, HD)),
        [vmem()] * 8,
        room=8,
    )(*sums)
    return (logits.T, query_down_grad, query_up_grad, value_down_grad, value_up_grad)


def solution(mesh):
    in_specs = (
        P("tm", "heads"),
        P("tm", "heads"),
        P(None, "heads"),
        P(None, "heads"),
        P(None, "heads"),
        P(),
        P(None, "heads"),
        P(),
        P(None, "heads"),
        P("heads", None),
        P("tm", None),
        P("tm"),
        P("tm", None),
    )
    out_specs = (
        P("tm", None),
        P(None, "heads"),
        P(None, "heads"),
        P(None, "heads"),
        P(None, "heads"),
    )
    fits = mesh.shape["heads"] == 4 and mesh.shape["tm"] == 8 == TOP * CAP
    local = fast if fits else general
    return jax.shard_map(local, mesh=mesh, in_specs=in_specs, out_specs=out_specs, check_vma=False)
```

```python
import jax
import jax.numpy as jnp
from jax import lax
from jax.experimental import pallas as pl
from jax.experimental.pallas import tpu as pltpu
from jax.sharding import PartitionSpec as P

HD = 128
RANK = 16
TOP = 8
BLK = 128
CAP = 1


HIGHEST = lax.Precision.HIGHEST


def attend(query, all_keys, all_values, split_row, out_grad):
    span_count, row_count, query_width = query.shape
    key_count, kv_width = (all_keys.shape[1], all_keys.shape[2])
    kv_heads = kv_width // HD
    group_size = query_width // kv_width
    score_scale = HD ** (-0.5)
    query_heads = query.reshape(span_count, row_count, kv_heads, group_size, HD)
    key_heads = all_keys.reshape(span_count, key_count, kv_heads, HD)
    value_heads = all_values.reshape(span_count, key_count, kv_heads, HD)
    grad_heads = out_grad.reshape(span_count, row_count, kv_heads, group_size, HD)
    scores = (
        jnp.einsum("crngd,cknd->cngrk", query_heads, key_heads, preferred_element_type=jnp.float32)
        * score_scale
    )
    row_ids = jnp.arange(row_count, dtype=jnp.int32)[:, None]
    col_ids = jnp.arange(BLK, dtype=jnp.int32)[None, :]
    edge_at = split_row[:, None, None]
    local_seen = (col_ids <= row_ids) & ((col_ids >= edge_at) | (row_ids < edge_at))
    visible = jnp.concatenate(
        [jnp.ones((span_count, row_count, key_count - BLK), jnp.bool_), local_seen], axis=2
    )
    scores = jnp.where(visible[:, None, None], scores, -jnp.inf)
    row_max = jnp.max(scores, axis=-1, keepdims=True)
    weights = jnp.exp(scores - row_max)
    probs = weights / jnp.sum(weights, axis=-1, keepdims=True)
    probs_low = probs.astype(jnp.bfloat16)
    attended = jnp.einsum(
        "cngrk,cknd->crngd", probs_low, value_heads, preferred_element_type=jnp.float32
    ).astype(jnp.bfloat16)
    prob_grad = jnp.einsum(
        "crngd,cknd->cngrk", grad_heads, value_heads, preferred_element_type=jnp.float32
    )
    row_dot = jnp.sum(grad_heads.astype(jnp.float32) * attended.astype(jnp.float32), axis=-1)
    row_dot = jnp.transpose(row_dot, (0, 2, 3, 1))[..., None]
    score_grad = (probs * (prob_grad - row_dot) * score_scale).astype(jnp.bfloat16)
    query_grad = jnp.einsum(
        "cngrk,cknd->crngd", score_grad, key_heads, preferred_element_type=jnp.float32
    ).astype(jnp.bfloat16)
    value_grad = jnp.einsum(
        "cngrk,crngd->cknd", probs_low, grad_heads, preferred_element_type=jnp.float32
    )
    return (
        attended.reshape(span_count, row_count, query_width),
        query_grad.reshape(span_count, row_count, query_width),
        value_grad.reshape(span_count, key_count, kv_width),
    )


def choose_slots(needed, places):
    slot_ids = jnp.arange(CAP, dtype=jnp.int32)
    return needed[:, None, :] * (places[:, None, :] == slot_ids[None, :, None]).astype(jnp.int32)


def general(
    slab_tokens,
    memory,
    query_weight,
    key_weight,
    value_weight,
    query_down,
    query_up,
    value_down,
    value_up,
    tag_weight,
    retrieval,
    boundary,
    grad_tags,
):
    tok_rows = slab_tokens.shape[0]
    mem_rows = memory.shape[0]
    query_width = query_weight.shape[1]
    kv_width = key_weight.shape[1]
    span_count = tok_rows // BLK
    block_count = mem_rows // BLK
    pair_weight = jnp.concatenate([key_weight, value_weight], 1)
    adapter_pair = jnp.concatenate([query_down, value_down], 0)
    contract_last = (((1,), (1,)), ((), ()))
    contract_first = (((0,), (0,)), ((), ()))
    token_piece = lax.all_gather(slab_tokens, "heads", axis=1, tiled=True)
    memory_piece = lax.all_gather(memory, "heads", axis=1, tiled=True)
    query_acc = jnp.dot(token_piece, query_weight, preferred_element_type=jnp.float32)
    pair_acc = jnp.dot(token_piece, pair_weight, preferred_element_type=jnp.float32)
    low_acc = lax.dot_general(
        token_piece, adapter_pair, contract_last, preferred_element_type=jnp.float32
    )
    memory_acc = jnp.dot(memory_piece, pair_weight, preferred_element_type=jnp.float32)
    memory_low_acc = lax.dot_general(
        memory_piece, adapter_pair[RANK:], contract_last, preferred_element_type=jnp.float32
    )
    query_acc, pair_acc, low_acc, memory_acc, memory_low_acc = (
        query_acc,
        pair_acc,
        low_acc,
        memory_acc,
        memory_low_acc,
    )
    low_tokens = low_acc.astype(jnp.bfloat16)
    low_query = low_tokens[:, :RANK]
    low_value = low_tokens[:, RANK:]
    queries = (query_acc + jnp.dot(low_query, query_up, preferred_element_type=jnp.float32)).astype(
        jnp.bfloat16
    )
    keys_local = pair_acc[:, :kv_width].astype(jnp.bfloat16)
    values_local = (
        pair_acc[:, kv_width:] + jnp.dot(low_value, value_up, preferred_element_type=jnp.float32)
    ).astype(jnp.bfloat16)
    memory_low = memory_low_acc.astype(jnp.bfloat16)
    memory_pair = (
        jnp.concatenate(
            [
                memory_acc[:, :kv_width],
                memory_acc[:, kv_width:]
                + jnp.dot(memory_low, value_up, preferred_element_type=jnp.float32),
            ],
            1,
        )
        .astype(jnp.bfloat16)
        .reshape(block_count, BLK, 2 * kv_width)
    )
    peer_count = lax.axis_size("tm")
    every_block = jnp.arange(peer_count * block_count, dtype=jnp.int32)
    wanted = (
        jnp.any(retrieval.reshape(-1, 1) == every_block[None, :], axis=0)
        .astype(jnp.int32)
        .reshape(peer_count, block_count)
    )
    places = jnp.cumsum(wanted, axis=1) - wanted
    requested = choose_slots(wanted, places)
    asked_for = lax.all_to_all(requested, "tm", split_axis=0, concat_axis=0, tiled=True)
    rows_needed = retrieval // block_count * CAP + jnp.take(places.reshape(-1), retrieval)
    asked_low = asked_for.astype(jnp.bfloat16)
    outgoing = jnp.einsum(
        "rcm,mbw->rcbw", asked_low, memory_pair, preferred_element_type=jnp.float32
    ).astype(jnp.bfloat16)
    fetched = lax.all_to_all(outgoing, "tm", split_axis=0, concat_axis=0, tiled=True)
    slot_rows = fetched.reshape(peer_count * CAP, BLK, 2 * kv_width)
    picked = jnp.take(slot_rows, rows_needed.reshape(-1), axis=0).reshape(
        span_count, TOP * BLK, 2 * kv_width
    )
    all_keys = jnp.concatenate(
        [picked[..., :kv_width], keys_local.reshape(span_count, BLK, kv_width)], 1
    )
    all_values = jnp.concatenate(
        [picked[..., kv_width:], values_local.reshape(span_count, BLK, kv_width)], 1
    )
    attended_grad = lax.dot_general(
        grad_tags, tag_weight.astype(jnp.float32), contract_last, precision=HIGHEST
    ).astype(jnp.bfloat16)
    attended, query_grad, value_grad = attend(
        queries.reshape(span_count, BLK, query_width),
        all_keys,
        all_values,
        boundary,
        attended_grad.reshape(span_count, BLK, query_width),
    )
    attended = attended.reshape(tok_rows, query_width)
    query_grad = query_grad.reshape(tok_rows, query_width)
    logits_out = lax.psum(
        jnp.dot(attended, tag_weight, preferred_element_type=jnp.float32), "heads"
    )
    local_grad = value_grad[:, TOP * BLK :].reshape(tok_rows, kv_width)
    slot_grads = value_grad[:, : TOP * BLK].reshape(span_count * TOP, BLK * kv_width)
    slot_hits = (
        rows_needed.reshape(-1, 1) == jnp.arange(peer_count * CAP, dtype=jnp.int32)[None, :]
    ).astype(jnp.float32)
    grad_buffer = lax.dot_general(slot_hits, slot_grads, contract_first, precision=HIGHEST).reshape(
        peer_count * CAP, BLK, kv_width
    )
    up_wide = value_up.astype(jnp.float32)
    returned = lax.all_to_all(
        grad_buffer.reshape(peer_count, CAP, BLK, kv_width),
        "tm",
        split_axis=0,
        concat_axis=0,
        tiled=True,
    )
    owned_grad = jnp.einsum(
        "rcm,rcbw->mbw", asked_for.astype(jnp.float32), returned, precision=HIGHEST
    ).reshape(mem_rows, kv_width)
    memory_cot = lax.dot_general(up_wide, owned_grad, contract_last, precision=HIGHEST)
    up_memory = lax.dot_general(
        memory_low.astype(jnp.float32), owned_grad, contract_first, precision=HIGHEST
    )
    query_cot = lax.dot_general(
        query_up, query_grad, contract_last, preferred_element_type=jnp.float32
    )
    value_cot = lax.dot_general(up_wide, local_grad, contract_last, precision=HIGHEST)
    query_cot, value_cot, memory_cot = lax.psum((query_cot, value_cot, memory_cot), "heads")
    query_down_grad = jnp.dot(
        query_cot.astype(jnp.bfloat16), slab_tokens, preferred_element_type=jnp.float32
    )
    value_down_grad = jnp.dot(
        value_cot.astype(jnp.bfloat16), slab_tokens, preferred_element_type=jnp.float32
    ) + jnp.dot(memory_cot.astype(jnp.bfloat16), memory, preferred_element_type=jnp.float32)
    query_up_grad = lax.dot_general(
        low_query, query_grad, contract_first, preferred_element_type=jnp.float32
    )
    value_up_grad = (
        lax.dot_general(
            low_value.astype(jnp.float32), local_grad, contract_first, precision=HIGHEST
        )
        + up_memory
    )
    query_down_grad, query_up_grad, value_down_grad, value_up_grad = lax.psum(
        (query_down_grad, query_up_grad, value_down_grad, value_up_grad), "tm"
    )
    return (logits_out, query_down_grad, query_up_grad, value_down_grad, value_up_grad)


LOG2E = 1.4426950408889634
NT = (((1,), (1,)), ((), ()))
PACK = 2 * BLK + RANK
STRIP = 16
PAIR = 2
MIB = 1024 * 1024
ROOM = 63.5


def dot_nt(a, b, precision=None):
    return lax.dot_general(a, b, NT, precision=precision, preferred_element_type=jnp.float32)


def dot_nn(a, b, precision=None):
    return jnp.dot(a, b, precision=precision, preferred_element_type=jnp.float32)


def piece_rows(place_ref, j, width):
    return pl.ds(pl.multiple_of(lax.bitwise_xor(place_ref[0], j) * width, width), width)


def start_copies(pairs, sems, first=0):
    copies = [pltpu.make_async_copy(src, dst, sems.at[first + n]) for n, (src, dst) in enumerate(pairs)]
    for copy in copies:
        copy.start()
    return copies


def wait_all(copies):
    for copy in copies:
        copy.wait()


def memory_pieces(place_ref, js, xs, hbm, scratch, sems):
    x_s, wk_s, wv_s, down_s = scratch
    width = x_s.shape[2]
    groups = []
    for n, j in enumerate(js):
        here = piece_rows(place_ref, j, width)
        pairs = [
            (xs[n], x_s.at[n]),
            (hbm[0].at[here, :], wk_s.at[n]),
            (hbm[1].at[here, :], wv_s.at[n]),
            (hbm[2].at[:, here], down_s.at[n]),
        ]
        groups.append(start_copies(pairs, sems, 4 * n))
    return groups


def memory_terms(n, scratch):
    x_s, wk_s, wv_s, down_s = scratch
    x = x_s[n]
    return dot_nn(x, jnp.concatenate([wk_s[n], wv_s[n]], 1)), dot_nt(x, down_s[n])


def memory_early_kernel(blocks, place_ref, named_ref, x0, x1, *refs):
    hbm, acc_ref, low_ref, wanted_ref, scratch, sems = refs[:3], refs[3], refs[4], refs[5], refs[6:10], refs[10]
    groups = memory_pieces(place_ref, (0, 1), (x0, x1), hbm, scratch, sems)
    for slot in range(TOP):
        block = named_ref[0, slot]
        wanted_ref[lax.div(block, blocks)] = lax.rem(block, blocks)
    for n in range(2):
        wait_all(groups[n])
        term, low_term = memory_terms(n, scratch)
        if n == 0:
            acc_ref[...] = term
            low_ref[...] = low_term
        else:
            acc_ref[...] += term
            low_ref[...] += low_term


def memory_middle_kernel(place_ref, x2, acc_hbm, low_hbm, *refs):
    hbm, acc_ref, low_ref, scratch, sems = refs[:3], refs[3], refs[4], refs[5:9], refs[9]
    acc_s, low_s, acc_sems = refs[10:13]
    groups = memory_pieces(place_ref, (2,), (x2,), hbm, scratch, sems)
    sums = start_copies([(acc_hbm, acc_s), (low_hbm, low_s)], acc_sems)
    wait_all(groups[0])
    term, low_term = memory_terms(0, scratch)
    wait_all(sums)
    acc_ref[...] = acc_s[...] + term
    low_ref[...] = low_s[...] + low_term


def memory_kernel(peers, place_ref, asked_ref, x3, acc_hbm, low_hbm, *refs):
    hbm, up_ref, out_ref = refs[:3], refs[3], refs[4]
    scratch, sems, acc_s, low_s, acc_sems, pair_ref = refs[5:9], refs[9], refs[10], refs[11], refs[12], refs[13]
    groups = memory_pieces(place_ref, (3,), (x3,), hbm, scratch, sems)
    sums = start_copies([(acc_hbm, acc_s), (low_hbm, low_s)], acc_sems)
    wait_all(groups[0])
    term, low_term = memory_terms(0, scratch)
    wait_all(sums)
    acc = acc_s[...] + term
    low = low_s[...] + low_term
    values = (acc[:, HD:] + dot_nn(low.astype(jnp.bfloat16), up_ref[...])).astype(jnp.bfloat16)
    keys = acc[:, :HD].astype(jnp.bfloat16)
    low_t = jnp.transpose(low).astype(jnp.bfloat16)
    for b in range(acc.shape[0] // BLK):
        at = slice(b * BLK, (b + 1) * BLK)
        pair_ref[b, 0:BLK, :] = keys[at]
        pair_ref[b, BLK : 2 * BLK, :] = values[at]
        pair_ref[b, 2 * BLK : PACK, :] = low_t[:, at]
    for r in range(peers):
        out_ref[r] = pair_ref[asked_ref[r]]


WQ_CUTS = 4


def project_pieces(place_ref, js, xs, hbm, scratch, sems):
    wq_hbm, wk_hbm, wv_hbm, qd_hbm, vd_hbm = hbm
    x_s, wq_s, wk_s, wv_s, qd_s, vd_s = scratch
    width = x_s.shape[2]
    part = width // WQ_CUTS
    groups = []
    for n, j in enumerate(js):
        here = piece_rows(place_ref, j, width)
        start = lax.bitwise_xor(place_ref[0], j) * width
        pairs = [(xs[n], x_s.at[n])]
        for m in range(WQ_CUTS):
            rows = pl.ds(pl.multiple_of(start + m * part, part), part)
            pairs.append((wq_hbm.at[rows, :], wq_s.at[n, pl.ds(m * part, part), :]))
        pairs += [
            (wk_hbm.at[here, :], wk_s.at[n]),
            (wv_hbm.at[here, :], wv_s.at[n]),
            (qd_hbm.at[:, here], qd_s.at[n]),
            (vd_hbm.at[:, here], vd_s.at[n]),
        ]
        groups.append(start_copies(pairs, sems, len(pairs) * n))
    return groups


def project_terms(n, scratch):
    x_s, wq_s, wk_s, wv_s, qd_s, vd_s = scratch
    x = x_s[n]
    return (
        dot_nn(x, wq_s[n]),
        dot_nn(x, jnp.concatenate([wk_s[n], wv_s[n]], 1)),
        dot_nt(x, jnp.concatenate([qd_s[n], vd_s[n]], 0)),
    )


def project_early_kernel(place_ref, x0, x1, *refs):
    hbm, (tag_ref, tags_t_ref), outs, (grad_ref, grad_t_ref) = refs[:5], refs[5:7], refs[8:11], refs[11:13]
    scratch, sems = refs[13:19], refs[19]
    groups = project_pieces(place_ref, (0, 1), (x0, x1), hbm, scratch, sems)
    first = (((0,), (0,)), ((), ()))
    tag = tag_ref[...].astype(jnp.float32)
    tags_t = tags_t_ref[...]
    f32 = jnp.float32
    grad_ref[...] = lax.dot_general(
        tags_t, tag, first, precision=HIGHEST, preferred_element_type=f32
    ).astype(jnp.bfloat16)
    grad_t_ref[...] = lax.dot_general(
        tag, tags_t, first, precision=HIGHEST, preferred_element_type=f32
    ).astype(jnp.bfloat16)
    for n in range(2):
        wait_all(groups[n])
        for ref, term in zip(outs, project_terms(n, scratch)):
            if n == 0:
                ref[...] = term
            else:
                ref[...] += term


def project_far_kernel(place_ref, x3, x2, *refs):
    hbm, early, (qup_ref, vup_ref), (q_ref, k_ref, v_ref, low_ref) = refs[:5], refs[5:8], refs[8:10], refs[10:14]
    scratch, sems, sum_refs, sum_sems = refs[14:20], refs[20], refs[21:24], refs[24]
    groups = project_pieces(place_ref, (3, 2), (x3, x2), hbm, scratch, sems)
    loads = start_copies(list(zip(early, sum_refs)), sum_sems)
    wait_all(groups[0])
    terms = project_terms(0, scratch)
    wait_all(loads)
    for ref, term in zip(sum_refs, terms):
        ref[...] += term
    wait_all(groups[1])
    q_acc, kv_acc, low_acc = [ref[...] + term for ref, term in zip(sum_refs, project_terms(1, scratch))]
    low = low_acc.astype(jnp.bfloat16)
    q_ref[...] = (q_acc + dot_nn(low[:, :RANK], qup_ref[...])).astype(jnp.bfloat16)
    k_ref[...] = kv_acc[:, :HD].astype(jnp.bfloat16)
    v_ref[...] = (kv_acc[:, HD:] + dot_nn(low[:, RANK:], vup_ref[...])).astype(jnp.bfloat16)
    low_ref[...] = jnp.transpose(low_acc).astype(jnp.bfloat16)


def attention_kernel(peers, heads, bound_ref, *refs):
    parts, got, grad_hbm, grad_t_hbm = refs[:4], refs[4], refs[5], refs[6]
    qup_ref, vup_ref, tag_ref, cot_ref, up_ref, mcot_ref = refs[7:13]
    (q_s, k_own, v_own, low_s, low_m_s, grad_ref, grad_t_ref, k_all, v_all, kt_all, vt_all, kt_own, vt_own, bias_s, s_s, dp_s,
     p_s, ds_s, att_s, dq_s, dv_s, more_sems) = refs[13:]
    seen = peers * BLK
    pairs = []
    for b in range(peers):
        at = slice(b * BLK, (b + 1) * BLK)
        pairs.append((got.at[b, pl.ds(0, BLK), :], k_all.at[at, :]))
        pairs.append((got.at[b, pl.ds(BLK, BLK), :], v_all.at[at, :]))
        pairs.append((got.at[b, pl.ds(2 * BLK, RANK), :], low_m_s.at[b]))
    pairs += list(zip(parts, (q_s, k_own, v_own, low_s))) + [(grad_hbm, grad_ref), (grad_t_hbm, grad_t_ref)]
    copies = start_copies(pairs, more_sems)
    wait_all(copies[: 3 * peers])
    for b in range(peers):
        at = slice(b * BLK, (b + 1) * BLK)
        kt_all[:, at] = jnp.transpose(k_all[at, :])
        vt_all[:, at] = jnp.transpose(v_all[at, :])
    wait_all(copies[3 * peers : -1])
    dv_s[...] = jnp.zeros_like(dv_s)
    up_ref[...] = jnp.zeros_like(up_ref)
    scale = HD ** (-0.5)
    up_wide = vup_ref[...].astype(jnp.float32)
    query_width = heads * HD

    def pair_step(c, carry):
        base = c * (PAIR * BLK)
        rows = pl.ds(pl.multiple_of(base, PAIR * BLK), PAIR * BLK)
        own_rows = [pl.ds(pl.multiple_of(base + b * BLK, BLK), BLK) for b in range(PAIR)]
        row_ids = lax.broadcasted_iota(jnp.int32, (BLK, BLK), 0)
        col_ids = lax.broadcasted_iota(jnp.int32, (BLK, BLK), 1)
        for b in range(PAIR):
            kt_own[:, b * BLK : (b + 1) * BLK] = jnp.transpose(k_own[own_rows[b], :])
            vt_own[:, b * BLK : (b + 1) * BLK] = jnp.transpose(v_own[own_rows[b], :])
            edge = bound_ref[c * PAIR + b]
            visible = (col_ids <= row_ids) & ((col_ids >= edge) | (row_ids < edge))
            bias_s[b * BLK : (b + 1) * BLK, :] = jnp.where(visible, 0.0, -jnp.inf)

        def head_cols(h):
            return slice(h * HD, (h + 1) * HD)

        def times_keys(out_ref, left_ref, h, all_t, own_t):
            out_ref[:, :seen] = dot_nn(left_ref[rows, head_cols(h)], all_t[...])
            for b in range(PAIR):
                at = slice(b * BLK, (b + 1) * BLK)
                out_ref[at, seen:] = dot_nn(left_ref[own_rows[b], head_cols(h)], own_t[:, at])

        def over_keys(left_ref, first, all_ref, own_ref):
            whole = dot_nn(left_ref[first : first + PAIR * BLK, :seen], all_ref[...])
            mine = [
                dot_nn(left_ref[first + b * BLK : first + (b + 1) * BLK, seen:], own_ref[own_rows[b], :])
                for b in range(PAIR)
            ]
            return (whole + jnp.concatenate(mine, 0)).astype(jnp.bfloat16)

        def scores(h):
            times_keys(s_s.at[h % 2], q_s, h, kt_all, kt_own)

        def prob_grads(h):
            times_keys(dp_s.at[h % 2], grad_ref, h, vt_all, vt_own)

        def strips(h):
            for r in range(0, PAIR * BLK, STRIP):
                at = slice(r, r + STRIP)
                s = s_s[h % 2, at, :]
                s = jnp.concatenate([s[:, :seen], s[:, seen:] + bias_s[at, :]], 1) * (scale * LOG2E)
                w = jnp.exp2(s - jnp.max(s, axis=1, keepdims=True))
                probs = w * (1.0 / jnp.sum(w, axis=1, keepdims=True))
                probs_low = probs.astype(jnp.bfloat16)
                first = h * PAIR * BLK + r
                p_s[first : first + STRIP, :] = probs_low
                dp = dp_s[h % 2, at, :]
                dot = jnp.sum(probs_low.astype(jnp.float32) * dp, axis=1, keepdims=True)
                ds_s[h % 2, at, :] = (probs * ((dp - dot) * scale)).astype(jnp.bfloat16)

        def finish_head(h):
            att_s[:, head_cols(h)] = over_keys(p_s, h * PAIR * BLK, v_all, v_own)
            dq_s[:, head_cols(h)] = over_keys(ds_s.at[h % 2], 0, k_all, k_own)

        scores(0)
        prob_grads(0)
        for h in range(heads + 1):
            if h + 1 < heads:
                scores(h + 1)
                prob_grads(h + 1)
            if h < heads:
                strips(h)
            if h > 0:
                finish_head(h - 1)
        pl.when(c == 0)(copies[-1].wait)
        g_t = jnp.concatenate([grad_t_ref[h * HD : (h + 1) * HD, rows] for h in range(heads)], 1)
        dv_s[...] += dot_nn(g_t, p_s[:, :seen])
        dv_own = []
        for b in range(PAIR):
            g_b = jnp.concatenate([grad_t_ref[h * HD : (h + 1) * HD, own_rows[b]] for h in range(heads)], 1)
            starts = [(h * PAIR + b) * BLK for h in range(heads)]
            p_b = jnp.concatenate([p_s[n : n + BLK, seen:] for n in starts], 0)
            dv_own.append(dot_nn(g_b, p_b))
        dv_own = jnp.concatenate(dv_own, 1)
        dq = dq_s[...]
        cot_ref[0:RANK, rows] = dot_nt(qup_ref[...], dq)
        cot_ref[RANK : 2 * RANK, rows] = dot_nn(up_wide, dv_own, HIGHEST)
        cot_ref[2 * RANK :, rows] = dot_nt(tag_ref[...], att_s[...])
        up_ref[:, :query_width] += dot_nn(low_s[0:RANK, rows], dq)
        up_ref[:, query_width:] += dot_nt(low_s[RANK:, rows].astype(jnp.float32), dv_own, HIGHEST)
        return carry

    lax.fori_loop(0, q_s.shape[0] // (PAIR * BLK), pair_step, 0)
    dv = dv_s[...]
    mcot = dot_nn(up_wide, dv, HIGHEST)
    low_m = jnp.concatenate([low_m_s[b] for b in range(peers)], 1).astype(jnp.float32)
    up_ref[:, query_width:] += dot_nt(low_m, dv, HIGHEST)
    for b in range(peers):
        mcot_ref[b] = mcot[:, b * BLK : (b + 1) * BLK]


def own_kernel(peers, asked_ref, back_ref, out_ref, sum_s):
    sum_s[...] = jnp.zeros_like(sum_s)
    for r in range(peers):
        block = asked_ref[r]
        sum_s[block] = sum_s[block] + back_ref[r]
    out_ref[...] = jnp.concatenate([sum_s[m] for m in range(sum_s.shape[0])], 1)


def first_down_kernel(c0, c1, c2, c3, slab_ref, up_ref, logit_ref, query_ref, value_ref):
    cot = (c0[...] + c1[...]) + (c2[...] + c3[...])
    logit_ref[...] = cot[2 * RANK :]
    both = dot_nn(cot[: 2 * RANK].astype(jnp.bfloat16), slab_ref[...])
    width = both.shape[1]
    query_ref[:, :width] = both[:RANK]
    query_ref[:, width:] = up_ref[...]
    value_ref[...] = both[RANK:]


def second_down_kernel(c0, c1, c2, c3, memory_ref, value_ref, out_ref):
    cot = (c0[...] + c1[...]) + (c2[...] + c3[...])
    out_ref[...] = value_ref[...] + dot_nn(cot.astype(jnp.bfloat16), memory_ref[...])


def finish_kernel(*refs):
    parts = [ref[...].astype(jnp.float32) for ref in refs[:6]]
    query = parts[0] + parts[1]
    value = (parts[2] + parts[3]) + (parts[4] + parts[5])
    query_down_ref, query_up_ref, value_down_ref, value_up_ref = refs[6:]
    value_down_ref[...] = value
    at = 0
    for out_ref in (query_down_ref, query_up_ref, value_up_ref):
        out_ref[...] = query[:, at : at + out_ref.shape[1]]
        at += out_ref.shape[1]


def swap(x, bit, axis="heads"):
    return lax.ppermute(x, axis, [(i, i ^ bit) for i in range(lax.axis_size(axis))])


def after(x, *deps):
    return pl.pallas_call(
        lambda *refs: None,
        out_shape=jax.ShapeDtypeStruct(x.shape, x.dtype),
        in_specs=[anywhere()] * (1 + len(deps)),
        out_specs=anywhere(),
        input_output_aliases={0: 0},
        name="in_order",
    )(x, *deps)


def anywhere():
    return pl.BlockSpec(memory_space=pl.ANY)


def smem():
    return pl.BlockSpec(memory_space=pltpu.SMEM)


def vmem():
    return pl.BlockSpec(memory_space=pltpu.VMEM)


def shaped(*shape, dtype=jnp.float32):
    return jax.ShapeDtypeStruct(shape, dtype)


def run(body, name, out_shape, in_specs, scratch=(), flops=0, moved=0, room=ROOM, out_specs=None):
    many = isinstance(out_shape, (tuple, list))
    return pl.pallas_call(
        body,
        out_shape=out_shape,
        in_specs=in_specs,
        out_specs=out_specs or (tuple(vmem() for _ in out_shape) if many else vmem()),
        scratch_shapes=list(scratch),
        compiler_params=pltpu.CompilerParams(vmem_limit_bytes=int(room * MIB)),
        cost_estimate=pl.CostEstimate(flops=flops, bytes_accessed=moved, transcendentals=0),
        name=name,
    )


def fast(
    slab_tokens,
    memory,
    query_weight,
    key_weight,
    value_weight,
    query_down,
    query_up,
    value_down,
    value_up,
    tag_weight,
    retrieval,
    boundary,
    grad_tags,
):
    tok_rows, width = slab_tokens.shape
    mem_rows = memory.shape[0]
    query_width = query_weight.shape[1]
    heads = query_width // HD
    spans = tok_rows // BLK
    blocks = mem_rows // BLK
    peers = lax.axis_size("tm")
    f32 = jnp.float32
    bf16 = jnp.bfloat16

    def memory_scratch(count):
        return [
            pltpu.VMEM((count, mem_rows, width), bf16),
            pltpu.VMEM((count, width, HD), bf16),
            pltpu.VMEM((count, width, HD), bf16),
            pltpu.VMEM((count, RANK, width), bf16),
            pltpu.SemaphoreType.DMA((4 * count,)),
        ]

    def project_scratch(count):
        return [
            pltpu.VMEM((count, tok_rows, width), bf16),
            pltpu.VMEM((count, width, query_width), bf16),
            pltpu.VMEM((count, width, HD), bf16),
            pltpu.VMEM((count, width, HD), bf16),
            pltpu.VMEM((count, RANK, width), bf16),
            pltpu.VMEM((count, RANK, width), bf16),
            pltpu.SemaphoreType.DMA((count * (WQ_CUTS + 5),)),
        ]

    memory_sums = [
        pltpu.VMEM((mem_rows, 2 * HD), f32),
        pltpu.VMEM((mem_rows, RANK), f32),
        pltpu.SemaphoreType.DMA((2,)),
    ]
    project_sums = [
        pltpu.VMEM((tok_rows, query_width), f32),
        pltpu.VMEM((tok_rows, 2 * HD), f32),
        pltpu.VMEM((tok_rows, 2 * RANK), f32),
    ]

    place = lax.axis_index("heads").astype(jnp.int32).reshape(1)
    tag_t = tag_weight.T
    tags = tag_t.shape[0]
    mem_far = swap(memory, 2)
    mem_near = swap(memory, 1)
    tok_near = swap(slab_tokens, 1)
    tok_far = swap(tok_near, 2)
    mem_acc, mem_low, wanted = run(
        lambda *refs: memory_early_kernel(blocks, *refs),
        "memory_near_half",
        (shaped(mem_rows, 2 * HD), shaped(mem_rows, RANK), shaped(peers, dtype=jnp.int32)),
        [smem()] * 2 + [anywhere()] * 5,
        memory_scratch(2),
        out_specs=(vmem(), vmem(), smem()),
    )(place, retrieval, memory, mem_near, key_weight, value_weight, value_down)
    asked = lax.all_to_all(wanted, "tm", split_axis=0, concat_axis=0, tiled=True)
    weights = (query_weight, key_weight, value_weight, query_down, value_down)
    mem_far = after(mem_far, asked)
    mem_cross = swap(mem_far, 1)
    mem_weights = (key_weight, value_weight, value_down)
    mem_acc, mem_low = run(
        memory_middle_kernel,
        "memory_far_quarter",
        (shaped(mem_rows, 2 * HD), shaped(mem_rows, RANK)),
        [smem()] + [anywhere()] * 6,
        memory_scratch(1) + memory_sums,
    )(place, mem_far, mem_acc, mem_low, *mem_weights)
    pairs = run(
        lambda *refs: memory_kernel(peers, *refs),
        "memory_pairs",
        shaped(peers, PACK, HD, dtype=bf16),
        [smem()] * 2 + [anywhere()] * 6 + [vmem()],
        memory_scratch(1) + memory_sums + [pltpu.VMEM((blocks, PACK, HD), bf16)],
    )(place, asked, mem_cross, mem_acc, mem_low, *mem_weights, value_up)
    got = lax.all_to_all(pairs, "tm", split_axis=0, concat_axis=0, tiled=True)
    *early, grad, grad_t = run(
        project_early_kernel,
        "project_near_half",
        (
            shaped(tok_rows, query_width),
            shaped(tok_rows, 2 * HD),
            shaped(tok_rows, 2 * RANK),
            shaped(tok_rows, query_width, dtype=bf16),
            shaped(query_width, tok_rows, dtype=bf16),
        ),
        [smem()] + [anywhere()] * 7 + [vmem()] * 2 + [anywhere()],
        project_scratch(2),
    )(place, slab_tokens, tok_near, *weights, tag_t, grad_tags.T, pairs)
    tok_far = after(tok_far, early[2])
    tok_cross = swap(tok_far, 1)
    parts = run(
        project_far_kernel,
        "project_far_half",
        (
            shaped(tok_rows, query_width, dtype=bf16),
            shaped(tok_rows, HD, dtype=bf16),
            shaped(tok_rows, HD, dtype=bf16),
            shaped(2 * RANK, tok_rows, dtype=bf16),
        ),
        [smem()] + [anywhere()] * 10 + [vmem()] * 2,
        project_scratch(2) + project_sums + [pltpu.SemaphoreType.DMA((3,))],
    )(place, tok_far, tok_cross, *weights, *early, query_up, value_up)

    seen = peers * BLK
    total = seen + BLK
    cot, ups, mcot = run(
        lambda *refs: attention_kernel(peers, heads, *refs),
        "span_attention",
        (shaped(2 * RANK + tags, tok_rows), shaped(RANK, query_width + HD), shaped(peers, RANK, BLK)),
        [smem()] + [anywhere()] * 7 + [vmem()] * 3,
        [
            pltpu.VMEM((tok_rows, query_width), bf16),
            pltpu.VMEM((tok_rows, HD), bf16),
            pltpu.VMEM((tok_rows, HD), bf16),
            pltpu.VMEM((2 * RANK, tok_rows), bf16),
            pltpu.VMEM((peers, RANK, BLK), bf16),
            pltpu.VMEM((tok_rows, query_width), bf16),
            pltpu.VMEM((query_width, tok_rows), bf16),
            pltpu.VMEM((seen, HD), bf16),
            pltpu.VMEM((seen, HD), bf16),
            pltpu.VMEM((HD, seen), bf16),
            pltpu.VMEM((HD, seen), bf16),
            pltpu.VMEM((HD, PAIR * BLK), bf16),
            pltpu.VMEM((HD, PAIR * BLK), bf16),
            pltpu.VMEM((PAIR * BLK, BLK), f32),
            pltpu.VMEM((2, PAIR * BLK, total), f32),
            pltpu.VMEM((2, PAIR * BLK, total), f32),
            pltpu.VMEM((heads * PAIR * BLK, total), bf16),
            pltpu.VMEM((2, PAIR * BLK, total), bf16),
            pltpu.VMEM((PAIR * BLK, query_width), bf16),
            pltpu.VMEM((PAIR * BLK, query_width), bf16),
            pltpu.VMEM((HD, seen), f32),
            pltpu.SemaphoreType.DMA((3 * peers + 6,)),
        ],
        flops=20 * tok_rows * query_width * total,
        moved=4 * tok_rows * query_width,
        room=60,
    )(boundary, *parts, got, grad, grad_t, query_up, value_up, tag_t)

    back = lax.all_to_all(mcot, "tm", split_axis=0, concat_axis=0, tiled=True)
    cots = [cot] + [swap(cot, d) for d in range(1, 4)]
    own = run(
        lambda *refs: own_kernel(peers, *refs),
        "owned_cotangent",
        shaped(RANK, mem_rows),
        [smem()] + [vmem()],
        [pltpu.VMEM((blocks, RANK, BLK), f32)],
        room=8,
    )(asked, back)
    logits, query_sum, value_part = run(
        first_down_kernel,
        "first_down",
        (shaped(tags, tok_rows), shaped(RANK, width + ups.shape[1]), shaped(RANK, width)),
        [vmem()] * 6,
        flops=4 * RANK * tok_rows * width,
        moved=2 * tok_rows * width,
        room=8,
    )(*cots, slab_tokens, ups)
    owns = [own] + [swap(own, d) for d in range(1, 4)]
    value_sum = run(
        second_down_kernel,
        "second_down",
        shaped(RANK, width),
        [vmem()] * 6,
        flops=2 * RANK * mem_rows * width,
        moved=2 * mem_rows * width,
        room=8,
    )(*owns, memory, value_part)
    query_sum = query_sum + swap(query_sum, 1, "tm")
    query_sum = (query_sum + swap(query_sum, 2, "tm")).astype(bf16)
    value_sum = (value_sum + swap(value_sum, 1, "tm")).astype(bf16)
    sums = [query_sum, swap(query_sum, 4, "tm"), value_sum] + [swap(value_sum, bit, "tm") for bit in (2, 4, 6)]
    query_down_grad, query_up_grad, value_down_grad, value_up_grad = run(
        finish_kernel,
        "finish_outputs",
        (shaped(RANK, width), shaped(RANK, query_width), shaped(RANK, width), shaped(RANK, HD)),
        [vmem()] * 6,
        room=8,
    )(*sums)
    return (logits.T, query_down_grad, query_up_grad, value_down_grad, value_up_grad)


def solution(mesh):
    in_specs = (
        P("tm", "heads"),
        P("tm", "heads"),
        P(None, "heads"),
        P(None, "heads"),
        P(None, "heads"),
        P(),
        P(None, "heads"),
        P(),
        P(None, "heads"),
        P("heads", None),
        P("tm", None),
        P("tm"),
        P("tm", None),
    )
    out_specs = (
        P("tm", None),
        P(None, "heads"),
        P(None, "heads"),
        P(None, "heads"),
        P(None, "heads"),
    )
    fits = mesh.shape["heads"] == 4 and mesh.shape["tm"] == 8 == TOP * CAP
    local = fast if fits else general
    return jax.shard_map(local, mesh=mesh, in_specs=in_specs, out_specs=out_specs, check_vma=False)
```

```python
import jax
import jax.numpy as jnp
from jax import lax
from jax.experimental import pallas as pl
from jax.experimental.pallas import tpu as pltpu
from jax.sharding import PartitionSpec as P

HD = 128
RANK = 16
TOP = 8
BLK = 128
CAP = 1


HIGHEST = lax.Precision.HIGHEST


def attend(query, all_keys, all_values, split_row, out_grad):
    span_count, row_count, query_width = query.shape
    key_count, kv_width = (all_keys.shape[1], all_keys.shape[2])
    kv_heads = kv_width // HD
    group_size = query_width // kv_width
    score_scale = HD ** (-0.5)
    query_heads = query.reshape(span_count, row_count, kv_heads, group_size, HD)
    key_heads = all_keys.reshape(span_count, key_count, kv_heads, HD)
    value_heads = all_values.reshape(span_count, key_count, kv_heads, HD)
    grad_heads = out_grad.reshape(span_count, row_count, kv_heads, group_size, HD)
    scores = (
        jnp.einsum("crngd,cknd->cngrk", query_heads, key_heads, preferred_element_type=jnp.float32)
        * score_scale
    )
    row_ids = jnp.arange(row_count, dtype=jnp.int32)[:, None]
    col_ids = jnp.arange(BLK, dtype=jnp.int32)[None, :]
    edge_at = split_row[:, None, None]
    local_seen = (col_ids <= row_ids) & ((col_ids >= edge_at) | (row_ids < edge_at))
    visible = jnp.concatenate(
        [jnp.ones((span_count, row_count, key_count - BLK), jnp.bool_), local_seen], axis=2
    )
    scores = jnp.where(visible[:, None, None], scores, -jnp.inf)
    row_max = jnp.max(scores, axis=-1, keepdims=True)
    weights = jnp.exp(scores - row_max)
    probs = weights / jnp.sum(weights, axis=-1, keepdims=True)
    probs_low = probs.astype(jnp.bfloat16)
    attended = jnp.einsum(
        "cngrk,cknd->crngd", probs_low, value_heads, preferred_element_type=jnp.float32
    ).astype(jnp.bfloat16)
    prob_grad = jnp.einsum(
        "crngd,cknd->cngrk", grad_heads, value_heads, preferred_element_type=jnp.float32
    )
    row_dot = jnp.sum(grad_heads.astype(jnp.float32) * attended.astype(jnp.float32), axis=-1)
    row_dot = jnp.transpose(row_dot, (0, 2, 3, 1))[..., None]
    score_grad = (probs * (prob_grad - row_dot) * score_scale).astype(jnp.bfloat16)
    query_grad = jnp.einsum(
        "cngrk,cknd->crngd", score_grad, key_heads, preferred_element_type=jnp.float32
    ).astype(jnp.bfloat16)
    value_grad = jnp.einsum(
        "cngrk,crngd->cknd", probs_low, grad_heads, preferred_element_type=jnp.float32
    )
    return (
        attended.reshape(span_count, row_count, query_width),
        query_grad.reshape(span_count, row_count, query_width),
        value_grad.reshape(span_count, key_count, kv_width),
    )


def choose_slots(needed, places):
    slot_ids = jnp.arange(CAP, dtype=jnp.int32)
    return needed[:, None, :] * (places[:, None, :] == slot_ids[None, :, None]).astype(jnp.int32)


def general(
    slab_tokens,
    memory,
    query_weight,
    key_weight,
    value_weight,
    query_down,
    query_up,
    value_down,
    value_up,
    tag_weight,
    retrieval,
    boundary,
    grad_tags,
):
    tok_rows = slab_tokens.shape[0]
    mem_rows = memory.shape[0]
    query_width = query_weight.shape[1]
    kv_width = key_weight.shape[1]
    span_count = tok_rows // BLK
    block_count = mem_rows // BLK
    pair_weight = jnp.concatenate([key_weight, value_weight], 1)
    adapter_pair = jnp.concatenate([query_down, value_down], 0)
    contract_last = (((1,), (1,)), ((), ()))
    contract_first = (((0,), (0,)), ((), ()))
    token_piece = lax.all_gather(slab_tokens, "heads", axis=1, tiled=True)
    memory_piece = lax.all_gather(memory, "heads", axis=1, tiled=True)
    query_acc = jnp.dot(token_piece, query_weight, preferred_element_type=jnp.float32)
    pair_acc = jnp.dot(token_piece, pair_weight, preferred_element_type=jnp.float32)
    low_acc = lax.dot_general(
        token_piece, adapter_pair, contract_last, preferred_element_type=jnp.float32
    )
    memory_acc = jnp.dot(memory_piece, pair_weight, preferred_element_type=jnp.float32)
    memory_low_acc = lax.dot_general(
        memory_piece, adapter_pair[RANK:], contract_last, preferred_element_type=jnp.float32
    )
    query_acc, pair_acc, low_acc, memory_acc, memory_low_acc = (
        query_acc,
        pair_acc,
        low_acc,
        memory_acc,
        memory_low_acc,
    )
    low_tokens = low_acc.astype(jnp.bfloat16)
    low_query = low_tokens[:, :RANK]
    low_value = low_tokens[:, RANK:]
    queries = (query_acc + jnp.dot(low_query, query_up, preferred_element_type=jnp.float32)).astype(
        jnp.bfloat16
    )
    keys_local = pair_acc[:, :kv_width].astype(jnp.bfloat16)
    values_local = (
        pair_acc[:, kv_width:] + jnp.dot(low_value, value_up, preferred_element_type=jnp.float32)
    ).astype(jnp.bfloat16)
    memory_low = memory_low_acc.astype(jnp.bfloat16)
    memory_pair = (
        jnp.concatenate(
            [
                memory_acc[:, :kv_width],
                memory_acc[:, kv_width:]
                + jnp.dot(memory_low, value_up, preferred_element_type=jnp.float32),
            ],
            1,
        )
        .astype(jnp.bfloat16)
        .reshape(block_count, BLK, 2 * kv_width)
    )
    peer_count = lax.axis_size("tm")
    every_block = jnp.arange(peer_count * block_count, dtype=jnp.int32)
    wanted = (
        jnp.any(retrieval.reshape(-1, 1) == every_block[None, :], axis=0)
        .astype(jnp.int32)
        .reshape(peer_count, block_count)
    )
    places = jnp.cumsum(wanted, axis=1) - wanted
    requested = choose_slots(wanted, places)
    asked_for = lax.all_to_all(requested, "tm", split_axis=0, concat_axis=0, tiled=True)
    rows_needed = retrieval // block_count * CAP + jnp.take(places.reshape(-1), retrieval)
    asked_low = asked_for.astype(jnp.bfloat16)
    outgoing = jnp.einsum(
        "rcm,mbw->rcbw", asked_low, memory_pair, preferred_element_type=jnp.float32
    ).astype(jnp.bfloat16)
    fetched = lax.all_to_all(outgoing, "tm", split_axis=0, concat_axis=0, tiled=True)
    slot_rows = fetched.reshape(peer_count * CAP, BLK, 2 * kv_width)
    picked = jnp.take(slot_rows, rows_needed.reshape(-1), axis=0).reshape(
        span_count, TOP * BLK, 2 * kv_width
    )
    all_keys = jnp.concatenate(
        [picked[..., :kv_width], keys_local.reshape(span_count, BLK, kv_width)], 1
    )
    all_values = jnp.concatenate(
        [picked[..., kv_width:], values_local.reshape(span_count, BLK, kv_width)], 1
    )
    attended_grad = lax.dot_general(
        grad_tags, tag_weight.astype(jnp.float32), contract_last, precision=HIGHEST
    ).astype(jnp.bfloat16)
    attended, query_grad, value_grad = attend(
        queries.reshape(span_count, BLK, query_width),
        all_keys,
        all_values,
        boundary,
        attended_grad.reshape(span_count, BLK, query_width),
    )
    attended = attended.reshape(tok_rows, query_width)
    query_grad = query_grad.reshape(tok_rows, query_width)
    logits_out = lax.psum(
        jnp.dot(attended, tag_weight, preferred_element_type=jnp.float32), "heads"
    )
    local_grad = value_grad[:, TOP * BLK :].reshape(tok_rows, kv_width)
    slot_grads = value_grad[:, : TOP * BLK].reshape(span_count * TOP, BLK * kv_width)
    slot_hits = (
        rows_needed.reshape(-1, 1) == jnp.arange(peer_count * CAP, dtype=jnp.int32)[None, :]
    ).astype(jnp.float32)
    grad_buffer = lax.dot_general(slot_hits, slot_grads, contract_first, precision=HIGHEST).reshape(
        peer_count * CAP, BLK, kv_width
    )
    up_wide = value_up.astype(jnp.float32)
    returned = lax.all_to_all(
        grad_buffer.reshape(peer_count, CAP, BLK, kv_width),
        "tm",
        split_axis=0,
        concat_axis=0,
        tiled=True,
    )
    owned_grad = jnp.einsum(
        "rcm,rcbw->mbw", asked_for.astype(jnp.float32), returned, precision=HIGHEST
    ).reshape(mem_rows, kv_width)
    memory_cot = lax.dot_general(up_wide, owned_grad, contract_last, precision=HIGHEST)
    up_memory = lax.dot_general(
        memory_low.astype(jnp.float32), owned_grad, contract_first, precision=HIGHEST
    )
    query_cot = lax.dot_general(
        query_up, query_grad, contract_last, preferred_element_type=jnp.float32
    )
    value_cot = lax.dot_general(up_wide, local_grad, contract_last, precision=HIGHEST)
    query_cot, value_cot, memory_cot = lax.psum((query_cot, value_cot, memory_cot), "heads")
    query_down_grad = jnp.dot(
        query_cot.astype(jnp.bfloat16), slab_tokens, preferred_element_type=jnp.float32
    )
    value_down_grad = jnp.dot(
        value_cot.astype(jnp.bfloat16), slab_tokens, preferred_element_type=jnp.float32
    ) + jnp.dot(memory_cot.astype(jnp.bfloat16), memory, preferred_element_type=jnp.float32)
    query_up_grad = lax.dot_general(
        low_query, query_grad, contract_first, preferred_element_type=jnp.float32
    )
    value_up_grad = (
        lax.dot_general(
            low_value.astype(jnp.float32), local_grad, contract_first, precision=HIGHEST
        )
        + up_memory
    )
    query_down_grad, query_up_grad, value_down_grad, value_up_grad = lax.psum(
        (query_down_grad, query_up_grad, value_down_grad, value_up_grad), "tm"
    )
    return (logits_out, query_down_grad, query_up_grad, value_down_grad, value_up_grad)


LOG2E = 1.4426950408889634
NT = (((1,), (1,)), ((), ()))
PACK = 2 * BLK + RANK
STRIP = 16
PAIR = 2
MIB = 1024 * 1024
ROOM = 63.5


def dot_nt(a, b, precision=None):
    return lax.dot_general(a, b, NT, precision=precision, preferred_element_type=jnp.float32)


def dot_nn(a, b, precision=None):
    return jnp.dot(a, b, precision=precision, preferred_element_type=jnp.float32)


def piece_rows(place_ref, j, width):
    return pl.ds(pl.multiple_of(lax.bitwise_xor(place_ref[0], j) * width, width), width)


def start_copies(pairs, sems, first=0):
    copies = [pltpu.make_async_copy(src, dst, sems.at[first + n]) for n, (src, dst) in enumerate(pairs)]
    for copy in copies:
        copy.start()
    return copies


def wait_all(copies):
    for copy in copies:
        copy.wait()


def memory_pieces(place_ref, js, xs, hbm, scratch, sems):
    x_s, wk_s, wv_s, down_s = scratch
    width = x_s.shape[2]
    groups = []
    for n, j in enumerate(js):
        here = piece_rows(place_ref, j, width)
        pairs = [
            (xs[n], x_s.at[n]),
            (hbm[0].at[here, :], wk_s.at[n]),
            (hbm[1].at[here, :], wv_s.at[n]),
            (hbm[2].at[:, here], down_s.at[n]),
        ]
        groups.append(start_copies(pairs, sems, 4 * n))
    return groups


def memory_terms(n, scratch):
    x_s, wk_s, wv_s, down_s = scratch
    x = x_s[n]
    return dot_nn(x, jnp.concatenate([wk_s[n], wv_s[n]], 1)), dot_nt(x, down_s[n])


def memory_early_kernel(blocks, place_ref, named_ref, x0, x1, *refs):
    hbm, acc_ref, low_ref, wanted_ref, scratch, sems = refs[:3], refs[3], refs[4], refs[5], refs[6:10], refs[10]
    groups = memory_pieces(place_ref, (0, 1), (x0, x1), hbm, scratch, sems)
    for slot in range(TOP):
        block = named_ref[0, slot]
        wanted_ref[lax.div(block, blocks)] = lax.rem(block, blocks)
    for n in range(2):
        wait_all(groups[n])
        term, low_term = memory_terms(n, scratch)
        if n == 0:
            acc_ref[...] = term
            low_ref[...] = low_term
        else:
            acc_ref[...] += term
            low_ref[...] += low_term


def memory_middle_kernel(place_ref, x2, acc_hbm, low_hbm, *refs):
    hbm, acc_ref, low_ref, scratch, sems = refs[:3], refs[3], refs[4], refs[5:9], refs[9]
    acc_s, low_s, acc_sems = refs[10:13]
    groups = memory_pieces(place_ref, (2,), (x2,), hbm, scratch, sems)
    sums = start_copies([(acc_hbm, acc_s), (low_hbm, low_s)], acc_sems)
    wait_all(groups[0])
    term, low_term = memory_terms(0, scratch)
    wait_all(sums)
    acc_ref[...] = acc_s[...] + term
    low_ref[...] = low_s[...] + low_term


def memory_kernel(peers, place_ref, asked_ref, x3, acc_hbm, low_hbm, *refs):
    hbm, up_ref, out_ref = refs[:3], refs[3], refs[4]
    scratch, sems, acc_s, low_s, acc_sems, pair_ref = refs[5:9], refs[9], refs[10], refs[11], refs[12], refs[13]
    groups = memory_pieces(place_ref, (3,), (x3,), hbm, scratch, sems)
    sums = start_copies([(acc_hbm, acc_s), (low_hbm, low_s)], acc_sems)
    wait_all(groups[0])
    term, low_term = memory_terms(0, scratch)
    wait_all(sums)
    acc = acc_s[...] + term
    low = low_s[...] + low_term
    values = (acc[:, HD:] + dot_nn(low.astype(jnp.bfloat16), up_ref[...])).astype(jnp.bfloat16)
    keys = acc[:, :HD].astype(jnp.bfloat16)
    low_t = jnp.transpose(low).astype(jnp.bfloat16)
    for b in range(acc.shape[0] // BLK):
        at = slice(b * BLK, (b + 1) * BLK)
        pair_ref[b, 0:BLK, :] = keys[at]
        pair_ref[b, BLK : 2 * BLK, :] = values[at]
        pair_ref[b, 2 * BLK : PACK, :] = low_t[:, at]
    for r in range(peers):
        out_ref[r] = pair_ref[asked_ref[r]]


WQ_CUTS = 4


def project_pieces(place_ref, js, xs, hbm, scratch, sems):
    wq_hbm, wk_hbm, wv_hbm, qd_hbm, vd_hbm = hbm
    x_s, wq_s, wk_s, wv_s, qd_s, vd_s = scratch
    width = x_s.shape[2]
    part = width // WQ_CUTS
    groups = []
    for n, j in enumerate(js):
        here = piece_rows(place_ref, j, width)
        start = lax.bitwise_xor(place_ref[0], j) * width
        pairs = [(xs[n], x_s.at[n])]
        for m in range(WQ_CUTS):
            rows = pl.ds(pl.multiple_of(start + m * part, part), part)
            pairs.append((wq_hbm.at[rows, :], wq_s.at[n, pl.ds(m * part, part), :]))
        pairs += [
            (wk_hbm.at[here, :], wk_s.at[n]),
            (wv_hbm.at[here, :], wv_s.at[n]),
            (qd_hbm.at[:, here], qd_s.at[n]),
            (vd_hbm.at[:, here], vd_s.at[n]),
        ]
        groups.append(start_copies(pairs, sems, len(pairs) * n))
    return groups


def project_terms(n, scratch):
    x_s, wq_s, wk_s, wv_s, qd_s, vd_s = scratch
    x = x_s[n]
    return (
        dot_nn(x, wq_s[n]),
        dot_nn(x, jnp.concatenate([wk_s[n], wv_s[n]], 1)),
        dot_nt(x, jnp.concatenate([qd_s[n], vd_s[n]], 0)),
    )


def project_early_kernel(place_ref, x0, x1, *refs):
    hbm, (tag_ref, tags_t_ref), outs, (grad_ref, grad_t_ref) = refs[:5], refs[5:7], refs[8:11], refs[11:13]
    scratch, sems = refs[13:19], refs[19]
    groups = project_pieces(place_ref, (0, 1), (x0, x1), hbm, scratch, sems)
    first = (((0,), (0,)), ((), ()))
    tag = tag_ref[...].astype(jnp.float32)
    tags_t = tags_t_ref[...]
    f32 = jnp.float32
    grad_ref[...] = lax.dot_general(
        tags_t, tag, first, precision=HIGHEST, preferred_element_type=f32
    ).astype(jnp.bfloat16)
    grad_t_ref[...] = lax.dot_general(
        tag, tags_t, first, precision=HIGHEST, preferred_element_type=f32
    ).astype(jnp.bfloat16)
    for n in range(2):
        wait_all(groups[n])
        for ref, term in zip(outs, project_terms(n, scratch)):
            if n == 0:
                ref[...] = term
            else:
                ref[...] += term


def project_far_kernel(place_ref, x3, x2, *refs):
    hbm, early, (qup_ref, vup_ref), (q_ref, k_ref, v_ref, low_ref) = refs[:5], refs[5:8], refs[8:10], refs[10:14]
    scratch, sems, sum_refs, sum_sems = refs[14:20], refs[20], refs[21:24], refs[24]
    groups = project_pieces(place_ref, (3, 2), (x3, x2), hbm, scratch, sems)
    loads = start_copies(list(zip(early, sum_refs)), sum_sems)
    wait_all(groups[0])
    terms = project_terms(0, scratch)
    wait_all(loads)
    for ref, term in zip(sum_refs, terms):
        ref[...] += term
    wait_all(groups[1])
    q_acc, kv_acc, low_acc = [ref[...] + term for ref, term in zip(sum_refs, project_terms(1, scratch))]
    low = low_acc.astype(jnp.bfloat16)
    q_ref[...] = (q_acc + dot_nn(low[:, :RANK], qup_ref[...])).astype(jnp.bfloat16)
    k_ref[...] = kv_acc[:, :HD].astype(jnp.bfloat16)
    v_ref[...] = (kv_acc[:, HD:] + dot_nn(low[:, RANK:], vup_ref[...])).astype(jnp.bfloat16)
    low_ref[...] = jnp.transpose(low_acc).astype(jnp.bfloat16)


def attention_kernel(peers, heads, bound_ref, *refs):
    parts, got, grad_hbm, grad_t_hbm = refs[:4], refs[4], refs[5], refs[6]
    qup_ref, vup_ref, tag_ref, cot_ref, mine_ref, mcot_ref = refs[7:13]
    (q_s, k_own, v_own, low_s, low_m_s, grad_ref, grad_t_ref, k_all, v_all, kt_all, vt_all, kt_own, vt_own, bias_s, s_s, dp_s,
     p_s, ds_s, att_s, dq_s, dv_s, up_ref, more_sems) = refs[13:]
    seen = peers * BLK
    pairs = []
    for b in range(peers):
        at = slice(b * BLK, (b + 1) * BLK)
        pairs.append((got.at[b, pl.ds(0, BLK), :], k_all.at[at, :]))
        pairs.append((got.at[b, pl.ds(BLK, BLK), :], v_all.at[at, :]))
        pairs.append((got.at[b, pl.ds(2 * BLK, RANK), :], low_m_s.at[b]))
    pairs += list(zip(parts, (q_s, k_own, v_own, low_s))) + [(grad_hbm, grad_ref), (grad_t_hbm, grad_t_ref)]
    copies = start_copies(pairs, more_sems)
    wait_all(copies[: 3 * peers])
    for b in range(peers):
        at = slice(b * BLK, (b + 1) * BLK)
        kt_all[:, at] = jnp.transpose(k_all[at, :])
        vt_all[:, at] = jnp.transpose(v_all[at, :])
    wait_all(copies[3 * peers : -1])
    dv_s[...] = jnp.zeros_like(dv_s)
    up_ref[...] = jnp.zeros_like(up_ref)
    scale = HD ** (-0.5)
    up_wide = vup_ref[...].astype(jnp.float32)
    query_width = heads * HD

    def pair_step(c, carry):
        base = c * (PAIR * BLK)
        rows = pl.ds(pl.multiple_of(base, PAIR * BLK), PAIR * BLK)
        own_rows = [pl.ds(pl.multiple_of(base + b * BLK, BLK), BLK) for b in range(PAIR)]
        row_ids = lax.broadcasted_iota(jnp.int32, (BLK, BLK), 0)
        col_ids = lax.broadcasted_iota(jnp.int32, (BLK, BLK), 1)
        for b in range(PAIR):
            kt_own[:, b * BLK : (b + 1) * BLK] = jnp.transpose(k_own[own_rows[b], :])
            vt_own[:, b * BLK : (b + 1) * BLK] = jnp.transpose(v_own[own_rows[b], :])
            edge = bound_ref[c * PAIR + b]
            visible = (col_ids <= row_ids) & ((col_ids >= edge) | (row_ids < edge))
            bias_s[b * BLK : (b + 1) * BLK, :] = jnp.where(visible, 0.0, -jnp.inf)

        def head_cols(h):
            return slice(h * HD, (h + 1) * HD)

        def times_keys(out_ref, left_ref, h, all_t, own_t):
            out_ref[:, :seen] = dot_nn(left_ref[rows, head_cols(h)], all_t[...])
            for b in range(PAIR):
                at = slice(b * BLK, (b + 1) * BLK)
                out_ref[at, seen:] = dot_nn(left_ref[own_rows[b], head_cols(h)], own_t[:, at])

        def over_keys(left_ref, first, all_ref, own_ref):
            whole = dot_nn(left_ref[first : first + PAIR * BLK, :seen], all_ref[...])
            mine = [
                dot_nn(left_ref[first + b * BLK : first + (b + 1) * BLK, seen:], own_ref[own_rows[b], :])
                for b in range(PAIR)
            ]
            return (whole + jnp.concatenate(mine, 0)).astype(jnp.bfloat16)

        def scores(h):
            times_keys(s_s.at[h % 2], q_s, h, kt_all, kt_own)

        def prob_grads(h):
            times_keys(dp_s.at[h % 2], grad_ref, h, vt_all, vt_own)

        def strips(h):
            for r in range(0, PAIR * BLK, STRIP):
                at = slice(r, r + STRIP)
                s = s_s[h % 2, at, :]
                s = jnp.concatenate([s[:, :seen], s[:, seen:] + bias_s[at, :]], 1) * (scale * LOG2E)
                w = jnp.exp2(s - jnp.max(s, axis=1, keepdims=True))
                probs = w * (1.0 / jnp.sum(w, axis=1, keepdims=True))
                probs_low = probs.astype(jnp.bfloat16)
                first = h * PAIR * BLK + r
                p_s[first : first + STRIP, :] = probs_low
                dp = dp_s[h % 2, at, :]
                dot = jnp.sum(probs_low.astype(jnp.float32) * dp, axis=1, keepdims=True)
                ds_s[h % 2, at, :] = (probs * ((dp - dot) * scale)).astype(jnp.bfloat16)

        def finish_head(h):
            att_s[:, head_cols(h)] = over_keys(p_s, h * PAIR * BLK, v_all, v_own)
            dq_s[:, head_cols(h)] = over_keys(ds_s.at[h % 2], 0, k_all, k_own)

        scores(0)
        prob_grads(0)
        for h in range(heads + 1):
            if h + 1 < heads:
                scores(h + 1)
                prob_grads(h + 1)
            if h < heads:
                strips(h)
            if h > 0:
                finish_head(h - 1)
        pl.when(c == 0)(copies[-1].wait)
        g_t = jnp.concatenate([grad_t_ref[h * HD : (h + 1) * HD, rows] for h in range(heads)], 1)
        dv_s[...] += dot_nn(g_t, p_s[:, :seen])
        dv_own = []
        for b in range(PAIR):
            g_b = jnp.concatenate([grad_t_ref[h * HD : (h + 1) * HD, own_rows[b]] for h in range(heads)], 1)
            starts = [(h * PAIR + b) * BLK for h in range(heads)]
            p_b = jnp.concatenate([p_s[n : n + BLK, seen:] for n in starts], 0)
            dv_own.append(dot_nn(g_b, p_b))
        dv_own = jnp.concatenate(dv_own, 1)
        dq = dq_s[...]
        cot_ref[0:RANK, rows] = dot_nt(qup_ref[...], dq)
        cot_ref[RANK : 2 * RANK, rows] = dot_nn(up_wide, dv_own, HIGHEST)
        cot_ref[2 * RANK :, rows] = dot_nt(tag_ref[...], att_s[...])
        up_ref[:, :query_width] += dot_nn(low_s[0:RANK, rows], dq)
        up_ref[:, query_width:] += dot_nt(low_s[RANK:, rows].astype(jnp.float32), dv_own, HIGHEST)
        return carry

    lax.fori_loop(0, q_s.shape[0] // (PAIR * BLK), pair_step, 0)
    dv = dv_s[...]
    mcot = dot_nn(up_wide, dv, HIGHEST)
    low_m = jnp.concatenate([low_m_s[b] for b in range(peers)], 1).astype(jnp.float32)
    up_ref[:, query_width:] += dot_nt(low_m, dv, HIGHEST)
    for b in range(peers):
        mcot_ref[b] = mcot[:, b * BLK : (b + 1) * BLK]
    at, wide = cot_ref.shape
    mine_ref[:at, :] = cot_ref[...]
    for n in range(0, up_ref.shape[1], wide):
        mine_ref[at : at + RANK, :] = up_ref[:, n : n + wide]
        at += RANK


def own_kernel(peers, asked_ref, back_ref, out_ref, sum_s):
    sum_s[...] = jnp.zeros_like(sum_s)
    for r in range(peers):
        block = asked_ref[r]
        sum_s[block] = sum_s[block] + back_ref[r]
    out_ref[...] = jnp.concatenate([sum_s[m] for m in range(sum_s.shape[0])], 1)


def first_down_kernel(mine_ref, c1, c2, c3, slab_ref, dep_ref, logit_ref, query_ref, value_ref):
    own, wide = c1.shape
    cot = (mine_ref[:own, :] + c1[...]) + (c2[...] + c3[...])
    logit_ref[...] = cot[2 * RANK :]
    both = dot_nn(cot[: 2 * RANK].astype(jnp.bfloat16), slab_ref[...])
    width = both.shape[1]
    query_ref[:, :width] = both[:RANK]
    for n, at in enumerate(range(own, mine_ref.shape[0], RANK)):
        query_ref[:, width + n * wide : width + (n + 1) * wide] = mine_ref[at : at + RANK, :]
    value_ref[...] = both[RANK:]


def second_down_kernel(c0, c1, c2, c3, memory_ref, value_ref, q0, q1, out_ref, query_ref):
    query_ref[...] = q0[...] + q1[...]
    cot = (c0[...] + c1[...]) + (c2[...] + c3[...])
    out_ref[...] = value_ref[...] + dot_nn(cot.astype(jnp.bfloat16), memory_ref[...])


def finish_kernel(*refs):
    parts = [ref[...].astype(jnp.float32) for ref in refs[:6]]
    query = parts[0] + parts[1]
    value = (parts[2] + parts[3]) + (parts[4] + parts[5])
    query_down_ref, query_up_ref, value_down_ref, value_up_ref = refs[6:]
    value_down_ref[...] = value
    at = 0
    for out_ref in (query_down_ref, query_up_ref, value_up_ref):
        out_ref[...] = query[:, at : at + out_ref.shape[1]]
        at += out_ref.shape[1]


def swap(x, bit, axis="heads"):
    return lax.ppermute(x, axis, [(i, i ^ bit) for i in range(lax.axis_size(axis))])


def after(x, *deps):
    return pl.pallas_call(
        lambda *refs: None,
        out_shape=jax.ShapeDtypeStruct(x.shape, x.dtype),
        in_specs=[anywhere()] * (1 + len(deps)),
        out_specs=anywhere(),
        input_output_aliases={0: 0},
        name="in_order",
    )(x, *deps)


def anywhere():
    return pl.BlockSpec(memory_space=pl.ANY)


def smem():
    return pl.BlockSpec(memory_space=pltpu.SMEM)


def vmem():
    return pl.BlockSpec(memory_space=pltpu.VMEM)


def shaped(*shape, dtype=jnp.float32):
    return jax.ShapeDtypeStruct(shape, dtype)


def run(body, name, out_shape, in_specs, scratch=(), flops=0, moved=0, room=ROOM, out_specs=None):
    many = isinstance(out_shape, (tuple, list))
    return pl.pallas_call(
        body,
        out_shape=out_shape,
        in_specs=in_specs,
        out_specs=out_specs or (tuple(vmem() for _ in out_shape) if many else vmem()),
        scratch_shapes=list(scratch),
        compiler_params=pltpu.CompilerParams(vmem_limit_bytes=int(room * MIB)),
        cost_estimate=pl.CostEstimate(flops=flops, bytes_accessed=moved, transcendentals=0),
        name=name,
    )


def fast(
    slab_tokens,
    memory,
    query_weight,
    key_weight,
    value_weight,
    query_down,
    query_up,
    value_down,
    value_up,
    tag_weight,
    retrieval,
    boundary,
    grad_tags,
):
    tok_rows, width = slab_tokens.shape
    mem_rows = memory.shape[0]
    query_width = query_weight.shape[1]
    heads = query_width // HD
    spans = tok_rows // BLK
    blocks = mem_rows // BLK
    peers = lax.axis_size("tm")
    f32 = jnp.float32
    bf16 = jnp.bfloat16

    def memory_scratch(count):
        return [
            pltpu.VMEM((count, mem_rows, width), bf16),
            pltpu.VMEM((count, width, HD), bf16),
            pltpu.VMEM((count, width, HD), bf16),
            pltpu.VMEM((count, RANK, width), bf16),
            pltpu.SemaphoreType.DMA((4 * count,)),
        ]

    def project_scratch(count):
        return [
            pltpu.VMEM((count, tok_rows, width), bf16),
            pltpu.VMEM((count, width, query_width), bf16),
            pltpu.VMEM((count, width, HD), bf16),
            pltpu.VMEM((count, width, HD), bf16),
            pltpu.VMEM((count, RANK, width), bf16),
            pltpu.VMEM((count, RANK, width), bf16),
            pltpu.SemaphoreType.DMA((count * (WQ_CUTS + 5),)),
        ]

    memory_sums = [
        pltpu.VMEM((mem_rows, 2 * HD), f32),
        pltpu.VMEM((mem_rows, RANK), f32),
        pltpu.SemaphoreType.DMA((2,)),
    ]
    project_sums = [
        pltpu.VMEM((tok_rows, query_width), f32),
        pltpu.VMEM((tok_rows, 2 * HD), f32),
        pltpu.VMEM((tok_rows, 2 * RANK), f32),
    ]

    place = lax.axis_index("heads").astype(jnp.int32).reshape(1)
    tag_t = tag_weight.T
    tags = tag_t.shape[0]
    mem_far = swap(memory, 2)
    mem_near = swap(memory, 1)
    tok_near = swap(slab_tokens, 1)
    tok_far = swap(tok_near, 2)
    mem_acc, mem_low, wanted = run(
        lambda *refs: memory_early_kernel(blocks, *refs),
        "memory_near_half",
        (shaped(mem_rows, 2 * HD), shaped(mem_rows, RANK), shaped(peers, dtype=jnp.int32)),
        [smem()] * 2 + [anywhere()] * 5,
        memory_scratch(2),
        out_specs=(vmem(), vmem(), smem()),
    )(place, retrieval, memory, mem_near, key_weight, value_weight, value_down)
    asked = lax.all_to_all(wanted, "tm", split_axis=0, concat_axis=0, tiled=True)
    weights = (query_weight, key_weight, value_weight, query_down, value_down)
    mem_far = after(mem_far, asked)
    mem_cross = swap(mem_far, 1)
    mem_weights = (key_weight, value_weight, value_down)
    mem_acc, mem_low = run(
        memory_middle_kernel,
        "memory_far_quarter",
        (shaped(mem_rows, 2 * HD), shaped(mem_rows, RANK)),
        [smem()] + [anywhere()] * 6,
        memory_scratch(1) + memory_sums,
    )(place, mem_far, mem_acc, mem_low, *mem_weights)
    pairs = run(
        lambda *refs: memory_kernel(peers, *refs),
        "memory_pairs",
        shaped(peers, PACK, HD, dtype=bf16),
        [smem()] * 2 + [anywhere()] * 6 + [vmem()],
        memory_scratch(1) + memory_sums + [pltpu.VMEM((blocks, PACK, HD), bf16)],
    )(place, asked, mem_cross, mem_acc, mem_low, *mem_weights, value_up)
    got = lax.all_to_all(pairs, "tm", split_axis=0, concat_axis=0, tiled=True)
    *early, grad, grad_t = run(
        project_early_kernel,
        "project_near_half",
        (
            shaped(tok_rows, query_width),
            shaped(tok_rows, 2 * HD),
            shaped(tok_rows, 2 * RANK),
            shaped(tok_rows, query_width, dtype=bf16),
            shaped(query_width, tok_rows, dtype=bf16),
        ),
        [smem()] + [anywhere()] * 7 + [vmem()] * 2 + [anywhere()],
        project_scratch(2),
    )(place, slab_tokens, tok_near, *weights, tag_t, grad_tags.T, pairs)
    tok_far = after(tok_far, early[2])
    tok_cross = swap(tok_far, 1)
    parts = run(
        project_far_kernel,
        "project_far_half",
        (
            shaped(tok_rows, query_width, dtype=bf16),
            shaped(tok_rows, HD, dtype=bf16),
            shaped(tok_rows, HD, dtype=bf16),
            shaped(2 * RANK, tok_rows, dtype=bf16),
        ),
        [smem()] + [anywhere()] * 10 + [vmem()] * 2,
        project_scratch(2) + project_sums + [pltpu.SemaphoreType.DMA((3,))],
    )(place, tok_far, tok_cross, *weights, *early, query_up, value_up)

    seen = peers * BLK
    total = seen + BLK
    cot, mine, mcot = run(
        lambda *refs: attention_kernel(peers, heads, *refs),
        "span_attention",
        (
            shaped(2 * RANK + tags, tok_rows),
            shaped(2 * RANK + tags + RANK * (query_width + HD) // tok_rows, tok_rows),
            shaped(peers, RANK, BLK),
        ),
        [smem()] + [anywhere()] * 7 + [vmem()] * 3,
        [
            pltpu.VMEM((tok_rows, query_width), bf16),
            pltpu.VMEM((tok_rows, HD), bf16),
            pltpu.VMEM((tok_rows, HD), bf16),
            pltpu.VMEM((2 * RANK, tok_rows), bf16),
            pltpu.VMEM((peers, RANK, BLK), bf16),
            pltpu.VMEM((tok_rows, query_width), bf16),
            pltpu.VMEM((query_width, tok_rows), bf16),
            pltpu.VMEM((seen, HD), bf16),
            pltpu.VMEM((seen, HD), bf16),
            pltpu.VMEM((HD, seen), bf16),
            pltpu.VMEM((HD, seen), bf16),
            pltpu.VMEM((HD, PAIR * BLK), bf16),
            pltpu.VMEM((HD, PAIR * BLK), bf16),
            pltpu.VMEM((PAIR * BLK, BLK), f32),
            pltpu.VMEM((2, PAIR * BLK, total), f32),
            pltpu.VMEM((2, PAIR * BLK, total), f32),
            pltpu.VMEM((heads * PAIR * BLK, total), bf16),
            pltpu.VMEM((2, PAIR * BLK, total), bf16),
            pltpu.VMEM((PAIR * BLK, query_width), bf16),
            pltpu.VMEM((PAIR * BLK, query_width), bf16),
            pltpu.VMEM((HD, seen), f32),
            pltpu.VMEM((RANK, query_width + HD), f32),
            pltpu.SemaphoreType.DMA((3 * peers + 6,)),
        ],
        flops=20 * tok_rows * query_width * total,
        moved=4 * tok_rows * query_width,
        room=60,
    )(boundary, *parts, got, grad, grad_t, query_up, value_up, tag_t)

    back = lax.all_to_all(mcot, "tm", split_axis=0, concat_axis=0, tiled=True)
    cots = [mine] + [swap(cot, d) for d in range(1, 4)]
    own = run(
        lambda *refs: own_kernel(peers, *refs),
        "owned_cotangent",
        shaped(RANK, mem_rows),
        [smem()] + [vmem()],
        [pltpu.VMEM((blocks, RANK, BLK), f32)],
        room=8,
    )(asked, back)
    logits, query_sum, value_part = run(
        first_down_kernel,
        "first_down",
        (shaped(tags, tok_rows), shaped(RANK, width + query_width + HD), shaped(RANK, width)),
        [vmem()] * 5 + [anywhere()],
        flops=4 * RANK * tok_rows * width,
        moved=2 * tok_rows * width,
        room=8,
    )(*cots, slab_tokens, own)
    owns = [own] + [swap(own, d) for d in range(1, 4)]
    value_sum, query_sum = run(
        second_down_kernel,
        "second_down",
        (shaped(RANK, width), shaped(*query_sum.shape)),
        [vmem()] * 8,
        flops=2 * RANK * mem_rows * width,
        moved=2 * mem_rows * width,
        room=8,
    )(*owns, memory, value_part, query_sum, swap(query_sum, 1, "tm"))
    query_sum = (query_sum + swap(query_sum, 2, "tm")).astype(bf16)
    value_sum = (value_sum + swap(value_sum, 1, "tm")).astype(bf16)
    sums = [query_sum, swap(query_sum, 4, "tm"), value_sum] + [swap(value_sum, bit, "tm") for bit in (2, 4, 6)]
    query_down_grad, query_up_grad, value_down_grad, value_up_grad = run(
        finish_kernel,
        "finish_outputs",
        (shaped(RANK, width), shaped(RANK, query_width), shaped(RANK, width), shaped(RANK, HD)),
        [vmem()] * 6,
        room=8,
    )(*sums)
    return (logits.T, query_down_grad, query_up_grad, value_down_grad, value_up_grad)


def solution(mesh):
    in_specs = (
        P("tm", "heads"),
        P("tm", "heads"),
        P(None, "heads"),
        P(None, "heads"),
        P(None, "heads"),
        P(),
        P(None, "heads"),
        P(),
        P(None, "heads"),
        P("heads", None),
        P("tm", None),
        P("tm"),
        P("tm", None),
    )
    out_specs = (
        P("tm", None),
        P(None, "heads"),
        P(None, "heads"),
        P(None, "heads"),
        P(None, "heads"),
    )
    fits = mesh.shape["heads"] == 4 and mesh.shape["tm"] == 8 == TOP * CAP
    local = fast if fits else general
    return jax.shard_map(local, mesh=mesh, in_specs=in_specs, out_specs=out_specs, check_vma=False)
```

```python
import jax
import jax.numpy as jnp
from jax import lax
from jax.experimental import pallas as pl
from jax.experimental.pallas import tpu as pltpu
from jax.sharding import PartitionSpec as P

HD = 128
RANK = 16
TOP = 8
BLK = 128
CAP = 1


HIGHEST = lax.Precision.HIGHEST


def attend(query, all_keys, all_values, split_row, out_grad):
    span_count, row_count, query_width = query.shape
    key_count, kv_width = (all_keys.shape[1], all_keys.shape[2])
    kv_heads = kv_width // HD
    group_size = query_width // kv_width
    score_scale = HD ** (-0.5)
    query_heads = query.reshape(span_count, row_count, kv_heads, group_size, HD)
    key_heads = all_keys.reshape(span_count, key_count, kv_heads, HD)
    value_heads = all_values.reshape(span_count, key_count, kv_heads, HD)
    grad_heads = out_grad.reshape(span_count, row_count, kv_heads, group_size, HD)
    scores = (
        jnp.einsum("crngd,cknd->cngrk", query_heads, key_heads, preferred_element_type=jnp.float32)
        * score_scale
    )
    row_ids = jnp.arange(row_count, dtype=jnp.int32)[:, None]
    col_ids = jnp.arange(BLK, dtype=jnp.int32)[None, :]
    edge_at = split_row[:, None, None]
    local_seen = (col_ids <= row_ids) & ((col_ids >= edge_at) | (row_ids < edge_at))
    visible = jnp.concatenate(
        [jnp.ones((span_count, row_count, key_count - BLK), jnp.bool_), local_seen], axis=2
    )
    scores = jnp.where(visible[:, None, None], scores, -jnp.inf)
    row_max = jnp.max(scores, axis=-1, keepdims=True)
    weights = jnp.exp(scores - row_max)
    probs = weights / jnp.sum(weights, axis=-1, keepdims=True)
    probs_low = probs.astype(jnp.bfloat16)
    attended = jnp.einsum(
        "cngrk,cknd->crngd", probs_low, value_heads, preferred_element_type=jnp.float32
    ).astype(jnp.bfloat16)
    prob_grad = jnp.einsum(
        "crngd,cknd->cngrk", grad_heads, value_heads, preferred_element_type=jnp.float32
    )
    row_dot = jnp.sum(grad_heads.astype(jnp.float32) * attended.astype(jnp.float32), axis=-1)
    row_dot = jnp.transpose(row_dot, (0, 2, 3, 1))[..., None]
    score_grad = (probs * (prob_grad - row_dot) * score_scale).astype(jnp.bfloat16)
    query_grad = jnp.einsum(
        "cngrk,cknd->crngd", score_grad, key_heads, preferred_element_type=jnp.float32
    ).astype(jnp.bfloat16)
    value_grad = jnp.einsum(
        "cngrk,crngd->cknd", probs_low, grad_heads, preferred_element_type=jnp.float32
    )
    return (
        attended.reshape(span_count, row_count, query_width),
        query_grad.reshape(span_count, row_count, query_width),
        value_grad.reshape(span_count, key_count, kv_width),
    )


def choose_slots(needed, places):
    slot_ids = jnp.arange(CAP, dtype=jnp.int32)
    return needed[:, None, :] * (places[:, None, :] == slot_ids[None, :, None]).astype(jnp.int32)


def general(
    slab_tokens,
    memory,
    query_weight,
    key_weight,
    value_weight,
    query_down,
    query_up,
    value_down,
    value_up,
    tag_weight,
    retrieval,
    boundary,
    grad_tags,
):
    tok_rows = slab_tokens.shape[0]
    mem_rows = memory.shape[0]
    query_width = query_weight.shape[1]
    kv_width = key_weight.shape[1]
    span_count = tok_rows // BLK
    block_count = mem_rows // BLK
    pair_weight = jnp.concatenate([key_weight, value_weight], 1)
    adapter_pair = jnp.concatenate([query_down, value_down], 0)
    contract_last = (((1,), (1,)), ((), ()))
    contract_first = (((0,), (0,)), ((), ()))
    token_piece = lax.all_gather(slab_tokens, "heads", axis=1, tiled=True)
    memory_piece = lax.all_gather(memory, "heads", axis=1, tiled=True)
    query_acc = jnp.dot(token_piece, query_weight, preferred_element_type=jnp.float32)
    pair_acc = jnp.dot(token_piece, pair_weight, preferred_element_type=jnp.float32)
    low_acc = lax.dot_general(
        token_piece, adapter_pair, contract_last, preferred_element_type=jnp.float32
    )
    memory_acc = jnp.dot(memory_piece, pair_weight, preferred_element_type=jnp.float32)
    memory_low_acc = lax.dot_general(
        memory_piece, adapter_pair[RANK:], contract_last, preferred_element_type=jnp.float32
    )
    query_acc, pair_acc, low_acc, memory_acc, memory_low_acc = (
        query_acc,
        pair_acc,
        low_acc,
        memory_acc,
        memory_low_acc,
    )
    low_tokens = low_acc.astype(jnp.bfloat16)
    low_query = low_tokens[:, :RANK]
    low_value = low_tokens[:, RANK:]
    queries = (query_acc + jnp.dot(low_query, query_up, preferred_element_type=jnp.float32)).astype(
        jnp.bfloat16
    )
    keys_local = pair_acc[:, :kv_width].astype(jnp.bfloat16)
    values_local = (
        pair_acc[:, kv_width:] + jnp.dot(low_value, value_up, preferred_element_type=jnp.float32)
    ).astype(jnp.bfloat16)
    memory_low = memory_low_acc.astype(jnp.bfloat16)
    memory_pair = (
        jnp.concatenate(
            [
                memory_acc[:, :kv_width],
                memory_acc[:, kv_width:]
                + jnp.dot(memory_low, value_up, preferred_element_type=jnp.float32),
            ],
            1,
        )
        .astype(jnp.bfloat16)
        .reshape(block_count, BLK, 2 * kv_width)
    )
    peer_count = lax.axis_size("tm")
    every_block = jnp.arange(peer_count * block_count, dtype=jnp.int32)
    wanted = (
        jnp.any(retrieval.reshape(-1, 1) == every_block[None, :], axis=0)
        .astype(jnp.int32)
        .reshape(peer_count, block_count)
    )
    places = jnp.cumsum(wanted, axis=1) - wanted
    requested = choose_slots(wanted, places)
    asked_for = lax.all_to_all(requested, "tm", split_axis=0, concat_axis=0, tiled=True)
    rows_needed = retrieval // block_count * CAP + jnp.take(places.reshape(-1), retrieval)
    asked_low = asked_for.astype(jnp.bfloat16)
    outgoing = jnp.einsum(
        "rcm,mbw->rcbw", asked_low, memory_pair, preferred_element_type=jnp.float32
    ).astype(jnp.bfloat16)
    fetched = lax.all_to_all(outgoing, "tm", split_axis=0, concat_axis=0, tiled=True)
    slot_rows = fetched.reshape(peer_count * CAP, BLK, 2 * kv_width)
    picked = jnp.take(slot_rows, rows_needed.reshape(-1), axis=0).reshape(
        span_count, TOP * BLK, 2 * kv_width
    )
    all_keys = jnp.concatenate(
        [picked[..., :kv_width], keys_local.reshape(span_count, BLK, kv_width)], 1
    )
    all_values = jnp.concatenate(
        [picked[..., kv_width:], values_local.reshape(span_count, BLK, kv_width)], 1
    )
    attended_grad = lax.dot_general(
        grad_tags, tag_weight.astype(jnp.float32), contract_last, precision=HIGHEST
    ).astype(jnp.bfloat16)
    attended, query_grad, value_grad = attend(
        queries.reshape(span_count, BLK, query_width),
        all_keys,
        all_values,
        boundary,
        attended_grad.reshape(span_count, BLK, query_width),
    )
    attended = attended.reshape(tok_rows, query_width)
    query_grad = query_grad.reshape(tok_rows, query_width)
    logits_out = lax.psum(
        jnp.dot(attended, tag_weight, preferred_element_type=jnp.float32), "heads"
    )
    local_grad = value_grad[:, TOP * BLK :].reshape(tok_rows, kv_width)
    slot_grads = value_grad[:, : TOP * BLK].reshape(span_count * TOP, BLK * kv_width)
    slot_hits = (
        rows_needed.reshape(-1, 1) == jnp.arange(peer_count * CAP, dtype=jnp.int32)[None, :]
    ).astype(jnp.float32)
    grad_buffer = lax.dot_general(slot_hits, slot_grads, contract_first, precision=HIGHEST).reshape(
        peer_count * CAP, BLK, kv_width
    )
    up_wide = value_up.astype(jnp.float32)
    returned = lax.all_to_all(
        grad_buffer.reshape(peer_count, CAP, BLK, kv_width),
        "tm",
        split_axis=0,
        concat_axis=0,
        tiled=True,
    )
    owned_grad = jnp.einsum(
        "rcm,rcbw->mbw", asked_for.astype(jnp.float32), returned, precision=HIGHEST
    ).reshape(mem_rows, kv_width)
    memory_cot = lax.dot_general(up_wide, owned_grad, contract_last, precision=HIGHEST)
    up_memory = lax.dot_general(
        memory_low.astype(jnp.float32), owned_grad, contract_first, precision=HIGHEST
    )
    query_cot = lax.dot_general(
        query_up, query_grad, contract_last, preferred_element_type=jnp.float32
    )
    value_cot = lax.dot_general(up_wide, local_grad, contract_last, precision=HIGHEST)
    query_cot, value_cot, memory_cot = lax.psum((query_cot, value_cot, memory_cot), "heads")
    query_down_grad = jnp.dot(
        query_cot.astype(jnp.bfloat16), slab_tokens, preferred_element_type=jnp.float32
    )
    value_down_grad = jnp.dot(
        value_cot.astype(jnp.bfloat16), slab_tokens, preferred_element_type=jnp.float32
    ) + jnp.dot(memory_cot.astype(jnp.bfloat16), memory, preferred_element_type=jnp.float32)
    query_up_grad = lax.dot_general(
        low_query, query_grad, contract_first, preferred_element_type=jnp.float32
    )
    value_up_grad = (
        lax.dot_general(
            low_value.astype(jnp.float32), local_grad, contract_first, precision=HIGHEST
        )
        + up_memory
    )
    query_down_grad, query_up_grad, value_down_grad, value_up_grad = lax.psum(
        (query_down_grad, query_up_grad, value_down_grad, value_up_grad), "tm"
    )
    return (logits_out, query_down_grad, query_up_grad, value_down_grad, value_up_grad)


LOG2E = 1.4426950408889634
NT = (((1,), (1,)), ((), ()))
PACK = 2 * BLK + RANK
STRIP = 16
PAIR = 2
MIB = 1024 * 1024
ROOM = 63.5


def dot_nt(a, b, precision=None):
    return lax.dot_general(a, b, NT, precision=precision, preferred_element_type=jnp.float32)


def dot_nn(a, b, precision=None):
    return jnp.dot(a, b, precision=precision, preferred_element_type=jnp.float32)


def piece_rows(place_ref, j, width):
    return pl.ds(pl.multiple_of(lax.bitwise_xor(place_ref[0], j) * width, width), width)


def start_copies(pairs, sems, first=0):
    copies = [pltpu.make_async_copy(src, dst, sems.at[first + n]) for n, (src, dst) in enumerate(pairs)]
    for copy in copies:
        copy.start()
    return copies


def wait_all(copies):
    for copy in copies:
        copy.wait()


def memory_pieces(place_ref, js, xs, hbm, scratch, sems):
    x_s, wk_s, wv_s, down_s = scratch
    width = x_s.shape[2]
    groups = []
    for n, j in enumerate(js):
        here = piece_rows(place_ref, j, width)
        pairs = [
            (xs[n], x_s.at[n]),
            (hbm[0].at[here, :], wk_s.at[n]),
            (hbm[1].at[here, :], wv_s.at[n]),
            (hbm[2].at[:, here], down_s.at[n]),
        ]
        groups.append(start_copies(pairs, sems, 4 * n))
    return groups


def memory_terms(n, scratch):
    x_s, wk_s, wv_s, down_s = scratch
    x = x_s[n]
    return dot_nn(x, jnp.concatenate([wk_s[n], wv_s[n]], 1)), dot_nt(x, down_s[n])


def memory_early_kernel(blocks, place_ref, named_ref, x0, x1, *refs):
    hbm, acc_ref, low_ref, wanted_ref, scratch, sems = refs[:3], refs[3], refs[4], refs[5], refs[6:10], refs[10]
    groups = memory_pieces(place_ref, (0, 1), (x0, x1), hbm, scratch, sems)
    for slot in range(TOP):
        block = named_ref[0, slot]
        wanted_ref[lax.div(block, blocks)] = lax.rem(block, blocks)
    for n in range(2):
        wait_all(groups[n])
        term, low_term = memory_terms(n, scratch)
        if n == 0:
            acc_ref[...] = term
            low_ref[...] = low_term
        else:
            acc_ref[...] += term
            low_ref[...] += low_term


def memory_middle_kernel(place_ref, x2, acc_hbm, low_hbm, *refs):
    hbm, acc_ref, low_ref, scratch, sems = refs[:3], refs[3], refs[4], refs[5:9], refs[9]
    acc_s, low_s, acc_sems = refs[10:13]
    groups = memory_pieces(place_ref, (2,), (x2,), hbm, scratch, sems)
    sums = start_copies([(acc_hbm, acc_s), (low_hbm, low_s)], acc_sems)
    wait_all(groups[0])
    term, low_term = memory_terms(0, scratch)
    wait_all(sums)
    acc_ref[...] = acc_s[...] + term
    low_ref[...] = low_s[...] + low_term


def memory_kernel(peers, place_ref, asked_ref, x3, acc_hbm, low_hbm, *refs):
    hbm, up_ref, out_ref = refs[:3], refs[3], refs[4]
    scratch, sems, acc_s, low_s, acc_sems, pair_ref = refs[5:9], refs[9], refs[10], refs[11], refs[12], refs[13]
    groups = memory_pieces(place_ref, (3,), (x3,), hbm, scratch, sems)
    sums = start_copies([(acc_hbm, acc_s), (low_hbm, low_s)], acc_sems)
    wait_all(groups[0])
    term, low_term = memory_terms(0, scratch)
    wait_all(sums)
    acc = acc_s[...] + term
    low = low_s[...] + low_term
    values = (acc[:, HD:] + dot_nn(low.astype(jnp.bfloat16), up_ref[...])).astype(jnp.bfloat16)
    keys = acc[:, :HD].astype(jnp.bfloat16)
    low_t = jnp.transpose(low).astype(jnp.bfloat16)
    for b in range(acc.shape[0] // BLK):
        at = slice(b * BLK, (b + 1) * BLK)
        pair_ref[b, 0:BLK, :] = keys[at]
        pair_ref[b, BLK : 2 * BLK, :] = values[at]
        pair_ref[b, 2 * BLK : PACK, :] = low_t[:, at]
    for r in range(peers):
        out_ref[r] = pair_ref[asked_ref[r]]


WQ_CUTS = 4


def project_pieces(place_ref, js, xs, hbm, scratch, sems):
    wq_hbm, wk_hbm, wv_hbm, qd_hbm, vd_hbm = hbm
    x_s, wq_s, wk_s, wv_s, qd_s, vd_s = scratch
    width = x_s.shape[2]
    part = width // WQ_CUTS
    groups = []
    for n, j in enumerate(js):
        here = piece_rows(place_ref, j, width)
        start = lax.bitwise_xor(place_ref[0], j) * width
        pairs = [(xs[n], x_s.at[n])]
        for m in range(WQ_CUTS):
            rows = pl.ds(pl.multiple_of(start + m * part, part), part)
            pairs.append((wq_hbm.at[rows, :], wq_s.at[n, pl.ds(m * part, part), :]))
        pairs += [
            (wk_hbm.at[here, :], wk_s.at[n]),
            (wv_hbm.at[here, :], wv_s.at[n]),
            (qd_hbm.at[:, here], qd_s.at[n]),
            (vd_hbm.at[:, here], vd_s.at[n]),
        ]
        groups.append(start_copies(pairs, sems, len(pairs) * n))
    return groups


def project_terms(n, scratch):
    x_s, wq_s, wk_s, wv_s, qd_s, vd_s = scratch
    x = x_s[n]
    return (
        dot_nn(x, wq_s[n]),
        dot_nn(x, jnp.concatenate([wk_s[n], wv_s[n]], 1)),
        dot_nt(x, jnp.concatenate([qd_s[n], vd_s[n]], 0)),
    )


def project_early_kernel(place_ref, x0, x1, *refs):
    hbm, (tag_ref, tags_t_ref), outs, (grad_ref, grad_t_ref) = refs[:5], refs[5:7], refs[8:11], refs[11:13]
    scratch, sems = refs[13:19], refs[19]
    groups = project_pieces(place_ref, (0, 1), (x0, x1), hbm, scratch, sems)
    first = (((0,), (0,)), ((), ()))
    tag = tag_ref[...].astype(jnp.float32)
    tags_t = tags_t_ref[...]
    f32 = jnp.float32
    grad_ref[...] = lax.dot_general(
        tags_t, tag, first, precision=HIGHEST, preferred_element_type=f32
    ).astype(jnp.bfloat16)
    grad_t_ref[...] = lax.dot_general(
        tag, tags_t, first, precision=HIGHEST, preferred_element_type=f32
    ).astype(jnp.bfloat16)
    for n in range(2):
        wait_all(groups[n])
        for ref, term in zip(outs, project_terms(n, scratch)):
            if n == 0:
                ref[...] = term
            else:
                ref[...] += term


def project_middle_kernel(place_ref, x3, *refs):
    hbm, early, outs, scratch, sems = refs[:5], refs[5:8], refs[8:11], refs[11:17], refs[17]
    sum_refs, sum_sems = refs[18:21], refs[21]
    groups = project_pieces(place_ref, (3,), (x3,), hbm, scratch, sems)
    loads = start_copies(list(zip(early, sum_refs)), sum_sems)
    wait_all(groups[0])
    terms = project_terms(0, scratch)
    wait_all(loads)
    for out, ref, term in zip(outs, sum_refs, terms):
        out[...] = ref[...] + term


def attention_kernel(peers, heads, place_ref, bound_ref, x2, *refs):
    hbm, early, got, grad_hbm, grad_t_hbm = refs[:5], refs[5:8], refs[8], refs[9], refs[10]
    qup_ref, vup_ref, tag_ref, cot_ref, mine_ref, mcot_ref = refs[11:17]
    scratch, sems, sum_refs = refs[17:23], refs[23], refs[24:27]
    (q_s, k_own, v_own, low_s, low_m_s, grad_ref, grad_t_ref, k_all, v_all, kt_all, vt_all, kt_own, vt_own, bias_s, s_s, dp_s,
     p_s, ds_s, att_s, dq_s, dv_s, up_ref, more_sems) = refs[27:]
    seen = peers * BLK
    groups = project_pieces(place_ref, (2,), (x2,), hbm, scratch, sems)
    pairs = list(zip(early, sum_refs))
    for b in range(peers):
        at = slice(b * BLK, (b + 1) * BLK)
        pairs.append((got.at[b, pl.ds(0, BLK), :], k_all.at[at, :]))
        pairs.append((got.at[b, pl.ds(BLK, BLK), :], v_all.at[at, :]))
        pairs.append((got.at[b, pl.ds(2 * BLK, RANK), :], low_m_s.at[b]))
    pairs += [(grad_hbm, grad_ref), (grad_t_hbm, grad_t_ref)]
    copies = start_copies(pairs, more_sems)
    wait_all(groups[0])
    terms = project_terms(0, scratch)
    wait_all(copies[:3])
    q_acc, kv_acc, low_acc = [ref[...] + term for ref, term in zip(sum_refs, terms)]
    low = low_acc.astype(jnp.bfloat16)
    q_s[...] = (q_acc + dot_nn(low[:, :RANK], qup_ref[...])).astype(jnp.bfloat16)
    k_own[...] = kv_acc[:, :HD].astype(jnp.bfloat16)
    v_own[...] = (kv_acc[:, HD:] + dot_nn(low[:, RANK:], vup_ref[...])).astype(jnp.bfloat16)
    low_s[...] = jnp.transpose(low_acc).astype(jnp.bfloat16)
    wait_all(copies[3 : 3 + 3 * peers])
    for b in range(peers):
        at = slice(b * BLK, (b + 1) * BLK)
        kt_all[:, at] = jnp.transpose(k_all[at, :])
        vt_all[:, at] = jnp.transpose(v_all[at, :])
    wait_all(copies[3 + 3 * peers : -1])
    dv_s[...] = jnp.zeros_like(dv_s)
    up_ref[...] = jnp.zeros_like(up_ref)
    scale = HD ** (-0.5)
    up_wide = vup_ref[...].astype(jnp.float32)
    query_width = heads * HD

    def pair_step(c, carry):
        base = c * (PAIR * BLK)
        rows = pl.ds(pl.multiple_of(base, PAIR * BLK), PAIR * BLK)
        own_rows = [pl.ds(pl.multiple_of(base + b * BLK, BLK), BLK) for b in range(PAIR)]
        row_ids = lax.broadcasted_iota(jnp.int32, (BLK, BLK), 0)
        col_ids = lax.broadcasted_iota(jnp.int32, (BLK, BLK), 1)
        for b in range(PAIR):
            kt_own[:, b * BLK : (b + 1) * BLK] = jnp.transpose(k_own[own_rows[b], :])
            vt_own[:, b * BLK : (b + 1) * BLK] = jnp.transpose(v_own[own_rows[b], :])
            edge = bound_ref[c * PAIR + b]
            visible = (col_ids <= row_ids) & ((col_ids >= edge) | (row_ids < edge))
            bias_s[b * BLK : (b + 1) * BLK, :] = jnp.where(visible, 0.0, -jnp.inf)

        def head_cols(h):
            return slice(h * HD, (h + 1) * HD)

        def times_keys(out_ref, left_ref, h, all_t, own_t):
            out_ref[:, :seen] = dot_nn(left_ref[rows, head_cols(h)], all_t[...])
            for b in range(PAIR):
                at = slice(b * BLK, (b + 1) * BLK)
                out_ref[at, seen:] = dot_nn(left_ref[own_rows[b], head_cols(h)], own_t[:, at])

        def over_keys(left_ref, first, all_ref, own_ref):
            whole = dot_nn(left_ref[first : first + PAIR * BLK, :seen], all_ref[...])
            mine = [
                dot_nn(left_ref[first + b * BLK : first + (b + 1) * BLK, seen:], own_ref[own_rows[b], :])
                for b in range(PAIR)
            ]
            return (whole + jnp.concatenate(mine, 0)).astype(jnp.bfloat16)

        def scores(h):
            times_keys(s_s.at[h % 2], q_s, h, kt_all, kt_own)

        def prob_grads(h):
            times_keys(dp_s.at[h % 2], grad_ref, h, vt_all, vt_own)

        def strips(h):
            for r in range(0, PAIR * BLK, STRIP):
                at = slice(r, r + STRIP)
                s = s_s[h % 2, at, :]
                s = jnp.concatenate([s[:, :seen], s[:, seen:] + bias_s[at, :]], 1) * (scale * LOG2E)
                w = jnp.exp2(s - jnp.max(s, axis=1, keepdims=True))
                probs = w * (1.0 / jnp.sum(w, axis=1, keepdims=True))
                probs_low = probs.astype(jnp.bfloat16)
                first = h * PAIR * BLK + r
                p_s[first : first + STRIP, :] = probs_low
                dp = dp_s[h % 2, at, :]
                dot = jnp.sum(probs_low.astype(jnp.float32) * dp, axis=1, keepdims=True)
                ds_s[h % 2, at, :] = (probs * ((dp - dot) * scale)).astype(jnp.bfloat16)

        def finish_head(h):
            att_s[:, head_cols(h)] = over_keys(p_s, h * PAIR * BLK, v_all, v_own)
            dq_s[:, head_cols(h)] = over_keys(ds_s.at[h % 2], 0, k_all, k_own)

        scores(0)
        prob_grads(0)
        for h in range(heads + 1):
            if h + 1 < heads:
                scores(h + 1)
                prob_grads(h + 1)
            if h < heads:
                strips(h)
            if h > 0:
                finish_head(h - 1)
        pl.when(c == 0)(copies[-1].wait)
        g_t = jnp.concatenate([grad_t_ref[h * HD : (h + 1) * HD, rows] for h in range(heads)], 1)
        dv_s[...] += dot_nn(g_t, p_s[:, :seen])
        dv_own = []
        for b in range(PAIR):
            g_b = jnp.concatenate([grad_t_ref[h * HD : (h + 1) * HD, own_rows[b]] for h in range(heads)], 1)
            starts = [(h * PAIR + b) * BLK for h in range(heads)]
            p_b = jnp.concatenate([p_s[n : n + BLK, seen:] for n in starts], 0)
            dv_own.append(dot_nn(g_b, p_b))
        dv_own = jnp.concatenate(dv_own, 1)
        dq = dq_s[...]
        cot_ref[0:RANK, rows] = dot_nt(qup_ref[...], dq)
        cot_ref[RANK : 2 * RANK, rows] = dot_nn(up_wide, dv_own, HIGHEST)
        cot_ref[2 * RANK :, rows] = dot_nt(tag_ref[...], att_s[...])
        up_ref[:, :query_width] += dot_nn(low_s[0:RANK, rows], dq)
        up_ref[:, query_width:] += dot_nt(low_s[RANK:, rows].astype(jnp.float32), dv_own, HIGHEST)
        return carry

    lax.fori_loop(0, q_s.shape[0] // (PAIR * BLK), pair_step, 0)
    dv = dv_s[...]
    mcot = dot_nn(up_wide, dv, HIGHEST)
    low_m = jnp.concatenate([low_m_s[b] for b in range(peers)], 1).astype(jnp.float32)
    up_ref[:, query_width:] += dot_nt(low_m, dv, HIGHEST)
    for b in range(peers):
        mcot_ref[b] = mcot[:, b * BLK : (b + 1) * BLK]
    at, wide = cot_ref.shape
    mine_ref[:at, :] = cot_ref[...]
    for n in range(0, up_ref.shape[1], wide):
        mine_ref[at : at + RANK, :] = up_ref[:, n : n + wide]
        at += RANK


def own_kernel(peers, asked_ref, back_ref, out_ref, sum_s):
    sum_s[...] = jnp.zeros_like(sum_s)
    for r in range(peers):
        block = asked_ref[r]
        sum_s[block] = sum_s[block] + back_ref[r]
    out_ref[...] = jnp.concatenate([sum_s[m] for m in range(sum_s.shape[0])], 1)


def first_down_kernel(mine_ref, c1, c2, c3, slab_ref, dep_ref, logit_ref, query_ref, value_ref):
    own, wide = c1.shape
    cot = (mine_ref[:own, :] + c1[...]) + (c2[...] + c3[...])
    logit_ref[...] = cot[2 * RANK :]
    both = dot_nn(cot[: 2 * RANK].astype(jnp.bfloat16), slab_ref[...])
    width = both.shape[1]
    query_ref[:, :width] = both[:RANK]
    for n, at in enumerate(range(own, mine_ref.shape[0], RANK)):
        query_ref[:, width + n * wide : width + (n + 1) * wide] = mine_ref[at : at + RANK, :]
    value_ref[...] = both[RANK:]


def second_down_kernel(c0, c1, c2, c3, memory_ref, value_ref, q0, q1, out_ref, query_ref):
    query_ref[...] = q0[...] + q1[...]
    cot = (c0[...] + c1[...]) + (c2[...] + c3[...])
    out_ref[...] = value_ref[...] + dot_nn(cot.astype(jnp.bfloat16), memory_ref[...])


def finish_kernel(*refs):
    parts = [ref[...].astype(jnp.float32) for ref in refs[:6]]
    query = parts[0] + parts[1]
    value = (parts[2] + parts[3]) + (parts[4] + parts[5])
    query_down_ref, query_up_ref, value_down_ref, value_up_ref = refs[6:]
    value_down_ref[...] = value
    at = 0
    for out_ref in (query_down_ref, query_up_ref, value_up_ref):
        out_ref[...] = query[:, at : at + out_ref.shape[1]]
        at += out_ref.shape[1]


def swap(x, bit, axis="heads"):
    return lax.ppermute(x, axis, [(i, i ^ bit) for i in range(lax.axis_size(axis))])


def after(x, *deps):
    return pl.pallas_call(
        lambda *refs: None,
        out_shape=jax.ShapeDtypeStruct(x.shape, x.dtype),
        in_specs=[anywhere()] * (1 + len(deps)),
        out_specs=anywhere(),
        input_output_aliases={0: 0},
        name="in_order",
    )(x, *deps)


def anywhere():
    return pl.BlockSpec(memory_space=pl.ANY)


def smem():
    return pl.BlockSpec(memory_space=pltpu.SMEM)


def vmem():
    return pl.BlockSpec(memory_space=pltpu.VMEM)


def shaped(*shape, dtype=jnp.float32):
    return jax.ShapeDtypeStruct(shape, dtype)


def run(body, name, out_shape, in_specs, scratch=(), flops=0, moved=0, room=ROOM, out_specs=None):
    many = isinstance(out_shape, (tuple, list))
    return pl.pallas_call(
        body,
        out_shape=out_shape,
        in_specs=in_specs,
        out_specs=out_specs or (tuple(vmem() for _ in out_shape) if many else vmem()),
        scratch_shapes=list(scratch),
        compiler_params=pltpu.CompilerParams(vmem_limit_bytes=int(room * MIB)),
        cost_estimate=pl.CostEstimate(flops=flops, bytes_accessed=moved, transcendentals=0),
        name=name,
    )


def fast(
    slab_tokens,
    memory,
    query_weight,
    key_weight,
    value_weight,
    query_down,
    query_up,
    value_down,
    value_up,
    tag_weight,
    retrieval,
    boundary,
    grad_tags,
):
    tok_rows, width = slab_tokens.shape
    mem_rows = memory.shape[0]
    query_width = query_weight.shape[1]
    heads = query_width // HD
    spans = tok_rows // BLK
    blocks = mem_rows // BLK
    peers = lax.axis_size("tm")
    f32 = jnp.float32
    bf16 = jnp.bfloat16

    def memory_scratch(count):
        return [
            pltpu.VMEM((count, mem_rows, width), bf16),
            pltpu.VMEM((count, width, HD), bf16),
            pltpu.VMEM((count, width, HD), bf16),
            pltpu.VMEM((count, RANK, width), bf16),
            pltpu.SemaphoreType.DMA((4 * count,)),
        ]

    def project_scratch(count):
        return [
            pltpu.VMEM((count, tok_rows, width), bf16),
            pltpu.VMEM((count, width, query_width), bf16),
            pltpu.VMEM((count, width, HD), bf16),
            pltpu.VMEM((count, width, HD), bf16),
            pltpu.VMEM((count, RANK, width), bf16),
            pltpu.VMEM((count, RANK, width), bf16),
            pltpu.SemaphoreType.DMA((count * (WQ_CUTS + 5),)),
        ]

    memory_sums = [
        pltpu.VMEM((mem_rows, 2 * HD), f32),
        pltpu.VMEM((mem_rows, RANK), f32),
        pltpu.SemaphoreType.DMA((2,)),
    ]
    project_sums = [
        pltpu.VMEM((tok_rows, query_width), f32),
        pltpu.VMEM((tok_rows, 2 * HD), f32),
        pltpu.VMEM((tok_rows, 2 * RANK), f32),
    ]

    place = lax.axis_index("heads").astype(jnp.int32).reshape(1)
    tag_t = tag_weight.T
    tags = tag_t.shape[0]
    mem_far = swap(memory, 2)
    mem_near = swap(memory, 1)
    tok_near = swap(slab_tokens, 1)
    tok_far = swap(tok_near, 2)
    mem_acc, mem_low, wanted = run(
        lambda *refs: memory_early_kernel(blocks, *refs),
        "memory_near_half",
        (shaped(mem_rows, 2 * HD), shaped(mem_rows, RANK), shaped(peers, dtype=jnp.int32)),
        [smem()] * 2 + [anywhere()] * 5,
        memory_scratch(2),
        out_specs=(vmem(), vmem(), smem()),
    )(place, retrieval, memory, mem_near, key_weight, value_weight, value_down)
    asked = lax.all_to_all(wanted, "tm", split_axis=0, concat_axis=0, tiled=True)
    weights = (query_weight, key_weight, value_weight, query_down, value_down)
    mem_far = after(mem_far, asked)
    mem_cross = swap(mem_far, 1)
    mem_weights = (key_weight, value_weight, value_down)
    mem_acc, mem_low = run(
        memory_middle_kernel,
        "memory_far_quarter",
        (shaped(mem_rows, 2 * HD), shaped(mem_rows, RANK)),
        [smem()] + [anywhere()] * 6,
        memory_scratch(1) + memory_sums,
    )(place, mem_far, mem_acc, mem_low, *mem_weights)
    pairs = run(
        lambda *refs: memory_kernel(peers, *refs),
        "memory_pairs",
        shaped(peers, PACK, HD, dtype=bf16),
        [smem()] * 2 + [anywhere()] * 6 + [vmem()],
        memory_scratch(1) + memory_sums + [pltpu.VMEM((blocks, PACK, HD), bf16)],
    )(place, asked, mem_cross, mem_acc, mem_low, *mem_weights, value_up)
    got = lax.all_to_all(pairs, "tm", split_axis=0, concat_axis=0, tiled=True)
    *early, grad, grad_t = run(
        project_early_kernel,
        "project_near_half",
        (
            shaped(tok_rows, query_width),
            shaped(tok_rows, 2 * HD),
            shaped(tok_rows, 2 * RANK),
            shaped(tok_rows, query_width, dtype=bf16),
            shaped(query_width, tok_rows, dtype=bf16),
        ),
        [smem()] + [anywhere()] * 7 + [vmem()] * 2 + [anywhere()],
        project_scratch(2),
    )(place, slab_tokens, tok_near, *weights, tag_t, grad_tags.T, pairs)
    tok_far = after(tok_far, early[2])
    tok_cross = swap(tok_far, 1)
    early = run(
        project_middle_kernel,
        "project_far_quarter",
        (shaped(tok_rows, query_width), shaped(tok_rows, 2 * HD), shaped(tok_rows, 2 * RANK)),
        [smem()] + [anywhere()] * 9,
        project_scratch(1) + project_sums + [pltpu.SemaphoreType.DMA((3,))],
    )(place, tok_far, *weights, *early)

    seen = peers * BLK
    total = seen + BLK
    cot, mine, mcot = run(
        lambda *refs: attention_kernel(peers, heads, *refs),
        "span_attention",
        (
            shaped(2 * RANK + tags, tok_rows),
            shaped(2 * RANK + tags + RANK * (query_width + HD) // tok_rows, tok_rows),
            shaped(peers, RANK, BLK),
        ),
        [smem()] * 2 + [anywhere()] * 12 + [vmem()] * 3,
        project_scratch(1)
        + project_sums
        + [
            pltpu.VMEM((tok_rows, query_width), bf16),
            pltpu.VMEM((tok_rows, HD), bf16),
            pltpu.VMEM((tok_rows, HD), bf16),
            pltpu.VMEM((2 * RANK, tok_rows), bf16),
            pltpu.VMEM((peers, RANK, BLK), bf16),
            pltpu.VMEM((tok_rows, query_width), bf16),
            pltpu.VMEM((query_width, tok_rows), bf16),
            pltpu.VMEM((seen, HD), bf16),
            pltpu.VMEM((seen, HD), bf16),
            pltpu.VMEM((HD, seen), bf16),
            pltpu.VMEM((HD, seen), bf16),
            pltpu.VMEM((HD, PAIR * BLK), bf16),
            pltpu.VMEM((HD, PAIR * BLK), bf16),
            pltpu.VMEM((PAIR * BLK, BLK), f32),
            pltpu.VMEM((2, PAIR * BLK, total), f32),
            pltpu.VMEM((2, PAIR * BLK, total), f32),
            pltpu.VMEM((heads * PAIR * BLK, total), bf16),
            pltpu.VMEM((2, PAIR * BLK, total), bf16),
            pltpu.VMEM((PAIR * BLK, query_width), bf16),
            pltpu.VMEM((PAIR * BLK, query_width), bf16),
            pltpu.VMEM((HD, seen), f32),
            pltpu.VMEM((RANK, query_width + HD), f32),
            pltpu.SemaphoreType.DMA((3 * peers + 5,)),
        ],
        flops=20 * tok_rows * query_width * total,
        moved=4 * tok_rows * query_width,
        room=60,
    )(place, boundary, tok_cross, *weights, *early, got, grad, grad_t, query_up, value_up, tag_t)

    back = lax.all_to_all(mcot, "tm", split_axis=0, concat_axis=0, tiled=True)
    cots = [mine] + [swap(cot, d) for d in range(1, 4)]
    own = run(
        lambda *refs: own_kernel(peers, *refs),
        "owned_cotangent",
        shaped(RANK, mem_rows),
        [smem()] + [vmem()],
        [pltpu.VMEM((blocks, RANK, BLK), f32)],
        room=8,
    )(asked, back)
    logits, query_sum, value_part = run(
        first_down_kernel,
        "first_down",
        (shaped(tags, tok_rows), shaped(RANK, width + query_width + HD), shaped(RANK, width)),
        [vmem()] * 5 + [anywhere()],
        flops=4 * RANK * tok_rows * width,
        moved=2 * tok_rows * width,
        room=8,
    )(*cots, slab_tokens, own)
    owns = [own] + [swap(own, d) for d in range(1, 4)]
    value_sum, query_sum = run(
        second_down_kernel,
        "second_down",
        (shaped(RANK, width), shaped(*query_sum.shape)),
        [vmem()] * 8,
        flops=2 * RANK * mem_rows * width,
        moved=2 * mem_rows * width,
        room=8,
    )(*owns, memory, value_part, query_sum, swap(query_sum, 1, "tm"))
    query_sum = (query_sum + swap(query_sum, 2, "tm")).astype(bf16)
    value_sum = (value_sum + swap(value_sum, 1, "tm")).astype(bf16)
    sums = [query_sum, swap(query_sum, 4, "tm"), value_sum] + [swap(value_sum, bit, "tm") for bit in (2, 4, 6)]
    query_down_grad, query_up_grad, value_down_grad, value_up_grad = run(
        finish_kernel,
        "finish_outputs",
        (shaped(RANK, width), shaped(RANK, query_width), shaped(RANK, width), shaped(RANK, HD)),
        [vmem()] * 6,
        room=8,
    )(*sums)
    return (logits.T, query_down_grad, query_up_grad, value_down_grad, value_up_grad)


def solution(mesh):
    in_specs = (
        P("tm", "heads"),
        P("tm", "heads"),
        P(None, "heads"),
        P(None, "heads"),
        P(None, "heads"),
        P(),
        P(None, "heads"),
        P(),
        P(None, "heads"),
        P("heads", None),
        P("tm", None),
        P("tm"),
        P("tm", None),
    )
    out_specs = (
        P("tm", None),
        P(None, "heads"),
        P(None, "heads"),
        P(None, "heads"),
        P(None, "heads"),
    )
    fits = mesh.shape["heads"] == 4 and mesh.shape["tm"] == 8 == TOP * CAP
    local = fast if fits else general
    return jax.shard_map(local, mesh=mesh, in_specs=in_specs, out_specs=out_specs, check_vma=False)
```

```python
import jax
import jax.numpy as jnp
from jax import lax
from jax.experimental import pallas as pl
from jax.experimental.pallas import tpu as pltpu
from jax.sharding import PartitionSpec as P

HD = 128
RANK = 16
TOP = 8
BLK = 128
CAP = 1


HIGHEST = lax.Precision.HIGHEST


def attend(query, all_keys, all_values, split_row, out_grad):
    span_count, row_count, query_width = query.shape
    key_count, kv_width = (all_keys.shape[1], all_keys.shape[2])
    kv_heads = kv_width // HD
    group_size = query_width // kv_width
    score_scale = HD ** (-0.5)
    query_heads = query.reshape(span_count, row_count, kv_heads, group_size, HD)
    key_heads = all_keys.reshape(span_count, key_count, kv_heads, HD)
    value_heads = all_values.reshape(span_count, key_count, kv_heads, HD)
    grad_heads = out_grad.reshape(span_count, row_count, kv_heads, group_size, HD)
    scores = (
        jnp.einsum("crngd,cknd->cngrk", query_heads, key_heads, preferred_element_type=jnp.float32)
        * score_scale
    )
    row_ids = jnp.arange(row_count, dtype=jnp.int32)[:, None]
    col_ids = jnp.arange(BLK, dtype=jnp.int32)[None, :]
    edge_at = split_row[:, None, None]
    local_seen = (col_ids <= row_ids) & ((col_ids >= edge_at) | (row_ids < edge_at))
    visible = jnp.concatenate(
        [jnp.ones((span_count, row_count, key_count - BLK), jnp.bool_), local_seen], axis=2
    )
    scores = jnp.where(visible[:, None, None], scores, -jnp.inf)
    row_max = jnp.max(scores, axis=-1, keepdims=True)
    weights = jnp.exp(scores - row_max)
    probs = weights / jnp.sum(weights, axis=-1, keepdims=True)
    probs_low = probs.astype(jnp.bfloat16)
    attended = jnp.einsum(
        "cngrk,cknd->crngd", probs_low, value_heads, preferred_element_type=jnp.float32
    ).astype(jnp.bfloat16)
    prob_grad = jnp.einsum(
        "crngd,cknd->cngrk", grad_heads, value_heads, preferred_element_type=jnp.float32
    )
    row_dot = jnp.sum(grad_heads.astype(jnp.float32) * attended.astype(jnp.float32), axis=-1)
    row_dot = jnp.transpose(row_dot, (0, 2, 3, 1))[..., None]
    score_grad = (probs * (prob_grad - row_dot) * score_scale).astype(jnp.bfloat16)
    query_grad = jnp.einsum(
        "cngrk,cknd->crngd", score_grad, key_heads, preferred_element_type=jnp.float32
    ).astype(jnp.bfloat16)
    value_grad = jnp.einsum(
        "cngrk,crngd->cknd", probs_low, grad_heads, preferred_element_type=jnp.float32
    )
    return (
        attended.reshape(span_count, row_count, query_width),
        query_grad.reshape(span_count, row_count, query_width),
        value_grad.reshape(span_count, key_count, kv_width),
    )


def choose_slots(needed, places):
    slot_ids = jnp.arange(CAP, dtype=jnp.int32)
    return needed[:, None, :] * (places[:, None, :] == slot_ids[None, :, None]).astype(jnp.int32)


def general(
    slab_tokens,
    memory,
    query_weight,
    key_weight,
    value_weight,
    query_down,
    query_up,
    value_down,
    value_up,
    tag_weight,
    retrieval,
    boundary,
    grad_tags,
):
    tok_rows = slab_tokens.shape[0]
    mem_rows = memory.shape[0]
    query_width = query_weight.shape[1]
    kv_width = key_weight.shape[1]
    span_count = tok_rows // BLK
    block_count = mem_rows // BLK
    pair_weight = jnp.concatenate([key_weight, value_weight], 1)
    adapter_pair = jnp.concatenate([query_down, value_down], 0)
    contract_last = (((1,), (1,)), ((), ()))
    contract_first = (((0,), (0,)), ((), ()))
    token_piece = lax.all_gather(slab_tokens, "heads", axis=1, tiled=True)
    memory_piece = lax.all_gather(memory, "heads", axis=1, tiled=True)
    query_acc = jnp.dot(token_piece, query_weight, preferred_element_type=jnp.float32)
    pair_acc = jnp.dot(token_piece, pair_weight, preferred_element_type=jnp.float32)
    low_acc = lax.dot_general(
        token_piece, adapter_pair, contract_last, preferred_element_type=jnp.float32
    )
    memory_acc = jnp.dot(memory_piece, pair_weight, preferred_element_type=jnp.float32)
    memory_low_acc = lax.dot_general(
        memory_piece, adapter_pair[RANK:], contract_last, preferred_element_type=jnp.float32
    )
    query_acc, pair_acc, low_acc, memory_acc, memory_low_acc = (
        query_acc,
        pair_acc,
        low_acc,
        memory_acc,
        memory_low_acc,
    )
    low_tokens = low_acc.astype(jnp.bfloat16)
    low_query = low_tokens[:, :RANK]
    low_value = low_tokens[:, RANK:]
    queries = (query_acc + jnp.dot(low_query, query_up, preferred_element_type=jnp.float32)).astype(
        jnp.bfloat16
    )
    keys_local = pair_acc[:, :kv_width].astype(jnp.bfloat16)
    values_local = (
        pair_acc[:, kv_width:] + jnp.dot(low_value, value_up, preferred_element_type=jnp.float32)
    ).astype(jnp.bfloat16)
    memory_low = memory_low_acc.astype(jnp.bfloat16)
    memory_pair = (
        jnp.concatenate(
            [
                memory_acc[:, :kv_width],
                memory_acc[:, kv_width:]
                + jnp.dot(memory_low, value_up, preferred_element_type=jnp.float32),
            ],
            1,
        )
        .astype(jnp.bfloat16)
        .reshape(block_count, BLK, 2 * kv_width)
    )
    peer_count = lax.axis_size("tm")
    every_block = jnp.arange(peer_count * block_count, dtype=jnp.int32)
    wanted = (
        jnp.any(retrieval.reshape(-1, 1) == every_block[None, :], axis=0)
        .astype(jnp.int32)
        .reshape(peer_count, block_count)
    )
    places = jnp.cumsum(wanted, axis=1) - wanted
    requested = choose_slots(wanted, places)
    asked_for = lax.all_to_all(requested, "tm", split_axis=0, concat_axis=0, tiled=True)
    rows_needed = retrieval // block_count * CAP + jnp.take(places.reshape(-1), retrieval)
    asked_low = asked_for.astype(jnp.bfloat16)
    outgoing = jnp.einsum(
        "rcm,mbw->rcbw", asked_low, memory_pair, preferred_element_type=jnp.float32
    ).astype(jnp.bfloat16)
    fetched = lax.all_to_all(outgoing, "tm", split_axis=0, concat_axis=0, tiled=True)
    slot_rows = fetched.reshape(peer_count * CAP, BLK, 2 * kv_width)
    picked = jnp.take(slot_rows, rows_needed.reshape(-1), axis=0).reshape(
        span_count, TOP * BLK, 2 * kv_width
    )
    all_keys = jnp.concatenate(
        [picked[..., :kv_width], keys_local.reshape(span_count, BLK, kv_width)], 1
    )
    all_values = jnp.concatenate(
        [picked[..., kv_width:], values_local.reshape(span_count, BLK, kv_width)], 1
    )
    attended_grad = lax.dot_general(
        grad_tags, tag_weight.astype(jnp.float32), contract_last, precision=HIGHEST
    ).astype(jnp.bfloat16)
    attended, query_grad, value_grad = attend(
        queries.reshape(span_count, BLK, query_width),
        all_keys,
        all_values,
        boundary,
        attended_grad.reshape(span_count, BLK, query_width),
    )
    attended = attended.reshape(tok_rows, query_width)
    query_grad = query_grad.reshape(tok_rows, query_width)
    logits_out = lax.psum(
        jnp.dot(attended, tag_weight, preferred_element_type=jnp.float32), "heads"
    )
    local_grad = value_grad[:, TOP * BLK :].reshape(tok_rows, kv_width)
    slot_grads = value_grad[:, : TOP * BLK].reshape(span_count * TOP, BLK * kv_width)
    slot_hits = (
        rows_needed.reshape(-1, 1) == jnp.arange(peer_count * CAP, dtype=jnp.int32)[None, :]
    ).astype(jnp.float32)
    grad_buffer = lax.dot_general(slot_hits, slot_grads, contract_first, precision=HIGHEST).reshape(
        peer_count * CAP, BLK, kv_width
    )
    up_wide = value_up.astype(jnp.float32)
    returned = lax.all_to_all(
        grad_buffer.reshape(peer_count, CAP, BLK, kv_width),
        "tm",
        split_axis=0,
        concat_axis=0,
        tiled=True,
    )
    owned_grad = jnp.einsum(
        "rcm,rcbw->mbw", asked_for.astype(jnp.float32), returned, precision=HIGHEST
    ).reshape(mem_rows, kv_width)
    memory_cot = lax.dot_general(up_wide, owned_grad, contract_last, precision=HIGHEST)
    up_memory = lax.dot_general(
        memory_low.astype(jnp.float32), owned_grad, contract_first, precision=HIGHEST
    )
    query_cot = lax.dot_general(
        query_up, query_grad, contract_last, preferred_element_type=jnp.float32
    )
    value_cot = lax.dot_general(up_wide, local_grad, contract_last, precision=HIGHEST)
    query_cot, value_cot, memory_cot = lax.psum((query_cot, value_cot, memory_cot), "heads")
    query_down_grad = jnp.dot(
        query_cot.astype(jnp.bfloat16), slab_tokens, preferred_element_type=jnp.float32
    )
    value_down_grad = jnp.dot(
        value_cot.astype(jnp.bfloat16), slab_tokens, preferred_element_type=jnp.float32
    ) + jnp.dot(memory_cot.astype(jnp.bfloat16), memory, preferred_element_type=jnp.float32)
    query_up_grad = lax.dot_general(
        low_query, query_grad, contract_first, preferred_element_type=jnp.float32
    )
    value_up_grad = (
        lax.dot_general(
            low_value.astype(jnp.float32), local_grad, contract_first, precision=HIGHEST
        )
        + up_memory
    )
    query_down_grad, query_up_grad, value_down_grad, value_up_grad = lax.psum(
        (query_down_grad, query_up_grad, value_down_grad, value_up_grad), "tm"
    )
    return (logits_out, query_down_grad, query_up_grad, value_down_grad, value_up_grad)


LOG2E = 1.4426950408889634
NT = (((1,), (1,)), ((), ()))
PACK = 2 * BLK + RANK
STRIP = 16
PAIR = 2
MIB = 1024 * 1024
ROOM = 63.5


def dot_nt(a, b, precision=None):
    return lax.dot_general(a, b, NT, precision=precision, preferred_element_type=jnp.float32)


def dot_nn(a, b, precision=None):
    return jnp.dot(a, b, precision=precision, preferred_element_type=jnp.float32)


def piece_rows(place_ref, j, width):
    return pl.ds(pl.multiple_of(lax.bitwise_xor(place_ref[0], j) * width, width), width)


def start_copies(pairs, sems, first=0):
    copies = [pltpu.make_async_copy(src, dst, sems.at[first + n]) for n, (src, dst) in enumerate(pairs)]
    for copy in copies:
        copy.start()
    return copies


def wait_all(copies):
    for copy in copies:
        copy.wait()


def memory_pieces(place_ref, js, xs, hbm, scratch, sems):
    x_s, wk_s, wv_s, down_s = scratch
    width = x_s.shape[2]
    groups = []
    for n, j in enumerate(js):
        here = piece_rows(place_ref, j, width)
        pairs = [
            (xs[n], x_s.at[n]),
            (hbm[0].at[here, :], wk_s.at[n]),
            (hbm[1].at[here, :], wv_s.at[n]),
            (hbm[2].at[:, here], down_s.at[n]),
        ]
        groups.append(start_copies(pairs, sems, 4 * n))
    return groups


def memory_terms(n, scratch):
    x_s, wk_s, wv_s, down_s = scratch
    x = x_s[n]
    return dot_nn(x, jnp.concatenate([wk_s[n], wv_s[n]], 1)), dot_nt(x, down_s[n])


def memory_early_kernel(blocks, place_ref, named_ref, x0, x1, *refs):
    hbm, acc_ref, low_ref, wanted_ref, scratch, sems = refs[:3], refs[3], refs[4], refs[5], refs[6:10], refs[10]
    groups = memory_pieces(place_ref, (0, 1), (x0, x1), hbm, scratch, sems)
    for slot in range(TOP):
        block = named_ref[0, slot]
        wanted_ref[lax.div(block, blocks)] = lax.rem(block, blocks)
    for n in range(2):
        wait_all(groups[n])
        term, low_term = memory_terms(n, scratch)
        if n == 0:
            acc_ref[...] = term
            low_ref[...] = low_term
        else:
            acc_ref[...] += term
            low_ref[...] += low_term


def memory_middle_kernel(place_ref, x2, acc_hbm, low_hbm, *refs):
    hbm, acc_ref, low_ref, scratch, sems = refs[:3], refs[3], refs[4], refs[5:9], refs[9]
    acc_s, low_s, acc_sems = refs[10:13]
    groups = memory_pieces(place_ref, (2,), (x2,), hbm, scratch, sems)
    sums = start_copies([(acc_hbm, acc_s), (low_hbm, low_s)], acc_sems)
    wait_all(groups[0])
    term, low_term = memory_terms(0, scratch)
    wait_all(sums)
    acc_ref[...] = acc_s[...] + term
    low_ref[...] = low_s[...] + low_term


def memory_kernel(peers, place_ref, asked_ref, x3, acc_hbm, low_hbm, *refs):
    hbm, up_ref, out_ref = refs[:3], refs[3], refs[4]
    scratch, sems, acc_s, low_s, acc_sems, pair_ref = refs[5:9], refs[9], refs[10], refs[11], refs[12], refs[13]
    groups = memory_pieces(place_ref, (3,), (x3,), hbm, scratch, sems)
    sums = start_copies([(acc_hbm, acc_s), (low_hbm, low_s)], acc_sems)
    wait_all(groups[0])
    term, low_term = memory_terms(0, scratch)
    wait_all(sums)
    acc = acc_s[...] + term
    low = low_s[...] + low_term
    values = (acc[:, HD:] + dot_nn(low.astype(jnp.bfloat16), up_ref[...])).astype(jnp.bfloat16)
    keys = acc[:, :HD].astype(jnp.bfloat16)
    low_t = jnp.transpose(low).astype(jnp.bfloat16)
    for b in range(acc.shape[0] // BLK):
        at = slice(b * BLK, (b + 1) * BLK)
        pair_ref[b, 0:BLK, :] = keys[at]
        pair_ref[b, BLK : 2 * BLK, :] = values[at]
        pair_ref[b, 2 * BLK : PACK, :] = low_t[:, at]
    for r in range(peers):
        out_ref[r] = pair_ref[asked_ref[r]]


WQ_CUTS = 4


def project_pieces(place_ref, js, xs, hbm, scratch, sems):
    wq_hbm, wk_hbm, wv_hbm, qd_hbm, vd_hbm = hbm
    x_s, wq_s, wk_s, wv_s, qd_s, vd_s = scratch
    width = x_s.shape[2]
    part = width // WQ_CUTS
    groups = []
    for n, j in enumerate(js):
        here = piece_rows(place_ref, j, width)
        start = lax.bitwise_xor(place_ref[0], j) * width
        pairs = [(xs[n], x_s.at[n])]
        for m in range(WQ_CUTS):
            rows = pl.ds(pl.multiple_of(start + m * part, part), part)
            pairs.append((wq_hbm.at[rows, :], wq_s.at[n, pl.ds(m * part, part), :]))
        pairs += [
            (wk_hbm.at[here, :], wk_s.at[n]),
            (wv_hbm.at[here, :], wv_s.at[n]),
            (qd_hbm.at[:, here], qd_s.at[n]),
            (vd_hbm.at[:, here], vd_s.at[n]),
        ]
        groups.append(start_copies(pairs, sems, len(pairs) * n))
    return groups


def project_terms(n, scratch):
    x_s, wq_s, wk_s, wv_s, qd_s, vd_s = scratch
    x = x_s[n]
    return (
        dot_nn(x, wq_s[n]),
        dot_nn(x, jnp.concatenate([wk_s[n], wv_s[n]], 1)),
        dot_nt(x, jnp.concatenate([qd_s[n], vd_s[n]], 0)),
    )


def project_early_kernel(place_ref, x0, x1, *refs):
    hbm, (tag_ref, tags_t_ref), outs, (grad_ref, grad_t_ref) = refs[:5], refs[5:7], refs[8:11], refs[11:13]
    scratch, sems = refs[13:19], refs[19]
    groups = project_pieces(place_ref, (0, 1), (x0, x1), hbm, scratch, sems)
    first = (((0,), (0,)), ((), ()))
    tag = tag_ref[...].astype(jnp.float32)
    tags_t = tags_t_ref[...]
    f32 = jnp.float32
    grad_ref[...] = lax.dot_general(
        tags_t, tag, first, precision=HIGHEST, preferred_element_type=f32
    ).astype(jnp.bfloat16)
    grad_t_ref[...] = lax.dot_general(
        tag, tags_t, first, precision=HIGHEST, preferred_element_type=f32
    ).astype(jnp.bfloat16)
    for n in range(2):
        wait_all(groups[n])
        for ref, term in zip(outs, project_terms(n, scratch)):
            if n == 0:
                ref[...] = term
            else:
                ref[...] += term


def project_middle_kernel(place_ref, x3, *refs):
    hbm, early, outs, scratch, sems = refs[:5], refs[5:8], refs[8:11], refs[11:17], refs[17]
    sum_refs, sum_sems = refs[18:21], refs[21]
    groups = project_pieces(place_ref, (3,), (x3,), hbm, scratch, sems)
    loads = start_copies(list(zip(early, sum_refs)), sum_sems)
    wait_all(groups[0])
    terms = project_terms(0, scratch)
    wait_all(loads)
    for out, ref, term in zip(outs, sum_refs, terms):
        out[...] = ref[...] + term


def attention_kernel(peers, heads, place_ref, bound_ref, x2, *refs):
    hbm, early, got, grad_hbm, grad_t_hbm = refs[:5], refs[5:8], refs[8], refs[9], refs[10]
    qup_ref, vup_ref, tag_ref, cot_ref, mine_ref, mcot_ref = refs[11:17]
    scratch, sems, sum_refs = refs[17:23], refs[23], refs[24:27]
    (q_s, k_own, v_own, low_s, low_m_s, grad_ref, grad_t_ref, k_all, v_all, kt_all, vt_all, kt_own, vt_own, bias_s, s_s, dp_s,
     p_s, ds_s, att_s, dq_s, dv_s, up_ref, more_sems) = refs[27:]
    seen = peers * BLK
    groups = project_pieces(place_ref, (2,), (x2,), hbm, scratch, sems)
    pairs = list(zip(early, sum_refs))
    for b in range(peers):
        at = slice(b * BLK, (b + 1) * BLK)
        pairs.append((got.at[b, pl.ds(0, BLK), :], k_all.at[at, :]))
        pairs.append((got.at[b, pl.ds(BLK, BLK), :], v_all.at[at, :]))
        pairs.append((got.at[b, pl.ds(2 * BLK, RANK), :], low_m_s.at[b]))
    pairs += [(grad_hbm, grad_ref), (grad_t_hbm, grad_t_ref)]
    copies = start_copies(pairs, more_sems)
    wait_all(groups[0])
    terms = project_terms(0, scratch)
    wait_all(copies[:3])
    q_acc, kv_acc, low_acc = [ref[...] + term for ref, term in zip(sum_refs, terms)]
    low = low_acc.astype(jnp.bfloat16)
    q_s[...] = (q_acc + dot_nn(low[:, :RANK], qup_ref[...])).astype(jnp.bfloat16)
    k_own[...] = kv_acc[:, :HD].astype(jnp.bfloat16)
    v_own[...] = (kv_acc[:, HD:] + dot_nn(low[:, RANK:], vup_ref[...])).astype(jnp.bfloat16)
    low_s[...] = jnp.transpose(low_acc).astype(jnp.bfloat16)
    wait_all(copies[3 : 3 + 3 * peers])
    for b in range(peers):
        at = slice(b * BLK, (b + 1) * BLK)
        kt_all[:, at] = jnp.transpose(k_all[at, :])
        vt_all[:, at] = jnp.transpose(v_all[at, :])
    wait_all(copies[3 + 3 * peers : -1])
    dv_s[...] = jnp.zeros_like(dv_s)
    up_ref[...] = jnp.zeros_like(up_ref)
    scale = HD ** (-0.5)
    up_wide = vup_ref[...].astype(jnp.float32)
    query_width = heads * HD

    def pair_step(c, carry):
        base = c * (PAIR * BLK)
        rows = pl.ds(pl.multiple_of(base, PAIR * BLK), PAIR * BLK)
        own_rows = [pl.ds(pl.multiple_of(base + b * BLK, BLK), BLK) for b in range(PAIR)]
        row_ids = lax.broadcasted_iota(jnp.int32, (BLK, BLK), 0)
        col_ids = lax.broadcasted_iota(jnp.int32, (BLK, BLK), 1)
        for b in range(PAIR):
            kt_own[:, b * BLK : (b + 1) * BLK] = jnp.transpose(k_own[own_rows[b], :])
            vt_own[:, b * BLK : (b + 1) * BLK] = jnp.transpose(v_own[own_rows[b], :])
            edge = bound_ref[c * PAIR + b]
            visible = (col_ids <= row_ids) & ((col_ids >= edge) | (row_ids < edge))
            bias_s[b * BLK : (b + 1) * BLK, :] = jnp.where(visible, 0.0, -jnp.inf)

        def head_cols(h):
            return slice(h * HD, (h + 1) * HD)

        def times_keys(out_ref, left_ref, h, all_t, own_t):
            out_ref[:, :seen] = dot_nn(left_ref[rows, head_cols(h)], all_t[...])
            for b in range(PAIR):
                at = slice(b * BLK, (b + 1) * BLK)
                out_ref[at, seen:] = dot_nn(left_ref[own_rows[b], head_cols(h)], own_t[:, at])

        def over_keys(left_ref, first, all_ref, own_ref):
            whole = dot_nn(left_ref[first : first + PAIR * BLK, :seen], all_ref[...])
            mine = [
                dot_nn(left_ref[first + b * BLK : first + (b + 1) * BLK, seen:], own_ref[own_rows[b], :])
                for b in range(PAIR)
            ]
            return (whole + jnp.concatenate(mine, 0)).astype(jnp.bfloat16)

        def scores(h):
            times_keys(s_s.at[h % 2], q_s, h, kt_all, kt_own)

        def prob_grads(h):
            times_keys(dp_s.at[h % 2], grad_ref, h, vt_all, vt_own)

        def strips(h):
            for r in range(0, PAIR * BLK, STRIP):
                at = slice(r, r + STRIP)
                s = s_s[h % 2, at, :]
                s = jnp.concatenate([s[:, :seen], s[:, seen:] + bias_s[at, :]], 1) * (scale * LOG2E)
                w = jnp.exp2(s - jnp.max(s, axis=1, keepdims=True))
                probs = w * (1.0 / jnp.sum(w, axis=1, keepdims=True))
                probs_low = probs.astype(jnp.bfloat16)
                first = h * PAIR * BLK + r
                p_s[first : first + STRIP, :] = probs_low
                dp = dp_s[h % 2, at, :]
                dot = jnp.sum(probs_low.astype(jnp.float32) * dp, axis=1, keepdims=True)
                ds_s[h % 2, at, :] = (probs * ((dp - dot) * scale)).astype(jnp.bfloat16)

        def finish_head(h):
            att_s[:, head_cols(h)] = over_keys(p_s, h * PAIR * BLK, v_all, v_own)
            dq_s[:, head_cols(h)] = over_keys(ds_s.at[h % 2], 0, k_all, k_own)

        scores(0)
        prob_grads(0)
        for h in range(heads + 1):
            if h + 1 < heads:
                scores(h + 1)
                prob_grads(h + 1)
            if h < heads:
                strips(h)
            if h > 0:
                finish_head(h - 1)
        pl.when(c == 0)(copies[-1].wait)
        g_t = jnp.concatenate([grad_t_ref[h * HD : (h + 1) * HD, rows] for h in range(heads)], 1)
        dv_s[...] += dot_nn(g_t, p_s[:, :seen])
        dv_own = []
        for b in range(PAIR):
            g_b = jnp.concatenate([grad_t_ref[h * HD : (h + 1) * HD, own_rows[b]] for h in range(heads)], 1)
            starts = [(h * PAIR + b) * BLK for h in range(heads)]
            p_b = jnp.concatenate([p_s[n : n + BLK, seen:] for n in starts], 0)
            dv_own.append(dot_nn(g_b, p_b))
        dv_own = jnp.concatenate(dv_own, 1)
        dq = dq_s[...]
        cot_ref[0:RANK, rows] = dot_nt(qup_ref[...], dq)
        cot_ref[RANK : 2 * RANK, rows] = dot_nn(up_wide, dv_own, HIGHEST)
        cot_ref[2 * RANK :, rows] = dot_nt(tag_ref[...], att_s[...])
        up_ref[:, :query_width] += dot_nn(low_s[0:RANK, rows], dq)
        up_ref[:, query_width:] += dot_nt(low_s[RANK:, rows].astype(jnp.float32), dv_own, HIGHEST)
        return carry

    lax.fori_loop(0, q_s.shape[0] // (PAIR * BLK), pair_step, 0)
    dv = dv_s[...]
    mcot = dot_nn(up_wide, dv, HIGHEST)
    low_m = jnp.concatenate([low_m_s[b] for b in range(peers)], 1).astype(jnp.float32)
    up_ref[:, query_width:] += dot_nt(low_m, dv, HIGHEST)
    for b in range(peers):
        mcot_ref[b] = mcot[:, b * BLK : (b + 1) * BLK]
    at, wide = cot_ref.shape
    mine_ref[:at, :] = cot_ref[...]
    for n in range(0, up_ref.shape[1], wide):
        mine_ref[at : at + RANK, :] = up_ref[:, n : n + wide]
        at += RANK


def own_kernel(peers, asked_ref, back_ref, out_ref, sum_s):
    sum_s[...] = jnp.zeros_like(sum_s)
    for r in range(peers):
        block = asked_ref[r]
        sum_s[block] = sum_s[block] + back_ref[r]
    out_ref[...] = jnp.concatenate([sum_s[m] for m in range(sum_s.shape[0])], 1)


def first_down_kernel(mine_ref, c1, c2, c3, slab_ref, dep_ref, logit_ref, query_ref, value_ref):
    own, wide = c1.shape
    cot = (mine_ref[:own, :] + c1[...]) + (c2[...] + c3[...])
    logit_ref[...] = cot[2 * RANK :]
    both = dot_nn(cot[: 2 * RANK].astype(jnp.bfloat16), slab_ref[...])
    width = both.shape[1]
    query_ref[:, :width] = both[:RANK]
    for n, at in enumerate(range(own, mine_ref.shape[0], RANK)):
        query_ref[:, width + n * wide : width + (n + 1) * wide] = mine_ref[at : at + RANK, :]
    value_ref[...] = both[RANK:]


def second_down_kernel(c0, c1, c2, c3, memory_ref, value_ref, q0, q1, out_ref, query_ref):
    query_ref[...] = q0[...] + q1[...]
    cot = (c0[...] + c1[...]) + (c2[...] + c3[...])
    out_ref[...] = value_ref[...] + dot_nn(cot.astype(jnp.bfloat16), memory_ref[...])


def pack_kernel(q0, q1, v0, v1, both_ref, value_ref):
    split = q0.shape[1]
    value = (v0[...] + v1[...]).astype(jnp.bfloat16)
    both_ref[:, :split] = (q0[...] + q1[...]).astype(jnp.bfloat16)
    both_ref[:, split:] = value
    value_ref[...] = value


def finish_kernel(here_ref, there_ref, v1, v3, query_down_ref, query_up_ref, value_down_ref, value_up_ref):
    here = here_ref[...].astype(jnp.float32)
    there = there_ref[...].astype(jnp.float32)
    split = here.shape[1] - value_down_ref.shape[1]
    value_down_ref[...] = (here[:, split:] + v1[...].astype(jnp.float32)) + (
        there[:, split:] + v3[...].astype(jnp.float32)
    )
    query = here[:, :split] + there[:, :split]
    at = 0
    for out_ref in (query_down_ref, query_up_ref, value_up_ref):
        out_ref[...] = query[:, at : at + out_ref.shape[1]]
        at += out_ref.shape[1]


def swap(x, bit, axis="heads"):
    return lax.ppermute(x, axis, [(i, i ^ bit) for i in range(lax.axis_size(axis))])


def after(x, *deps):
    return pl.pallas_call(
        lambda *refs: None,
        out_shape=jax.ShapeDtypeStruct(x.shape, x.dtype),
        in_specs=[anywhere()] * (1 + len(deps)),
        out_specs=anywhere(),
        input_output_aliases={0: 0},
        name="in_order",
    )(x, *deps)


def anywhere():
    return pl.BlockSpec(memory_space=pl.ANY)


def smem():
    return pl.BlockSpec(memory_space=pltpu.SMEM)


def vmem():
    return pl.BlockSpec(memory_space=pltpu.VMEM)


def shaped(*shape, dtype=jnp.float32):
    return jax.ShapeDtypeStruct(shape, dtype)


def run(body, name, out_shape, in_specs, scratch=(), flops=0, moved=0, room=ROOM, out_specs=None):
    many = isinstance(out_shape, (tuple, list))
    return pl.pallas_call(
        body,
        out_shape=out_shape,
        in_specs=in_specs,
        out_specs=out_specs or (tuple(vmem() for _ in out_shape) if many else vmem()),
        scratch_shapes=list(scratch),
        compiler_params=pltpu.CompilerParams(vmem_limit_bytes=int(room * MIB)),
        cost_estimate=pl.CostEstimate(flops=flops, bytes_accessed=moved, transcendentals=0),
        name=name,
    )


def fast(
    slab_tokens,
    memory,
    query_weight,
    key_weight,
    value_weight,
    query_down,
    query_up,
    value_down,
    value_up,
    tag_weight,
    retrieval,
    boundary,
    grad_tags,
):
    tok_rows, width = slab_tokens.shape
    mem_rows = memory.shape[0]
    query_width = query_weight.shape[1]
    heads = query_width // HD
    spans = tok_rows // BLK
    blocks = mem_rows // BLK
    peers = lax.axis_size("tm")
    f32 = jnp.float32
    bf16 = jnp.bfloat16

    def memory_scratch(count):
        return [
            pltpu.VMEM((count, mem_rows, width), bf16),
            pltpu.VMEM((count, width, HD), bf16),
            pltpu.VMEM((count, width, HD), bf16),
            pltpu.VMEM((count, RANK, width), bf16),
            pltpu.SemaphoreType.DMA((4 * count,)),
        ]

    def project_scratch(count):
        return [
            pltpu.VMEM((count, tok_rows, width), bf16),
            pltpu.VMEM((count, width, query_width), bf16),
            pltpu.VMEM((count, width, HD), bf16),
            pltpu.VMEM((count, width, HD), bf16),
            pltpu.VMEM((count, RANK, width), bf16),
            pltpu.VMEM((count, RANK, width), bf16),
            pltpu.SemaphoreType.DMA((count * (WQ_CUTS + 5),)),
        ]

    memory_sums = [
        pltpu.VMEM((mem_rows, 2 * HD), f32),
        pltpu.VMEM((mem_rows, RANK), f32),
        pltpu.SemaphoreType.DMA((2,)),
    ]
    project_sums = [
        pltpu.VMEM((tok_rows, query_width), f32),
        pltpu.VMEM((tok_rows, 2 * HD), f32),
        pltpu.VMEM((tok_rows, 2 * RANK), f32),
    ]

    place = lax.axis_index("heads").astype(jnp.int32).reshape(1)
    tag_t = tag_weight.T
    tags = tag_t.shape[0]
    mem_far = swap(memory, 2)
    mem_near = swap(memory, 1)
    tok_near = swap(slab_tokens, 1)
    tok_far = swap(tok_near, 2)
    mem_acc, mem_low, wanted = run(
        lambda *refs: memory_early_kernel(blocks, *refs),
        "memory_near_half",
        (shaped(mem_rows, 2 * HD), shaped(mem_rows, RANK), shaped(peers, dtype=jnp.int32)),
        [smem()] * 2 + [anywhere()] * 5,
        memory_scratch(2),
        out_specs=(vmem(), vmem(), smem()),
    )(place, retrieval, memory, mem_near, key_weight, value_weight, value_down)
    asked = lax.all_to_all(wanted, "tm", split_axis=0, concat_axis=0, tiled=True)
    weights = (query_weight, key_weight, value_weight, query_down, value_down)
    mem_far = after(mem_far, asked)
    mem_cross = swap(mem_far, 1)
    mem_weights = (key_weight, value_weight, value_down)
    mem_acc, mem_low = run(
        memory_middle_kernel,
        "memory_far_quarter",
        (shaped(mem_rows, 2 * HD), shaped(mem_rows, RANK)),
        [smem()] + [anywhere()] * 6,
        memory_scratch(1) + memory_sums,
    )(place, mem_far, mem_acc, mem_low, *mem_weights)
    pairs = run(
        lambda *refs: memory_kernel(peers, *refs),
        "memory_pairs",
        shaped(peers, PACK, HD, dtype=bf16),
        [smem()] * 2 + [anywhere()] * 6 + [vmem()],
        memory_scratch(1) + memory_sums + [pltpu.VMEM((blocks, PACK, HD), bf16)],
    )(place, asked, mem_cross, mem_acc, mem_low, *mem_weights, value_up)
    got = lax.all_to_all(pairs, "tm", split_axis=0, concat_axis=0, tiled=True)
    *early, grad, grad_t = run(
        project_early_kernel,
        "project_near_half",
        (
            shaped(tok_rows, query_width),
            shaped(tok_rows, 2 * HD),
            shaped(tok_rows, 2 * RANK),
            shaped(tok_rows, query_width, dtype=bf16),
            shaped(query_width, tok_rows, dtype=bf16),
        ),
        [smem()] + [anywhere()] * 7 + [vmem()] * 2 + [anywhere()],
        project_scratch(2),
    )(place, slab_tokens, tok_near, *weights, tag_t, grad_tags.T, pairs)
    tok_far = after(tok_far, early[2])
    tok_cross = swap(tok_far, 1)
    early = run(
        project_middle_kernel,
        "project_far_quarter",
        (shaped(tok_rows, query_width), shaped(tok_rows, 2 * HD), shaped(tok_rows, 2 * RANK)),
        [smem()] + [anywhere()] * 9,
        project_scratch(1) + project_sums + [pltpu.SemaphoreType.DMA((3,))],
    )(place, tok_far, *weights, *early)

    seen = peers * BLK
    total = seen + BLK
    cot, mine, mcot = run(
        lambda *refs: attention_kernel(peers, heads, *refs),
        "span_attention",
        (
            shaped(2 * RANK + tags, tok_rows),
            shaped(2 * RANK + tags + RANK * (query_width + HD) // tok_rows, tok_rows),
            shaped(peers, RANK, BLK),
        ),
        [smem()] * 2 + [anywhere()] * 12 + [vmem()] * 3,
        project_scratch(1)
        + project_sums
        + [
            pltpu.VMEM((tok_rows, query_width), bf16),
            pltpu.VMEM((tok_rows, HD), bf16),
            pltpu.VMEM((tok_rows, HD), bf16),
            pltpu.VMEM((2 * RANK, tok_rows), bf16),
            pltpu.VMEM((peers, RANK, BLK), bf16),
            pltpu.VMEM((tok_rows, query_width), bf16),
            pltpu.VMEM((query_width, tok_rows), bf16),
            pltpu.VMEM((seen, HD), bf16),
            pltpu.VMEM((seen, HD), bf16),
            pltpu.VMEM((HD, seen), bf16),
            pltpu.VMEM((HD, seen), bf16),
            pltpu.VMEM((HD, PAIR * BLK), bf16),
            pltpu.VMEM((HD, PAIR * BLK), bf16),
            pltpu.VMEM((PAIR * BLK, BLK), f32),
            pltpu.VMEM((2, PAIR * BLK, total), f32),
            pltpu.VMEM((2, PAIR * BLK, total), f32),
            pltpu.VMEM((heads * PAIR * BLK, total), bf16),
            pltpu.VMEM((2, PAIR * BLK, total), bf16),
            pltpu.VMEM((PAIR * BLK, query_width), bf16),
            pltpu.VMEM((PAIR * BLK, query_width), bf16),
            pltpu.VMEM((HD, seen), f32),
            pltpu.VMEM((RANK, query_width + HD), f32),
            pltpu.SemaphoreType.DMA((3 * peers + 5,)),
        ],
        flops=20 * tok_rows * query_width * total,
        moved=4 * tok_rows * query_width,
        room=60,
    )(place, boundary, tok_cross, *weights, *early, got, grad, grad_t, query_up, value_up, tag_t)

    back = lax.all_to_all(mcot, "tm", split_axis=0, concat_axis=0, tiled=True)
    cots = [mine] + [swap(cot, d) for d in range(1, 4)]
    own = run(
        lambda *refs: own_kernel(peers, *refs),
        "owned_cotangent",
        shaped(RANK, mem_rows),
        [smem()] + [vmem()],
        [pltpu.VMEM((blocks, RANK, BLK), f32)],
        room=8,
    )(asked, back)
    logits, query_sum, value_part = run(
        first_down_kernel,
        "first_down",
        (shaped(tags, tok_rows), shaped(RANK, width + query_width + HD), shaped(RANK, width)),
        [vmem()] * 5 + [anywhere()],
        flops=4 * RANK * tok_rows * width,
        moved=2 * tok_rows * width,
        room=8,
    )(*cots, slab_tokens, own)
    owns = [own] + [swap(own, d) for d in range(1, 4)]
    value_sum, query_sum = run(
        second_down_kernel,
        "second_down",
        (shaped(RANK, width), shaped(*query_sum.shape)),
        [vmem()] * 8,
        flops=2 * RANK * mem_rows * width,
        moved=2 * mem_rows * width,
        room=8,
    )(*owns, memory, value_part, query_sum, swap(query_sum, 1, "tm"))
    split = query_sum.shape[1]
    both, value_low = run(
        pack_kernel,
        "pack_sums",
        (shaped(RANK, split + width, dtype=bf16), shaped(RANK, width, dtype=bf16)),
        [vmem()] * 4,
        room=8,
    )(query_sum, swap(query_sum, 2, "tm"), value_sum, swap(value_sum, 1, "tm"))
    sums = [both, swap(both, 4, "tm"), swap(value_low, 2, "tm"), swap(value_low, 6, "tm")]
    query_down_grad, query_up_grad, value_down_grad, value_up_grad = run(
        finish_kernel,
        "finish_outputs",
        (shaped(RANK, width), shaped(RANK, query_width), shaped(RANK, width), shaped(RANK, HD)),
        [vmem()] * 4,
        room=8,
    )(*sums)
    return (logits.T, query_down_grad, query_up_grad, value_down_grad, value_up_grad)


def solution(mesh):
    in_specs = (
        P("tm", "heads"),
        P("tm", "heads"),
        P(None, "heads"),
        P(None, "heads"),
        P(None, "heads"),
        P(),
        P(None, "heads"),
        P(),
        P(None, "heads"),
        P("heads", None),
        P("tm", None),
        P("tm"),
        P("tm", None),
    )
    out_specs = (
        P("tm", None),
        P(None, "heads"),
        P(None, "heads"),
        P(None, "heads"),
        P(None, "heads"),
    )
    fits = mesh.shape["heads"] == 4 and mesh.shape["tm"] == 8 == TOP * CAP
    local = fast if fits else general
    return jax.shard_map(local, mesh=mesh, in_specs=in_specs, out_specs=out_specs, check_vma=False)
```

```python
import jax
import jax.numpy as jnp
from jax import lax
from jax.experimental import pallas as pl
from jax.experimental.pallas import tpu as pltpu
from jax.sharding import PartitionSpec as P

HD = 128
RANK = 16
TOP = 8
BLK = 128
CAP = 1


HIGHEST = lax.Precision.HIGHEST


def attend(query, all_keys, all_values, split_row, out_grad):
    span_count, row_count, query_width = query.shape
    key_count, kv_width = (all_keys.shape[1], all_keys.shape[2])
    kv_heads = kv_width // HD
    group_size = query_width // kv_width
    score_scale = HD ** (-0.5)
    query_heads = query.reshape(span_count, row_count, kv_heads, group_size, HD)
    key_heads = all_keys.reshape(span_count, key_count, kv_heads, HD)
    value_heads = all_values.reshape(span_count, key_count, kv_heads, HD)
    grad_heads = out_grad.reshape(span_count, row_count, kv_heads, group_size, HD)
    scores = (
        jnp.einsum("crngd,cknd->cngrk", query_heads, key_heads, preferred_element_type=jnp.float32)
        * score_scale
    )
    row_ids = jnp.arange(row_count, dtype=jnp.int32)[:, None]
    col_ids = jnp.arange(BLK, dtype=jnp.int32)[None, :]
    edge_at = split_row[:, None, None]
    local_seen = (col_ids <= row_ids) & ((col_ids >= edge_at) | (row_ids < edge_at))
    visible = jnp.concatenate(
        [jnp.ones((span_count, row_count, key_count - BLK), jnp.bool_), local_seen], axis=2
    )
    scores = jnp.where(visible[:, None, None], scores, -jnp.inf)
    row_max = jnp.max(scores, axis=-1, keepdims=True)
    weights = jnp.exp(scores - row_max)
    probs = weights / jnp.sum(weights, axis=-1, keepdims=True)
    probs_low = probs.astype(jnp.bfloat16)
    attended = jnp.einsum(
        "cngrk,cknd->crngd", probs_low, value_heads, preferred_element_type=jnp.float32
    ).astype(jnp.bfloat16)
    prob_grad = jnp.einsum(
        "crngd,cknd->cngrk", grad_heads, value_heads, preferred_element_type=jnp.float32
    )
    row_dot = jnp.sum(grad_heads.astype(jnp.float32) * attended.astype(jnp.float32), axis=-1)
    row_dot = jnp.transpose(row_dot, (0, 2, 3, 1))[..., None]
    score_grad = (probs * (prob_grad - row_dot) * score_scale).astype(jnp.bfloat16)
    query_grad = jnp.einsum(
        "cngrk,cknd->crngd", score_grad, key_heads, preferred_element_type=jnp.float32
    ).astype(jnp.bfloat16)
    value_grad = jnp.einsum(
        "cngrk,crngd->cknd", probs_low, grad_heads, preferred_element_type=jnp.float32
    )
    return (
        attended.reshape(span_count, row_count, query_width),
        query_grad.reshape(span_count, row_count, query_width),
        value_grad.reshape(span_count, key_count, kv_width),
    )


def choose_slots(needed, places):
    slot_ids = jnp.arange(CAP, dtype=jnp.int32)
    return needed[:, None, :] * (places[:, None, :] == slot_ids[None, :, None]).astype(jnp.int32)


def general(
    slab_tokens,
    memory,
    query_weight,
    key_weight,
    value_weight,
    query_down,
    query_up,
    value_down,
    value_up,
    tag_weight,
    retrieval,
    boundary,
    grad_tags,
):
    tok_rows = slab_tokens.shape[0]
    mem_rows = memory.shape[0]
    query_width = query_weight.shape[1]
    kv_width = key_weight.shape[1]
    span_count = tok_rows // BLK
    block_count = mem_rows // BLK
    pair_weight = jnp.concatenate([key_weight, value_weight], 1)
    adapter_pair = jnp.concatenate([query_down, value_down], 0)
    contract_last = (((1,), (1,)), ((), ()))
    contract_first = (((0,), (0,)), ((), ()))
    token_piece = lax.all_gather(slab_tokens, "heads", axis=1, tiled=True)
    memory_piece = lax.all_gather(memory, "heads", axis=1, tiled=True)
    query_acc = jnp.dot(token_piece, query_weight, preferred_element_type=jnp.float32)
    pair_acc = jnp.dot(token_piece, pair_weight, preferred_element_type=jnp.float32)
    low_acc = lax.dot_general(
        token_piece, adapter_pair, contract_last, preferred_element_type=jnp.float32
    )
    memory_acc = jnp.dot(memory_piece, pair_weight, preferred_element_type=jnp.float32)
    memory_low_acc = lax.dot_general(
        memory_piece, adapter_pair[RANK:], contract_last, preferred_element_type=jnp.float32
    )
    query_acc, pair_acc, low_acc, memory_acc, memory_low_acc = (
        query_acc,
        pair_acc,
        low_acc,
        memory_acc,
        memory_low_acc,
    )
    low_tokens = low_acc.astype(jnp.bfloat16)
    low_query = low_tokens[:, :RANK]
    low_value = low_tokens[:, RANK:]
    queries = (query_acc + jnp.dot(low_query, query_up, preferred_element_type=jnp.float32)).astype(
        jnp.bfloat16
    )
    keys_local = pair_acc[:, :kv_width].astype(jnp.bfloat16)
    values_local = (
        pair_acc[:, kv_width:] + jnp.dot(low_value, value_up, preferred_element_type=jnp.float32)
    ).astype(jnp.bfloat16)
    memory_low = memory_low_acc.astype(jnp.bfloat16)
    memory_pair = (
        jnp.concatenate(
            [
                memory_acc[:, :kv_width],
                memory_acc[:, kv_width:]
                + jnp.dot(memory_low, value_up, preferred_element_type=jnp.float32),
            ],
            1,
        )
        .astype(jnp.bfloat16)
        .reshape(block_count, BLK, 2 * kv_width)
    )
    peer_count = lax.axis_size("tm")
    every_block = jnp.arange(peer_count * block_count, dtype=jnp.int32)
    wanted = (
        jnp.any(retrieval.reshape(-1, 1) == every_block[None, :], axis=0)
        .astype(jnp.int32)
        .reshape(peer_count, block_count)
    )
    places = jnp.cumsum(wanted, axis=1) - wanted
    requested = choose_slots(wanted, places)
    asked_for = lax.all_to_all(requested, "tm", split_axis=0, concat_axis=0, tiled=True)
    rows_needed = retrieval // block_count * CAP + jnp.take(places.reshape(-1), retrieval)
    asked_low = asked_for.astype(jnp.bfloat16)
    outgoing = jnp.einsum(
        "rcm,mbw->rcbw", asked_low, memory_pair, preferred_element_type=jnp.float32
    ).astype(jnp.bfloat16)
    fetched = lax.all_to_all(outgoing, "tm", split_axis=0, concat_axis=0, tiled=True)
    slot_rows = fetched.reshape(peer_count * CAP, BLK, 2 * kv_width)
    picked = jnp.take(slot_rows, rows_needed.reshape(-1), axis=0).reshape(
        span_count, TOP * BLK, 2 * kv_width
    )
    all_keys = jnp.concatenate(
        [picked[..., :kv_width], keys_local.reshape(span_count, BLK, kv_width)], 1
    )
    all_values = jnp.concatenate(
        [picked[..., kv_width:], values_local.reshape(span_count, BLK, kv_width)], 1
    )
    attended_grad = lax.dot_general(
        grad_tags, tag_weight.astype(jnp.float32), contract_last, precision=HIGHEST
    ).astype(jnp.bfloat16)
    attended, query_grad, value_grad = attend(
        queries.reshape(span_count, BLK, query_width),
        all_keys,
        all_values,
        boundary,
        attended_grad.reshape(span_count, BLK, query_width),
    )
    attended = attended.reshape(tok_rows, query_width)
    query_grad = query_grad.reshape(tok_rows, query_width)
    logits_out = lax.psum(
        jnp.dot(attended, tag_weight, preferred_element_type=jnp.float32), "heads"
    )
    local_grad = value_grad[:, TOP * BLK :].reshape(tok_rows, kv_width)
    slot_grads = value_grad[:, : TOP * BLK].reshape(span_count * TOP, BLK * kv_width)
    slot_hits = (
        rows_needed.reshape(-1, 1) == jnp.arange(peer_count * CAP, dtype=jnp.int32)[None, :]
    ).astype(jnp.float32)
    grad_buffer = lax.dot_general(slot_hits, slot_grads, contract_first, precision=HIGHEST).reshape(
        peer_count * CAP, BLK, kv_width
    )
    up_wide = value_up.astype(jnp.float32)
    returned = lax.all_to_all(
        grad_buffer.reshape(peer_count, CAP, BLK, kv_width),
        "tm",
        split_axis=0,
        concat_axis=0,
        tiled=True,
    )
    owned_grad = jnp.einsum(
        "rcm,rcbw->mbw", asked_for.astype(jnp.float32), returned, precision=HIGHEST
    ).reshape(mem_rows, kv_width)
    memory_cot = lax.dot_general(up_wide, owned_grad, contract_last, precision=HIGHEST)
    up_memory = lax.dot_general(
        memory_low.astype(jnp.float32), owned_grad, contract_first, precision=HIGHEST
    )
    query_cot = lax.dot_general(
        query_up, query_grad, contract_last, preferred_element_type=jnp.float32
    )
    value_cot = lax.dot_general(up_wide, local_grad, contract_last, precision=HIGHEST)
    query_cot, value_cot, memory_cot = lax.psum((query_cot, value_cot, memory_cot), "heads")
    query_down_grad = jnp.dot(
        query_cot.astype(jnp.bfloat16), slab_tokens, preferred_element_type=jnp.float32
    )
    value_down_grad = jnp.dot(
        value_cot.astype(jnp.bfloat16), slab_tokens, preferred_element_type=jnp.float32
    ) + jnp.dot(memory_cot.astype(jnp.bfloat16), memory, preferred_element_type=jnp.float32)
    query_up_grad = lax.dot_general(
        low_query, query_grad, contract_first, preferred_element_type=jnp.float32
    )
    value_up_grad = (
        lax.dot_general(
            low_value.astype(jnp.float32), local_grad, contract_first, precision=HIGHEST
        )
        + up_memory
    )
    query_down_grad, query_up_grad, value_down_grad, value_up_grad = lax.psum(
        (query_down_grad, query_up_grad, value_down_grad, value_up_grad), "tm"
    )
    return (logits_out, query_down_grad, query_up_grad, value_down_grad, value_up_grad)


LOG2E = 1.4426950408889634
NT = (((1,), (1,)), ((), ()))
PACK = 2 * BLK + RANK
STRIP = 16
PAIR = 2
MIB = 1024 * 1024
ROOM = 63.5


def dot_nt(a, b, precision=None):
    return lax.dot_general(a, b, NT, precision=precision, preferred_element_type=jnp.float32)


def dot_nn(a, b, precision=None):
    return jnp.dot(a, b, precision=precision, preferred_element_type=jnp.float32)


def piece_rows(place_ref, j, width):
    return pl.ds(pl.multiple_of(lax.bitwise_xor(place_ref[0], j) * width, width), width)


def start_copies(pairs, sems, first=0):
    copies = [pltpu.make_async_copy(src, dst, sems.at[first + n]) for n, (src, dst) in enumerate(pairs)]
    for copy in copies:
        copy.start()
    return copies


def wait_all(copies):
    for copy in copies:
        copy.wait()


def memory_pieces(place_ref, js, xs, hbm, scratch, sems):
    x_s, wk_s, wv_s, down_s = scratch
    width = x_s.shape[2]
    groups = []
    for n, j in enumerate(js):
        here = piece_rows(place_ref, j, width)
        pairs = [
            (xs[n], x_s.at[n]),
            (hbm[0].at[here, :], wk_s.at[n]),
            (hbm[1].at[here, :], wv_s.at[n]),
            (hbm[2].at[:, here], down_s.at[n]),
        ]
        groups.append(start_copies(pairs, sems, 4 * n))
    return groups


def memory_terms(n, scratch):
    x_s, wk_s, wv_s, down_s = scratch
    x = x_s[n]
    return dot_nn(x, jnp.concatenate([wk_s[n], wv_s[n]], 1)), dot_nt(x, down_s[n])


def memory_early_kernel(blocks, place_ref, named_ref, x0, x1, *refs):
    hbm, acc_ref, low_ref, wanted_ref, scratch, sems = refs[:3], refs[3], refs[4], refs[5], refs[6:10], refs[10]
    groups = memory_pieces(place_ref, (0, 1), (x0, x1), hbm, scratch, sems)
    for slot in range(TOP):
        block = named_ref[0, slot]
        wanted_ref[lax.div(block, blocks)] = lax.rem(block, blocks)
    for n in range(2):
        wait_all(groups[n])
        term, low_term = memory_terms(n, scratch)
        if n == 0:
            acc_ref[...] = term
            low_ref[...] = low_term
        else:
            acc_ref[...] += term
            low_ref[...] += low_term


def memory_middle_kernel(place_ref, x2, acc_hbm, low_hbm, *refs):
    hbm, acc_ref, low_ref, scratch, sems = refs[:3], refs[3], refs[4], refs[5:9], refs[9]
    acc_s, low_s, acc_sems = refs[10:13]
    groups = memory_pieces(place_ref, (2,), (x2,), hbm, scratch, sems)
    sums = start_copies([(acc_hbm, acc_s), (low_hbm, low_s)], acc_sems)
    wait_all(groups[0])
    term, low_term = memory_terms(0, scratch)
    wait_all(sums)
    acc_ref[...] = acc_s[...] + term
    low_ref[...] = low_s[...] + low_term


def memory_kernel(peers, place_ref, asked_ref, x3, acc_hbm, low_hbm, *refs):
    hbm, up_ref, out_ref = refs[:3], refs[3], refs[4]
    scratch, sems, acc_s, low_s, acc_sems, pair_ref = refs[5:9], refs[9], refs[10], refs[11], refs[12], refs[13]
    groups = memory_pieces(place_ref, (3,), (x3,), hbm, scratch, sems)
    sums = start_copies([(acc_hbm, acc_s), (low_hbm, low_s)], acc_sems)
    wait_all(groups[0])
    term, low_term = memory_terms(0, scratch)
    wait_all(sums)
    acc = acc_s[...] + term
    low = low_s[...] + low_term
    values = (acc[:, HD:] + dot_nn(low.astype(jnp.bfloat16), up_ref[...])).astype(jnp.bfloat16)
    keys = acc[:, :HD].astype(jnp.bfloat16)
    low_t = jnp.transpose(low).astype(jnp.bfloat16)
    for b in range(acc.shape[0] // BLK):
        at = slice(b * BLK, (b + 1) * BLK)
        pair_ref[b, 0:BLK, :] = keys[at]
        pair_ref[b, BLK : 2 * BLK, :] = values[at]
        pair_ref[b, 2 * BLK : PACK, :] = low_t[:, at]
    for r in range(peers):
        out_ref[r] = pair_ref[asked_ref[r]]


WQ_CUTS = 4


def project_pieces(place_ref, js, xs, hbm, scratch, sems):
    wq_hbm, wk_hbm, wv_hbm, qd_hbm, vd_hbm = hbm
    x_s, wq_s, wk_s, wv_s, qd_s, vd_s = scratch
    width = x_s.shape[2]
    part = width // WQ_CUTS
    groups = []
    for n, j in enumerate(js):
        here = piece_rows(place_ref, j, width)
        start = lax.bitwise_xor(place_ref[0], j) * width
        pairs = [(xs[n], x_s.at[n])]
        for m in range(WQ_CUTS):
            rows = pl.ds(pl.multiple_of(start + m * part, part), part)
            pairs.append((wq_hbm.at[rows, :], wq_s.at[n, pl.ds(m * part, part), :]))
        pairs += [
            (wk_hbm.at[here, :], wk_s.at[n]),
            (wv_hbm.at[here, :], wv_s.at[n]),
            (qd_hbm.at[:, here], qd_s.at[n]),
            (vd_hbm.at[:, here], vd_s.at[n]),
        ]
        groups.append(start_copies(pairs, sems, len(pairs) * n))
    return groups


def project_terms(n, scratch):
    x_s, wq_s, wk_s, wv_s, qd_s, vd_s = scratch
    x = x_s[n]
    return (
        dot_nn(x, wq_s[n]),
        dot_nn(x, jnp.concatenate([wk_s[n], wv_s[n]], 1)),
        dot_nt(x, jnp.concatenate([qd_s[n], vd_s[n]], 0)),
    )


def project_early_kernel(place_ref, x0, x1, *refs):
    hbm, (tag_ref, tags_t_ref), outs, (grad_ref, grad_t_ref) = refs[:5], refs[5:7], refs[8:11], refs[11:13]
    scratch, sems = refs[13:19], refs[19]
    groups = project_pieces(place_ref, (0, 1), (x0, x1), hbm, scratch, sems)
    first = (((0,), (0,)), ((), ()))
    tag = tag_ref[...].astype(jnp.float32)
    tags_t = tags_t_ref[...]
    f32 = jnp.float32
    grad_ref[...] = lax.dot_general(
        tags_t, tag, first, precision=HIGHEST, preferred_element_type=f32
    ).astype(jnp.bfloat16)
    grad_t_ref[...] = lax.dot_general(
        tag, tags_t, first, precision=HIGHEST, preferred_element_type=f32
    ).astype(jnp.bfloat16)
    for n in range(2):
        wait_all(groups[n])
        for ref, term in zip(outs, project_terms(n, scratch)):
            if n == 0:
                ref[...] = term
            else:
                ref[...] += term


def project_middle_kernel(place_ref, x3, *refs):
    hbm, early, outs, scratch, sems = refs[:5], refs[5:8], refs[8:11], refs[11:17], refs[17]
    sum_refs, sum_sems = refs[18:21], refs[21]
    groups = project_pieces(place_ref, (3,), (x3,), hbm, scratch, sems)
    loads = start_copies(list(zip(early, sum_refs)), sum_sems)
    wait_all(groups[0])
    terms = project_terms(0, scratch)
    wait_all(loads)
    for out, ref, term in zip(outs, sum_refs, terms):
        out[...] = ref[...] + term


def attention_kernel(peers, heads, place_ref, bound_ref, x2, *refs):
    hbm, early, got, grad_hbm, grad_t_hbm = refs[:5], refs[5:8], refs[8], refs[9], refs[10]
    qup_ref, vup_ref, tag_ref, cot_ref, mine_ref, mcot_ref = refs[11:17]
    scratch, sems, sum_refs = refs[17:23], refs[23], refs[24:27]
    (q_s, k_own, v_own, low_s, low_m_s, grad_ref, grad_t_ref, k_all, v_all, kt_all, vt_all, kt_own, vt_own, bias_s, s_s, dp_s,
     p_s, ds_s, att_s, dq_s, dv_s, up_ref, more_sems) = refs[27:]
    seen = peers * BLK
    pairs = []
    for b in range(peers):
        at = slice(b * BLK, (b + 1) * BLK)
        pairs.append((got.at[b, pl.ds(0, BLK), :], k_all.at[at, :]))
        pairs.append((got.at[b, pl.ds(BLK, BLK), :], v_all.at[at, :]))
        pairs.append((got.at[b, pl.ds(2 * BLK, RANK), :], low_m_s.at[b]))
    fetched = start_copies(pairs, more_sems)
    groups = project_pieces(place_ref, (2,), (x2,), hbm, scratch, sems)
    pairs = list(zip(early, sum_refs)) + [(grad_hbm, grad_ref), (grad_t_hbm, grad_t_ref)]
    copies = start_copies(pairs, more_sems, len(fetched))
    wait_all(fetched)
    for b in range(peers):
        at = slice(b * BLK, (b + 1) * BLK)
        kt_all[:, at] = jnp.transpose(k_all[at, :])
        vt_all[:, at] = jnp.transpose(v_all[at, :])
    wait_all(groups[0])
    terms = project_terms(0, scratch)
    wait_all(copies[:3])
    q_acc, kv_acc, low_acc = [ref[...] + term for ref, term in zip(sum_refs, terms)]
    low = low_acc.astype(jnp.bfloat16)
    q_s[...] = (q_acc + dot_nn(low[:, :RANK], qup_ref[...])).astype(jnp.bfloat16)
    k_own[...] = kv_acc[:, :HD].astype(jnp.bfloat16)
    v_own[...] = (kv_acc[:, HD:] + dot_nn(low[:, RANK:], vup_ref[...])).astype(jnp.bfloat16)
    low_s[...] = jnp.transpose(low_acc).astype(jnp.bfloat16)
    wait_all(copies[3:-1])
    dv_s[...] = jnp.zeros_like(dv_s)
    up_ref[...] = jnp.zeros_like(up_ref)
    scale = HD ** (-0.5)
    up_wide = vup_ref[...].astype(jnp.float32)
    query_width = heads * HD

    def pair_step(c, carry):
        base = c * (PAIR * BLK)
        rows = pl.ds(pl.multiple_of(base, PAIR * BLK), PAIR * BLK)
        own_rows = [pl.ds(pl.multiple_of(base + b * BLK, BLK), BLK) for b in range(PAIR)]
        row_ids = lax.broadcasted_iota(jnp.int32, (BLK, BLK), 0)
        col_ids = lax.broadcasted_iota(jnp.int32, (BLK, BLK), 1)
        for b in range(PAIR):
            kt_own[:, b * BLK : (b + 1) * BLK] = jnp.transpose(k_own[own_rows[b], :])
            vt_own[:, b * BLK : (b + 1) * BLK] = jnp.transpose(v_own[own_rows[b], :])
            edge = bound_ref[c * PAIR + b]
            visible = (col_ids <= row_ids) & ((col_ids >= edge) | (row_ids < edge))
            bias_s[b * BLK : (b + 1) * BLK, :] = jnp.where(visible, 0.0, -jnp.inf)

        def head_cols(h):
            return slice(h * HD, (h + 1) * HD)

        def times_keys(out_ref, left_ref, h, all_t, own_t):
            out_ref[:, :seen] = dot_nn(left_ref[rows, head_cols(h)], all_t[...])
            for b in range(PAIR):
                at = slice(b * BLK, (b + 1) * BLK)
                out_ref[at, seen:] = dot_nn(left_ref[own_rows[b], head_cols(h)], own_t[:, at])

        def over_keys(left_ref, first, all_ref, own_ref):
            whole = dot_nn(left_ref[first : first + PAIR * BLK, :seen], all_ref[...])
            mine = [
                dot_nn(left_ref[first + b * BLK : first + (b + 1) * BLK, seen:], own_ref[own_rows[b], :])
                for b in range(PAIR)
            ]
            return (whole + jnp.concatenate(mine, 0)).astype(jnp.bfloat16)

        def scores(h):
            times_keys(s_s.at[h % 2], q_s, h, kt_all, kt_own)

        def prob_grads(h):
            times_keys(dp_s.at[h % 2], grad_ref, h, vt_all, vt_own)

        def strips(h):
            for r in range(0, PAIR * BLK, STRIP):
                at = slice(r, r + STRIP)
                s = s_s[h % 2, at, :]
                s = jnp.concatenate([s[:, :seen], s[:, seen:] + bias_s[at, :]], 1) * (scale * LOG2E)
                w = jnp.exp2(s - jnp.max(s, axis=1, keepdims=True))
                probs = w * (1.0 / jnp.sum(w, axis=1, keepdims=True))
                probs_low = probs.astype(jnp.bfloat16)
                first = h * PAIR * BLK + r
                p_s[first : first + STRIP, :] = probs_low
                dp = dp_s[h % 2, at, :]
                dot = jnp.sum(probs_low.astype(jnp.float32) * dp, axis=1, keepdims=True)
                ds_s[h % 2, at, :] = (probs * ((dp - dot) * scale)).astype(jnp.bfloat16)

        def finish_head(h):
            att_s[:, head_cols(h)] = over_keys(p_s, h * PAIR * BLK, v_all, v_own)
            dq_s[:, head_cols(h)] = over_keys(ds_s.at[h % 2], 0, k_all, k_own)

        scores(0)
        prob_grads(0)
        for h in range(heads + 1):
            if h + 1 < heads:
                scores(h + 1)
                prob_grads(h + 1)
            if h < heads:
                strips(h)
            if h > 0:
                finish_head(h - 1)
        pl.when(c == 0)(copies[-1].wait)
        g_t = jnp.concatenate([grad_t_ref[h * HD : (h + 1) * HD, rows] for h in range(heads)], 1)
        dv_s[...] += dot_nn(g_t, p_s[:, :seen])
        dv_own = []
        for b in range(PAIR):
            g_b = jnp.concatenate([grad_t_ref[h * HD : (h + 1) * HD, own_rows[b]] for h in range(heads)], 1)
            starts = [(h * PAIR + b) * BLK for h in range(heads)]
            p_b = jnp.concatenate([p_s[n : n + BLK, seen:] for n in starts], 0)
            dv_own.append(dot_nn(g_b, p_b))
        dv_own = jnp.concatenate(dv_own, 1)
        dq = dq_s[...]
        cot_ref[0:RANK, rows] = dot_nt(qup_ref[...], dq)
        cot_ref[RANK : 2 * RANK, rows] = dot_nn(up_wide, dv_own, HIGHEST)
        cot_ref[2 * RANK :, rows] = dot_nt(tag_ref[...], att_s[...])
        up_ref[:, :query_width] += dot_nn(low_s[0:RANK, rows], dq)
        up_ref[:, query_width:] += dot_nt(low_s[RANK:, rows].astype(jnp.float32), dv_own, HIGHEST)
        return carry

    lax.fori_loop(0, q_s.shape[0] // (PAIR * BLK), pair_step, 0)
    dv = dv_s[...]
    mcot = dot_nn(up_wide, dv, HIGHEST)
    low_m = jnp.concatenate([low_m_s[b] for b in range(peers)], 1).astype(jnp.float32)
    up_ref[:, query_width:] += dot_nt(low_m, dv, HIGHEST)
    for b in range(peers):
        mcot_ref[b] = mcot[:, b * BLK : (b + 1) * BLK]
    at, wide = cot_ref.shape
    mine_ref[:at, :] = cot_ref[...]
    for n in range(0, up_ref.shape[1], wide):
        mine_ref[at : at + RANK, :] = up_ref[:, n : n + wide]
        at += RANK


def own_kernel(peers, asked_ref, back_ref, mine_hbm, out_ref, mine_ref, sum_s, sem):
    copy = pltpu.make_async_copy(mine_hbm, mine_ref, sem)
    copy.start()
    sum_s[...] = jnp.zeros_like(sum_s)
    for r in range(peers):
        block = asked_ref[r]
        sum_s[block] = sum_s[block] + back_ref[r]
    out_ref[...] = jnp.concatenate([sum_s[m] for m in range(sum_s.shape[0])], 1)
    copy.wait()


def first_down_kernel(mine_ref, c1, c2, c3, slab_ref, logit_ref, query_ref, value_ref):
    own, wide = c1.shape
    cot = (mine_ref[:own, :] + c1[...]) + (c2[...] + c3[...])
    logit_ref[...] = cot[2 * RANK :]
    both = dot_nn(cot[: 2 * RANK].astype(jnp.bfloat16), slab_ref[...])
    width = both.shape[1]
    query_ref[:, :width] = both[:RANK]
    for n, at in enumerate(range(own, mine_ref.shape[0], RANK)):
        query_ref[:, width + n * wide : width + (n + 1) * wide] = mine_ref[at : at + RANK, :]
    value_ref[...] = both[RANK:]


def second_down_kernel(c0, c1, c2, c3, memory_ref, value_ref, q0, q1, out_ref, query_ref):
    query_ref[...] = q0[...] + q1[...]
    cot = (c0[...] + c1[...]) + (c2[...] + c3[...])
    out_ref[...] = value_ref[...] + dot_nn(cot.astype(jnp.bfloat16), memory_ref[...])


def pack_kernel(q0, q1, v0, v1, both_ref, value_ref):
    split = q0.shape[1]
    value = (v0[...] + v1[...]).astype(jnp.bfloat16)
    both_ref[:, :split] = (q0[...] + q1[...]).astype(jnp.bfloat16)
    both_ref[:, split:] = value
    value_ref[...] = value


def finish_kernel(here_ref, there_ref, v1, v3, query_down_ref, query_up_ref, value_down_ref, value_up_ref):
    here = here_ref[...].astype(jnp.float32)
    there = there_ref[...].astype(jnp.float32)
    split = here.shape[1] - value_down_ref.shape[1]
    value_down_ref[...] = (here[:, split:] + v1[...].astype(jnp.float32)) + (
        there[:, split:] + v3[...].astype(jnp.float32)
    )
    query = here[:, :split] + there[:, :split]
    at = 0
    for out_ref in (query_down_ref, query_up_ref, value_up_ref):
        out_ref[...] = query[:, at : at + out_ref.shape[1]]
        at += out_ref.shape[1]


def swap(x, bit, axis="heads"):
    return lax.ppermute(x, axis, [(i, i ^ bit) for i in range(lax.axis_size(axis))])


def after(x, *deps):
    return pl.pallas_call(
        lambda *refs: None,
        out_shape=jax.ShapeDtypeStruct(x.shape, x.dtype),
        in_specs=[anywhere()] * (1 + len(deps)),
        out_specs=anywhere(),
        input_output_aliases={0: 0},
        name="in_order",
    )(x, *deps)


def anywhere():
    return pl.BlockSpec(memory_space=pl.ANY)


def smem():
    return pl.BlockSpec(memory_space=pltpu.SMEM)


def vmem():
    return pl.BlockSpec(memory_space=pltpu.VMEM)


def shaped(*shape, dtype=jnp.float32):
    return jax.ShapeDtypeStruct(shape, dtype)


def run(body, name, out_shape, in_specs, scratch=(), flops=0, moved=0, room=ROOM, out_specs=None):
    many = isinstance(out_shape, (tuple, list))
    return pl.pallas_call(
        body,
        out_shape=out_shape,
        in_specs=in_specs,
        out_specs=out_specs or (tuple(vmem() for _ in out_shape) if many else vmem()),
        scratch_shapes=list(scratch),
        compiler_params=pltpu.CompilerParams(vmem_limit_bytes=int(room * MIB)),
        cost_estimate=pl.CostEstimate(flops=flops, bytes_accessed=moved, transcendentals=0),
        name=name,
    )


def fast(
    slab_tokens,
    memory,
    query_weight,
    key_weight,
    value_weight,
    query_down,
    query_up,
    value_down,
    value_up,
    tag_weight,
    retrieval,
    boundary,
    grad_tags,
):
    tok_rows, width = slab_tokens.shape
    mem_rows = memory.shape[0]
    query_width = query_weight.shape[1]
    heads = query_width // HD
    spans = tok_rows // BLK
    blocks = mem_rows // BLK
    peers = lax.axis_size("tm")
    f32 = jnp.float32
    bf16 = jnp.bfloat16

    def memory_scratch(count):
        return [
            pltpu.VMEM((count, mem_rows, width), bf16),
            pltpu.VMEM((count, width, HD), bf16),
            pltpu.VMEM((count, width, HD), bf16),
            pltpu.VMEM((count, RANK, width), bf16),
            pltpu.SemaphoreType.DMA((4 * count,)),
        ]

    def project_scratch(count):
        return [
            pltpu.VMEM((count, tok_rows, width), bf16),
            pltpu.VMEM((count, width, query_width), bf16),
            pltpu.VMEM((count, width, HD), bf16),
            pltpu.VMEM((count, width, HD), bf16),
            pltpu.VMEM((count, RANK, width), bf16),
            pltpu.VMEM((count, RANK, width), bf16),
            pltpu.SemaphoreType.DMA((count * (WQ_CUTS + 5),)),
        ]

    memory_sums = [
        pltpu.VMEM((mem_rows, 2 * HD), f32),
        pltpu.VMEM((mem_rows, RANK), f32),
        pltpu.SemaphoreType.DMA((2,)),
    ]
    project_sums = [
        pltpu.VMEM((tok_rows, query_width), f32),
        pltpu.VMEM((tok_rows, 2 * HD), f32),
        pltpu.VMEM((tok_rows, 2 * RANK), f32),
    ]

    place = lax.axis_index("heads").astype(jnp.int32).reshape(1)
    tag_t = tag_weight.T
    tags = tag_t.shape[0]
    mem_far = swap(memory, 2)
    mem_near = swap(memory, 1)
    tok_near = swap(slab_tokens, 1)
    tok_far = swap(tok_near, 2)
    mem_acc, mem_low, wanted = run(
        lambda *refs: memory_early_kernel(blocks, *refs),
        "memory_near_half",
        (shaped(mem_rows, 2 * HD), shaped(mem_rows, RANK), shaped(peers, dtype=jnp.int32)),
        [smem()] * 2 + [anywhere()] * 5,
        memory_scratch(2),
        out_specs=(vmem(), vmem(), smem()),
    )(place, retrieval, memory, mem_near, key_weight, value_weight, value_down)
    asked = lax.all_to_all(wanted, "tm", split_axis=0, concat_axis=0, tiled=True)
    weights = (query_weight, key_weight, value_weight, query_down, value_down)
    mem_far = after(mem_far, asked)
    mem_cross = swap(mem_far, 1)
    mem_weights = (key_weight, value_weight, value_down)
    mem_acc, mem_low = run(
        memory_middle_kernel,
        "memory_far_quarter",
        (shaped(mem_rows, 2 * HD), shaped(mem_rows, RANK)),
        [smem()] + [anywhere()] * 6,
        memory_scratch(1) + memory_sums,
    )(place, mem_far, mem_acc, mem_low, *mem_weights)
    pairs = run(
        lambda *refs: memory_kernel(peers, *refs),
        "memory_pairs",
        shaped(peers, PACK, HD, dtype=bf16),
        [smem()] * 2 + [anywhere()] * 6 + [vmem()],
        memory_scratch(1) + memory_sums + [pltpu.VMEM((blocks, PACK, HD), bf16)],
    )(place, asked, mem_cross, mem_acc, mem_low, *mem_weights, value_up)
    got = lax.all_to_all(pairs, "tm", split_axis=0, concat_axis=0, tiled=True)
    *early, grad, grad_t = run(
        project_early_kernel,
        "project_near_half",
        (
            shaped(tok_rows, query_width),
            shaped(tok_rows, 2 * HD),
            shaped(tok_rows, 2 * RANK),
            shaped(tok_rows, query_width, dtype=bf16),
            shaped(query_width, tok_rows, dtype=bf16),
        ),
        [smem()] + [anywhere()] * 7 + [vmem()] * 2 + [anywhere()],
        project_scratch(2),
    )(place, slab_tokens, tok_near, *weights, tag_t, grad_tags.T, pairs)
    tok_far = after(tok_far, early[2])
    tok_cross = swap(tok_far, 1)
    early = run(
        project_middle_kernel,
        "project_far_quarter",
        (shaped(tok_rows, query_width), shaped(tok_rows, 2 * HD), shaped(tok_rows, 2 * RANK)),
        [smem()] + [anywhere()] * 9,
        project_scratch(1) + project_sums + [pltpu.SemaphoreType.DMA((3,))],
    )(place, tok_far, *weights, *early)

    seen = peers * BLK
    total = seen + BLK
    cot, mine, mcot = run(
        lambda *refs: attention_kernel(peers, heads, *refs),
        "span_attention",
        (
            shaped(2 * RANK + tags, tok_rows),
            shaped(2 * RANK + tags + RANK * (query_width + HD) // tok_rows, tok_rows),
            shaped(peers, RANK, BLK),
        ),
        [smem()] * 2 + [anywhere()] * 12 + [vmem()] * 3,
        project_scratch(1)
        + project_sums
        + [
            pltpu.VMEM((tok_rows, query_width), bf16),
            pltpu.VMEM((tok_rows, HD), bf16),
            pltpu.VMEM((tok_rows, HD), bf16),
            pltpu.VMEM((2 * RANK, tok_rows), bf16),
            pltpu.VMEM((peers, RANK, BLK), bf16),
            pltpu.VMEM((tok_rows, query_width), bf16),
            pltpu.VMEM((query_width, tok_rows), bf16),
            pltpu.VMEM((seen, HD), bf16),
            pltpu.VMEM((seen, HD), bf16),
            pltpu.VMEM((HD, seen), bf16),
            pltpu.VMEM((HD, seen), bf16),
            pltpu.VMEM((HD, PAIR * BLK), bf16),
            pltpu.VMEM((HD, PAIR * BLK), bf16),
            pltpu.VMEM((PAIR * BLK, BLK), f32),
            pltpu.VMEM((2, PAIR * BLK, total), f32),
            pltpu.VMEM((2, PAIR * BLK, total), f32),
            pltpu.VMEM((heads * PAIR * BLK, total), bf16),
            pltpu.VMEM((2, PAIR * BLK, total), bf16),
            pltpu.VMEM((PAIR * BLK, query_width), bf16),
            pltpu.VMEM((PAIR * BLK, query_width), bf16),
            pltpu.VMEM((HD, seen), f32),
            pltpu.VMEM((RANK, query_width + HD), f32),
            pltpu.SemaphoreType.DMA((3 * peers + 5,)),
        ],
        flops=20 * tok_rows * query_width * total,
        moved=4 * tok_rows * query_width,
        room=60,
    )(place, boundary, tok_cross, *weights, *early, got, grad, grad_t, query_up, value_up, tag_t)

    back = lax.all_to_all(mcot, "tm", split_axis=0, concat_axis=0, tiled=True)
    own, mine = run(
        lambda *refs: own_kernel(peers, *refs),
        "owned_cotangent",
        (shaped(RANK, mem_rows), shaped(*mine.shape)),
        [smem(), vmem(), anywhere()],
        [pltpu.VMEM((blocks, RANK, BLK), f32), pltpu.SemaphoreType.DMA],
        room=8,
    )(asked, back, mine)
    cots = [mine] + [swap(cot, d) for d in range(1, 4)]
    logits, query_sum, value_part = run(
        first_down_kernel,
        "first_down",
        (shaped(tags, tok_rows), shaped(RANK, width + query_width + HD), shaped(RANK, width)),
        [vmem()] * 5,
        flops=4 * RANK * tok_rows * width,
        moved=2 * tok_rows * width,
        room=8,
    )(*cots, slab_tokens)
    owns = [own] + [swap(own, d) for d in range(1, 4)]
    value_sum, query_sum = run(
        second_down_kernel,
        "second_down",
        (shaped(RANK, width), shaped(*query_sum.shape)),
        [vmem()] * 8,
        flops=2 * RANK * mem_rows * width,
        moved=2 * mem_rows * width,
        room=8,
    )(*owns, memory, value_part, query_sum, swap(query_sum, 1, "tm"))
    split = query_sum.shape[1]
    both, value_low = run(
        pack_kernel,
        "pack_sums",
        (shaped(RANK, split + width, dtype=bf16), shaped(RANK, width, dtype=bf16)),
        [vmem()] * 4,
        room=8,
    )(query_sum, swap(query_sum, 2, "tm"), value_sum, swap(value_sum, 1, "tm"))
    sums = [both, swap(both, 4, "tm"), swap(value_low, 2, "tm"), swap(value_low, 6, "tm")]
    query_down_grad, query_up_grad, value_down_grad, value_up_grad = run(
        finish_kernel,
        "finish_outputs",
        (shaped(RANK, width), shaped(RANK, query_width), shaped(RANK, width), shaped(RANK, HD)),
        [vmem()] * 4,
        room=8,
    )(*sums)
    return (logits.T, query_down_grad, query_up_grad, value_down_grad, value_up_grad)


def solution(mesh):
    in_specs = (
        P("tm", "heads"),
        P("tm", "heads"),
        P(None, "heads"),
        P(None, "heads"),
        P(None, "heads"),
        P(),
        P(None, "heads"),
        P(),
        P(None, "heads"),
        P("heads", None),
        P("tm", None),
        P("tm"),
        P("tm", None),
    )
    out_specs = (
        P("tm", None),
        P(None, "heads"),
        P(None, "heads"),
        P(None, "heads"),
        P(None, "heads"),
    )
    fits = mesh.shape["heads"] == 4 and mesh.shape["tm"] == 8 == TOP * CAP
    local = fast if fits else general
    return jax.shard_map(local, mesh=mesh, in_specs=in_specs, out_specs=out_specs, check_vma=False)
```
